32 devices in a mesh: seq: 8 (over z, core), row: 4 (over y, x).
Axes of the slice: x: 2, y: 2, z: 4, core: 2. Of those that a mesh axis runs over, the one named last changes fastest.
Arguments:
- inputs: bfloat16 [32, 1024, 512], P('row', 'seq'), may hold values from -6 to 6
- lengths: int32 [32], P('row'), may hold values from 128 to 1024, as said below
- norm_gain: float32 [512], replicated, may hold values from 0.5 to 1.5
- conv_weight: float32 [4, 512], replicated, may hold values from -3 to 3
- gate_weight: bfloat16 [512, 1024], replicated, may hold values from -0.25 to 0.25
- gate_bias: float32 [1024], replicated, may hold values from -9.5 to -2.5
- cand_weight: bfloat16 [512, 1024], replicated, may hold values from -0.25 to 0.25
- out_weight: bfloat16 [1024, 512], replicated, may hold values from -1.5 to 1.5
- mlp_gain: float32 [512], replicated, may hold values from 0.5 to 1.5
- up_weight: bfloat16 [512, 2048], replicated, may hold values from -0.25 to 0.25
- down_weight: bfloat16 [2048, 512], replicated, may hold values from -0.125 to 0.125
- cotangent: bfloat16 [32, 1024, 512], P('row', 'seq'), may hold values from -6 to 6
Outputs:
- output: bfloat16 [32, 1024, 512], P('row', 'seq')
- input_grad: bfloat16 [32, 1024, 512], P('row', 'seq')
- norm_gain_grad: float32 [512], replicated
- conv_weight_grad: float32 [4, 512], replicated
- gate_weight_grad: float32 [512, 1024], replicated
- gate_bias_grad: float32 [1024], replicated
- cand_weight_grad: float32 [512, 1024], replicated
- out_weight_grad: float32 [1024, 512], replicated
- mlp_gain_grad: float32 [512], replicated
- up_weight_grad: float32 [512, 2048], replicated
- down_weight_grad: float32 [2048, 512], replicated
The draws below stay inside these ranges and needn't reach their ends.
Inputs may be any that keep to these rules, and one draw needn't show every extreme that they name: `lengths`: within each aligned block of 8 rows at least one row has length 1024.
All inputs are finite; a program needn't handle non-finite values.
Results may differ from the reference program's by a relative error of at most 0.018.
Values may be sent and summed in bfloat16 or wider, within the bound.
No kernel may reach another device: no remote copies, remote signals or barrier semaphores. Data moves between devices by JAX's collectives and lax.ppermute only.
A program may use at most 128 MiB of HBM per device.

```python
import jax
import jax.numpy as jnp
from jax import lax

D = 512
H = 1024
F = 2048
KCONV = 4
ROW_DEV = 8
SEQ = 1024
ROWS = 32
LEN_MIN = 128


def draw_lengths(key, part):
    key = jax.random.fold_in(key, 7)
    key_level, key_extra, key_pick = jax.random.split(key, 3)
    level_exp = jax.random.randint(key_level, (ROWS,), 0, 4)
    spread = LEN_MIN * 2 ** level_exp
    extra_len = jax.random.randint(key_extra, (ROWS,), 0, spread)
    ragged = jnp.minimum(LEN_MIN + extra_len, SEQ)
    chosen = jax.random.randint(key_pick, (ROWS // ROW_DEV,), 0, ROW_DEV)
    longest = jnp.arange(ROWS) % ROW_DEV == jnp.repeat(chosen, ROW_DEV)
    return jnp.where(longest, SEQ, ragged).astype(jnp.int32)


def draw_gate_bias(key, part):
    key = jax.random.fold_in(key, 11)
    values = jax.random.uniform(key, (H,), jnp.float32, -8.0, -2.5)
    return values.astype(jnp.float32)


def block_scale(stream_key, dims, cuts, least, top_value):
    def one(dim, blocks):
        steps = jax.random.uniform(jax.random.fold_in(jax.random.fold_in(stream_key, 6), dim), (blocks,), jnp.float32, least / len(cuts), top_value / len(cuts))
        return jnp.repeat(jnp.exp(steps), dims[dim] // blocks).reshape((-1,) + (1,) * (len(dims) - dim - 1))

    factor_of = one(*cuts[0])
    for cut in cuts[1:]:
        factor_of = factor_of * one(*cut)
    return factor_of


def scatter_about(stream_key, shape, deviation, most, cuts=(), kind=jnp.bfloat16):
    values = deviation * jax.random.normal(stream_key, shape, jnp.float32)
    if cuts:
        values = values * block_scale(stream_key, shape, cuts, -0.22, 0.18)
    return jnp.clip(values, -most, most).astype(kind)


def setup_inputs(seed: int = 0) -> dict:
    seeds = jax.random.split(jax.random.key(seed), 13)
    return {
        "inputs": scatter_about(seeds[0], (ROWS, SEQ, D), 1.0, 6.0, ((0, 4), (1, 8))),
        "lengths": draw_lengths(jax.random.fold_in(seeds[12], 71), 0),
        "norm_gain": jnp.clip(1.0 + 0.1 * jax.random.normal(seeds[2], (D,), jnp.float32), 0.5, 1.5),
        "conv_weight": scatter_about(seeds[3], (KCONV, D), 0.5, 3.0, (), jnp.float32),
        "gate_weight": scatter_about(seeds[4], (D, H), D ** -0.5, 0.25),
        "gate_bias": draw_gate_bias(jax.random.fold_in(seeds[12], 71), 0),
        "cand_weight": scatter_about(seeds[6], (D, H), D ** -0.5, 0.25),
        "out_weight": scatter_about(seeds[7], (H, D), (H // 64) ** -0.5, 1.5),
        "mlp_gain": jnp.clip(1.0 + 0.1 * jax.random.normal(seeds[8], (D,), jnp.float32), 0.5, 1.5),
        "up_weight": scatter_about(seeds[9], (D, F), D ** -0.5, 0.25),
        "down_weight": scatter_about(seeds[10], (F, D), F ** -0.5, 0.125),
        "cotangent": scatter_about(seeds[11], (ROWS, SEQ, D), 1.0, 6.0, ((0, 4), (1, 8))),
    }


epsilon = 1e-06

@jax.custom_vjp
def low(v):
    return lax.optimization_barrier(v.astype(jnp.bfloat16)).astype(jnp.float32)

@jax.custom_vjp
def low_back(v):
    return v

def low_keep(v):
    return (low(v), None)

def low_pass(kept, grad):
    return (grad,)

def back_keep(v):
    return (v, None)

def back_low(kept, grad):
    return (low(grad),)
low.defvjp(low_keep, low_pass)
low_back.defvjp(back_keep, back_low)

def exact_dot(left, right):
    return jnp.dot(left, right, preferred_element_type=jnp.float32, precision=lax.Precision.HIGHEST)

def rms_norm(values, gain_vec):
    return values * lax.rsqrt(lax.optimization_barrier(jnp.mean(values * values, -1, keepdims=True)) + epsilon) * gain_vec

def combine(earlier, later):
    return (earlier[0] + later[0], later[1] + jnp.exp(later[0]) * earlier[1])

def minimal_block(group_in, live_mask, weights):
    norm_gain, conv_weight, gate_weight, gate_bias, cand_weight, out_weight, mlp_gain, up_weight, down_weight = weights
    count, length, width = group_in.shape
    normed = low(rms_norm(group_in, norm_gain))
    padded = jnp.pad(normed, ((0, 0), (KCONV - 1, 0), (0, 0)))
    conv = sum((conv_weight[offset] * padded[:, KCONV - 1 - offset:KCONV - 1 - offset + length] for offset in range(KCONV)))
    conv_rows = low(conv).reshape(count * length, width)
    gate_pre = low_back(exact_dot(conv_rows, gate_weight) + gate_bias).reshape(count, length, H)
    cand_pre = low_back(exact_dot(conv_rows, cand_weight)).reshape(count, length, H)
    log_decay = -jax.nn.softplus(gate_pre) * live_mask
    inputs_b = jax.nn.sigmoid(gate_pre) * cand_pre * live_mask
    cum_log, full_state = lax.associative_scan(combine, (log_decay, inputs_b), axis=1)
    mixed_low = low(full_state * live_mask).reshape(count * length, H)
    mixer_out = low_back(exact_dot(mixed_low, out_weight)).reshape(count, length, width)
    residual = group_in + mixer_out
    normed_two = low(rms_norm(residual, mlp_gain)).reshape(count * length, width)
    hidden_pre = low_back(exact_dot(normed_two, up_weight))
    active = low(jax.nn.gelu(hidden_pre))
    mlp_out = low_back(exact_dot(active, down_weight)).reshape(count, length, width)
    return residual + mlp_out

def reference(inputs, lengths, norm_gain, conv_weight, gate_weight, gate_bias, cand_weight, out_weight, mlp_gain, up_weight, down_weight, cotangent):
    weights = (norm_gain.astype(jnp.float32), conv_weight.astype(jnp.float32), gate_weight.astype(jnp.float32), gate_bias.astype(jnp.float32), cand_weight.astype(jnp.float32), out_weight.astype(jnp.float32), mlp_gain.astype(jnp.float32), up_weight.astype(jnp.float32), down_weight.astype(jnp.float32))
    positions = jnp.arange(SEQ, dtype=jnp.int32)
    live_masks = (positions[None, :] < lengths[:, None]).astype(jnp.float32)[:, :, None]
    groups = ROWS // 2
    grouped_in = inputs.reshape(groups, 2, SEQ, D)
    grouped_mask = live_masks.reshape(groups, 2, SEQ, 1)
    grouped_cot = cotangent.reshape(groups, 2, SEQ, D)

    def step(totals, batch_item):
        group_in, group_mask, group_cot = batch_item
        result, pullback = jax.vjp(lambda value_in, *params: minimal_block(value_in, group_mask, params), group_in.astype(jnp.float32), *weights)
        grads = pullback(group_cot.astype(jnp.float32))
        totals = tuple((total_one + grad_one for total_one, grad_one in zip(totals, grads[1:])))
        return (totals, (result.astype(jnp.bfloat16), grads[0].astype(jnp.bfloat16)))
    start_totals = tuple((jnp.zeros_like(param) for param in weights))
    totals, (outputs, input_grads) = lax.scan(step, start_totals, (grouped_in, grouped_mask, grouped_cot))
    return (outputs.reshape(ROWS, SEQ, D), input_grads.reshape(ROWS, SEQ, D), totals[0], totals[1], totals[2], totals[3], totals[4], totals[5], totals[6], totals[7], totals[8])
```

```python
import functools

import jax
import jax.numpy as jnp
import numpy as np
from jax import lax
from jax.experimental import pallas as pl
from jax.experimental.pallas import tpu as pltpu
from jax.sharding import PartitionSpec as P

epsilon = 1e-06
f32 = jnp.float32
bf16 = jnp.bfloat16
R = 8
PERM = 256


def nn(a, b):
    return lax.dot_general(a, b, (((1,), (0,)), ((), ())), preferred_element_type=f32)


def nt(a, b):
    return lax.dot_general(a, b, (((1,), (1,)), ((), ())), preferred_element_type=f32)


def tn(a, b):
    return lax.dot_general(a, b, (((0,), (0,)), ((), ())), preferred_element_type=f32)


def to_pm_matrix():
    out = lax.broadcasted_iota(jnp.int32, (PERM, PERM), 0)
    src = lax.broadcasted_iota(jnp.int32, (PERM, PERM), 1)
    span = PERM // R
    return ((out // R == src % span) & (out % R == src // span)).astype(f32).astype(bf16)


def to_rm_matrix():
    out = lax.broadcasted_iota(jnp.int32, (PERM, PERM), 0)
    src = lax.broadcasted_iota(jnp.int32, (PERM, PERM), 1)
    span = PERM // R
    return ((src // R == out % span) & (src % R == out // span)).astype(f32).astype(bf16)


def position_major(perm, block):
    span = PERM // R
    parts = []
    for s in range(block.shape[1] // span):
        part = block[:, s * span : (s + 1) * span, :].reshape(PERM, block.shape[2])
        parts.append(nn(perm, part))
    return parts[0] if len(parts) == 1 else jnp.concatenate(parts, 0)


def row_major(perm, tokens):
    span = PERM // R
    parts = []
    for s in range(tokens.shape[0] // PERM):
        part = nn(perm, tokens[s * PERM : (s + 1) * PERM]).astype(bf16)
        parts.append(part.reshape(R, span, tokens.shape[1]))
    return parts[0] if len(parts) == 1 else jnp.concatenate(parts, 1)


def eight(t):
    return pl.ds(pl.multiple_of(t * R, R), R)


def sixteen(t):
    return pl.ds(pl.multiple_of(t * 2 * R, 2 * R), 2 * R)


def front_kernel(scal, lens, x, before, gain, convw, wg, bias, wc, c_out, zl_out, kh_out, ends, ext, state):
    step = pl.program_id(0)
    tb = x.shape[1]
    m = tb * R
    halo = before.shape[0]
    taps = convw.shape[0]

    @pl.when(step == 0)
    def _():
        ext[0:halo, :] = before[...]
        state[0:R, :] = jnp.ones((R, state.shape[1]), f32)
        state[R:, :] = jnp.zeros((R, state.shape[1]), f32)

    xp = position_major(to_pm_matrix(), x[...])
    inv = lax.rsqrt(jnp.mean(xp * xp, -1, keepdims=True) + epsilon)
    ext[halo:, :] = (xp * inv * gain[...]).astype(bf16).astype(f32)
    conv = convw[0:1, :] * ext[halo:, :]
    for k in range(1, taps):
        lo = halo - k * R
        conv = conv + convw[k : k + 1, :] * ext[lo : lo + m, :]
    ext[0:halo, :] = ext[m : m + halo, :]
    cb = conv.astype(bf16)
    c_out[...] = cb
    kz = nn(cb, wg[...]) + bias[...]
    zs = 1.0 / (1.0 + jnp.exp(-kz))
    width = zs.shape[1]
    zs = zs.reshape(tb, R, width)
    pos = scal[0] + step * tb + lax.broadcasted_iota(jnp.int32, (tb, R, width), 0)
    zl_out[...] = jnp.where(pos < lens[...][None], zs, 0.0).reshape(m, width)
    kh_out[...] = nn(cb, wc[...])

    def body(t, carry):
        prod, h = carry
        zl = zl_out[eight(t), :]
        a = 1.0 - zl
        return prod * a, h * a + zl * kh_out[eight(t), :]

    prod, h = lax.fori_loop(0, tb, body, (state[0:R, :], state[R:, :]), unroll=4)
    state[0:R, :] = prod
    state[R:, :] = h
    ends[0:R, :] = prod
    ends[R:, :] = h


def gelu_parts(p):
    k0 = 0.7978845608028654
    p2 = p * p
    th = jnp.tanh(p * (k0 + (k0 * 0.044715) * p2))
    ht = 0.5 + 0.5 * th
    return p * ht, ht + (2.0 * p) * (ht - ht * ht) * (k0 + (3.0 * k0 * 0.044715) * p2)


def ffn_kernel(
    scal, lens, x, g, zl, kh, gathered, wo, mgain, wu, wd,
    out, r1_out, gl_out, y_out, hp_out, dp_out, dgrad, ugrad,
    state, act, dps, n2s, gls,
    *, blocks, fchunk,
):
    step = pl.program_id(0)
    tb = x.shape[1]
    m = tb * R
    feed = wu.shape[1]

    @pl.when(step == 0)
    def _():
        h = jnp.zeros((R, zl.shape[1]), f32)
        for j in range(gathered.shape[0]):
            h = jnp.where(j < scal[1], gathered[j, 0:R, :] * h + gathered[j, R:, :], h)
        state[...] = h

    @pl.when(step < blocks)
    def _():
        first = scal[0] + step * tb
        limit = lens[...]

        def body(u, h):
            t = u * 2
            za = zl[eight(t), :]
            ha = h - za * h + za * kh[eight(t), :]
            zb = zl[eight(t + 1), :]
            hb = ha - zb * ha + zb * kh[eight(t + 1), :]
            hp_out[sixteen(u), :] = jnp.concatenate([h, ha], 0).astype(bf16)
            ya = jnp.where(first + t < limit, ha, 0.0)
            yb = jnp.where(first + t + 1 < limit, hb, 0.0)
            y_out[sixteen(u), :] = jnp.concatenate([ya, yb], 0).astype(bf16)
            return hb

        state[...] = lax.fori_loop(0, tb // 2, body, state[...], unroll=2)
        to_pm = to_pm_matrix()
        gl = position_major(to_pm, g[...]).astype(bf16)
        gl_out[...] = gl
        r1 = position_major(to_pm, x[...]) + nn(y_out[...], wo[...])
        r1_out[...] = r1
        inv = lax.rsqrt(jnp.mean(r1 * r1, -1, keepdims=True) + epsilon)
        n2 = (r1 * inv * mgain[...]).astype(bf16)
        rows = pl.ds(pl.multiple_of(step * m, m), m)
        n2s[rows, :] = n2
        gls[rows, :] = gl
        for f in range(0, feed, fchunk):
            cols = slice(f, f + fchunk)
            a, slope = gelu_parts(nn(n2, wu[:, cols]))
            ab = a.astype(bf16)
            act[rows, cols] = ab
            dpb = (nt(gl, wd[cols, :]) * slope).astype(bf16)
            dps[rows, cols] = dpb
            dp_out[:, cols] = dpb
        total = r1 + nn(act[rows, :], wd[...])
        out[...] = row_major(to_rm_matrix(), total.astype(bf16))

    @pl.when(step >= blocks)
    def _():
        j = step - blocks
        wide = dgrad.shape[0]
        cols = pl.ds(pl.multiple_of(j * wide, wide), wide)
        dgrad[...] = tn(act[:, cols], gls[...]).astype(bf16)
        ugrad[...] = tn(n2s[...], dps[:, cols]).astype(bf16)


def mid_kernel(
    scal, lens, dp, r1, gl, zl, y, mgain, wu, wo,
    dh_out, dr1_out, ograd, back, mg_out,
    state, ys, dms,
    *, blocks,
):
    step = pl.program_id(0)
    m = r1.shape[0]
    tb = m // R
    block = blocks - 1 - step

    @pl.when(step == 0)
    def _():
        state[...] = jnp.zeros(state.shape, f32)
        mg_out[...] = jnp.zeros(mg_out.shape, f32)

    @pl.when(step < blocks)
    def _():
        dn2 = nt(dp[...], wu[...])
        r1v = r1[...]
        width = r1v.shape[1]
        inv = lax.rsqrt(jnp.mean(r1v * r1v, -1, keepdims=True) + epsilon)
        mg_out[...] += jnp.sum((dn2 * r1v * inv).reshape(tb, R, width), 0)
        s = mgain[...] * dn2
        mean = jnp.mean(s * r1v, -1, keepdims=True)
        dr1 = gl[...].astype(f32) + inv * (s - r1v * (inv * inv * mean))
        dr1_out[...] = dr1
        dm = dr1.astype(bf16)
        rows = pl.ds(pl.multiple_of(block * m, m), m)
        dms[rows, :] = dm
        ys[rows, :] = y[...]
        dh = nt(dm, wo[...])
        hidden = dh.shape[1]
        dh = dh.reshape(tb, R, hidden)
        pos = scal[0] + block * tb + lax.broadcasted_iota(jnp.int32, (tb, R, hidden), 0)
        dh_out[...] = jnp.where(pos < lens[...][None], dh, 0.0).reshape(m, hidden)

        def body(u, mm):
            t = tb - 1 - u
            lam = dh_out[eight(t), :] + mm
            return lam - zl[eight(t), :] * lam

        last = lax.fori_loop(0, tb, body, state[...], unroll=4)
        state[...] = last
        back[...] = last

    @pl.when(step >= blocks)
    def _():
        j = step - blocks
        wide = ograd.shape[0]
        cols = pl.ds(pl.multiple_of(j * wide, wide), wide)
        ograd[...] = tn(ys[:, cols], dms[...]).astype(bf16)


def gate_kernel(
    scal, dh, zl, kh, hp, c, fgath, bgath, wg, wc,
    ggrad, cgrad, dc_out, bias_out,
    state, cs, dkz, dkh,
    *, blocks,
):
    step = pl.program_id(0)
    m = dh.shape[0]
    tb = m // R
    block = blocks - 1 - step

    @pl.when(step == 0)
    def _():
        mm = jnp.zeros(state.shape, f32)
        for j in range(fgath.shape[0] - 1, -1, -1):
            mm = jnp.where(j > scal[1], bgath[j] + fgath[j, 0:R, :] * mm, mm)
        state[...] = mm
        bias_out[...] = jnp.zeros(bias_out.shape, f32)

    @pl.when(step < blocks)
    def _():
        base = block * tb

        def body(u, carry):
            mm, bias = carry
            w = tb // 2 - 1 - u
            t = w * 2
            hpv = hp[sixteen(w), :].astype(f32)
            zb = zl[eight(t + 1), :]
            lam = dh[eight(t + 1), :] + mm
            sb = lam * zb
            mm = lam - sb
            kb = (sb - sb * zb) * (kh[eight(t + 1), :] - hpv[R:, :])
            za = zl[eight(t), :]
            lam = dh[eight(t), :] + mm
            sa = lam * za
            mm = lam - sa
            ka = (sa - sa * za) * (kh[eight(t), :] - hpv[:R, :])
            kk = jnp.concatenate([ka, kb], 0).astype(bf16)
            ss = jnp.concatenate([sa, sb], 0).astype(bf16)
            dkz[sixteen(base // 2 + w), :] = kk
            dkh[sixteen(base // 2 + w), :] = ss
            kf = kk.astype(f32)
            return mm, bias + kf[:R, :] + kf[R:, :]

        mm, bias = lax.fori_loop(0, tb // 2, body, (state[...], bias_out[...]), unroll=2)
        state[...] = mm
        bias_out[...] = bias
        rows = pl.ds(pl.multiple_of(block * m, m), m)
        cs[rows, :] = c[...]
        dc_out[...] = nt(dkz[rows, :], wg[...]) + nt(dkh[rows, :], wc[...])

    @pl.when(step >= blocks)
    def _():
        j = step - blocks
        wide = ggrad.shape[1]
        cols = pl.ds(pl.multiple_of(j * wide, wide), wide)
        ggrad[...] = tn(cs[...], dkz[:, cols]).astype(bf16)
        cgrad[...] = tn(cs[...], dkh[:, cols]).astype(bf16)


def tail_kernel(x, dr1, dc, before, after, gain, convw, grad, sums, uext, dext, *, blocks):
    step = pl.program_id(0)
    tb = x.shape[1]
    m = tb * R
    halo = before.shape[0]
    taps = convw.shape[0]
    width = gain.shape[1]

    @pl.when(step == 0)
    def _():
        uext[0:halo, :] = before[...]
        dext[0 : dc.shape[0], :] = dc[...]
        dext[dc.shape[0] :, :] = after[...]
        sums[...] = jnp.zeros(sums.shape, f32)

    xp = position_major(to_pm_matrix(), x[...])
    inv = lax.rsqrt(jnp.mean(xp * xp, -1, keepdims=True) + epsilon)
    xn = xp * inv
    uext[halo:, :] = (xn * gain[...]).astype(bf16).astype(f32)
    start = step * m
    here = dext[pl.ds(pl.multiple_of(start, R), m), :]
    du = convw[0:1, :] * here
    for k in range(taps):
        lo = halo - k * R
        part = (here * uext[lo : lo + m, :]).reshape(tb, R, width)
        sums[(k + 1) * R : (k + 2) * R, :] += jnp.sum(part, 0)
        if k:
            du = du + convw[k : k + 1, :] * dext[pl.ds(pl.multiple_of(start + k * R, R), m), :]
    uext[0:halo, :] = uext[m : m + halo, :]
    sums[0:R, :] += jnp.sum((du * xn).reshape(tb, R, width), 0)
    s1 = gain[...] * du
    mean = jnp.mean(s1 * xn, -1, keepdims=True)
    gin = dr1[...] + inv * (s1 - xn * mean)
    grad[...] = row_major(to_rm_matrix(), gin.astype(bf16))


def params(mib):
    return pltpu.CompilerParams(
        dimension_semantics=("arbitrary",), vmem_limit_bytes=mib * 1024 * 1024
    )


def shape(dims, kind=f32):
    return jax.ShapeDtypeStruct(dims, kind)


def whole(array):
    zeros = (0,) * array.ndim
    return pl.BlockSpec(array.shape, lambda *a: zeros, pipeline_mode=pl.Buffered(1))


def passed_along(value, axis, steps):
    count = lax.axis_size(axis)
    leading, last = (max(0, -steps), min(count, count - steps))
    return lax.ppermute(value, axis, [(source, source + steps) for source in range(leading, last)])


def per_device(
    inputs,
    lengths,
    norm_gain,
    conv_weight,
    gate_weight,
    gate_bias,
    cand_weight,
    out_weight,
    mlp_gain,
    up_weight,
    down_weight,
    cotangent,
):
    rows, span, width = inputs.shape
    hidden = gate_weight.shape[1]
    feed = up_weight.shape[1]
    taps = conv_weight.shape[0]
    margin = taps - 1
    tokens = rows * span
    tb = 32
    blocks = span // tb
    m = tb * R
    seq = lax.axis_index("seq")
    count = lax.axis_size("seq")
    scal = jnp.stack([seq * span, seq]).astype(jnp.int32)
    lens = jnp.broadcast_to(lengths[:, None], (rows, hidden))
    gain1 = norm_gain.reshape(1, width)
    gain2 = mlp_gain.reshape(1, width)
    bias = gate_bias.reshape(1, hidden)

    edge = inputs[:, span - margin :, :].astype(f32)
    edge_inv = lax.rsqrt(jnp.mean(edge * edge, -1, keepdims=True) + epsilon)
    edge_u = (edge * edge_inv * norm_gain).astype(bf16)
    before = passed_along(edge_u, "seq", 1)
    before = before.swapaxes(0, 1).reshape(margin * rows, width).astype(f32)

    clamp = lambda i: jnp.minimum(i, blocks - 1)
    rm_block = pl.BlockSpec((rows, tb, width), lambda i, s: (0, clamp(i), 0))

    def tok(w):
        return pl.BlockSpec((m, w), lambda i, s: (clamp(i), 0))

    def rtok(w):
        return pl.BlockSpec((m, w), lambda i, s: (blocks - 1 - clamp(i), 0))

    def fixed(dims):
        zeros = (0,) * len(dims)
        return pl.BlockSpec(dims, lambda i, s: zeros)

    c, zl, kh, ends = pl.pallas_call(
        front_kernel,
        grid_spec=pltpu.PrefetchScalarGridSpec(
            num_scalar_prefetch=1,
            grid=(blocks,),
            in_specs=[
                whole(lens), rm_block, whole(before), whole(gain1), whole(conv_weight),
                whole(gate_weight), whole(bias), whole(cand_weight),
            ],
            out_specs=[tok(width), tok(hidden), tok(hidden), fixed((2 * R, hidden))],
            scratch_shapes=[
                pltpu.VMEM((margin * R + m, width), f32),
                pltpu.VMEM((2 * R, hidden), f32),
            ],
        ),
        out_shape=[
            shape((tokens, width), bf16), shape((tokens, hidden)), shape((tokens, hidden)),
            shape((2 * R, hidden)),
        ],
        compiler_params=params(40),
        name="front",
    )(scal, lens, inputs, before, gain1, conv_weight, gate_weight, bias, cand_weight)

    fgath = lax.all_gather(ends, "seq", axis=0)

    gsteps = 4
    gtile = feed // gsteps
    late = lambda i: jnp.maximum(i - blocks, 0)
    output, r1, gl, y, hp, dp, dgrad, ugrad = pl.pallas_call(
        functools.partial(ffn_kernel, blocks=blocks, fchunk=512),
        grid_spec=pltpu.PrefetchScalarGridSpec(
            num_scalar_prefetch=1,
            grid=(blocks + gsteps,),
            in_specs=[
                whole(lens), rm_block, rm_block, tok(hidden), tok(hidden), whole(fgath),
                whole(out_weight), whole(gain2), whole(up_weight), whole(down_weight),
            ],
            out_specs=[
                rm_block, tok(width), tok(width), tok(hidden), tok(hidden), tok(feed),
                pl.BlockSpec((gtile, width), lambda i, s: (late(i), 0)),
                pl.BlockSpec((width, gtile), lambda i, s: (0, late(i))),
            ],
            scratch_shapes=[
                pltpu.VMEM((R, hidden), f32),
                pltpu.VMEM((tokens, feed), bf16),
                pltpu.VMEM((tokens, feed), bf16),
                pltpu.VMEM((tokens, width), bf16),
                pltpu.VMEM((tokens, width), bf16),
            ],
        ),
        out_shape=[
            shape((rows, span, width), bf16), shape((tokens, width)), shape((tokens, width), bf16),
            shape((tokens, hidden), bf16), shape((tokens, hidden), bf16),
            shape((tokens, feed), bf16),
            shape((feed, width), bf16), shape((width, feed), bf16),
        ],
        compiler_params=params(52),
        name="ffn",
    )(scal, lens, inputs, cotangent, zl, kh, fgath, out_weight, gain2, up_weight, down_weight)

    osteps = 2
    otile = hidden // osteps
    dh, dr1, ograd, back, mg = pl.pallas_call(
        functools.partial(mid_kernel, blocks=blocks),
        grid_spec=pltpu.PrefetchScalarGridSpec(
            num_scalar_prefetch=1,
            grid=(blocks + osteps,),
            in_specs=[
                whole(lens), rtok(feed), rtok(width), rtok(width), rtok(hidden), rtok(hidden),
                whole(gain2), whole(up_weight), whole(out_weight),
            ],
            out_specs=[
                rtok(hidden), rtok(width),
                pl.BlockSpec((otile, width), lambda i, s: (late(i), 0)),
                fixed((R, hidden)), fixed((R, width)),
            ],
            scratch_shapes=[
                pltpu.VMEM((R, hidden), f32),
                pltpu.VMEM((tokens, hidden), bf16),
                pltpu.VMEM((tokens, width), bf16),
            ],
        ),
        out_shape=[
            shape((tokens, hidden)), shape((tokens, width)), shape((hidden, width), bf16),
            shape((R, hidden)), shape((R, width)),
        ],
        compiler_params=params(40),
        name="mid",
    )(scal, lens, dp, r1, gl, zl, y, gain2, up_weight, out_weight)

    bgath = lax.all_gather(back, "seq", axis=0)

    ksteps = 2
    ktile = hidden // ksteps
    ggrad, cgrad, dc, bias_part = pl.pallas_call(
        functools.partial(gate_kernel, blocks=blocks),
        grid_spec=pltpu.PrefetchScalarGridSpec(
            num_scalar_prefetch=1,
            grid=(blocks + ksteps,),
            in_specs=[
                rtok(hidden), rtok(hidden), rtok(hidden), rtok(hidden), rtok(width),
                whole(fgath), whole(bgath), whole(gate_weight), whole(cand_weight),
            ],
            out_specs=[
                pl.BlockSpec((width, ktile), lambda i, s: (0, late(i))),
                pl.BlockSpec((width, ktile), lambda i, s: (0, late(i))),
                rtok(width), fixed((R, hidden)),
            ],
            scratch_shapes=[
                pltpu.VMEM((R, hidden), f32),
                pltpu.VMEM((tokens, width), bf16),
                pltpu.VMEM((tokens, hidden), bf16),
                pltpu.VMEM((tokens, hidden), bf16),
            ],
        ),
        out_shape=[
            shape((width, hidden), bf16), shape((width, hidden), bf16), shape((tokens, width)),
            shape((R, hidden)),
        ],
        compiler_params=params(40),
        name="gates",
    )(scal, dh, zl, kh, hp, c, fgath, bgath, gate_weight, cand_weight)

    after = passed_along(dc[: margin * R].astype(bf16), "seq", -1).astype(f32)
    rm1 = pl.BlockSpec((rows, tb, width), lambda i: (0, i, 0))
    input_grad, sums = pl.pallas_call(
        functools.partial(tail_kernel, blocks=blocks),
        grid=(blocks,),
        in_specs=[
            rm1, pl.BlockSpec((m, width), lambda i: (i, 0)), whole(dc), whole(before),
            whole(after), whole(gain1), whole(conv_weight),
        ],
        out_specs=[rm1, pl.BlockSpec(((taps + 1) * R, width), lambda i: (0, 0))],
        scratch_shapes=[
            pltpu.VMEM((margin * R + m, width), f32),
            pltpu.VMEM((margin * R + tokens, width), f32),
        ],
        out_shape=[shape((rows, span, width), bf16), shape(((taps + 1) * R, width))],
        compiler_params=params(40),
        name="tail",
    )(inputs, dr1, dc, before, after, gain1, conv_weight)

    both = ("seq", "row")
    dgrad, ugrad = lax.psum((dgrad, ugrad), both)
    ograd, ggrad, cgrad = lax.psum((ograd, ggrad, cgrad), both)
    small = jnp.concatenate(
        [
            sums.reshape(taps + 1, R, width).sum(1).reshape(-1),
            mg.sum(0),
            bias_part.sum(0),
        ]
    )
    small = lax.psum(small, both)
    lo = (taps + 1) * width
    return (
        output,
        input_grad,
        small[:width],
        small[width:lo].reshape(taps, width),
        ggrad.astype(f32),
        small[lo + width :],
        cgrad.astype(f32),
        ograd.astype(f32),
        small[lo : lo + width],
        ugrad.astype(f32),
        dgrad.astype(f32),
    )


def solution(mesh):
    sharded = P("row", "seq", None)
    in_specs = (sharded, P("row")) + (P(),) * 9 + (sharded,)
    out_specs = (sharded, sharded) + (P(),) * 9
    return jax.shard_map(
        per_device, mesh=mesh, in_specs=in_specs, out_specs=out_specs, check_vma=False
    )
```

```python
import functools

import jax
import jax.numpy as jnp
import numpy as np
from jax import lax
from jax.experimental import pallas as pl
from jax.experimental.pallas import tpu as pltpu
from jax.sharding import PartitionSpec as P

epsilon = 1e-06
f32 = jnp.float32
bf16 = jnp.bfloat16
R = 8
PERM = 256
SLOTS = 32
PIECE1 = 128
PIECE2 = 96


def nn(a, b):
    return lax.dot_general(a, b, (((1,), (0,)), ((), ())), preferred_element_type=f32)


def nt(a, b):
    return lax.dot_general(a, b, (((1,), (1,)), ((), ())), preferred_element_type=f32)


def tn(a, b):
    return lax.dot_general(a, b, (((0,), (0,)), ((), ())), preferred_element_type=f32)


def to_pm_matrix():
    out = lax.broadcasted_iota(jnp.int32, (PERM, PERM), 0)
    src = lax.broadcasted_iota(jnp.int32, (PERM, PERM), 1)
    span = PERM // R
    return ((out // R == src % span) & (out % R == src // span)).astype(f32).astype(bf16)


def to_rm_matrix():
    out = lax.broadcasted_iota(jnp.int32, (PERM, PERM), 0)
    src = lax.broadcasted_iota(jnp.int32, (PERM, PERM), 1)
    span = PERM // R
    return ((src // R == out % span) & (src % R == out // span)).astype(f32).astype(bf16)


def position_major(perm, block):
    span = PERM // R
    parts = []
    for s in range(block.shape[1] // span):
        part = block[:, s * span : (s + 1) * span, :].reshape(PERM, block.shape[2])
        parts.append(nn(perm, part))
    return parts[0] if len(parts) == 1 else jnp.concatenate(parts, 0)


def row_major(perm, tokens):
    span = PERM // R
    parts = []
    for s in range(tokens.shape[0] // PERM):
        part = nn(perm, tokens[s * PERM : (s + 1) * PERM]).astype(bf16)
        parts.append(part.reshape(R, span, tokens.shape[1]))
    return parts[0] if len(parts) == 1 else jnp.concatenate(parts, 1)


def eight(t):
    return pl.ds(pl.multiple_of(t * R, R), R)


def sixteen(t):
    return pl.ds(pl.multiple_of(t * 2 * R, 2 * R), 2 * R)


def front_kernel(scal, lens, x, before, gain, convw, wg, bias, wc, c_out, zl_out, kh_out, ends, ext, state):
    step = pl.program_id(0)
    tb = x.shape[1]
    m = tb * R
    halo = before.shape[0]
    taps = convw.shape[0]

    @pl.when(step == 0)
    def _():
        ext[0:halo, :] = before[...]
        state[0:R, :] = jnp.ones((R, state.shape[1]), f32)
        state[R:, :] = jnp.zeros((R, state.shape[1]), f32)

    xp = position_major(to_pm_matrix(), x[...])
    inv = lax.rsqrt(jnp.mean(xp * xp, -1, keepdims=True) + epsilon)
    ext[halo:, :] = (xp * inv * gain[...]).astype(bf16).astype(f32)
    conv = convw[0:1, :] * ext[halo:, :]
    for k in range(1, taps):
        lo = halo - k * R
        conv = conv + convw[k : k + 1, :] * ext[lo : lo + m, :]
    ext[0:halo, :] = ext[m : m + halo, :]
    cb = conv.astype(bf16)
    c_out[...] = cb
    kz = nn(cb, wg[...]) + bias[...]
    zs = 1.0 / (1.0 + jnp.exp(-kz))
    width = zs.shape[1]
    zs = zs.reshape(tb, R, width)
    pos = scal[0] + step * tb + lax.broadcasted_iota(jnp.int32, (tb, R, width), 0)
    zl_out[...] = jnp.where(pos < lens[...][None], zs, 0.0).reshape(m, width)
    kh_out[...] = nn(cb, wc[...])

    def body(t, carry):
        prod, h = carry
        zl = zl_out[eight(t), :]
        a = 1.0 - zl
        return prod * a, h * a + zl * kh_out[eight(t), :]

    prod, h = lax.fori_loop(0, tb, body, (state[0:R, :], state[R:, :]), unroll=4)
    state[0:R, :] = prod
    state[R:, :] = h
    ends[0:R, :] = prod
    ends[R:, :] = h


def gelu_parts(p):
    k0 = 0.7978845608028654
    p2 = p * p
    th = jnp.tanh(p * (k0 + (k0 * 0.044715) * p2))
    ht = 0.5 + 0.5 * th
    return p * ht, ht + (2.0 * p) * (ht - ht * ht) * (k0 + (3.0 * k0 * 0.044715) * p2)


def ffn_kernel(scal, lens, x, g, zl, kh, other, *refs, blocks, fchunk, hops):
    msgs = refs[:hops]
    wo, mgain, wu, wd = refs[hops : hops + 4]
    out, r1_out, gl_out, y_out, hp_out, dp_out, send, keep = refs[hops + 4 : hops + 12]
    state, act, dps, n2s, gls = refs[hops + 12 :]
    step = pl.program_id(0)
    tb = x.shape[1]
    m = tb * R
    feed = wu.shape[1]

    @pl.when(step == 0)
    def _():
        h = jnp.zeros((R, zl.shape[1]), f32)
        for msg in reversed(msgs):
            both = msg[...].astype(f32)
            h = jnp.exp(both[0:R, :]) * h + both[R:, :]
        state[...] = jnp.where(scal[1] == 1, other[0:R, :] * h + other[R:, :], h)

    @pl.when(step < blocks)
    def _():
        first = scal[0] + step * tb
        limit = lens[...]

        def body(u, h):
            t = u * 2
            za = zl[eight(t), :]
            ha = h - za * h + za * kh[eight(t), :]
            zb = zl[eight(t + 1), :]
            hb = ha - zb * ha + zb * kh[eight(t + 1), :]
            hp_out[sixteen(u), :] = jnp.concatenate([h, ha], 0).astype(bf16)
            ya = jnp.where(first + t < limit, ha, 0.0)
            yb = jnp.where(first + t + 1 < limit, hb, 0.0)
            y_out[sixteen(u), :] = jnp.concatenate([ya, yb], 0).astype(bf16)
            return hb

        state[...] = lax.fori_loop(0, tb // 2, body, state[...], unroll=2)
        to_pm = to_pm_matrix()
        gl = position_major(to_pm, g[...]).astype(bf16)
        gl_out[...] = gl
        r1 = position_major(to_pm, x[...]) + nn(y_out[...], wo[...])
        r1_out[...] = r1
        inv = lax.rsqrt(jnp.mean(r1 * r1, -1, keepdims=True) + epsilon)
        n2 = (r1 * inv * mgain[...]).astype(bf16)
        rows = pl.ds(pl.multiple_of(step * m, m), m)
        n2s[rows, :] = n2
        gls[rows, :] = gl
        for f in range(0, feed, fchunk):
            cols = slice(f, f + fchunk)
            a, slope = gelu_parts(nn(n2, wu[:, cols]))
            ab = a.astype(bf16)
            act[rows, cols] = ab
            dpb = (nt(gl, wd[cols, :]) * slope).astype(bf16)
            dps[rows, cols] = dpb
            dp_out[:, cols] = dpb
        total = r1 + nn(act[rows, :], wd[...])
        out[...] = row_major(to_rm_matrix(), total.astype(bf16))

    def emit(dst, half, sel, j):
        acols = pl.ds(pl.multiple_of(half * (feed // 2) + j * (feed // 4), feed // 4), feed // 4)
        part = tn(act[:, acols], gls[...]).astype(bf16)
        slot_rows = feed // SLOTS
        per = (feed // 4) // slot_rows
        for i in range(per):
            pos = ((j * per + i) ^ sel) * PIECE1
            dst[pl.ds(pl.multiple_of(pos, 16), slot_rows), :] = part[i * slot_rows : (i + 1) * slot_rows]
        width = n2s.shape[1]
        ncols = pl.ds(pl.multiple_of(half * (width // 2), width // 2), width // 2)
        urows = width // SLOTS
        for q in range(2):
            at = j * 2 + q
            fcols = pl.ds(pl.multiple_of(at * width, width), width)
            part = tn(n2s[:, ncols], dps[:, fcols]).astype(bf16)
            for i in range(SLOTS // 2):
                pos = (i ^ sel) * PIECE1 + slot_rows + at * urows
                dst[pl.ds(pl.multiple_of(pos, 16), urows), :] = part[i * urows : (i + 1) * urows]

    @pl.when((step >= blocks) & (step < blocks + 2))
    def _():
        emit(send, 1 - scal[1], scal[3], step - blocks)

    @pl.when(step >= blocks + 2)
    def _():
        emit(keep, scal[1], scal[2], step - blocks - 2)


def mid_kernel(
    scal, lens, dp, r1, gl, zl, mgain, wu, wo,
    dh_out, dr1_out, dm_out, back, mg_out,
    state,
    *, blocks,
):
    step = pl.program_id(0)
    m = r1.shape[0]
    tb = m // R
    block = blocks - 1 - step

    @pl.when(step == 0)
    def _():
        state[...] = jnp.zeros(state.shape, f32)
        mg_out[...] = jnp.zeros(mg_out.shape, f32)

    dn2 = nt(dp[...], wu[...])
    r1v = r1[...]
    width = r1v.shape[1]
    inv = lax.rsqrt(jnp.mean(r1v * r1v, -1, keepdims=True) + epsilon)
    mg_out[...] += jnp.sum((dn2 * r1v * inv).reshape(tb, R, width), 0)
    s = mgain[...] * dn2
    mean = jnp.mean(s * r1v, -1, keepdims=True)
    dr1 = gl[...].astype(f32) + inv * (s - r1v * (inv * inv * mean))
    dr1_out[...] = dr1
    dm = dr1.astype(bf16)
    dm_out[...] = dm
    dh = nt(dm, wo[...])
    hidden = dh.shape[1]
    dh = dh.reshape(tb, R, hidden)
    pos = scal[0] + block * tb + lax.broadcasted_iota(jnp.int32, (tb, R, hidden), 0)
    dh_out[...] = jnp.where(pos < lens[...][None], dh, 0.0).reshape(m, hidden)

    def body(u, mm):
        t = tb - 1 - u
        lam = dh_out[eight(t), :] + mm
        return lam - zl[eight(t), :] * lam

    last = lax.fori_loop(0, tb, body, state[...], unroll=4)
    state[...] = last
    back[...] = last


def out_grad_kernel(y, dm, grad):
    grad[...] = tn(y[...], dm[...]).astype(bf16)


def gate_kernel(scal, dh, zl, kh, hp, c, ograd, other, fother, *refs, blocks, hops):
    msgs = refs[:hops]
    plogs = refs[hops : 2 * hops]
    wg, wc = refs[2 * hops : 2 * hops + 2]
    send, keep, dc_out, bias_out = refs[2 * hops + 2 : 2 * hops + 6]
    state, cs, dkz, dkh = refs[2 * hops + 6 :]
    step = pl.program_id(0)
    m = dh.shape[0]
    tb = m // R
    block = blocks - 1 - step

    @pl.when(step == 0)
    def _():
        mm = jnp.zeros(state.shape, f32)
        for msg, plog in zip(reversed(msgs), reversed(plogs)):
            mm = msg[...].astype(f32) + jnp.exp(plog[...].astype(f32)) * mm
        state[...] = jnp.where(scal[1] == 0, fother[...] + other[0:R, :] * mm, mm)
        bias_out[...] = jnp.zeros(bias_out.shape, f32)

    @pl.when(step < blocks)
    def _():
        base = block * tb

        def body(u, carry):
            mm, bias = carry
            w = tb // 2 - 1 - u
            t = w * 2
            hpv = hp[sixteen(w), :].astype(f32)
            zb = zl[eight(t + 1), :]
            lam = dh[eight(t + 1), :] + mm
            sb = lam * zb
            mm = lam - sb
            kb = (sb - sb * zb) * (kh[eight(t + 1), :] - hpv[R:, :])
            za = zl[eight(t), :]
            lam = dh[eight(t), :] + mm
            sa = lam * za
            mm = lam - sa
            ka = (sa - sa * za) * (kh[eight(t), :] - hpv[:R, :])
            kk = jnp.concatenate([ka, kb], 0).astype(bf16)
            ss = jnp.concatenate([sa, sb], 0).astype(bf16)
            dkz[sixteen(base // 2 + w), :] = kk
            dkh[sixteen(base // 2 + w), :] = ss
            kf = kk.astype(f32)
            return mm, bias + kf[:R, :] + kf[R:, :]

        mm, bias = lax.fori_loop(0, tb // 2, body, (state[...], bias_out[...]), unroll=2)
        state[...] = mm
        bias_out[...] = bias
        rows = pl.ds(pl.multiple_of(block * m, m), m)
        cs[rows, :] = c[...]
        dc_out[...] = nt(dkz[rows, :], wg[...]) + nt(dkh[rows, :], wc[...])

    def emit(dst, half, sel):
        width = cs.shape[1]
        hidden = dkz.shape[1]
        ccols = pl.ds(pl.multiple_of(half * (width // 2), width // 2), width // 2)
        cvals = cs[:, ccols]
        rows = width // SLOTS
        at = 0
        for grads in (dkz, dkh):
            for q in range(hidden // width):
                part = tn(cvals, grads[:, q * width : (q + 1) * width]).astype(bf16)
                for i in range(SLOTS // 2):
                    pos = (i ^ sel) * PIECE2 + at
                    dst[pl.ds(pl.multiple_of(pos, 16), rows), :] = part[i * rows : (i + 1) * rows]
                at += rows
        orows = hidden // SLOTS
        for i in range(SLOTS // 2):
            pos = (i ^ sel) * PIECE2 + at
            src = pl.multiple_of(half * (hidden // 2) + i * orows, 16)
            dst[pl.ds(pl.multiple_of(pos, 16), orows), :] = ograd[pl.ds(src, orows), :]

    @pl.when(step == blocks)
    def _():
        emit(send, 1 - scal[1], scal[3])

    @pl.when(step == blocks + 1)
    def _():
        emit(keep, scal[1], scal[2])


def tail_kernel(x, dr1, dc, before, after, gain, convw, grad, sums, uext, dext, *, blocks):
    step = pl.program_id(0)
    tb = x.shape[1]
    m = tb * R
    halo = before.shape[0]
    taps = convw.shape[0]
    width = gain.shape[1]

    @pl.when(step == 0)
    def _():
        uext[0:halo, :] = before[...]
        dext[0 : dc.shape[0], :] = dc[...]
        dext[dc.shape[0] :, :] = after[...]
        sums[...] = jnp.zeros(sums.shape, f32)

    xp = position_major(to_pm_matrix(), x[...])
    inv = lax.rsqrt(jnp.mean(xp * xp, -1, keepdims=True) + epsilon)
    xn = xp * inv
    uext[halo:, :] = (xn * gain[...]).astype(bf16).astype(f32)
    start = step * m
    here = dext[pl.ds(pl.multiple_of(start, R), m), :]
    du = convw[0:1, :] * here
    for k in range(taps):
        lo = halo - k * R
        part = (here * uext[lo : lo + m, :]).reshape(tb, R, width)
        sums[(k + 1) * R : (k + 2) * R, :] += jnp.sum(part, 0)
        if k:
            du = du + convw[k : k + 1, :] * dext[pl.ds(pl.multiple_of(start + k * R, R), m), :]
    uext[0:halo, :] = uext[m : m + halo, :]
    sums[0:R, :] += jnp.sum((du * xn).reshape(tb, R, width), 0)
    s1 = gain[...] * du
    mean = jnp.mean(s1 * xn, -1, keepdims=True)
    gin = dr1[...] + inv * (s1 - xn * mean)
    grad[...] = row_major(to_rm_matrix(), gin.astype(bf16))


def spread_kernel(scal, mine, theirs, *outs, piece, plan):
    group = pl.program_id(0)
    mine_now = (group >> 2) == scal[1]

    def emit(src, low):
        for a in range(4):
            base = (a ^ low) * piece
            at = 0
            for out, rows, columns in plan:
                ref = outs[out]
                for q in range(columns):
                    width = src.shape[1]
                    part = src[pl.ds(pl.multiple_of(base + at, 16), rows), :].astype(f32)
                    ref[a * rows : (a + 1) * rows, q * width : (q + 1) * width] = part
                    at += rows

    @pl.when(mine_now)
    def _():
        emit(mine, scal[2] & 3)

    @pl.when(jnp.logical_not(mine_now))
    def _():
        emit(theirs, scal[3] & 3)


def spread(scal, mine, theirs, piece, plan, shapes, name):
    width = mine.shape[1]
    near = lambda g, s: (jnp.clip(g - 4 * s[1], 0, 3) ^ (s[2] >> 2), 0)
    far = lambda g, s: (jnp.clip(g - 4 * (1 - s[1]), 0, 3) ^ (s[3] >> 2), 0)
    return pl.pallas_call(
        functools.partial(spread_kernel, piece=piece, plan=plan),
        grid_spec=pltpu.PrefetchScalarGridSpec(
            num_scalar_prefetch=1,
            grid=(8,),
            in_specs=[pl.BlockSpec((4 * piece, width), near), pl.BlockSpec((4 * piece, width), far)],
            out_specs=[pl.BlockSpec((dims[0] // 8, dims[1]), lambda g, s: (g, 0)) for dims in shapes],
        ),
        out_shape=[shape(dims) for dims in shapes],
        compiler_params=params(60),
        cost_estimate=cost(0, 6 * sum(dims[0] * dims[1] for dims in shapes)),
        name=name,
    )(scal, mine, theirs)


def params(mib):
    return pltpu.CompilerParams(
        dimension_semantics=("arbitrary",), vmem_limit_bytes=mib * 1024 * 1024
    )


def cost(flops, moved):
    return pl.CostEstimate(flops=flops, bytes_accessed=moved, transcendentals=0)


def shape(dims, kind=f32):
    return jax.ShapeDtypeStruct(dims, kind)


def whole(array):
    zeros = (0,) * array.ndim
    return pl.BlockSpec(array.shape, lambda *a: zeros, pipeline_mode=pl.Buffered(1))


def passed_along(value, axis, steps):
    count = lax.axis_size(axis)
    leading, last = (max(0, -steps), min(count, count - steps))
    return lax.ppermute(value, axis, [(source, source + steps) for source in range(leading, last)])


def flat_permute(value, pairs):
    return lax.ppermute(value, ("seq", "row"), pairs)


def stage_bits():
    row_bits = lax.axis_size("row").bit_length() - 1
    seq_bits = lax.axis_size("seq").bit_length() - 1
    plane = list(range(row_bits))
    line = [row_bits + 1 + z for z in range(seq_bits - 1)]
    cut = row_bits // 2
    return (plane + line, plane[cut:] + plane[:cut] + line[::-1])


def slot_of(flat, bits):
    slot = 0
    for k in range(4):
        slot = slot * 2 + ((flat >> bits[k]) & 1)
    return slot


def halving_pairs(stage):
    row_bits = lax.axis_size("row").bit_length() - 1
    orders = stage_bits()
    devices = lax.axis_size("row") * lax.axis_size("seq")
    return [(d, d ^ (1 << orders[(d >> row_bits) & 1][stage])) for d in range(devices)]


def core_pairs():
    row_bits = lax.axis_size("row").bit_length() - 1
    devices = lax.axis_size("row") * lax.axis_size("seq")
    return [(d, d ^ (1 << row_bits)) for d in range(devices)]


def added(a, b):
    return (a.astype(f32) + b.astype(f32)).astype(bf16)


def summed_pieces(send, keep):
    stages = len(stage_bits()[0])
    recv = flat_permute(send, core_pairs())
    for k in range(4):
        half = keep.shape[0] // 2
        send = added(keep[half:], recv[half:])
        recv_next = flat_permute(send, halving_pairs(k))
        keep = added(keep[:half], recv[:half])
        recv = recv_next
    total = added(keep, recv)
    for k in range(4, stages):
        total = added(total, flat_permute(total, halving_pairs(k)))
    for k in range(3, -1, -1):
        total = jnp.concatenate([total, flat_permute(total, halving_pairs(k))], 0)
    return total, flat_permute(total, core_pairs())


def summed_small(value):
    value = value + flat_permute(value, core_pairs())
    for k in range(len(stage_bits()[0])):
        value = value + flat_permute(value, halving_pairs(k))
    return value


def chip_shift(value, steps):
    return passed_along(value, "seq", 2 * steps)


def per_device(
    inputs,
    lengths,
    norm_gain,
    conv_weight,
    gate_weight,
    gate_bias,
    cand_weight,
    out_weight,
    mlp_gain,
    up_weight,
    down_weight,
    cotangent,
):
    rows, span, width = inputs.shape
    hidden = gate_weight.shape[1]
    feed = up_weight.shape[1]
    taps = conv_weight.shape[0]
    margin = taps - 1
    tokens = rows * span
    tb = 32
    blocks = span // tb
    m = tb * R
    seq = lax.axis_index("seq")
    core = seq & 1
    chips = lax.axis_size("seq") // 2
    hops = chips - 1
    flat = seq * lax.axis_size("row") + lax.axis_index("row")
    slots = [slot_of(flat, bits) for bits in stage_bits()]
    here = jnp.where(core == 0, slots[0], slots[1])
    mate = jnp.where(core == 0, slots[1], slots[0])
    scal = jnp.stack([seq * span, core, here, mate]).astype(jnp.int32)
    lens = jnp.broadcast_to(lengths[:, None], (rows, hidden))
    gain1 = norm_gain.reshape(1, width)
    gain2 = mlp_gain.reshape(1, width)
    bias = gate_bias.reshape(1, hidden)

    edge = inputs[:, span - margin :, :].astype(f32)
    edge_inv = lax.rsqrt(jnp.mean(edge * edge, -1, keepdims=True) + epsilon)
    edge_u = (edge * edge_inv * norm_gain).astype(bf16)
    before = passed_along(edge_u, "seq", 1)
    before = before.swapaxes(0, 1).reshape(margin * rows, width).astype(f32)

    clamp = lambda i: jnp.minimum(i, blocks - 1)
    rm_block = pl.BlockSpec((rows, tb, width), lambda i, s: (0, clamp(i), 0))

    def tok(w):
        return pl.BlockSpec((m, w), lambda i, s: (clamp(i), 0))

    def rtok(w):
        return pl.BlockSpec((m, w), lambda i, s: (blocks - 1 - clamp(i), 0))

    def fixed(dims):
        zeros = (0,) * len(dims)
        return pl.BlockSpec(dims, lambda i, s: zeros)

    c, zl, kh, ends = pl.pallas_call(
        front_kernel,
        grid_spec=pltpu.PrefetchScalarGridSpec(
            num_scalar_prefetch=1,
            grid=(blocks,),
            in_specs=[
                whole(lens), rm_block, whole(before), whole(gain1), whole(conv_weight),
                whole(gate_weight), whole(bias), whole(cand_weight),
            ],
            out_specs=[tok(width), tok(hidden), tok(hidden), fixed((2 * R, hidden))],
            scratch_shapes=[
                pltpu.VMEM((margin * R + m, width), f32),
                pltpu.VMEM((2 * R, hidden), f32),
            ],
        ),
        out_shape=[
            shape((tokens, width), bf16), shape((tokens, hidden)), shape((tokens, hidden)),
            shape((2 * R, hidden)),
        ],
        compiler_params=params(60),
        cost_estimate=cost(4 * tokens * width * hidden, 16 * tokens * hidden),
        name="front",
    )(scal, lens, inputs, before, gain1, conv_weight, gate_weight, bias, cand_weight)

    other = flat_permute(ends, core_pairs())
    first = jnp.where(core == 0, ends, other)
    second = jnp.where(core == 0, other, ends)
    decay = jnp.log(jnp.maximum(ends[:R] * other[:R], 1e-37))
    message = jnp.concatenate([decay, second[:R] * first[R:] + second[R:]], 0).astype(bf16)
    forward = [chip_shift(message, k) for k in range(1, chips)]
    plogs = [chip_shift(message[:R], -k) for k in range(1, chips)]

    gsteps = 4
    late = lambda i: jnp.maximum(i - blocks, 0)
    output, r1, gl, y, hp, dp, send1, keep1 = pl.pallas_call(
        functools.partial(ffn_kernel, blocks=blocks, fchunk=512, hops=hops),
        grid_spec=pltpu.PrefetchScalarGridSpec(
            num_scalar_prefetch=1,
            grid=(blocks + gsteps,),
            in_specs=[
                whole(lens), rm_block, rm_block, tok(hidden), tok(hidden), whole(other),
                *[whole(f) for f in forward], whole(out_weight), whole(gain2), whole(up_weight), whole(down_weight),
            ],
            out_specs=[
                rm_block, tok(width), tok(width), tok(hidden), tok(hidden), tok(feed),
                fixed((SLOTS // 2 * PIECE1, width)), fixed((SLOTS // 2 * PIECE1, width)),
            ],
            scratch_shapes=[
                pltpu.VMEM((R, hidden), f32),
                pltpu.VMEM((tokens, feed), bf16),
                pltpu.VMEM((tokens, feed), bf16),
                pltpu.VMEM((tokens, width), bf16),
                pltpu.VMEM((tokens, width), bf16),
            ],
        ),
        out_shape=[
            shape((rows, span, width), bf16), shape((tokens, width)), shape((tokens, width), bf16),
            shape((tokens, hidden), bf16), shape((tokens, hidden), bf16),
            shape((tokens, feed), bf16),
            shape((SLOTS // 2 * PIECE1, width), bf16), shape((SLOTS // 2 * PIECE1, width), bf16),
        ],
        compiler_params=params(60),
        cost_estimate=cost(2 * tokens * width * (hidden + 5 * feed), 64 * tokens * hidden),
        name="ffn",
    )(scal, lens, inputs, cotangent, zl, kh, other, *forward, out_weight, gain2, up_weight, down_weight)
    mine1, theirs1 = summed_pieces(send1, keep1)

    dh, dr1, dm, back, mg = pl.pallas_call(
        functools.partial(mid_kernel, blocks=blocks),
        grid_spec=pltpu.PrefetchScalarGridSpec(
            num_scalar_prefetch=1,
            grid=(blocks,),
            in_specs=[
                whole(lens), rtok(feed), rtok(width), rtok(width), rtok(hidden),
                whole(gain2), whole(up_weight), whole(out_weight),
            ],
            out_specs=[
                rtok(hidden), rtok(width), rtok(width), fixed((R, hidden)), fixed((R, width)),
            ],
            scratch_shapes=[pltpu.VMEM((R, hidden), f32)],
        ),
        out_shape=[
            shape((tokens, hidden)), shape((tokens, width)), shape((tokens, width), bf16),
            shape((R, hidden)), shape((R, width)),
        ],
        compiler_params=params(60),
        cost_estimate=cost(2 * tokens * width * (hidden + feed), 32 * tokens * hidden),
        name="mid",
    )(scal, lens, dp, r1, gl, zl, gain2, up_weight, out_weight)

    fother = flat_permute(back, core_pairs())
    lower = jnp.where(core == 0, back, fother)
    upper = jnp.where(core == 0, fother, back)
    message = (lower + first[:R] * upper).astype(bf16)
    backward = [chip_shift(message, -k) for k in range(1, chips)]

    osteps = 2
    otile = hidden // osteps
    ograd = pl.pallas_call(
        out_grad_kernel,
        grid=(osteps,),
        in_specs=[pl.BlockSpec((tokens, otile), lambda i: (0, i)), whole(dm)],
        out_specs=pl.BlockSpec((otile, width), lambda i: (i, 0)),
        out_shape=shape((hidden, width), bf16),
        compiler_params=params(60),
        cost_estimate=cost(2 * tokens * width * hidden, 4 * tokens * hidden),
        name="out_grad",
    )(y, dm)

    send2, keep2, dc, bias_part = pl.pallas_call(
        functools.partial(gate_kernel, blocks=blocks, hops=hops),
        grid_spec=pltpu.PrefetchScalarGridSpec(
            num_scalar_prefetch=1,
            grid=(blocks + 2,),
            in_specs=[
                rtok(hidden), rtok(hidden), rtok(hidden), rtok(hidden), rtok(width),
                whole(ograd), whole(other), whole(fother), *[whole(f) for f in backward],
                *[whole(f) for f in plogs], whole(gate_weight), whole(cand_weight),
            ],
            out_specs=[
                fixed((SLOTS // 2 * PIECE2, width)), fixed((SLOTS // 2 * PIECE2, width)),
                rtok(width), fixed((R, hidden)),
            ],
            scratch_shapes=[
                pltpu.VMEM((R, hidden), f32),
                pltpu.VMEM((tokens, width), bf16),
                pltpu.VMEM((tokens, hidden), bf16),
                pltpu.VMEM((tokens, hidden), bf16),
            ],
        ),
        out_shape=[
            shape((SLOTS // 2 * PIECE2, width), bf16), shape((SLOTS // 2 * PIECE2, width), bf16),
            shape((tokens, width)), shape((R, hidden)),
        ],
        compiler_params=params(60),
        cost_estimate=cost(8 * tokens * width * hidden, 24 * tokens * hidden),
        name="gates",
    )(scal, dh, zl, kh, hp, c, ograd, other, fother, *backward, *plogs, gate_weight, cand_weight)
    mine2, theirs2 = summed_pieces(send2, keep2)

    after = passed_along(dc[: margin * R].astype(bf16), "seq", -1).astype(f32)
    rm1 = pl.BlockSpec((rows, tb, width), lambda i: (0, i, 0))
    input_grad, sums = pl.pallas_call(
        functools.partial(tail_kernel, blocks=blocks),
        grid=(blocks,),
        in_specs=[
            rm1, pl.BlockSpec((m, width), lambda i: (i, 0)), whole(dc), whole(before),
            whole(after), whole(gain1), whole(conv_weight),
        ],
        out_specs=[rm1, pl.BlockSpec(((taps + 1) * R, width), lambda i: (0, 0))],
        scratch_shapes=[
            pltpu.VMEM((margin * R + m, width), f32),
            pltpu.VMEM((margin * R + tokens, width), f32),
        ],
        out_shape=[shape((rows, span, width), bf16), shape(((taps + 1) * R, width))],
        compiler_params=params(60),
        cost_estimate=cost(4 * tokens * width * width, 16 * tokens * width),
        name="tail",
    )(inputs, dr1, dc, before, after, gain1, conv_weight)

    small = jnp.concatenate(
        [
            sums.reshape(taps + 1, R, width).sum(1),
            mg.sum(0, keepdims=True),
            bias_part.sum(0).reshape(hidden // width, width),
        ],
        0,
    )
    small = summed_small(small)
    dgrad, ugrad = spread(
        scal, mine1, theirs1, PIECE1,
        ((0, feed // SLOTS, 1), (1, width // SLOTS, feed // width)),
        ((feed, width), (width, feed)), "spread_ffn",
    )
    ggrad, cgrad, ograd = spread(
        scal, mine2, theirs2, PIECE2,
        ((0, width // SLOTS, hidden // width), (1, width // SLOTS, hidden // width),
         (2, hidden // SLOTS, 1)),
        ((width, hidden), (width, hidden), (hidden, width)), "spread_gates",
    )
    return (
        output,
        input_grad,
        small[0],
        small[1 : taps + 1],
        ggrad,
        small[taps + 2 :].reshape(hidden),
        cgrad,
        ograd,
        small[taps + 1],
        ugrad,
        dgrad,
    )


def solution(mesh):
    sharded = P("row", "seq", None)
    in_specs = (sharded, P("row")) + (P(),) * 9 + (sharded,)
    out_specs = (sharded, sharded) + (P(),) * 9
    return jax.shard_map(
        per_device, mesh=mesh, in_specs=in_specs, out_specs=out_specs, check_vma=False
    )
```

```python
import functools

import jax
import jax.numpy as jnp
import numpy as np
from jax import lax
from jax.experimental import pallas as pl
from jax.experimental.pallas import tpu as pltpu
from jax.sharding import PartitionSpec as P

epsilon = 1e-06
f32 = jnp.float32
bf16 = jnp.bfloat16
R = 8
PERM = 256
SCALARS = 4
SLOTS = 32
PIECE1 = 128
PIECE2 = 96


def nn(a, b):
    return lax.dot_general(a, b, (((1,), (0,)), ((), ())), preferred_element_type=f32)


def nt(a, b):
    return lax.dot_general(a, b, (((1,), (1,)), ((), ())), preferred_element_type=f32)


def tn(a, b):
    return lax.dot_general(a, b, (((0,), (0,)), ((), ())), preferred_element_type=f32)


def to_pm_matrix():
    out = lax.broadcasted_iota(jnp.int32, (PERM, PERM), 0)
    src = lax.broadcasted_iota(jnp.int32, (PERM, PERM), 1)
    span = PERM // R
    return ((out // R == src % span) & (out % R == src // span)).astype(f32).astype(bf16)


def to_rm_matrix():
    out = lax.broadcasted_iota(jnp.int32, (PERM, PERM), 0)
    src = lax.broadcasted_iota(jnp.int32, (PERM, PERM), 1)
    span = PERM // R
    return ((src // R == out % span) & (src % R == out // span)).astype(f32).astype(bf16)


def position_major(perm, block):
    span = PERM // R
    parts = []
    for s in range(block.shape[1] // span):
        part = block[:, s * span : (s + 1) * span, :].reshape(PERM, block.shape[2])
        parts.append(nn(perm, part))
    return parts[0] if len(parts) == 1 else jnp.concatenate(parts, 0)


def row_major(perm, tokens):
    span = PERM // R
    parts = []
    for s in range(tokens.shape[0] // PERM):
        part = nn(perm, tokens[s * PERM : (s + 1) * PERM]).astype(bf16)
        parts.append(part.reshape(R, span, tokens.shape[1]))
    return parts[0] if len(parts) == 1 else jnp.concatenate(parts, 1)


def eight(t):
    return pl.ds(pl.multiple_of(t * R, R), R)


def sixteen(t):
    return pl.ds(pl.multiple_of(t * 2 * R, 2 * R), 2 * R)


def normed_edge(edge, gain):
    e = edge.astype(f32)
    inv = lax.rsqrt(jnp.mean(e * e, -1, keepdims=True) + epsilon)
    return (e * inv * gain).astype(bf16).astype(f32)


def set_limits(scal, limit):
    row = lax.broadcasted_iota(jnp.int32, limit.shape, 0)
    value = jnp.zeros(limit.shape, jnp.int32)
    for r in range(R):
        value = jnp.where(row == r, scal[SCALARS + r], value)
    limit[...] = value


def halves(ref, pair):
    both = ref[sixteen(pair), :].astype(f32)
    return both[:R], both[R:]


def front_kernel(scal, x, edge, gain, convw, wg, bias, wc, c_out, zl_out, kh_out, ends, ext, state, limit):
    step = pl.program_id(0)
    tb = x.shape[1]
    m = tb * R
    halo = edge.shape[0]
    taps = convw.shape[0]

    @pl.when(step == 0)
    def _():
        set_limits(scal, limit)
        ext[0:halo, :] = normed_edge(edge[...], gain[...])
        state[0:R, :] = jnp.ones((R, state.shape[1]), f32)
        state[R:, :] = jnp.zeros((R, state.shape[1]), f32)

    xp = position_major(to_pm_matrix(), x[...])
    inv = lax.rsqrt(jnp.mean(xp * xp, -1, keepdims=True) + epsilon)
    ext[halo:, :] = (xp * inv * gain[...]).astype(bf16).astype(f32)
    conv = convw[0:1, :] * ext[halo:, :]
    for k in range(1, taps):
        lo = halo - k * R
        conv = conv + convw[k : k + 1, :] * ext[lo : lo + m, :]
    ext[0:halo, :] = ext[m : m + halo, :]
    cb = conv.astype(bf16)
    c_out[...] = cb
    kz = nn(cb, wg[...]) + bias[...]
    zs = 1.0 / (1.0 + jnp.exp(-kz))
    width = zs.shape[1]
    zs = zs.reshape(tb, R, width)
    pos = scal[0] + step * tb + lax.broadcasted_iota(jnp.int32, (tb, R, width), 0)
    zl_out[...] = jnp.where(pos < limit[...][None], zs, 0.0).reshape(m, width).astype(bf16)
    kh_out[...] = nn(cb, wc[...]).astype(bf16)

    def body(u, carry):
        prod, h = carry
        za, zb = halves(zl_out, u)
        ka, kb = halves(kh_out, u)
        a = 1.0 - za
        b = 1.0 - zb
        return prod * (a * b), (h * a + za * ka) * b + zb * kb

    prod, h = lax.fori_loop(0, tb // 2, body, (state[0:R, :], state[R:, :]), unroll=4)
    state[0:R, :] = prod
    state[R:, :] = h
    ends[0:R, :] = prod
    ends[R:, :] = h


def gelu_parts(p):
    k0 = 0.7978845608028654
    p2 = p * p
    th = jnp.tanh(p * (k0 + (k0 * 0.044715) * p2))
    ht = 0.5 + 0.5 * th
    return p * ht, ht + (2.0 * p) * (ht - ht * ht) * (k0 + (3.0 * k0 * 0.044715) * p2)


def da_kernel(g, wd, gl_out, da_out):
    gl = position_major(to_pm_matrix(), g[...]).astype(bf16)
    gl_out[...] = gl
    da_out[...] = nt(gl, wd[...]).astype(bf16)


def ffn_kernel(scal, x, gl, da, zl, kh, other, *refs, blocks, fchunk, hops):
    msgs = refs[:hops]
    wo, mgain, wu, wd = refs[hops : hops + 4]
    out, r1_out, y_out, hp_out, dp_out, send, keep = refs[hops + 4 : hops + 11]
    state, limit, act, dps, n2s, gls = refs[hops + 11 :]
    step = pl.program_id(0)
    tb = x.shape[1]
    m = tb * R
    feed = wu.shape[1]

    @pl.when(step == 0)
    def _():
        set_limits(scal, limit)
        h = jnp.zeros((R, zl.shape[1]), f32)
        for msg in reversed(msgs):
            both = msg[...].astype(f32)
            h = jnp.exp(both[0:R, :]) * h + both[R:, :]
        state[...] = jnp.where(scal[1] == 1, other[0:R, :] * h + other[R:, :], h)

    @pl.when(step < blocks)
    def _():
        first = scal[0] + step * tb
        lens = limit[...]

        def body(u, h):
            t = u * 2
            za, zb = halves(zl, u)
            ka, kb = halves(kh, u)
            ha = h - za * h + za * ka
            hb = ha - zb * ha + zb * kb
            hp_out[sixteen(u), :] = jnp.concatenate([h, ha], 0).astype(bf16)
            ya = jnp.where(first + t < lens, ha, 0.0)
            yb = jnp.where(first + t + 1 < lens, hb, 0.0)
            y_out[sixteen(u), :] = jnp.concatenate([ya, yb], 0).astype(bf16)
            return hb

        state[...] = lax.fori_loop(0, tb // 2, body, state[...], unroll=2)
        to_pm = to_pm_matrix()
        r1 = position_major(to_pm, x[...]) + nn(y_out[...], wo[...])
        r1_out[...] = r1
        inv = lax.rsqrt(jnp.mean(r1 * r1, -1, keepdims=True) + epsilon)
        n2 = (r1 * inv * mgain[...]).astype(bf16)
        rows = pl.ds(pl.multiple_of(step * m, m), m)
        n2s[rows, :] = n2
        gls[rows, :] = gl[...]
        for f in range(0, feed, fchunk):
            cols = slice(f, f + fchunk)
            a, slope = gelu_parts(nn(n2, wu[:, cols]))
            ab = a.astype(bf16)
            act[rows, cols] = ab
            dpb = (da[:, cols].astype(f32) * slope).astype(bf16)
            dps[rows, cols] = dpb
            dp_out[:, cols] = dpb
        total = r1 + nn(act[rows, :], wd[...])
        out[...] = row_major(to_rm_matrix(), total.astype(bf16))

    def emit(dst, half, sel, j):
        acols = pl.ds(pl.multiple_of(half * (feed // 2) + j * (feed // 4), feed // 4), feed // 4)
        part = tn(act[:, acols], gls[...]).astype(bf16)
        slot_rows = feed // SLOTS
        per = (feed // 4) // slot_rows
        for i in range(per):
            pos = ((j * per + i) ^ sel) * PIECE1
            dst[pl.ds(pl.multiple_of(pos, 16), slot_rows), :] = part[i * slot_rows : (i + 1) * slot_rows]
        width = n2s.shape[1]
        ncols = pl.ds(pl.multiple_of(half * (width // 2), width // 2), width // 2)
        urows = width // SLOTS
        for q in range(2):
            at = j * 2 + q
            fcols = pl.ds(pl.multiple_of(at * width, width), width)
            part = tn(n2s[:, ncols], dps[:, fcols]).astype(bf16)
            for i in range(SLOTS // 2):
                pos = (i ^ sel) * PIECE1 + slot_rows + at * urows
                dst[pl.ds(pl.multiple_of(pos, 16), urows), :] = part[i * urows : (i + 1) * urows]

    @pl.when((step >= blocks) & (step < blocks + 2))
    def _():
        emit(send, 1 - scal[1], scal[3], step - blocks)

    @pl.when(step >= blocks + 2)
    def _():
        emit(keep, scal[1], scal[2], step - blocks - 2)


def mid_kernel(
    scal, dp, r1, gl, zl, mgain, wu, wo, *refs, top, carried
):
    step = pl.program_id(0)
    m = r1.shape[0]
    tb = m // R
    block = top - step
    if carried:
        back_in, mg_in = refs[:2]
        refs = refs[3:]
    dh_out, dr1_out, dm_out, back, mg_out, state, limit = refs

    @pl.when(step == 0)
    def _():
        set_limits(scal, limit)
        state[...] = back_in[...] if carried else jnp.zeros(state.shape, f32)
        mg_out[...] = mg_in[...] if carried else jnp.zeros(mg_out.shape, f32)

    dn2 = nt(dp[...], wu[...])
    r1v = r1[...]
    width = r1v.shape[1]
    inv = lax.rsqrt(jnp.mean(r1v * r1v, -1, keepdims=True) + epsilon)
    mg_out[...] += jnp.sum((dn2 * r1v * inv).reshape(tb, R, width), 0)
    s = mgain[...] * dn2
    mean = jnp.mean(s * r1v, -1, keepdims=True)
    dr1 = gl[...].astype(f32) + inv * (s - r1v * (inv * inv * mean))
    dr1_out[...] = dr1
    dm = dr1.astype(bf16)
    dm_out[...] = dm
    dh = nt(dm, wo[...])
    hidden = dh.shape[1]
    dh = dh.reshape(tb, R, hidden)
    pos = scal[0] + block * tb + lax.broadcasted_iota(jnp.int32, (tb, R, hidden), 0)
    dh_out[...] = jnp.where(pos < limit[...][None], dh, 0.0).reshape(m, hidden).astype(bf16)

    def body(u, mm):
        w = tb // 2 - 1 - u
        za, zb = halves(zl, w)
        da, db = halves(dh_out, w)
        lam = db + mm
        lam = da + (lam - zb * lam)
        return lam - za * lam

    last = lax.fori_loop(0, tb // 2, body, state[...], unroll=4)
    state[...] = last
    back[...] = last


def out_grad_kernel(y, dm_a, dm_b, grad):
    dm = jnp.concatenate([dm_a[...], dm_b[...]], 0)
    grad[...] = tn(y[...], dm).astype(bf16)


def gate_kernel(scal, dh_a, dh_b, zl, kh, hp, c, ograd, other, fother, *refs, blocks, hops, low):
    msgs = refs[:hops]
    plogs = refs[hops : 2 * hops]
    wg, wc = refs[2 * hops : 2 * hops + 2]
    send, keep, dc_out, bias_out = refs[2 * hops + 3 : 2 * hops + 7]
    state, cs, dkz, dkh = refs[2 * hops + 7 :]
    step = pl.program_id(0)
    m = dh_a.shape[0]
    tb = m // R
    block = blocks - 1 - step

    @pl.when(step == 0)
    def _():
        mm = jnp.zeros(state.shape, f32)
        for msg, plog in zip(reversed(msgs), reversed(plogs)):
            mm = msg[...].astype(f32) + jnp.exp(plog[...].astype(f32)) * mm
        state[...] = jnp.where(scal[1] == 0, fother[...] + other[0:R, :] * mm, mm)
        bias_out[...] = jnp.zeros(bias_out.shape, f32)

    def adjoint(dh):
        base = block * tb

        def body(u, carry):
            mm, bias = carry
            w = tb // 2 - 1 - u
            ha, hb = halves(hp, w)
            za, zb = halves(zl, w)
            da, db = halves(dh, w)
            ka, kb = halves(kh, w)
            lam = db + mm
            sb = lam * zb
            mm = lam - sb
            kb = (sb - sb * zb) * (kb - hb)
            lam = da + mm
            sa = lam * za
            mm = lam - sa
            ka = (sa - sa * za) * (ka - ha)
            kk = jnp.concatenate([ka, kb], 0).astype(bf16)
            ss = jnp.concatenate([sa, sb], 0).astype(bf16)
            dkz[sixteen(base // 2 + w), :] = kk
            dkh[sixteen(base // 2 + w), :] = ss
            kf = kk.astype(f32)
            return mm, bias + kf[:R, :] + kf[R:, :]

        mm, bias = lax.fori_loop(0, tb // 2, body, (state[...], bias_out[...]), unroll=2)
        state[...] = mm
        bias_out[...] = bias
        rows = pl.ds(pl.multiple_of(block * m, m), m)
        cs[rows, :] = c[...]
        dc_out[...] = nt(dkz[rows, :], wg[...]) + nt(dkh[rows, :], wc[...])

    @pl.when((step < blocks) & (block >= low))
    def _():
        adjoint(dh_b)

    @pl.when((step < blocks) & (block < low))
    def _():
        adjoint(dh_a)

    def emit(dst, half, sel):
        width = cs.shape[1]
        hidden = dkz.shape[1]
        ccols = pl.ds(pl.multiple_of(half * (width // 2), width // 2), width // 2)
        cvals = cs[:, ccols]
        rows = width // SLOTS
        at = 0
        for grads in (dkz, dkh):
            for q in range(hidden // width):
                part = tn(cvals, grads[:, q * width : (q + 1) * width]).astype(bf16)
                for i in range(SLOTS // 2):
                    pos = (i ^ sel) * PIECE2 + at
                    dst[pl.ds(pl.multiple_of(pos, 16), rows), :] = part[i * rows : (i + 1) * rows]
                at += rows
        orows = hidden // SLOTS
        for i in range(SLOTS // 2):
            pos = (i ^ sel) * PIECE2 + at
            src = pl.multiple_of(half * (hidden // 2) + i * orows, 16)
            dst[pl.ds(pl.multiple_of(pos, 16), orows), :] = ograd[pl.ds(src, orows), :]

    @pl.when(step == blocks)
    def _():
        emit(send, 1 - scal[1], scal[3])

    @pl.when(step == blocks + 1)
    def _():
        emit(keep, scal[1], scal[2])


def tail_kernel(x, dr1_a, dr1_b, dc, edge, after, gain, convw, order, grad, sums, uext, dext, *, low):
    step = pl.program_id(0)
    tb = x.shape[1]
    m = tb * R
    halo = edge.shape[0]
    taps = convw.shape[0]
    width = gain.shape[1]

    @pl.when(step == 0)
    def _():
        uext[0:halo, :] = normed_edge(edge[...], gain[...])
        dext[0 : dc.shape[0], :] = dc[...]
        dext[dc.shape[0] :, :] = after[...].astype(f32)
        sums[...] = jnp.zeros(sums.shape, f32)

    xp = position_major(to_pm_matrix(), x[...])
    inv = lax.rsqrt(jnp.mean(xp * xp, -1, keepdims=True) + epsilon)
    xn = xp * inv
    uext[halo:, :] = (xn * gain[...]).astype(bf16).astype(f32)
    start = step * m
    here = dext[pl.ds(pl.multiple_of(start, R), m), :]
    du = convw[0:1, :] * here
    for k in range(taps):
        lo = halo - k * R
        part = (here * uext[lo : lo + m, :]).reshape(tb, R, width)
        sums[(k + 1) * R : (k + 2) * R, :] += jnp.sum(part, 0)
        if k:
            du = du + convw[k : k + 1, :] * dext[pl.ds(pl.multiple_of(start + k * R, R), m), :]
    uext[0:halo, :] = uext[m : m + halo, :]
    sums[0:R, :] += jnp.sum((du * xn).reshape(tb, R, width), 0)
    s1 = gain[...] * du
    mean = jnp.mean(s1 * xn, -1, keepdims=True)
    dr1 = jnp.where(step < low, dr1_a[...], dr1_b[...])
    gin = dr1 + inv * (s1 - xn * mean)
    grad[...] = row_major(to_rm_matrix(), gin.astype(bf16))


def spread_kernel(scal, mine, theirs, *outs, piece, plan):
    mine_now = (pl.program_id(0) >> 1) == scal[1]

    def emit(src, low):
        for a in range(8):
            base = (a ^ low) * piece
            at = 0
            for out, rows, columns in plan:
                ref = outs[out]
                for q in range(columns):
                    width = src.shape[1]
                    part = src[pl.ds(pl.multiple_of(base + at, 16), rows), :].astype(f32)
                    ref[a * rows : (a + 1) * rows, q * width : (q + 1) * width] = part
                    at += rows

    @pl.when(mine_now)
    def _():
        emit(mine, scal[2] & 7)

    @pl.when(jnp.logical_not(mine_now))
    def _():
        emit(theirs, scal[3] & 7)


def spread(scal, mine, theirs, piece, plan, shapes, name):
    width = mine.shape[1]
    near = lambda g, s: (jnp.clip(g - 2 * s[1], 0, 1) ^ (s[2] >> 3), 0)
    far = lambda g, s: (jnp.clip(g - 2 * (1 - s[1]), 0, 1) ^ (s[3] >> 3), 0)
    return pl.pallas_call(
        functools.partial(spread_kernel, piece=piece, plan=plan),
        grid_spec=pltpu.PrefetchScalarGridSpec(
            num_scalar_prefetch=1,
            grid=(4,),
            in_specs=[pl.BlockSpec((8 * piece, width), near), pl.BlockSpec((8 * piece, width), far)],
            out_specs=[pl.BlockSpec((dims[0] // 4, dims[1]), lambda g, s: (g, 0)) for dims in shapes],
        ),
        out_shape=[shape(dims) for dims in shapes],
        compiler_params=params(60),
        cost_estimate=cost(0, 6 * sum(dims[0] * dims[1] for dims in shapes)),
        name=name,
    )(scal, mine, theirs)


def params(mib):
    return pltpu.CompilerParams(
        dimension_semantics=("arbitrary",), vmem_limit_bytes=mib * 1024 * 1024
    )


def cost(flops, moved):
    return pl.CostEstimate(flops=flops, bytes_accessed=moved, transcendentals=0)


def shape(dims, kind=f32):
    return jax.ShapeDtypeStruct(dims, kind)


ORDER = pl.BlockSpec(memory_space=pl.ANY)


def whole(array):
    zeros = (0,) * array.ndim
    return pl.BlockSpec(array.shape, lambda *a: zeros, pipeline_mode=pl.Buffered(1))


def passed_along(value, axis, steps):
    count = lax.axis_size(axis)
    leading, last = (max(0, -steps), min(count, count - steps))
    return lax.ppermute(value, axis, [(source, source + steps) for source in range(leading, last)])


def flat_permute(value, pairs):
    return lax.ppermute(value, ("seq", "row"), pairs)


def stage_bits():
    row_bits = lax.axis_size("row").bit_length() - 1
    seq_bits = lax.axis_size("seq").bit_length() - 1
    plane = list(range(row_bits))
    line = [row_bits + 1 + z for z in range(seq_bits - 1)]
    cut = row_bits // 2
    return (plane + line, plane[cut:] + plane[:cut] + line[::-1])


def slot_of(flat, bits):
    slot = 0
    for k in range(4):
        slot = slot * 2 + ((flat >> bits[k]) & 1)
    return slot


def halving_pairs(stage):
    row_bits = lax.axis_size("row").bit_length() - 1
    orders = stage_bits()
    devices = lax.axis_size("row") * lax.axis_size("seq")
    return [(d, d ^ (1 << orders[(d >> row_bits) & 1][stage])) for d in range(devices)]


def core_pairs():
    row_bits = lax.axis_size("row").bit_length() - 1
    devices = lax.axis_size("row") * lax.axis_size("seq")
    return [(d, d ^ (1 << row_bits)) for d in range(devices)]


def added(a, b):
    return (a.astype(f32) + b.astype(f32)).astype(bf16)


class Halving:
    def __init__(self, send, keep):
        self.stage = 0
        self.keep = keep
        self.recv = flat_permute(send, core_pairs())
        self.total = None

    def advance(self, *order):
        if order:
            self.recv, *_ = lax.optimization_barrier((self.recv,) + order)
        stages = len(stage_bits()[0])
        k = self.stage
        self.stage += 1
        if k < 4:
            half = self.keep.shape[0] // 2
            self.send = added(self.keep[half:], self.recv[half:])
            self.keep = added(self.keep[:half], self.recv[:half])
            self.recv = flat_permute(self.send, halving_pairs(k))
            return
        if k == 4:
            self.total = added(self.keep, self.recv)
            for extra in range(4, stages):
                self.total = added(self.total, flat_permute(self.total, halving_pairs(extra)))
        else:
            self.total = jnp.concatenate([self.total, self.recv], 0)
        self.recv = flat_permute(self.total, halving_pairs(7 - k) if k < 8 else core_pairs())

    def finished(self):
        while self.stage < 9:
            self.advance()
        return self.total, self.recv


def chip_shift(value, steps):
    return passed_along(value, "seq", 2 * steps)


def per_device(
    inputs,
    lengths,
    norm_gain,
    conv_weight,
    gate_weight,
    gate_bias,
    cand_weight,
    out_weight,
    mlp_gain,
    up_weight,
    down_weight,
    cotangent,
):
    rows, span, width = inputs.shape
    hidden = gate_weight.shape[1]
    feed = up_weight.shape[1]
    taps = conv_weight.shape[0]
    margin = taps - 1
    tokens = rows * span
    tb = 32
    blocks = span // tb
    m = tb * R
    seq = lax.axis_index("seq")
    core = seq & 1
    chips = lax.axis_size("seq") // 2
    hops = chips - 1
    flat = seq * lax.axis_size("row") + lax.axis_index("row")
    slots = [slot_of(flat, bits) for bits in stage_bits()]
    here = jnp.where(core == 0, slots[0], slots[1])
    mate = jnp.where(core == 0, slots[1], slots[0])
    scal = jnp.concatenate([jnp.stack([seq * span, core, here, mate]).astype(jnp.int32), lengths])
    gain1 = norm_gain.reshape(1, width)
    gain2 = mlp_gain.reshape(1, width)
    bias = gate_bias.reshape(1, hidden)

    edge = inputs[:, span - margin :, :].swapaxes(0, 1).reshape(margin * rows, width)
    edge = passed_along(edge, "seq", 1)

    clamp = lambda i: jnp.minimum(i, blocks - 1)
    rm_block = pl.BlockSpec((rows, tb, width), lambda i, s: (0, clamp(i), 0))

    def tok(w):
        return pl.BlockSpec((m, w), lambda i, s: (clamp(i), 0))

    def rtok(w):
        return pl.BlockSpec((m, w), lambda i, s: (blocks - 1 - clamp(i), 0))

    def fixed(dims):
        zeros = (0,) * len(dims)
        return pl.BlockSpec(dims, lambda i, s: zeros)

    c, zl, kh, ends = pl.pallas_call(
        front_kernel,
        grid_spec=pltpu.PrefetchScalarGridSpec(
            num_scalar_prefetch=1,
            grid=(blocks,),
            in_specs=[
                rm_block, whole(edge), whole(gain1), whole(conv_weight),
                whole(gate_weight), whole(bias), whole(cand_weight),
            ],
            out_specs=[tok(width), tok(hidden), tok(hidden), fixed((2 * R, hidden))],
            scratch_shapes=[
                pltpu.VMEM((margin * R + m, width), f32),
                pltpu.VMEM((2 * R, hidden), f32),
                pltpu.VMEM((R, hidden), jnp.int32),
            ],
        ),
        out_shape=[
            shape((tokens, width), bf16), shape((tokens, hidden), bf16), shape((tokens, hidden), bf16),
            shape((2 * R, hidden)),
        ],
        compiler_params=params(60),
        cost_estimate=cost(4 * tokens * width * hidden, 16 * tokens * hidden),
        name="front",
    )(scal, inputs, edge, gain1, conv_weight, gate_weight, bias, cand_weight)

    other = flat_permute(ends, core_pairs())
    first = jnp.where(core == 0, ends, other)
    second = jnp.where(core == 0, other, ends)
    decay = jnp.log(jnp.maximum(ends[:R] * other[:R], 1e-37))
    message = jnp.concatenate([decay, second[:R] * first[R:] + second[R:]], 0).astype(bf16)
    forward = [chip_shift(message, k) for k in range(1, chips)]
    plogs = [chip_shift(message[:R], -k) for k in range(1, chips)]

    flat_rm = pl.BlockSpec((rows, tb, width), lambda i: (0, i, 0))
    gl, da = pl.pallas_call(
        da_kernel,
        grid=(blocks,),
        in_specs=[flat_rm, whole(down_weight)],
        out_specs=[pl.BlockSpec((m, width), lambda i: (i, 0)), pl.BlockSpec((m, feed), lambda i: (i, 0))],
        out_shape=[shape((tokens, width), bf16), shape((tokens, feed), bf16)],
        compiler_params=params(60),
        cost_estimate=cost(2 * tokens * width * feed, 8 * tokens * hidden),
        name="da",
    )(cotangent, down_weight)

    gsteps = 4
    late = lambda i: jnp.maximum(i - blocks, 0)
    output, r1, y, hp, dp, send1, keep1 = pl.pallas_call(
        functools.partial(ffn_kernel, blocks=blocks, fchunk=512, hops=hops),
        grid_spec=pltpu.PrefetchScalarGridSpec(
            num_scalar_prefetch=1,
            grid=(blocks + gsteps,),
            in_specs=[
                rm_block, tok(width), tok(feed), tok(hidden), tok(hidden), whole(other),
                *[whole(f) for f in forward], whole(out_weight), whole(gain2), whole(up_weight), whole(down_weight),
            ],
            out_specs=[
                rm_block, tok(width), tok(hidden), tok(hidden), tok(feed),
                fixed((SLOTS // 2 * PIECE1, width)), fixed((SLOTS // 2 * PIECE1, width)),
            ],
            scratch_shapes=[
                pltpu.VMEM((R, hidden), f32),
                pltpu.VMEM((R, hidden), jnp.int32),
                pltpu.VMEM((tokens, feed), bf16),
                pltpu.VMEM((tokens, feed), bf16),
                pltpu.VMEM((tokens, width), bf16),
                pltpu.VMEM((tokens, width), bf16),
            ],
        ),
        out_shape=[
            shape((rows, span, width), bf16), shape((tokens, width)),
            shape((tokens, hidden), bf16), shape((tokens, hidden), bf16),
            shape((tokens, feed), bf16),
            shape((SLOTS // 2 * PIECE1, width), bf16), shape((SLOTS // 2 * PIECE1, width), bf16),
        ],
        compiler_params=params(60),
        cost_estimate=cost(2 * tokens * width * (hidden + 5 * feed), 64 * tokens * hidden),
        name="ffn",
    )(scal, inputs, gl, da, zl, kh, other, *forward, out_weight, gain2, up_weight, down_weight)
    def mid(top, count, carry):
        at = lambda w: pl.BlockSpec((m, w), lambda i, s: (top - i, 0))
        to = lambda w: pl.BlockSpec((m, w), lambda i, s: (count - 1 - i, 0))
        operands = (scal, dp, r1, gl, zl, gain2, up_weight, out_weight) + carry
        local = count * m
        return pl.pallas_call(
            functools.partial(mid_kernel, top=top, carried=bool(carry)),
            grid_spec=pltpu.PrefetchScalarGridSpec(
                num_scalar_prefetch=1,
                grid=(count,),
                in_specs=[
                    at(feed), at(width), at(width), at(hidden),
                    whole(gain2), whole(up_weight), whole(out_weight),
                ] + ([whole(carry[0]), whole(carry[1]), ORDER] if carry else []),
                out_specs=[to(hidden), to(width), to(width), fixed((R, hidden)), fixed((R, width))],
                scratch_shapes=[pltpu.VMEM((R, hidden), f32), pltpu.VMEM((R, hidden), jnp.int32)],
            ),
            out_shape=[
                shape((local, hidden), bf16), shape((local, width)), shape((local, width), bf16),
                shape((R, hidden)), shape((R, width)),
            ],
            compiler_params=params(60),
            cost_estimate=cost(
                2 * local * width * (hidden + feed), 32 * local * hidden
            ),
            name="mid_late" if not carry else "mid_early",
        )(*operands)

    chunk1 = Halving(send1, keep1)
    upper_half = blocks // 2
    dh_b, dr1_b, dm_b, back, mg = mid(blocks - 1, upper_half, ())
    chunk1.advance(back)
    dh_a, dr1_a, dm_a, back, mg = mid(blocks - 1 - upper_half, blocks - upper_half, (back, mg, chunk1.send))

    fother = flat_permute(back, core_pairs())
    lower = jnp.where(core == 0, back, fother)
    upper = jnp.where(core == 0, fother, back)
    message = (lower + first[:R] * upper).astype(bf16)
    backward = [chip_shift(message, -k) for k in range(1, chips)]

    osteps = 2
    otile = hidden // osteps
    ograd = pl.pallas_call(
        out_grad_kernel,
        grid=(osteps,),
        in_specs=[pl.BlockSpec((tokens, otile), lambda i: (0, i)), whole(dm_a), whole(dm_b)],
        out_specs=pl.BlockSpec((otile, width), lambda i: (i, 0)),
        out_shape=shape((hidden, width), bf16),
        compiler_params=params(60),
        cost_estimate=cost(2 * tokens * width * hidden, 4 * tokens * hidden),
        name="out_grad",
    )(y, dm_a, dm_b)

    chunk1.advance()
    low = blocks - upper_half
    top_block = pl.BlockSpec((m, hidden), lambda i, s: (jnp.maximum(blocks - 1 - clamp(i) - low, 0), 0))
    low_block = pl.BlockSpec((m, hidden), lambda i, s: (jnp.minimum(blocks - 1 - clamp(i), low - 1), 0))
    send2, keep2, dc, bias_part = pl.pallas_call(
        functools.partial(gate_kernel, blocks=blocks, hops=hops, low=low),
        grid_spec=pltpu.PrefetchScalarGridSpec(
            num_scalar_prefetch=1,
            grid=(blocks + 2,),
            in_specs=[
                low_block, top_block, rtok(hidden), rtok(hidden), rtok(hidden), rtok(width),
                whole(ograd), whole(other), whole(fother), *[whole(f) for f in backward],
                *[whole(f) for f in plogs], whole(gate_weight), whole(cand_weight), ORDER,
            ],
            out_specs=[
                fixed((SLOTS // 2 * PIECE2, width)), fixed((SLOTS // 2 * PIECE2, width)),
                rtok(width), fixed((R, hidden)),
            ],
            scratch_shapes=[
                pltpu.VMEM((R, hidden), f32),
                pltpu.VMEM((tokens, width), bf16),
                pltpu.VMEM((tokens, hidden), bf16),
                pltpu.VMEM((tokens, hidden), bf16),
            ],
        ),
        out_shape=[
            shape((SLOTS // 2 * PIECE2, width), bf16), shape((SLOTS // 2 * PIECE2, width), bf16),
            shape((tokens, width)), shape((R, hidden)),
        ],
        compiler_params=params(60),
        cost_estimate=cost(8 * tokens * width * hidden, 24 * tokens * hidden),
        name="gates",
    )(
        scal, dh_a, dh_b, zl, kh, hp, c, ograd, other, fother, *backward, *plogs,
        gate_weight, cand_weight, chunk1.send,
    )
    send2, chunk1.recv = lax.optimization_barrier((send2, chunk1.recv))
    chunk2 = Halving(send2, keep2)
    after = passed_along(dc[: margin * R].astype(bf16), "seq", -1)
    chunk1.advance()
    rm1 = pl.BlockSpec((rows, tb, width), lambda i: (0, i, 0))
    input_grad, sums = pl.pallas_call(
        functools.partial(tail_kernel, low=low),
        grid=(blocks,),
        in_specs=[
            rm1,
            pl.BlockSpec((m, width), lambda i: (jnp.minimum(i, low - 1), 0)),
            pl.BlockSpec((m, width), lambda i: (jnp.maximum(i - low, 0), 0)),
            whole(dc), whole(edge), whole(after), whole(gain1), whole(conv_weight), ORDER,
        ],
        out_specs=[rm1, pl.BlockSpec(((taps + 1) * R, width), lambda i: (0, 0))],
        scratch_shapes=[
            pltpu.VMEM((margin * R + m, width), f32),
            pltpu.VMEM((margin * R + tokens, width), f32),
        ],
        out_shape=[shape((rows, span, width), bf16), shape(((taps + 1) * R, width))],
        compiler_params=params(60),
        cost_estimate=cost(4 * tokens * width * width, 16 * tokens * width),
        name="tail",
    )(inputs, dr1_a, dr1_b, dc, edge, after, gain1, conv_weight, chunk1.send)

    small = jnp.concatenate(
        [
            sums.reshape(taps + 1, R, width).sum(1),
            mg.sum(0, keepdims=True),
            bias_part.sum(0).reshape(hidden // width, width),
        ],
        0,
    )
    chunk2.advance(small)
    small = small + flat_permute(small, core_pairs())
    for k in range(len(stage_bits()[0])):
        if k < 8:
            chunk2.advance(small)
        small = small + flat_permute(small, halving_pairs(k))
    mine2, theirs2 = chunk2.finished()
    mine1, theirs1 = chunk1.finished()
    dgrad, ugrad = spread(
        scal, mine1, theirs1, PIECE1,
        ((0, feed // SLOTS, 1), (1, width // SLOTS, feed // width)),
        ((feed, width), (width, feed)), "spread_ffn",
    )
    ggrad, cgrad, ograd = spread(
        scal, mine2, theirs2, PIECE2,
        ((0, width // SLOTS, hidden // width), (1, width // SLOTS, hidden // width),
         (2, hidden // SLOTS, 1)),
        ((width, hidden), (width, hidden), (hidden, width)), "spread_gates",
    )
    return (
        output,
        input_grad,
        small[0],
        small[1 : taps + 1],
        ggrad,
        small[taps + 2 :].reshape(hidden),
        cgrad,
        ograd,
        small[taps + 1],
        ugrad,
        dgrad,
    )


def solution(mesh):
    sharded = P("row", "seq", None)
    in_specs = (sharded, P("row")) + (P(),) * 9 + (sharded,)
    out_specs = (sharded, sharded) + (P(),) * 9
    return jax.shard_map(
        per_device, mesh=mesh, in_specs=in_specs, out_specs=out_specs, check_vma=False
    )
```

```python
import functools

import jax
import jax.numpy as jnp
import numpy as np
from jax import lax
from jax.experimental import pallas as pl
from jax.experimental.pallas import tpu as pltpu
from jax.sharding import PartitionSpec as P

epsilon = 1e-06
f32 = jnp.float32
bf16 = jnp.bfloat16
R = 8
PERM = 256
SCALARS = 4
SLOTS = 32
PIECE1 = 128
PIECE2 = 96


def nn(a, b):
    return lax.dot_general(a, b, (((1,), (0,)), ((), ())), preferred_element_type=f32)


def nt(a, b):
    return lax.dot_general(a, b, (((1,), (1,)), ((), ())), preferred_element_type=f32)


def tn(a, b):
    return lax.dot_general(a, b, (((0,), (0,)), ((), ())), preferred_element_type=f32)


def token_order():
    out = np.arange(PERM)
    source = (out % R) * (PERM // R) + out // R
    to_pm = np.zeros((PERM, PERM), np.float32)
    to_pm[out, source] = 1
    return jnp.asarray(to_pm, bf16), jnp.asarray(to_pm.T, bf16)


def position_major(perm, block):
    span = PERM // R
    parts = []
    for s in range(block.shape[1] // span):
        part = block[:, s * span : (s + 1) * span, :].reshape(PERM, block.shape[2])
        parts.append(nn(perm, part))
    return parts[0] if len(parts) == 1 else jnp.concatenate(parts, 0)


def row_major(perm, tokens):
    span = PERM // R
    parts = []
    for s in range(tokens.shape[0] // PERM):
        part = nn(perm, tokens[s * PERM : (s + 1) * PERM]).astype(bf16)
        parts.append(part.reshape(R, span, tokens.shape[1]))
    return parts[0] if len(parts) == 1 else jnp.concatenate(parts, 1)


def eight(t):
    return pl.ds(pl.multiple_of(t * R, R), R)


def sixteen(t):
    return pl.ds(pl.multiple_of(t * 2 * R, 2 * R), 2 * R)


def normed_edge(edge, gain):
    e = edge.astype(f32)
    inv = lax.rsqrt(jnp.mean(e * e, -1, keepdims=True) + epsilon)
    return (e * inv * gain).astype(bf16).astype(f32)


def set_limits(scal, limit):
    row = lax.broadcasted_iota(jnp.int32, limit.shape, 0)
    value = jnp.zeros(limit.shape, jnp.int32)
    for r in range(R):
        value = jnp.where(row == r, scal[SCALARS + r], value)
    limit[...] = value


def halves(ref, pair):
    both = ref[sixteen(pair), :].astype(f32)
    return both[:R], both[R:]


def front_kernel(scal, x, perm, edge, gain, convw, wg, bias, wc, c_out, zl_out, kh_out, ends, ext, state, limit):
    step = pl.program_id(0)
    tb = x.shape[1]
    m = tb * R
    halo = edge.shape[0]
    taps = convw.shape[0]

    @pl.when(step == 0)
    def _():
        set_limits(scal, limit)
        ext[0:halo, :] = normed_edge(edge[...], gain[...])
        state[0:R, :] = jnp.ones((R, state.shape[1]), f32)
        state[R:, :] = jnp.zeros((R, state.shape[1]), f32)

    xp = position_major(perm[...], x[...])
    inv = lax.rsqrt(jnp.mean(xp * xp, -1, keepdims=True) + epsilon)
    ext[halo:, :] = (xp * inv * gain[...]).astype(bf16).astype(f32)
    conv = convw[0:1, :] * ext[halo:, :]
    for k in range(1, taps):
        lo = halo - k * R
        conv = conv + convw[k : k + 1, :] * ext[lo : lo + m, :]
    ext[0:halo, :] = ext[m : m + halo, :]
    cb = conv.astype(bf16)
    c_out[...] = cb
    kz = nn(cb, wg[...]) + bias[...]
    zs = 1.0 / (1.0 + jnp.exp(-kz))
    width = zs.shape[1]
    zs = zs.reshape(tb, R, width)
    pos = scal[0] + step * tb + lax.broadcasted_iota(jnp.int32, (tb, R, width), 0)
    zl_out[...] = jnp.where(pos < limit[...][None], zs, 0.0).reshape(m, width).astype(bf16)
    kh_out[...] = nn(cb, wc[...]).astype(bf16)

    def body(u, carry):
        prod, h = carry
        za, zb = halves(zl_out, u)
        ka, kb = halves(kh_out, u)
        a = 1.0 - za
        b = 1.0 - zb
        return prod * (a * b), (h * a + za * ka) * b + zb * kb

    prod, h = lax.fori_loop(0, tb // 2, body, (state[0:R, :], state[R:, :]), unroll=4)
    state[0:R, :] = prod
    state[R:, :] = h
    ends[0:R, :] = prod
    ends[R:, :] = h


def gelu_parts(p):
    k0 = 0.7978845608028654
    p2 = p * p
    th = jnp.tanh(p * (k0 + (k0 * 0.044715) * p2))
    ht = 0.5 + 0.5 * th
    return p * ht, ht + (2.0 * p) * (ht - ht * ht) * (k0 + (3.0 * k0 * 0.044715) * p2)


def da_kernel(g, perm, wd, gl_out, da_out):
    gl = position_major(perm[...], g[...]).astype(bf16)
    gl_out[...] = gl
    da_out[...] = nt(gl, wd[...]).astype(bf16)


def core_kernel(scal, x, perm, gl, da, zl, kh, other, *refs, fchunk, hops):
    msgs = refs[:hops]
    wo, mgain, wu = refs[hops : hops + 3]
    r1_out, y_out, hp_out, n2_out, act_out, dp_out, dm_out, dr1_out, dh_out, back, mg = refs[hops + 3 : hops + 14]
    state, limit, run = refs[hops + 14 :]
    step = pl.program_id(0)
    tb = x.shape[1]
    m = tb * R
    width, feed = wu.shape
    hidden = wo.shape[0]

    @pl.when(step == 0)
    def _():
        set_limits(scal, limit)
        h = jnp.zeros((R, hidden), f32)
        for msg in reversed(msgs):
            both = msg[...].astype(f32)
            h = jnp.exp(both[0:R, :]) * h + both[R:, :]
        state[...] = jnp.where(scal[1] == 1, other[0:R, :] * h + other[R:, :], h)
        run[...] = jnp.ones((R, hidden), f32)
        back[...] = jnp.zeros(back.shape, f32)
        mg[...] = jnp.zeros(mg.shape, f32)

    first = scal[0] + step * tb
    lens = limit[...]

    def body(u, h):
        t = u * 2
        za, zb = halves(zl, u)
        ka, kb = halves(kh, u)
        ha = h - za * h + za * ka
        hb = ha - zb * ha + zb * kb
        hp_out[sixteen(u), :] = jnp.concatenate([h, ha], 0).astype(bf16)
        ya = jnp.where(first + t < lens, ha, 0.0)
        yb = jnp.where(first + t + 1 < lens, hb, 0.0)
        y_out[sixteen(u), :] = jnp.concatenate([ya, yb], 0).astype(bf16)
        return hb

    state[...] = lax.fori_loop(0, tb // 2, body, state[...], unroll=2)
    r1 = position_major(perm[...], x[...]) + nn(y_out[...], wo[...])
    r1_out[...] = r1
    inv = lax.rsqrt(jnp.mean(r1 * r1, -1, keepdims=True) + epsilon)
    n2 = (r1 * inv * mgain[...]).astype(bf16)
    n2_out[...] = n2
    for f in range(0, feed, fchunk):
        cols = slice(f, f + fchunk)
        a, slope = gelu_parts(nn(n2, wu[:, cols]))
        act_out[:, cols] = a.astype(bf16)
        dp_out[:, cols] = (da[:, cols].astype(f32) * slope).astype(bf16)
    dn2 = nt(dp_out[...], wu[...])
    r1 = r1_out[...]
    mg[...] += jnp.sum((dn2 * r1 * inv).reshape(tb, R, width), 0)
    s = mgain[...] * dn2
    mean = jnp.mean(s * r1, -1, keepdims=True)
    dr1 = gl[...].astype(f32) + inv * (s - r1 * (inv * inv * mean))
    dr1_out[...] = dr1
    dm = dr1.astype(bf16)
    dm_out[...] = dm
    dh = nt(dm, wo[...]).reshape(tb, R, hidden)
    pos = first + lax.broadcasted_iota(jnp.int32, (tb, R, hidden), 0)
    dh_out[...] = jnp.where(pos < lens[None], dh, 0.0).reshape(m, hidden).astype(bf16)

    def adjoint(u, carry):
        prod, total = carry
        za, zb = halves(zl, u)
        da, db = halves(dh_out, u)
        pa = prod - za * prod
        pb = pa - zb * pa
        return pb, total + (pa * da + pb * db)

    prod, total = lax.fori_loop(0, tb // 2, adjoint, (run[...], back[...]), unroll=4)
    run[...] = prod
    back[...] = total


def ffn_grad_kernel(scal, act, gl, n2, dp, send, keep, tile):
    step = pl.program_id(0)
    width = n2.shape[1]
    rows1 = act.shape[1] * 4 // SLOTS
    rows2 = width // SLOTS
    part = tn(act[...], gl[...]).astype(bf16)
    per = act.shape[1] // rows1

    def rows_of_half(dst, sel):
        for i in range(per):
            pos = (((step & 1) * per + i) ^ sel) * PIECE1
            dst[pl.ds(pl.multiple_of(pos, 16), rows1), :] = part[i * rows1 : (i + 1) * rows1]

    @pl.when(step < 2)
    def _():
        rows_of_half(send, scal[3])

    @pl.when(step >= 2)
    def _():
        rows_of_half(keep, scal[2])

    tile[...] = tn(n2[...], dp[...]).astype(bf16)
    for dst, half, sel in ((send, 1 - scal[1], scal[3]), (keep, scal[1], scal[2])):
        for i in range(SLOTS // 2):
            src = pl.multiple_of(half * (width // 2) + i * rows2, 16)
            pos = (i ^ sel) * PIECE1 + rows1 + step * rows2
            dst[pl.ds(pl.multiple_of(pos, 16), rows2), :] = tile[pl.ds(src, rows2), :]


def out_grad_kernel(y, dm, grad):
    grad[...] = tn(y[...], dm[...]).astype(bf16)


def gate_kernel(scal, dh, zl, kh, hp, c, ograd, other, fother, *refs, blocks, hops):
    msgs = refs[:hops]
    wg, wc = refs[hops : hops + 2]
    send, keep, dkz_out, dkh_out, edge_out, bias_out = refs[hops + 3 : hops + 9]
    state, cs, dkz, dkh = refs[hops + 9 :]
    step = pl.program_id(0)
    m = dh.shape[0]
    tb = m // R
    block = blocks - 1 - step

    @pl.when(step == 0)
    def _():
        mm = jnp.zeros(state.shape, f32)
        for msg in reversed(msgs):
            both = msg[...].astype(f32)
            mm = jnp.exp(both[0:R, :]) * mm + both[R:, :]
        state[...] = jnp.where(scal[1] == 0, fother[...] + other[0:R, :] * mm, mm)
        bias_out[...] = jnp.zeros(bias_out.shape, f32)

    @pl.when(step < blocks)
    def _():
        def body(u, carry):
            mm, bias = carry
            w = tb // 2 - 1 - u
            ha, hb = halves(hp, w)
            za, zb = halves(zl, w)
            da, db = halves(dh, w)
            ka, kb = halves(kh, w)
            lam = db + mm
            sb = lam * zb
            mm = lam - sb
            kb = (sb - sb * zb) * (kb - hb)
            lam = da + mm
            sa = lam * za
            mm = lam - sa
            ka = (sa - sa * za) * (ka - ha)
            kk = jnp.concatenate([ka, kb], 0).astype(bf16)
            dkz_out[sixteen(w), :] = kk
            dkh_out[sixteen(w), :] = jnp.concatenate([sa, sb], 0).astype(bf16)
            kf = kk.astype(f32)
            return mm, bias + kf[:R, :] + kf[R:, :]

        mm, bias = lax.fori_loop(0, tb // 2, body, (state[...], bias_out[...]), unroll=2)
        state[...] = mm
        bias_out[...] = bias
        rows = pl.ds(pl.multiple_of(block * m, m), m)
        dkz[rows, :] = dkz_out[...]
        dkh[rows, :] = dkh_out[...]
        cs[rows, :] = c[...]

    def emit(dst, half, sel):
        width = cs.shape[1]
        hidden = dkz.shape[1]
        ccols = pl.ds(pl.multiple_of(half * (width // 2), width // 2), width // 2)
        cvals = cs[:, ccols]
        rows = width // SLOTS
        at = 0
        for grads in (dkz, dkh):
            for q in range(hidden // width):
                part = tn(cvals, grads[:, q * width : (q + 1) * width]).astype(bf16)
                for i in range(SLOTS // 2):
                    pos = (i ^ sel) * PIECE2 + at
                    dst[pl.ds(pl.multiple_of(pos, 16), rows), :] = part[i * rows : (i + 1) * rows]
                at += rows
        orows = hidden // SLOTS
        for i in range(SLOTS // 2):
            pos = (i ^ sel) * PIECE2 + at
            src = pl.multiple_of(half * (hidden // 2) + i * orows, 16)
            dst[pl.ds(pl.multiple_of(pos, 16), orows), :] = ograd[pl.ds(src, orows), :]

    @pl.when(step == blocks)
    def _():
        emit(send, 1 - scal[1], scal[3])

    @pl.when(step == blocks + 1)
    def _():
        emit(keep, scal[1], scal[2])
        span = edge_out.shape[0]
        edge_out[...] = (nt(dkz[0:span, :], wg[...]) + nt(dkh[0:span, :], wc[...])).astype(bf16)


def tail_kernel(x, dr1, dkz, dkh, pm, back_pm, edge, after, gain, convw, wg, wc, order, grad, sums, uext, dext, *, blocks):
    step = pl.program_id(0)
    tb = x.shape[1]
    m = tb * R
    halo = edge.shape[0]
    taps = convw.shape[0]
    width = gain.shape[1]

    @pl.when(step == 0)
    def _():
        uext[0:halo, :] = normed_edge(edge[...], gain[...])
        dext[blocks * m :, :] = after[...].astype(f32)
        sums[...] = jnp.zeros(sums.shape, f32)

    @pl.when(step < blocks)
    def _():
        rows = pl.ds(pl.multiple_of(step * m, m), m)
        dext[rows, :] = nt(dkz[...], wg[...]) + nt(dkh[...], wc[...])

    @pl.when(step >= blocks)
    def _():
        xp = position_major(pm[...], x[...])
        inv = lax.rsqrt(jnp.mean(xp * xp, -1, keepdims=True) + epsilon)
        xn = xp * inv
        uext[halo:, :] = (xn * gain[...]).astype(bf16).astype(f32)
        start = (step - blocks) * m
        here = dext[pl.ds(pl.multiple_of(start, R), m), :]
        du = convw[0:1, :] * here
        for k in range(taps):
            lo = halo - k * R
            part = (here * uext[lo : lo + m, :]).reshape(tb, R, width)
            sums[(k + 1) * R : (k + 2) * R, :] += jnp.sum(part, 0)
            if k:
                du = du + convw[k : k + 1, :] * dext[pl.ds(pl.multiple_of(start + k * R, R), m), :]
        uext[0:halo, :] = uext[m : m + halo, :]
        sums[0:R, :] += jnp.sum((du * xn).reshape(tb, R, width), 0)
        s1 = gain[...] * du
        mean = jnp.mean(s1 * xn, -1, keepdims=True)
        gin = dr1[...] + inv * (s1 - xn * mean)
        grad[...] = row_major(back_pm[...], gin.astype(bf16))


def output_kernel(r1, act, perm, wd, order, out):
    total = r1[...] + nn(act[...], wd[...])
    out[...] = row_major(perm[...], total.astype(bf16))


def spread_kernel(scal, mine, theirs, *outs, piece, plan):
    mine_now = (pl.program_id(0) >> 1) == scal[1]

    def emit(src, low):
        for a in range(8):
            base = (a ^ low) * piece
            at = 0
            for out, rows, columns in plan:
                ref = outs[out]
                for q in range(columns):
                    width = src.shape[1]
                    part = src[pl.ds(pl.multiple_of(base + at, 16), rows), :].astype(f32)
                    ref[a * rows : (a + 1) * rows, q * width : (q + 1) * width] = part
                    at += rows

    @pl.when(mine_now)
    def _():
        emit(mine, scal[2] & 7)

    @pl.when(jnp.logical_not(mine_now))
    def _():
        emit(theirs, scal[3] & 7)


def spread(scal, mine, theirs, piece, plan, shapes, name):
    width = mine.shape[1]
    near = lambda g, s: (jnp.clip(g - 2 * s[1], 0, 1) ^ (s[2] >> 3), 0)
    far = lambda g, s: (jnp.clip(g - 2 * (1 - s[1]), 0, 1) ^ (s[3] >> 3), 0)
    return pl.pallas_call(
        functools.partial(spread_kernel, piece=piece, plan=plan),
        grid_spec=pltpu.PrefetchScalarGridSpec(
            num_scalar_prefetch=1,
            grid=(4,),
            in_specs=[pl.BlockSpec((8 * piece, width), near), pl.BlockSpec((8 * piece, width), far)],
            out_specs=[pl.BlockSpec((dims[0] // 4, dims[1]), lambda g, s: (g, 0)) for dims in shapes],
        ),
        out_shape=[shape(dims) for dims in shapes],
        compiler_params=params(60),
        cost_estimate=cost(0, 6 * sum(dims[0] * dims[1] for dims in shapes)),
        name=name,
    )(scal, mine, theirs)


def params(mib):
    return pltpu.CompilerParams(
        dimension_semantics=("arbitrary",), vmem_limit_bytes=mib * 1024 * 1024
    )


def cost(flops, moved):
    return pl.CostEstimate(flops=flops, bytes_accessed=moved, transcendentals=0)


def shape(dims, kind=f32):
    return jax.ShapeDtypeStruct(dims, kind)


ORDER = pl.BlockSpec(memory_space=pl.ANY)


def whole(array):
    zeros = (0,) * array.ndim
    return pl.BlockSpec(array.shape, lambda *a: zeros, pipeline_mode=pl.Buffered(1))


def passed_along(value, axis, steps):
    count = lax.axis_size(axis)
    leading, last = (max(0, -steps), min(count, count - steps))
    return lax.ppermute(value, axis, [(source, source + steps) for source in range(leading, last)])


def flat_permute(value, pairs):
    return lax.ppermute(value, ("seq", "row"), pairs)


def stage_bits():
    row_bits = lax.axis_size("row").bit_length() - 1
    seq_bits = lax.axis_size("seq").bit_length() - 1
    plane = list(range(row_bits))
    line = [row_bits + 1 + z for z in range(seq_bits - 1)]
    cut = row_bits // 2
    return (plane + line, plane[cut:] + plane[:cut] + line[::-1])


def slot_of(flat, bits):
    slot = 0
    for k in range(4):
        slot = slot * 2 + ((flat >> bits[k]) & 1)
    return slot


def halving_pairs(stage):
    row_bits = lax.axis_size("row").bit_length() - 1
    orders = stage_bits()
    devices = lax.axis_size("row") * lax.axis_size("seq")
    return [(d, d ^ (1 << orders[(d >> row_bits) & 1][stage])) for d in range(devices)]


def core_pairs():
    row_bits = lax.axis_size("row").bit_length() - 1
    devices = lax.axis_size("row") * lax.axis_size("seq")
    return [(d, d ^ (1 << row_bits)) for d in range(devices)]


def added(a, b):
    return (a.astype(f32) + b.astype(f32)).astype(bf16)


class Halving:
    def __init__(self, send, keep):
        self.stage = 0
        self.keep = keep
        self.recv = flat_permute(send, core_pairs())
        self.total = None

    def advance(self, *order):
        if order:
            self.recv, *_ = lax.optimization_barrier((self.recv,) + order)
        stages = len(stage_bits()[0])
        k = self.stage
        self.stage += 1
        if k < 4:
            half = self.keep.shape[0] // 2
            self.send = added(self.keep[half:], self.recv[half:])
            self.keep = added(self.keep[:half], self.recv[:half])
            self.recv = flat_permute(self.send, halving_pairs(k))
            return
        if k == 4:
            self.total = added(self.keep, self.recv)
            for extra in range(4, stages):
                self.total = added(self.total, flat_permute(self.total, halving_pairs(extra)))
        else:
            self.total = jnp.concatenate([self.total, self.recv], 0)
        self.recv = flat_permute(self.total, halving_pairs(7 - k) if k < 8 else core_pairs())

    def finished(self):
        while self.stage < 9:
            self.advance()
        return self.total, self.recv


def chip_shift(value, steps):
    return passed_along(value, "seq", 2 * steps)


def per_device(
    inputs,
    lengths,
    norm_gain,
    conv_weight,
    gate_weight,
    gate_bias,
    cand_weight,
    out_weight,
    mlp_gain,
    up_weight,
    down_weight,
    cotangent,
):
    rows, span, width = inputs.shape
    hidden = gate_weight.shape[1]
    feed = up_weight.shape[1]
    taps = conv_weight.shape[0]
    margin = taps - 1
    tokens = rows * span
    tb = 32
    blocks = span // tb
    m = tb * R
    seq = lax.axis_index("seq")
    core = seq & 1
    chips = lax.axis_size("seq") // 2
    hops = chips - 1
    flat = seq * lax.axis_size("row") + lax.axis_index("row")
    slots = [slot_of(flat, bits) for bits in stage_bits()]
    here = jnp.where(core == 0, slots[0], slots[1])
    mate = jnp.where(core == 0, slots[1], slots[0])
    scal = jnp.concatenate([jnp.stack([seq * span, core, here, mate]).astype(jnp.int32), lengths])
    gain1 = norm_gain.reshape(1, width)
    gain2 = mlp_gain.reshape(1, width)
    bias = gate_bias.reshape(1, hidden)
    to_pm, to_rm = token_order()

    edge = inputs[:, span - margin :, :].swapaxes(0, 1).reshape(margin * rows, width)
    edge = passed_along(edge, "seq", 1)

    last = blocks - 1
    clamp = lambda i: jnp.minimum(i, last)
    late = lambda i: jnp.maximum(i - blocks, 0)

    def rm(index):
        return pl.BlockSpec((rows, tb, width), lambda i, *s: (0, index(i), 0))

    def tok(w, index=clamp):
        return pl.BlockSpec((m, w), lambda i, *s: (index(i), 0))

    def rtok(w):
        return tok(w, lambda i: last - clamp(i))

    def fixed(dims):
        zeros = (0,) * len(dims)
        return pl.BlockSpec(dims, lambda i, *s: zeros)

    def call(kernel, name, grid, ins, outs, scratch, operands, estimate, scalars=True):
        spec = pltpu.PrefetchScalarGridSpec(
            num_scalar_prefetch=int(scalars),
            grid=(grid,),
            in_specs=ins,
            out_specs=[o[1] for o in outs],
            scratch_shapes=scratch,
        )
        return pl.pallas_call(
            kernel,
            grid_spec=spec,
            out_shape=[o[0] for o in outs],
            compiler_params=params(60),
            cost_estimate=estimate,
            name=name,
        )(*operands)

    def rows_of(w, kind, spec=tok):
        return shape((tokens, w), kind), spec(w)

    c, zl, kh, ends = call(
        front_kernel, "front", blocks,
        [
            rm(clamp), whole(to_pm), whole(edge), whole(gain1), whole(conv_weight),
            whole(gate_weight), whole(bias), whole(cand_weight),
        ],
        [
            rows_of(width, bf16), rows_of(hidden, bf16), rows_of(hidden, bf16),
            (shape((2 * R, hidden)), fixed((2 * R, hidden))),
        ],
        [
            pltpu.VMEM((margin * R + m, width), f32),
            pltpu.VMEM((2 * R, hidden), f32),
            pltpu.VMEM((R, hidden), jnp.int32),
        ],
        (scal, inputs, to_pm, edge, gain1, conv_weight, gate_weight, bias, cand_weight),
        cost(4 * tokens * width * hidden, 16 * tokens * hidden),
    )

    other = flat_permute(ends, core_pairs())
    first = jnp.where(core == 0, ends, other)
    second = jnp.where(core == 0, other, ends)
    decay = jnp.log(jnp.maximum(ends[:R] * other[:R], 1e-37))
    message = jnp.concatenate([decay, second[:R] * first[R:] + second[R:]], 0).astype(bf16)
    forward = [chip_shift(message, k) for k in range(1, chips)]

    gl, da = call(
        da_kernel, "da", blocks,
        [rm(clamp), whole(to_pm), whole(down_weight)],
        [rows_of(width, bf16), rows_of(feed, bf16)],
        [],
        (cotangent, to_pm, down_weight),
        cost(2 * tokens * width * feed, 8 * tokens * hidden),
        scalars=False,
    )

    r1, y, hp, n2, act, dp, dm, dr1, dh, back, mg = call(
        functools.partial(core_kernel, fchunk=512, hops=hops), "core", blocks,
        [
            rm(clamp), whole(to_pm), tok(width), tok(feed), tok(hidden), tok(hidden), whole(other),
            *[whole(f) for f in forward], whole(out_weight), whole(gain2), whole(up_weight),
        ],
        [
            rows_of(width, f32), rows_of(hidden, bf16), rows_of(hidden, bf16), rows_of(width, bf16),
            rows_of(feed, bf16), rows_of(feed, bf16), rows_of(width, bf16), rows_of(width, f32),
            rows_of(hidden, bf16),
            (shape((R, hidden)), fixed((R, hidden))), (shape((R, width)), fixed((R, width))),
        ],
        [
            pltpu.VMEM((R, hidden), f32),
            pltpu.VMEM((R, hidden), jnp.int32),
            pltpu.VMEM((R, hidden), f32),
        ],
        (scal, inputs, to_pm, gl, da, zl, kh, other, *forward, out_weight, gain2, up_weight),
        cost(4 * tokens * width * (hidden + feed), 48 * tokens * hidden),
    )

    fother = flat_permute(back, core_pairs())
    lower = jnp.where(core == 0, back, fother)
    upper = jnp.where(core == 0, fother, back)
    message = jnp.concatenate([decay, lower + first[:R] * upper], 0).astype(bf16)
    act, message = lax.optimization_barrier((act, message))
    backward = [chip_shift(message, -k) for k in range(1, chips)]

    quarter = feed // 4
    half1 = (shape((SLOTS // 2 * PIECE1, width), bf16), fixed((SLOTS // 2 * PIECE1, width)))
    act_block = lambda i, s: (0, jnp.where(i < 2, 1 - s[1], s[1]) * 2 + (i & 1))
    send1, keep1 = call(
        ffn_grad_kernel, "ffn_grad", 4,
        [
            pl.BlockSpec((tokens, quarter), act_block), whole(gl), whole(n2),
            pl.BlockSpec((tokens, quarter), lambda i, s: (0, i)),
        ],
        [half1, half1],
        [pltpu.VMEM((width, quarter), bf16)],
        (scal, act, gl, n2, dp),
        cost(4 * tokens * width * feed, 12 * tokens * hidden),
    )
    send1, *backward = lax.optimization_barrier((send1, *backward))
    chunk1 = Halving(send1, keep1)

    otile = hidden // 2
    (ograd,) = call(
        out_grad_kernel, "out_grad", 2,
        [pl.BlockSpec((tokens, otile), lambda i: (0, i)), whole(dm)],
        [(shape((hidden, width), bf16), pl.BlockSpec((otile, width), lambda i: (i, 0)))],
        [],
        (y, dm),
        cost(2 * tokens * width * hidden, 4 * tokens * hidden),
        scalars=False,
    )
    chunk1.advance(ograd)

    half2 = (shape((SLOTS // 2 * PIECE2, width), bf16), fixed((SLOTS // 2 * PIECE2, width)))
    send2, keep2, dkz, dkh, edge_dc, bias_part = call(
        functools.partial(gate_kernel, blocks=blocks, hops=hops), "gates", blocks + 2,
        [
            rtok(hidden), rtok(hidden), rtok(hidden), rtok(hidden), rtok(width),
            whole(ograd), whole(other), whole(fother), *[whole(f) for f in backward],
            whole(gate_weight), whole(cand_weight), ORDER,
        ],
        [
            half2, half2, rows_of(hidden, bf16, rtok), rows_of(hidden, bf16, rtok),
            (shape((4 * R, width), bf16), fixed((4 * R, width))),
            (shape((R, hidden)), fixed((R, hidden))),
        ],
        [
            pltpu.VMEM((R, hidden), f32),
            pltpu.VMEM((tokens, width), bf16),
            pltpu.VMEM((tokens, hidden), bf16),
            pltpu.VMEM((tokens, hidden), bf16),
        ],
        (
            scal, dh, zl, kh, hp, c, ograd, other, fother, *backward,
            gate_weight, cand_weight, chunk1.send,
        ),
        cost(8 * tokens * width * hidden, 24 * tokens * hidden),
    )
    send2, chunk1.recv = lax.optimization_barrier((send2, chunk1.recv))
    chunk2 = Halving(send2, keep2)
    after = passed_along(edge_dc[: margin * R], "seq", -1)
    chunk1.advance()

    input_grad, sums = call(
        functools.partial(tail_kernel, blocks=blocks), "tail", 2 * blocks,
        [
            rm(late), tok(width, late), tok(hidden), tok(hidden), whole(to_pm), whole(to_rm), whole(edge),
            whole(after), whole(gain1), whole(conv_weight), whole(gate_weight), whole(cand_weight),
            ORDER,
        ],
        [
            (shape((rows, span, width), bf16), rm(late)),
            (shape(((taps + 1) * R, width)), fixed(((taps + 1) * R, width))),
        ],
        [
            pltpu.VMEM((margin * R + m, width), f32),
            pltpu.VMEM((margin * R + tokens, width), f32),
        ],
        (
            inputs, dr1, dkz, dkh, to_pm, to_rm, edge, after, gain1, conv_weight, gate_weight, cand_weight,
            chunk1.send,
        ),
        cost(4 * tokens * width * hidden, 24 * tokens * width),
        scalars=False,
    )
    small = jnp.concatenate(
        [
            sums.reshape(taps + 1, R, width).sum(1),
            mg.sum(0, keepdims=True),
            bias_part.sum(0).reshape(hidden // width, width),
        ],
        0,
    )
    chunk2.advance(small)
    (output,) = call(
        output_kernel, "output", blocks,
        [tok(width), tok(feed), whole(to_rm), whole(down_weight), ORDER],
        [(shape((rows, span, width), bf16), rm(clamp))],
        [],
        (r1, act, to_rm, down_weight, chunk2.send),
        cost(2 * tokens * width * feed, 8 * tokens * hidden),
        scalars=False,
    )
    small, output = lax.optimization_barrier((small + flat_permute(small, core_pairs()), output))
    for k in range(len(stage_bits()[0])):
        if k < 8:
            chunk2.advance(small)
        small = small + flat_permute(small, halving_pairs(k))
    mine2, theirs2 = chunk2.finished()
    mine1, theirs1 = chunk1.finished()
    dgrad, ugrad = spread(
        scal, mine1, theirs1, PIECE1,
        ((0, feed // SLOTS, 1), (1, width // SLOTS, feed // width)),
        ((feed, width), (width, feed)), "spread_ffn",
    )
    ggrad, cgrad, ograd = spread(
        scal, mine2, theirs2, PIECE2,
        ((0, width // SLOTS, hidden // width), (1, width // SLOTS, hidden // width),
         (2, hidden // SLOTS, 1)),
        ((width, hidden), (width, hidden), (hidden, width)), "spread_gates",
    )
    return (
        output,
        input_grad,
        small[0],
        small[1 : taps + 1],
        ggrad,
        small[taps + 2 :].reshape(hidden),
        cgrad,
        ograd,
        small[taps + 1],
        ugrad,
        dgrad,
    )


def solution(mesh):
    sharded = P("row", "seq", None)
    in_specs = (sharded, P("row")) + (P(),) * 9 + (sharded,)
    out_specs = (sharded, sharded) + (P(),) * 9
    return jax.shard_map(
        per_device, mesh=mesh, in_specs=in_specs, out_specs=out_specs, check_vma=False
    )
```

```python
import functools

import jax
import jax.numpy as jnp
import numpy as np
from jax import lax
from jax.experimental import pallas as pl
from jax.experimental.pallas import tpu as pltpu
from jax.sharding import PartitionSpec as P

epsilon = 1e-06
f32 = jnp.float32
bf16 = jnp.bfloat16
R = 8
PERM = 256
SCALARS = 4
SLOTS = 32
PIECE1 = 128
PIECE2 = 96


def nn(a, b):
    return lax.dot_general(a, b, (((1,), (0,)), ((), ())), preferred_element_type=f32)


def nt(a, b):
    return lax.dot_general(a, b, (((1,), (1,)), ((), ())), preferred_element_type=f32)


def tn(a, b):
    return lax.dot_general(a, b, (((0,), (0,)), ((), ())), preferred_element_type=f32)


def token_order():
    out = np.arange(PERM)
    source = (out % R) * (PERM // R) + out // R
    to_pm = np.zeros((PERM, PERM), np.float32)
    to_pm[out, source] = 1
    return jnp.asarray(to_pm, bf16), jnp.asarray(to_pm.T, bf16)


def position_major(perm, block):
    span = PERM // R
    parts = []
    for s in range(block.shape[1] // span):
        part = block[:, s * span : (s + 1) * span, :].reshape(PERM, block.shape[2])
        parts.append(nn(perm, part))
    return parts[0] if len(parts) == 1 else jnp.concatenate(parts, 0)


def row_major(perm, tokens):
    span = PERM // R
    parts = []
    for s in range(tokens.shape[0] // PERM):
        part = nn(perm, tokens[s * PERM : (s + 1) * PERM]).astype(bf16)
        parts.append(part.reshape(R, span, tokens.shape[1]))
    return parts[0] if len(parts) == 1 else jnp.concatenate(parts, 1)


def eight(t):
    return pl.ds(pl.multiple_of(t * R, R), R)


def sixteen(t):
    return pl.ds(pl.multiple_of(t * 2 * R, 2 * R), 2 * R)


def normed_edge(edge, gain):
    e = edge.astype(f32)
    inv = lax.rsqrt(jnp.mean(e * e, -1, keepdims=True) + epsilon)
    return (e * inv * gain).astype(bf16).astype(f32)


def set_limits(scal, limit):
    row = lax.broadcasted_iota(jnp.int32, limit.shape, 0)
    value = jnp.zeros(limit.shape, jnp.int32)
    for r in range(R):
        value = jnp.where(row == r, scal[SCALARS + r], value)
    limit[...] = value


def halves(ref, pair):
    both = ref[sixteen(pair), :].astype(f32)
    return both[:R], both[R:]


def front_kernel(scal, x, perm, edge, gain, convw, wg, bias, wc, c_out, zl_out, kh_out, ends, ext, state, limit):
    step = pl.program_id(0)
    tb = x.shape[1]
    m = tb * R
    halo = edge.shape[0]
    taps = convw.shape[0]

    @pl.when(step == 0)
    def _():
        set_limits(scal, limit)
        ext[0:halo, :] = normed_edge(edge[...], gain[...])
        state[0:R, :] = jnp.ones((R, state.shape[1]), f32)
        state[R:, :] = jnp.zeros((R, state.shape[1]), f32)

    xp = position_major(perm[...], x[...])
    inv = lax.rsqrt(jnp.mean(xp * xp, -1, keepdims=True) + epsilon)
    ext[halo:, :] = (xp * inv * gain[...]).astype(bf16).astype(f32)
    conv = convw[0:1, :] * ext[halo:, :]
    for k in range(1, taps):
        lo = halo - k * R
        conv = conv + convw[k : k + 1, :] * ext[lo : lo + m, :]
    ext[0:halo, :] = ext[m : m + halo, :]
    cb = conv.astype(bf16)
    c_out[...] = cb
    kz = nn(cb, wg[...]) + bias[...]
    zs = 1.0 / (1.0 + jnp.exp(-kz))
    width = zs.shape[1]
    zs = zs.reshape(tb, R, width)
    pos = scal[0] + step * tb + lax.broadcasted_iota(jnp.int32, (tb, R, width), 0)
    zl_out[...] = jnp.where(pos < limit[...][None], zs, 0.0).reshape(m, width).astype(bf16)
    kh_out[...] = nn(cb, wc[...]).astype(bf16)

    def body(u, carry):
        prod, h = carry
        za, zb = halves(zl_out, u)
        ka, kb = halves(kh_out, u)
        a = 1.0 - za
        b = 1.0 - zb
        return prod * (a * b), (h * a + za * ka) * b + zb * kb

    prod, h = lax.fori_loop(0, tb // 2, body, (state[0:R, :], state[R:, :]), unroll=4)
    state[0:R, :] = prod
    state[R:, :] = h
    ends[0:R, :] = prod
    ends[R:, :] = h


def gelu_parts(p):
    k0 = 0.7978845608028654
    p2 = p * p
    th = jnp.tanh(p * (k0 + (k0 * 0.044715) * p2))
    ht = 0.5 + 0.5 * th
    return p * ht, ht + (2.0 * p) * (ht - ht * ht) * (k0 + (3.0 * k0 * 0.044715) * p2)


def da_kernel(g, perm, wd, gl_out, da_out):
    gl = position_major(perm[...], g[...]).astype(bf16)
    gl_out[...] = gl
    da_out[...] = nt(gl, wd[...]).astype(bf16)


def core_kernel(scal, x, perm, gl, da, zl, kh, other, *refs, fchunk, hops):
    msgs = refs[:hops]
    wo, mgain, wu = refs[hops : hops + 3]
    r1_out, y_out, hp_out, n2_out, act_out, dp_out, dm_out, dr1_out, dh_out, back, mg = refs[hops + 3 : hops + 14]
    state, limit, run = refs[hops + 14 :]
    step = pl.program_id(0)
    tb = x.shape[1]
    m = tb * R
    width, feed = wu.shape
    hidden = wo.shape[0]

    @pl.when(step == 0)
    def _():
        set_limits(scal, limit)
        h = jnp.zeros((R, hidden), f32)
        for msg in reversed(msgs):
            both = msg[...].astype(f32)
            h = jnp.exp(both[0:R, :]) * h + both[R:, :]
        state[...] = jnp.where(scal[1] == 1, other[0:R, :] * h + other[R:, :], h)
        run[...] = jnp.ones((R, hidden), f32)
        back[...] = jnp.zeros(back.shape, f32)
        mg[...] = jnp.zeros(mg.shape, f32)

    first = scal[0] + step * tb
    lens = limit[...]

    def body(u, h):
        t = u * 2
        za, zb = halves(zl, u)
        ka, kb = halves(kh, u)
        ha = h - za * h + za * ka
        hb = ha - zb * ha + zb * kb
        hp_out[sixteen(u), :] = jnp.concatenate([h, ha], 0).astype(bf16)
        ya = jnp.where(first + t < lens, ha, 0.0)
        yb = jnp.where(first + t + 1 < lens, hb, 0.0)
        y_out[sixteen(u), :] = jnp.concatenate([ya, yb], 0).astype(bf16)
        return hb

    state[...] = lax.fori_loop(0, tb // 2, body, state[...], unroll=2)
    r1 = position_major(perm[...], x[...]) + nn(y_out[...], wo[...])
    r1_out[...] = r1
    inv = lax.rsqrt(jnp.mean(r1 * r1, -1, keepdims=True) + epsilon)
    n2 = (r1 * inv * mgain[...]).astype(bf16)
    n2_out[...] = n2
    for f in range(0, feed, fchunk):
        cols = slice(f, f + fchunk)
        a, slope = gelu_parts(nn(n2, wu[:, cols]))
        act_out[:, cols] = a.astype(bf16)
        dp_out[:, cols] = (da[:, cols].astype(f32) * slope).astype(bf16)
    dn2 = nt(dp_out[...], wu[...])
    r1 = r1_out[...]
    mg[...] += jnp.sum((dn2 * r1 * inv).reshape(tb, R, width), 0)
    s = mgain[...] * dn2
    mean = jnp.mean(s * r1, -1, keepdims=True)
    dr1 = gl[...].astype(f32) + inv * (s - r1 * (inv * inv * mean))
    dr1_out[...] = dr1
    dm = dr1.astype(bf16)
    dm_out[...] = dm
    dh = nt(dm, wo[...]).reshape(tb, R, hidden)
    pos = first + lax.broadcasted_iota(jnp.int32, (tb, R, hidden), 0)
    dh_out[...] = jnp.where(pos < lens[None], dh, 0.0).reshape(m, hidden).astype(bf16)

    def adjoint(u, carry):
        prod, total = carry
        za, zb = halves(zl, u)
        da, db = halves(dh_out, u)
        pa = prod - za * prod
        pb = pa - zb * pa
        return pb, total + (pa * da + pb * db)

    prod, total = lax.fori_loop(0, tb // 2, adjoint, (run[...], back[...]), unroll=4)
    run[...] = prod
    back[...] = total


def ffn_grad_kernel(scal, act, gl, n2, dp, send, keep, tile):
    step = pl.program_id(0)
    width = n2.shape[1]
    rows1 = act.shape[1] * 4 // SLOTS
    rows2 = width // SLOTS
    part = tn(act[...], gl[...]).astype(bf16)
    per = act.shape[1] // rows1

    def rows_of_half(dst, sel):
        for i in range(per):
            pos = (((step & 1) * per + i) ^ sel) * PIECE1
            dst[pl.ds(pl.multiple_of(pos, 16), rows1), :] = part[i * rows1 : (i + 1) * rows1]

    @pl.when(step < 2)
    def _():
        rows_of_half(send, scal[3])

    @pl.when(step >= 2)
    def _():
        rows_of_half(keep, scal[2])

    tile[...] = tn(n2[...], dp[...]).astype(bf16)
    for dst, half, sel in ((send, 1 - scal[1], scal[3]), (keep, scal[1], scal[2])):
        for i in range(SLOTS // 2):
            src = pl.multiple_of(half * (width // 2) + i * rows2, 16)
            pos = (i ^ sel) * PIECE1 + rows1 + step * rows2
            dst[pl.ds(pl.multiple_of(pos, 16), rows2), :] = tile[pl.ds(src, rows2), :]


def out_grad_kernel(y, dm, grad):
    grad[...] = tn(y[...], dm[...]).astype(bf16)


def gate_kernel(scal, dh, zl, kh, hp, c, ograd, other, fother, *refs, blocks, hops):
    msgs = refs[:hops]
    wg, wc = refs[hops : hops + 2]
    send, keep, dkz_out, dkh_out, edge_out, bias_out = refs[hops + 3 : hops + 9]
    state, cs, dkz, dkh = refs[hops + 9 :]
    step = pl.program_id(0)
    m = dh.shape[0]
    tb = m // R
    block = blocks - 1 - step

    @pl.when(step == 0)
    def _():
        mm = jnp.zeros(state.shape, f32)
        for msg in reversed(msgs):
            both = msg[...].astype(f32)
            mm = jnp.exp(both[0:R, :]) * mm + both[R:, :]
        state[...] = jnp.where(scal[1] == 0, fother[...] + other[0:R, :] * mm, mm)
        bias_out[...] = jnp.zeros(bias_out.shape, f32)

    @pl.when(step < blocks)
    def _():
        def body(u, carry):
            mm, bias = carry
            w = tb // 2 - 1 - u
            ha, hb = halves(hp, w)
            za, zb = halves(zl, w)
            da, db = halves(dh, w)
            ka, kb = halves(kh, w)
            lam = db + mm
            sb = lam * zb
            mm = lam - sb
            kb = (sb - sb * zb) * (kb - hb)
            lam = da + mm
            sa = lam * za
            mm = lam - sa
            ka = (sa - sa * za) * (ka - ha)
            kk = jnp.concatenate([ka, kb], 0).astype(bf16)
            dkz_out[sixteen(w), :] = kk
            dkh_out[sixteen(w), :] = jnp.concatenate([sa, sb], 0).astype(bf16)
            kf = kk.astype(f32)
            return mm, bias + kf[:R, :] + kf[R:, :]

        mm, bias = lax.fori_loop(0, tb // 2, body, (state[...], bias_out[...]), unroll=2)
        state[...] = mm
        bias_out[...] = bias
        rows = pl.ds(pl.multiple_of(block * m, m), m)
        dkz[rows, :] = dkz_out[...]
        dkh[rows, :] = dkh_out[...]
        cs[rows, :] = c[...]

    def emit(dst, half, sel):
        width = cs.shape[1]
        hidden = dkz.shape[1]
        ccols = pl.ds(pl.multiple_of(half * (width // 2), width // 2), width // 2)
        cvals = cs[:, ccols]
        rows = width // SLOTS
        at = 0
        for grads in (dkz, dkh):
            for q in range(hidden // width):
                part = tn(cvals, grads[:, q * width : (q + 1) * width]).astype(bf16)
                for i in range(SLOTS // 2):
                    pos = (i ^ sel) * PIECE2 + at
                    dst[pl.ds(pl.multiple_of(pos, 16), rows), :] = part[i * rows : (i + 1) * rows]
                at += rows
        orows = hidden // SLOTS
        for i in range(SLOTS // 2):
            pos = (i ^ sel) * PIECE2 + at
            src = pl.multiple_of(half * (hidden // 2) + i * orows, 16)
            dst[pl.ds(pl.multiple_of(pos, 16), orows), :] = ograd[pl.ds(src, orows), :]

    @pl.when(step == blocks)
    def _():
        emit(send, 1 - scal[1], scal[3])

    @pl.when(step == blocks + 1)
    def _():
        emit(keep, scal[1], scal[2])
        span = edge_out.shape[0]
        edge_out[...] = (nt(dkz[0:span, :], wg[...]) + nt(dkh[0:span, :], wc[...])).astype(bf16)


def tail_kernel(x, dr1, dkz, dkh, pm, back_pm, edge, after, gain, convw, wg, wc, order, grad, sums, uext, dext, *, blocks):
    step = pl.program_id(0)
    tb = x.shape[1]
    m = tb * R
    halo = edge.shape[0]
    taps = convw.shape[0]
    width = gain.shape[1]

    @pl.when(step == 0)
    def _():
        uext[0:halo, :] = normed_edge(edge[...], gain[...])
        dext[blocks * m :, :] = after[...].astype(f32)
        sums[...] = jnp.zeros(sums.shape, f32)

    @pl.when(step < blocks)
    def _():
        rows = pl.ds(pl.multiple_of(step * m, m), m)
        dext[rows, :] = nt(dkz[...], wg[...]) + nt(dkh[...], wc[...])

    @pl.when(step >= blocks)
    def _():
        xp = position_major(pm[...], x[...])
        inv = lax.rsqrt(jnp.mean(xp * xp, -1, keepdims=True) + epsilon)
        xn = xp * inv
        uext[halo:, :] = (xn * gain[...]).astype(bf16).astype(f32)
        start = (step - blocks) * m
        here = dext[pl.ds(pl.multiple_of(start, R), m), :]
        du = convw[0:1, :] * here
        for k in range(taps):
            lo = halo - k * R
            part = (here * uext[lo : lo + m, :]).reshape(tb, R, width)
            sums[(k + 1) * R : (k + 2) * R, :] += jnp.sum(part, 0)
            if k:
                du = du + convw[k : k + 1, :] * dext[pl.ds(pl.multiple_of(start + k * R, R), m), :]
        uext[0:halo, :] = uext[m : m + halo, :]
        sums[0:R, :] += jnp.sum((du * xn).reshape(tb, R, width), 0)
        s1 = gain[...] * du
        mean = jnp.mean(s1 * xn, -1, keepdims=True)
        gin = dr1[...] + inv * (s1 - xn * mean)
        grad[...] = row_major(back_pm[...], gin.astype(bf16))


def output_kernel(r1, act, perm, wd, order, out):
    total = r1[...] + nn(act[...], wd[...])
    out[...] = row_major(perm[...], total.astype(bf16))


def spread_kernel(scal, mine, theirs, *outs, piece, plan):
    mine_now = (pl.program_id(0) >> 1) == scal[1]

    def emit(src, low):
        for a in range(8):
            base = (a ^ low) * piece
            at = 0
            for out, rows, columns in plan:
                ref = outs[out]
                for q in range(columns):
                    width = src.shape[1]
                    part = src[pl.ds(pl.multiple_of(base + at, 16), rows), :].astype(f32)
                    ref[a * rows : (a + 1) * rows, q * width : (q + 1) * width] = part
                    at += rows

    @pl.when(mine_now)
    def _():
        emit(mine, scal[2] & 7)

    @pl.when(jnp.logical_not(mine_now))
    def _():
        emit(theirs, scal[3] & 7)


def spread(scal, mine, theirs, piece, plan, shapes, name):
    width = mine.shape[1]
    near = lambda g, s: (jnp.clip(g - 2 * s[1], 0, 1) ^ (s[2] >> 3), 0)
    far = lambda g, s: (jnp.clip(g - 2 * (1 - s[1]), 0, 1) ^ (s[3] >> 3), 0)
    return pl.pallas_call(
        functools.partial(spread_kernel, piece=piece, plan=plan),
        grid_spec=pltpu.PrefetchScalarGridSpec(
            num_scalar_prefetch=1,
            grid=(4,),
            in_specs=[pl.BlockSpec((8 * piece, width), near), pl.BlockSpec((8 * piece, width), far)],
            out_specs=[pl.BlockSpec((dims[0] // 4, dims[1]), lambda g, s: (g, 0)) for dims in shapes],
        ),
        out_shape=[shape(dims) for dims in shapes],
        compiler_params=params(16),
        cost_estimate=cost(0, 6 * sum(dims[0] * dims[1] for dims in shapes)),
        name=name,
    )(scal, mine, theirs)


def params(mib):
    return pltpu.CompilerParams(
        dimension_semantics=("arbitrary",), vmem_limit_bytes=mib * 1024 * 1024
    )


def cost(flops, moved):
    return pl.CostEstimate(flops=flops, bytes_accessed=moved, transcendentals=0)


def shape(dims, kind=f32):
    return jax.ShapeDtypeStruct(dims, kind)


ORDER = pl.BlockSpec(memory_space=pl.ANY)


def whole(array):
    zeros = (0,) * array.ndim
    return pl.BlockSpec(array.shape, lambda *a: zeros, pipeline_mode=pl.Buffered(1))


def passed_along(value, axis, steps):
    count = lax.axis_size(axis)
    leading, last = (max(0, -steps), min(count, count - steps))
    return lax.ppermute(value, axis, [(source, source + steps) for source in range(leading, last)])


def flat_permute(value, pairs):
    return lax.ppermute(value, ("seq", "row"), pairs)


def stage_bits():
    row_bits = lax.axis_size("row").bit_length() - 1
    seq_bits = lax.axis_size("seq").bit_length() - 1
    plane = list(range(row_bits))
    line = [row_bits + 1 + z for z in range(seq_bits - 1)]
    cut = row_bits // 2
    return (plane + line, plane[cut:] + plane[:cut] + line[::-1])


def slot_of(flat, bits):
    slot = 0
    for k in range(4):
        slot = slot * 2 + ((flat >> bits[k]) & 1)
    return slot


def halving_pairs(stage):
    row_bits = lax.axis_size("row").bit_length() - 1
    orders = stage_bits()
    devices = lax.axis_size("row") * lax.axis_size("seq")
    return [(d, d ^ (1 << orders[(d >> row_bits) & 1][stage])) for d in range(devices)]


def core_pairs():
    row_bits = lax.axis_size("row").bit_length() - 1
    devices = lax.axis_size("row") * lax.axis_size("seq")
    return [(d, d ^ (1 << row_bits)) for d in range(devices)]


def added(a, b):
    return (a.astype(f32) + b.astype(f32)).astype(bf16)


class Halving:
    def __init__(self, send, keep):
        self.stage = 0
        self.keep = keep
        self.recv = flat_permute(send, core_pairs())
        self.total = None

    def advance(self, *order):
        if order:
            self.recv, *_ = lax.optimization_barrier((self.recv,) + order)
        stages = len(stage_bits()[0])
        k = self.stage
        self.stage += 1
        if k < 4:
            half = self.keep.shape[0] // 2
            self.send = added(self.keep[half:], self.recv[half:])
            self.keep = added(self.keep[:half], self.recv[:half])
            self.recv = flat_permute(self.send, halving_pairs(k))
            return
        if k == 4:
            self.total = added(self.keep, self.recv)
            for extra in range(4, stages):
                self.total = added(self.total, flat_permute(self.total, halving_pairs(extra)))
        else:
            self.total = jnp.concatenate([self.total, self.recv], 0)
        self.recv = flat_permute(self.total, halving_pairs(7 - k) if k < 8 else core_pairs())

    def finished(self):
        while self.stage < 9:
            self.advance()
        return self.total, self.recv


def chip_shift(value, steps):
    return passed_along(value, "seq", 2 * steps)


def per_device(
    inputs,
    lengths,
    norm_gain,
    conv_weight,
    gate_weight,
    gate_bias,
    cand_weight,
    out_weight,
    mlp_gain,
    up_weight,
    down_weight,
    cotangent,
):
    rows, span, width = inputs.shape
    hidden = gate_weight.shape[1]
    feed = up_weight.shape[1]
    taps = conv_weight.shape[0]
    margin = taps - 1
    tokens = rows * span
    tb = 32
    blocks = span // tb
    m = tb * R
    seq = lax.axis_index("seq")
    core = seq & 1
    chips = lax.axis_size("seq") // 2
    hops = chips - 1
    flat = seq * lax.axis_size("row") + lax.axis_index("row")
    slots = [slot_of(flat, bits) for bits in stage_bits()]
    here = jnp.where(core == 0, slots[0], slots[1])
    mate = jnp.where(core == 0, slots[1], slots[0])
    scal = jnp.concatenate([jnp.stack([seq * span, core, here, mate]).astype(jnp.int32), lengths])
    gain1 = norm_gain.reshape(1, width)
    gain2 = mlp_gain.reshape(1, width)
    bias = gate_bias.reshape(1, hidden)
    to_pm, to_rm = token_order()

    edge = inputs[:, span - margin :, :].swapaxes(0, 1).reshape(margin * rows, width)
    edge = passed_along(edge, "seq", 1)

    last = blocks - 1
    clamp = lambda i: jnp.minimum(i, last)
    late = lambda i: jnp.maximum(i - blocks, 0)

    def rm(index):
        return pl.BlockSpec((rows, tb, width), lambda i, *s: (0, index(i), 0))

    def tok(w, index=clamp):
        return pl.BlockSpec((m, w), lambda i, *s: (index(i), 0))

    def rtok(w):
        return tok(w, lambda i: last - clamp(i))

    def fixed(dims):
        zeros = (0,) * len(dims)
        return pl.BlockSpec(dims, lambda i, *s: zeros)

    def call(kernel, name, grid, ins, outs, scratch, operands, estimate, scalars=True):
        spec = pltpu.PrefetchScalarGridSpec(
            num_scalar_prefetch=int(scalars),
            grid=(grid,),
            in_specs=ins,
            out_specs=[o[1] for o in outs],
            scratch_shapes=scratch,
        )
        return pl.pallas_call(
            kernel,
            grid_spec=spec,
            out_shape=[o[0] for o in outs],
            compiler_params=params(16),
            cost_estimate=estimate,
            name=name,
        )(*operands)

    def rows_of(w, kind, spec=tok):
        return shape((tokens, w), kind), spec(w)

    c, zl, kh, ends = call(
        front_kernel, "front", blocks,
        [
            rm(clamp), whole(to_pm), whole(edge), whole(gain1), whole(conv_weight),
            whole(gate_weight), whole(bias), whole(cand_weight),
        ],
        [
            rows_of(width, bf16), rows_of(hidden, bf16), rows_of(hidden, bf16),
            (shape((2 * R, hidden)), fixed((2 * R, hidden))),
        ],
        [
            pltpu.VMEM((margin * R + m, width), f32),
            pltpu.VMEM((2 * R, hidden), f32),
            pltpu.VMEM((R, hidden), jnp.int32),
        ],
        (scal, inputs, to_pm, edge, gain1, conv_weight, gate_weight, bias, cand_weight),
        cost(4 * tokens * width * hidden, 16 * tokens * hidden),
    )

    other = flat_permute(ends, core_pairs())
    first = jnp.where(core == 0, ends, other)
    second = jnp.where(core == 0, other, ends)
    decay = jnp.log(jnp.maximum(ends[:R] * other[:R], 1e-37))
    message = jnp.concatenate([decay, second[:R] * first[R:] + second[R:]], 0).astype(bf16)
    forward = [chip_shift(message, k) for k in range(1, chips)]

    gl, da = call(
        da_kernel, "da", blocks,
        [rm(clamp), whole(to_pm), whole(down_weight)],
        [rows_of(width, bf16), rows_of(feed, bf16)],
        [],
        (cotangent, to_pm, down_weight),
        cost(2 * tokens * width * feed, 8 * tokens * hidden),
        scalars=False,
    )

    r1, y, hp, n2, act, dp, dm, dr1, dh, back, mg = call(
        functools.partial(core_kernel, fchunk=512, hops=hops), "core", blocks,
        [
            rm(clamp), whole(to_pm), tok(width), tok(feed), tok(hidden), tok(hidden), whole(other),
            *[whole(f) for f in forward], whole(out_weight), whole(gain2), whole(up_weight),
        ],
        [
            rows_of(width, f32), rows_of(hidden, bf16), rows_of(hidden, bf16), rows_of(width, bf16),
            rows_of(feed, bf16), rows_of(feed, bf16), rows_of(width, bf16), rows_of(width, f32),
            rows_of(hidden, bf16),
            (shape((R, hidden)), fixed((R, hidden))), (shape((R, width)), fixed((R, width))),
        ],
        [
            pltpu.VMEM((R, hidden), f32),
            pltpu.VMEM((R, hidden), jnp.int32),
            pltpu.VMEM((R, hidden), f32),
        ],
        (scal, inputs, to_pm, gl, da, zl, kh, other, *forward, out_weight, gain2, up_weight),
        cost(4 * tokens * width * (hidden + feed), 48 * tokens * hidden),
    )

    fother = flat_permute(back, core_pairs())
    lower = jnp.where(core == 0, back, fother)
    upper = jnp.where(core == 0, fother, back)
    message = jnp.concatenate([decay, lower + first[:R] * upper], 0).astype(bf16)
    act, message = lax.optimization_barrier((act, message))
    backward = [chip_shift(message, -k) for k in range(1, chips)]

    quarter = feed // 4
    half1 = (shape((SLOTS // 2 * PIECE1, width), bf16), fixed((SLOTS // 2 * PIECE1, width)))
    act_block = lambda i, s: (0, jnp.where(i < 2, 1 - s[1], s[1]) * 2 + (i & 1))
    send1, keep1 = call(
        ffn_grad_kernel, "ffn_grad", 4,
        [
            pl.BlockSpec((tokens, quarter), act_block), whole(gl), whole(n2),
            pl.BlockSpec((tokens, quarter), lambda i, s: (0, i)),
        ],
        [half1, half1],
        [pltpu.VMEM((width, quarter), bf16)],
        (scal, act, gl, n2, dp),
        cost(4 * tokens * width * feed, 12 * tokens * hidden),
    )
    send1, *backward = lax.optimization_barrier((send1, *backward))
    chunk1 = Halving(send1, keep1)

    otile = hidden // 2
    (ograd,) = call(
        out_grad_kernel, "out_grad", 2,
        [pl.BlockSpec((tokens, otile), lambda i: (0, i)), whole(dm)],
        [(shape((hidden, width), bf16), pl.BlockSpec((otile, width), lambda i: (i, 0)))],
        [],
        (y, dm),
        cost(2 * tokens * width * hidden, 4 * tokens * hidden),
        scalars=False,
    )
    chunk1.advance(ograd)

    half2 = (shape((SLOTS // 2 * PIECE2, width), bf16), fixed((SLOTS // 2 * PIECE2, width)))
    send2, keep2, dkz, dkh, edge_dc, bias_part = call(
        functools.partial(gate_kernel, blocks=blocks, hops=hops), "gates", blocks + 2,
        [
            rtok(hidden), rtok(hidden), rtok(hidden), rtok(hidden), rtok(width),
            whole(ograd), whole(other), whole(fother), *[whole(f) for f in backward],
            whole(gate_weight), whole(cand_weight), ORDER,
        ],
        [
            half2, half2, rows_of(hidden, bf16, rtok), rows_of(hidden, bf16, rtok),
            (shape((4 * R, width), bf16), fixed((4 * R, width))),
            (shape((R, hidden)), fixed((R, hidden))),
        ],
        [
            pltpu.VMEM((R, hidden), f32),
            pltpu.VMEM((tokens, width), bf16),
            pltpu.VMEM((tokens, hidden), bf16),
            pltpu.VMEM((tokens, hidden), bf16),
        ],
        (
            scal, dh, zl, kh, hp, c, ograd, other, fother, *backward,
            gate_weight, cand_weight, chunk1.send,
        ),
        cost(8 * tokens * width * hidden, 24 * tokens * hidden),
    )
    send2, chunk1.recv = lax.optimization_barrier((send2, chunk1.recv))
    chunk2 = Halving(send2, keep2)
    after = passed_along(edge_dc[: margin * R], "seq", -1)
    chunk1.advance()

    input_grad, sums = call(
        functools.partial(tail_kernel, blocks=blocks), "tail", 2 * blocks,
        [
            rm(late), tok(width, late), tok(hidden), tok(hidden), whole(to_pm), whole(to_rm), whole(edge),
            whole(after), whole(gain1), whole(conv_weight), whole(gate_weight), whole(cand_weight),
            ORDER,
        ],
        [
            (shape((rows, span, width), bf16), rm(late)),
            (shape(((taps + 1) * R, width)), fixed(((taps + 1) * R, width))),
        ],
        [
            pltpu.VMEM((margin * R + m, width), f32),
            pltpu.VMEM((margin * R + tokens, width), f32),
        ],
        (
            inputs, dr1, dkz, dkh, to_pm, to_rm, edge, after, gain1, conv_weight, gate_weight, cand_weight,
            chunk1.send,
        ),
        cost(4 * tokens * width * hidden, 24 * tokens * width),
        scalars=False,
    )
    small = jnp.concatenate(
        [
            sums.reshape(taps + 1, R, width).sum(1),
            mg.sum(0, keepdims=True),
            bias_part.sum(0).reshape(hidden // width, width),
        ],
        0,
    )
    chunk2.advance(small)
    (output,) = call(
        output_kernel, "output", blocks,
        [tok(width), tok(feed), whole(to_rm), whole(down_weight), ORDER],
        [(shape((rows, span, width), bf16), rm(clamp))],
        [],
        (r1, act, to_rm, down_weight, chunk2.send),
        cost(2 * tokens * width * feed, 8 * tokens * hidden),
        scalars=False,
    )
    small, output = lax.optimization_barrier((small + flat_permute(small, core_pairs()), output))
    for k in range(len(stage_bits()[0])):
        if k < 8:
            chunk2.advance(small)
        small = small + flat_permute(small, halving_pairs(k))
    mine2, theirs2 = chunk2.finished()
    mine1, theirs1 = chunk1.finished()
    dgrad, ugrad = spread(
        scal, mine1, theirs1, PIECE1,
        ((0, feed // SLOTS, 1), (1, width // SLOTS, feed // width)),
        ((feed, width), (width, feed)), "spread_ffn",
    )
    ggrad, cgrad, ograd = spread(
        scal, mine2, theirs2, PIECE2,
        ((0, width // SLOTS, hidden // width), (1, width // SLOTS, hidden // width),
         (2, hidden // SLOTS, 1)),
        ((width, hidden), (width, hidden), (hidden, width)), "spread_gates",
    )
    return (
        output,
        input_grad,
        small[0],
        small[1 : taps + 1],
        ggrad,
        small[taps + 2 :].reshape(hidden),
        cgrad,
        ograd,
        small[taps + 1],
        ugrad,
        dgrad,
    )


def solution(mesh):
    sharded = P("row", "seq", None)
    in_specs = (sharded, P("row")) + (P(),) * 9 + (sharded,)
    out_specs = (sharded, sharded) + (P(),) * 9
    return jax.shard_map(
        per_device, mesh=mesh, in_specs=in_specs, out_specs=out_specs, check_vma=False
    )
```

```python
import functools

import jax
import jax.numpy as jnp
import numpy as np
from jax import lax
from jax.experimental import pallas as pl
from jax.experimental.pallas import tpu as pltpu
from jax.sharding import PartitionSpec as P

epsilon = 1e-06
f32 = jnp.float32
bf16 = jnp.bfloat16
R = 8
PERM = 256
SCALARS = 4
SLOTS = 32
PIECE1 = 128
PIECE2 = 96


def nn(a, b):
    return lax.dot_general(a, b, (((1,), (0,)), ((), ())), preferred_element_type=f32)


def nt(a, b):
    return lax.dot_general(a, b, (((1,), (1,)), ((), ())), preferred_element_type=f32)


def tn(a, b):
    return lax.dot_general(a, b, (((0,), (0,)), ((), ())), preferred_element_type=f32)


def token_order():
    out = np.arange(PERM)
    source = (out % R) * (PERM // R) + out // R
    to_pm = np.zeros((PERM, PERM), np.float32)
    to_pm[out, source] = 1
    return jnp.asarray(to_pm, bf16), jnp.asarray(to_pm.T, bf16)


def position_major(perm, block):
    span = PERM // R
    parts = []
    for s in range(block.shape[1] // span):
        part = block[:, s * span : (s + 1) * span, :].reshape(PERM, block.shape[2])
        parts.append(nn(perm, part))
    return parts[0] if len(parts) == 1 else jnp.concatenate(parts, 0)


def row_major(perm, tokens):
    span = PERM // R
    parts = []
    for s in range(tokens.shape[0] // PERM):
        part = nn(perm, tokens[s * PERM : (s + 1) * PERM]).astype(bf16)
        parts.append(part.reshape(R, span, tokens.shape[1]))
    return parts[0] if len(parts) == 1 else jnp.concatenate(parts, 1)


def eight(t):
    return pl.ds(pl.multiple_of(t * R, R), R)


def sixteen(t):
    return pl.ds(pl.multiple_of(t * 2 * R, 2 * R), 2 * R)


def normed_edge(edge, gain):
    e = edge.astype(f32)
    inv = lax.rsqrt(jnp.mean(e * e, -1, keepdims=True) + epsilon)
    return (e * inv * gain).astype(bf16).astype(f32)


def set_limits(scal, limit):
    row = lax.broadcasted_iota(jnp.int32, limit.shape, 0)
    value = jnp.zeros(limit.shape, jnp.int32)
    for r in range(R):
        value = jnp.where(row == r, scal[SCALARS + r], value)
    limit[...] = value


def halves(ref, pair):
    both = ref[sixteen(pair), :].astype(f32)
    return both[:R], both[R:]


def front_kernel(scal, x, perm, edge, gain, convw, wg, bias, wc, c_out, zl_out, kh_out, ends, ext, state, limit):
    step = pl.program_id(0)
    tb = x.shape[1]
    m = tb * R
    halo = edge.shape[0]
    taps = convw.shape[0]

    @pl.when(step == 0)
    def _():
        set_limits(scal, limit)
        ext[0:halo, :] = normed_edge(edge[...], gain[...])
        state[0:R, :] = jnp.ones((R, state.shape[1]), f32)
        state[R:, :] = jnp.zeros((R, state.shape[1]), f32)

    xp = position_major(perm[...], x[...])
    inv = lax.rsqrt(jnp.mean(xp * xp, -1, keepdims=True) + epsilon)
    ext[halo:, :] = (xp * inv * gain[...]).astype(bf16).astype(f32)
    conv = convw[0:1, :] * ext[halo:, :]
    for k in range(1, taps):
        lo = halo - k * R
        conv = conv + convw[k : k + 1, :] * ext[lo : lo + m, :]
    ext[0:halo, :] = ext[m : m + halo, :]
    cb = conv.astype(bf16)
    c_out[...] = cb
    kz = nn(cb, wg[...]) + bias[...]
    zs = 1.0 / (1.0 + jnp.exp(-kz))
    width = zs.shape[1]
    zs = zs.reshape(tb, R, width)
    pos = scal[0] + step * tb + lax.broadcasted_iota(jnp.int32, (tb, R, width), 0)
    zl_out[...] = jnp.where(pos < limit[...][None], zs, 0.0).reshape(m, width).astype(bf16)
    kh_out[...] = nn(cb, wc[...]).astype(bf16)

    def body(u, carry):
        prod, h = carry
        za, zb = halves(zl_out, u)
        ka, kb = halves(kh_out, u)
        a = 1.0 - za
        b = 1.0 - zb
        return prod * (a * b), (h * a + za * ka) * b + zb * kb

    prod, h = lax.fori_loop(0, tb // 2, body, (state[0:R, :], state[R:, :]), unroll=4)
    state[0:R, :] = prod
    state[R:, :] = h
    ends[0:R, :] = prod
    ends[R:, :] = h


def gelu_parts(p):
    k0 = 0.7978845608028654
    p2 = p * p
    th = jnp.tanh(p * (k0 + (k0 * 0.044715) * p2))
    ht = 0.5 + 0.5 * th
    return p * ht, ht + (2.0 * p) * (ht - ht * ht) * (k0 + (3.0 * k0 * 0.044715) * p2)


def da_kernel(g, perm, wd, gl_out, da_out):
    gl = position_major(perm[...], g[...]).astype(bf16)
    gl_out[...] = gl
    da_out[...] = nt(gl, wd[...]).astype(bf16)


def core_kernel(scal, x, perm, gl, da, zl, kh, other, *refs, fchunk, hops):
    msgs = refs[:hops]
    wo, mgain, wu = refs[hops : hops + 3]
    r1_out, y_out, hp_out, n2_out, act_out, dp_out, dm_out, dr1_out, dh_out, back, mg = refs[hops + 3 : hops + 14]
    state, limit, run = refs[hops + 14 :]
    step = pl.program_id(0)
    tb = x.shape[1]
    m = tb * R
    width, feed = wu.shape
    hidden = wo.shape[0]

    @pl.when(step == 0)
    def _():
        set_limits(scal, limit)
        h = jnp.zeros((R, hidden), f32)
        for msg in reversed(msgs):
            both = msg[...].astype(f32)
            h = jnp.exp(both[0:R, :]) * h + both[R:, :]
        state[...] = jnp.where(scal[1] == 1, other[0:R, :] * h + other[R:, :], h)
        run[...] = jnp.ones((R, hidden), f32)
        back[...] = jnp.zeros(back.shape, f32)
        mg[...] = jnp.zeros(mg.shape, f32)

    first = scal[0] + step * tb
    lens = limit[...]

    def body(u, h):
        t = u * 2
        za, zb = halves(zl, u)
        ka, kb = halves(kh, u)
        ha = h - za * h + za * ka
        hb = ha - zb * ha + zb * kb
        hp_out[sixteen(u), :] = jnp.concatenate([h, ha], 0).astype(bf16)
        ya = jnp.where(first + t < lens, ha, 0.0)
        yb = jnp.where(first + t + 1 < lens, hb, 0.0)
        y_out[sixteen(u), :] = jnp.concatenate([ya, yb], 0).astype(bf16)
        return hb

    state[...] = lax.fori_loop(0, tb // 2, body, state[...], unroll=2)
    r1 = position_major(perm[...], x[...]) + nn(y_out[...], wo[...])
    r1_out[...] = r1
    inv = lax.rsqrt(jnp.mean(r1 * r1, -1, keepdims=True) + epsilon)
    n2 = (r1 * inv * mgain[...]).astype(bf16)
    n2_out[...] = n2
    for f in range(0, feed, fchunk):
        cols = slice(f, f + fchunk)
        a, slope = gelu_parts(nn(n2, wu[:, cols]))
        act_out[:, cols] = a.astype(bf16)
        dp_out[:, cols] = (da[:, cols].astype(f32) * slope).astype(bf16)
    dn2 = nt(dp_out[...], wu[...])
    r1 = r1_out[...]
    mg[...] += jnp.sum((dn2 * r1 * inv).reshape(tb, R, width), 0)
    s = mgain[...] * dn2
    mean = jnp.mean(s * r1, -1, keepdims=True)
    dr1 = gl[...].astype(f32) + inv * (s - r1 * (inv * inv * mean))
    dr1_out[...] = dr1
    dm = dr1.astype(bf16)
    dm_out[...] = dm
    dh = nt(dm, wo[...]).reshape(tb, R, hidden)
    pos = first + lax.broadcasted_iota(jnp.int32, (tb, R, hidden), 0)
    dh_out[...] = jnp.where(pos < lens[None], dh, 0.0).reshape(m, hidden).astype(bf16)

    def adjoint(u, carry):
        prod, total = carry
        za, zb = halves(zl, u)
        da, db = halves(dh_out, u)
        pa = prod - za * prod
        pb = pa - zb * pa
        return pb, total + (pa * da + pb * db)

    prod, total = lax.fori_loop(0, tb // 2, adjoint, (run[...], back[...]), unroll=4)
    run[...] = prod
    back[...] = total


def put_rows(dst, sel, piece, at, rows, part):
    for i in range(SLOTS // 2):
        pos = pl.multiple_of((i ^ sel) * piece + at, 16)
        dst[pl.ds(pos, rows), :] = part[i * rows : (i + 1) * rows]


def ffn_grad_kernel(scal, act, gl, n2, dp, dst, *, pick):
    step = pl.program_id(0)
    sel = scal[2 + pick]
    width = gl.shape[1]
    rows1 = act.shape[1] * 4 // SLOTS
    rows2 = n2.shape[1] * 2 // SLOTS
    part = tn(act[...], gl[...]).astype(bf16)
    per = act.shape[1] // rows1
    for i in range(per):
        pos = ((step * per + i) ^ sel) * PIECE1
        dst[pl.ds(pl.multiple_of(pos, 16), rows1), :] = part[i * rows1 : (i + 1) * rows1]
    columns = dp.shape[1] // width
    for q in range(columns):
        part = tn(n2[...], dp[:, q * width : (q + 1) * width]).astype(bf16)
        put_rows(dst, sel, PIECE1, rows1 + (step * columns + q) * rows2, rows2, part)


def gate_grad_kernel(scal, c, dkz, dkh, y, dm, dst, *, pick):
    sel = scal[2 + pick]
    width = dm.shape[1]
    rows = c.shape[1] * 2 // SLOTS
    at = 0
    for grads in (dkz, dkh):
        for q in range(grads.shape[1] // width):
            part = tn(c[...], grads[:, q * width : (q + 1) * width]).astype(bf16)
            put_rows(dst, sel, PIECE2, at, rows, part)
            at += rows
    put_rows(dst, sel, PIECE2, at, y.shape[1] * 2 // SLOTS, tn(y[...], dm[...]).astype(bf16))


def gate_kernel(scal, dh, zl, kh, hp, other, fother, *refs, blocks, hops):
    msgs = refs[:hops]
    wg, wc = refs[hops : hops + 2]
    dkz, dkh, edge_out, bias_out = refs[hops + 3 : hops + 7]
    state = refs[hops + 7]
    step = pl.program_id(0)
    m = dh.shape[0]
    tb = m // R
    block = blocks - 1 - step

    @pl.when(step == 0)
    def _():
        mm = jnp.zeros(state.shape, f32)
        for msg in reversed(msgs):
            both = msg[...].astype(f32)
            mm = jnp.exp(both[0:R, :]) * mm + both[R:, :]
        state[...] = jnp.where(scal[1] == 0, fother[...] + other[0:R, :] * mm, mm)
        bias_out[...] = jnp.zeros(bias_out.shape, f32)

    def body(u, carry):
        mm, bias = carry
        w = tb // 2 - 1 - u
        ha, hb = halves(hp, w)
        za, zb = halves(zl, w)
        da, db = halves(dh, w)
        ka, kb = halves(kh, w)
        lam = db + mm
        sb = lam * zb
        mm = lam - sb
        kb = (sb - sb * zb) * (kb - hb)
        lam = da + mm
        sa = lam * za
        mm = lam - sa
        ka = (sa - sa * za) * (ka - ha)
        kk = jnp.concatenate([ka, kb], 0).astype(bf16)
        dkz[sixteen(w), :] = kk
        dkh[sixteen(w), :] = jnp.concatenate([sa, sb], 0).astype(bf16)
        kf = kk.astype(f32)
        return mm, bias + kf[:R, :] + kf[R:, :]

    mm, bias = lax.fori_loop(0, tb // 2, body, (state[...], bias_out[...]), unroll=2)
    state[...] = mm
    bias_out[...] = bias

    @pl.when(block == 0)
    def _():
        span = edge_out.shape[0]
        edge_out[...] = (nt(dkz[0:span, :], wg[...]) + nt(dkh[0:span, :], wc[...])).astype(bf16)


def tail_kernel(x, dr1, dkz, dkh, pm, back_pm, edge, after, gain, convw, wg, wc, grad, sums, uext, dext, *, blocks):
    step = pl.program_id(0)
    tb = x.shape[1]
    m = tb * R
    halo = edge.shape[0]
    taps = convw.shape[0]
    width = gain.shape[1]

    @pl.when(step == 0)
    def _():
        uext[0:halo, :] = normed_edge(edge[...], gain[...])
        dext[blocks * m :, :] = after[...].astype(f32)
        sums[...] = jnp.zeros(sums.shape, f32)

    @pl.when(step < blocks)
    def _():
        rows = pl.ds(pl.multiple_of(step * m, m), m)
        dext[rows, :] = nt(dkz[...], wg[...]) + nt(dkh[...], wc[...])

    @pl.when(step >= blocks)
    def _():
        xp = position_major(pm[...], x[...])
        inv = lax.rsqrt(jnp.mean(xp * xp, -1, keepdims=True) + epsilon)
        xn = xp * inv
        uext[halo:, :] = (xn * gain[...]).astype(bf16).astype(f32)
        start = (step - blocks) * m
        here = dext[pl.ds(pl.multiple_of(start, R), m), :]
        du = convw[0:1, :] * here
        for k in range(taps):
            lo = halo - k * R
            part = (here * uext[lo : lo + m, :]).reshape(tb, R, width)
            sums[(k + 1) * R : (k + 2) * R, :] += jnp.sum(part, 0)
            if k:
                du = du + convw[k : k + 1, :] * dext[pl.ds(pl.multiple_of(start + k * R, R), m), :]
        uext[0:halo, :] = uext[m : m + halo, :]
        sums[0:R, :] += jnp.sum((du * xn).reshape(tb, R, width), 0)
        s1 = gain[...] * du
        mean = jnp.mean(s1 * xn, -1, keepdims=True)
        gin = dr1[...] + inv * (s1 - xn * mean)
        grad[...] = row_major(back_pm[...], gin.astype(bf16))


def output_kernel(r1, act, perm, wd, out):
    total = r1[...] + nn(act[...], wd[...])
    out[...] = row_major(perm[...], total.astype(bf16))


def spread_kernel(scal, src, *refs, piece, plan, mate):
    low = scal[2 + mate] & 7
    for a in range(8):
        base = (a ^ low) * piece
        at = 0
        for out, rows, columns in plan:
            ref = refs[len(refs) - len(plan) + out]
            for q in range(columns):
                width = src.shape[1]
                part = src[pl.ds(pl.multiple_of(base + at, 16), rows), :].astype(f32)
                ref[a * rows : (a + 1) * rows, q * width : (q + 1) * width] = part
                at += rows


def spread(scal, src, held, mate, flip, piece, plan, shapes, name):
    def block(g, s):
        return ((s[1] ^ mate) * 2 + ((s[2 + mate] >> 3) ^ flip), 0)

    count = len(held)
    return pl.pallas_call(
        functools.partial(spread_kernel, piece=piece, plan=plan, mate=mate),
        grid_spec=pltpu.PrefetchScalarGridSpec(
            num_scalar_prefetch=1,
            grid=(1,),
            in_specs=[whole(src)] + [ORDER] * count,
            out_specs=[pl.BlockSpec((dims[0] // 4, dims[1]), block) for dims in shapes],
        ),
        out_shape=[pltpu.HBM(dims, f32) for dims in shapes],
        input_output_aliases={2 + k: k for k in range(count)},
        compiler_params=params(16),
        cost_estimate=LITTLE,
        name=name,
    )(scal, src, *held)


def params(mib):
    return pltpu.CompilerParams(
        dimension_semantics=("arbitrary",), vmem_limit_bytes=mib * 1024 * 1024
    )


def shape(dims, kind=f32):
    return jax.ShapeDtypeStruct(dims, kind)


LITTLE = pl.CostEstimate(flops=1024, bytes_accessed=1024, transcendentals=0)
ORDER = pl.BlockSpec(memory_space=pl.ANY)


def far(array):
    return pltpu.with_memory_space_constraint(array, pltpu.HBM)


def whole(array):
    zeros = (0,) * array.ndim
    return pl.BlockSpec(array.shape, lambda *a: zeros, pipeline_mode=pl.Buffered(1))


def passed_along(value, axis, steps):
    count = lax.axis_size(axis)
    leading, last = (max(0, -steps), min(count, count - steps))
    return lax.ppermute(value, axis, [(source, source + steps) for source in range(leading, last)])


def flat_permute(value, pairs):
    return lax.ppermute(value, ("seq", "row"), pairs)


def stage_bits():
    row_bits = lax.axis_size("row").bit_length() - 1
    seq_bits = lax.axis_size("seq").bit_length() - 1
    plane = list(range(row_bits))
    line = [row_bits + 1 + z for z in range(seq_bits - 1)]
    cut = row_bits // 2
    return (plane + line, plane[cut:] + plane[:cut] + line[::-1])


def slot_of(flat, bits):
    slot = 0
    for k in range(4):
        slot = slot * 2 + ((flat >> bits[k]) & 1)
    return slot


def halving_pairs(stage):
    row_bits = lax.axis_size("row").bit_length() - 1
    orders = stage_bits()
    devices = lax.axis_size("row") * lax.axis_size("seq")
    return [(d, d ^ (1 << orders[(d >> row_bits) & 1][stage])) for d in range(devices)]


def core_pairs():
    row_bits = lax.axis_size("row").bit_length() - 1
    devices = lax.axis_size("row") * lax.axis_size("seq")
    return [(d, d ^ (1 << row_bits)) for d in range(devices)]


def added(a, b):
    return (a.astype(f32) + b.astype(f32)).astype(bf16)


class Sequence:
    def __init__(self, token):
        self.token = token

    def after(self, *arrays):
        *arrays, _ = lax.optimization_barrier((*arrays, self.token))
        return arrays[0] if len(arrays) == 1 else arrays

    def did(self, array):
        self.token = array
        return array


class Halving:
    def __init__(self, seq, send):
        self.seq = seq
        self.recv = flat_permute(send, core_pairs())
        self.stage = 0
        self.stages = len(stage_bits()[0])

    def step(self, *beside):
        k = self.stage
        self.stage += 1
        recv, *beside = self.seq.after(self.recv, *beside) if beside else (self.seq.after(self.recv),)
        if k < 4:
            half = self.keep.shape[0] // 2
            send = self.seq.did(added(self.keep[half:], recv[half:]))
            self.recv = flat_permute(send, halving_pairs(k))
            self.keep = added(self.keep[:half], recv[:half])
        elif k == 4:
            total = added(self.keep, recv)
            for extra in range(4, self.stages):
                total = added(total, flat_permute(total, halving_pairs(extra)))
            self.total = self.seq.did(total)
            self.recv = flat_permute(total, halving_pairs(3))
        elif k < 8:
            self.total = self.seq.did(jnp.concatenate([self.total, recv], 0))
            self.recv = flat_permute(self.total, halving_pairs(7 - k))
            if k == 7:
                self.theirs = flat_permute(self.total, core_pairs())
        else:
            self.rest = recv
            self.their_rest = flat_permute(recv, core_pairs())
        return beside


def chip_shift(value, steps):
    return passed_along(value, "seq", 2 * steps)


def per_device(
    inputs,
    lengths,
    norm_gain,
    conv_weight,
    gate_weight,
    gate_bias,
    cand_weight,
    out_weight,
    mlp_gain,
    up_weight,
    down_weight,
    cotangent,
):
    rows, span, width = inputs.shape
    hidden = gate_weight.shape[1]
    feed = up_weight.shape[1]
    taps = conv_weight.shape[0]
    margin = taps - 1
    tokens = rows * span
    tb = 32
    blocks = span // tb
    m = tb * R
    seq = lax.axis_index("seq")
    core = seq & 1
    chips = lax.axis_size("seq") // 2
    hops = chips - 1
    flat = seq * lax.axis_size("row") + lax.axis_index("row")
    slots = [slot_of(flat, bits) for bits in stage_bits()]
    here = jnp.where(core == 0, slots[0], slots[1])
    mate = jnp.where(core == 0, slots[1], slots[0])
    scal = jnp.concatenate([jnp.stack([seq * span, core, here, mate]).astype(jnp.int32), lengths])
    gain1 = norm_gain.reshape(1, width)
    gain2 = mlp_gain.reshape(1, width)
    bias = gate_bias.reshape(1, hidden)
    to_pm, to_rm = token_order()

    edge = inputs[:, span - margin :, :].swapaxes(0, 1).reshape(margin * rows, width)
    edge = passed_along(edge, "seq", 1)

    last = blocks - 1
    clamp = lambda i: jnp.minimum(i, last)
    late = lambda i: jnp.maximum(i - blocks, 0)

    def rm(index):
        return pl.BlockSpec((rows, tb, width), lambda i, *s: (0, index(i), 0))

    def tok(w, index=clamp):
        return pl.BlockSpec((m, w), lambda i, *s: (index(i), 0))

    def rtok(w):
        return tok(w, lambda i: last - clamp(i))

    def fixed(dims):
        zeros = (0,) * len(dims)
        return pl.BlockSpec(dims, lambda i, *s: zeros)

    def call(kernel, name, grid, ins, outs, scratch, operands, scalars=True):
        spec = pltpu.PrefetchScalarGridSpec(
            num_scalar_prefetch=int(scalars),
            grid=(grid,),
            in_specs=ins,
            out_specs=[o[1] for o in outs],
            scratch_shapes=scratch,
        )
        return pl.pallas_call(
            kernel,
            grid_spec=spec,
            out_shape=[o[0] for o in outs],
            compiler_params=params(16),
            cost_estimate=LITTLE,
            name=name,
        )(*operands)

    def rows_of(w, kind, spec=tok, kept=shape):
        return kept((tokens, w), kind), spec(w)

    c, zl, kh, ends = call(
        front_kernel, "front", blocks,
        [
            rm(clamp), whole(to_pm), whole(edge), whole(gain1), whole(conv_weight),
            whole(gate_weight), whole(bias), whole(cand_weight),
        ],
        [
            rows_of(width, bf16), rows_of(hidden, bf16), rows_of(hidden, bf16),
            (shape((2 * R, hidden)), fixed((2 * R, hidden))),
        ],
        [
            pltpu.VMEM((margin * R + m, width), f32),
            pltpu.VMEM((2 * R, hidden), f32),
            pltpu.VMEM((R, hidden), jnp.int32),
        ],
        (
            scal, far(inputs), far(to_pm), edge, far(gain1), far(conv_weight), far(gate_weight),
            far(bias), far(cand_weight),
        ),
    )

    other = flat_permute(ends, core_pairs())
    first = jnp.where(core == 0, ends, other)
    second = jnp.where(core == 0, other, ends)
    decay = jnp.log(jnp.maximum(ends[:R] * other[:R], 1e-37))
    message = jnp.concatenate([decay, second[:R] * first[R:] + second[R:]], 0).astype(bf16)
    forward = [chip_shift(message, k) for k in range(1, chips)]

    gl, da = call(
        da_kernel, "da", blocks,
        [rm(clamp), whole(to_pm), whole(down_weight)],
        [rows_of(width, bf16), rows_of(feed, bf16)],
        [],
        (cotangent, to_pm, down_weight),
        scalars=False,
    )

    r1, y, hp, n2, act, dp, dm, dr1, dh, back, mg = call(
        functools.partial(core_kernel, fchunk=512, hops=hops), "core", blocks,
        [
            rm(clamp), whole(to_pm), tok(width), tok(feed), tok(hidden), tok(hidden), whole(other),
            *[whole(f) for f in forward], whole(out_weight), whole(gain2), whole(up_weight),
        ],
        [
            rows_of(width, f32, kept=pltpu.HBM), rows_of(hidden, bf16), rows_of(hidden, bf16),
            rows_of(width, bf16), rows_of(feed, bf16), rows_of(feed, bf16), rows_of(width, bf16),
            rows_of(width, f32, kept=pltpu.HBM),
            rows_of(hidden, bf16),
            (shape((R, hidden)), fixed((R, hidden))), (shape((R, width)), fixed((R, width))),
        ],
        [
            pltpu.VMEM((R, hidden), f32),
            pltpu.VMEM((R, hidden), jnp.int32),
            pltpu.VMEM((R, hidden), f32),
        ],
        (scal, inputs, to_pm, gl, da, zl, kh, other, *forward, out_weight, gain2, up_weight),
    )

    order = Sequence(back)
    quarter = feed // 4

    def ffn_grads(pick):
        half = lambda s: s[1] if pick == 0 else 1 - s[1]
        a, d = order.after(act, dp)
        (piece,) = call(
            functools.partial(ffn_grad_kernel, pick=pick), "ffn_grad", 2,
            [
                pl.BlockSpec((tokens, quarter), lambda i, s: (0, half(s) * 2 + i)), whole(gl),
                pl.BlockSpec((tokens, width // 2), lambda i, s: (0, half(s))),
                pl.BlockSpec((tokens, feed // 2), lambda i, s: (0, i)),
            ],
            [(shape((SLOTS // 2 * PIECE1, width), bf16), fixed((SLOTS // 2 * PIECE1, width)))],
            [],
            (scal, a, gl, n2, d),
        )
        return order.did(piece)

    def gate_grads(pick):
        half = lambda s: s[1] if pick == 0 else 1 - s[1]
        z, h = order.after(dkz, dkh)
        (piece,) = call(
            functools.partial(gate_grad_kernel, pick=pick), "gate_grad", 1,
            [
                pl.BlockSpec((tokens, width // 2), lambda i, s: (0, half(s))),
                whole(z), whole(h),
                pl.BlockSpec((tokens, hidden // 2), lambda i, s: (0, half(s))), whole(dm),
            ],
            [(shape((SLOTS // 2 * PIECE2, width), bf16), fixed((SLOTS // 2 * PIECE2, width)))],
            [],
            (scal, c, z, h, y, dm),
        )
        return order.did(piece)

    fother = flat_permute(back, core_pairs())
    chunk1 = Halving(order, ffn_grads(1))
    fother = order.after(fother)
    lower = jnp.where(core == 0, back, fother)
    upper = jnp.where(core == 0, fother, back)
    message = jnp.concatenate([decay, lower + first[:R] * upper], 0).astype(bf16)
    backward = [chip_shift(order.did(message), -k) for k in range(1, chips)]
    chunk1.keep = ffn_grads(0)
    backward = chunk1.step(*backward)

    dkz, dkh, edge_dc, bias_part = call(
        functools.partial(gate_kernel, blocks=blocks, hops=hops), "gates", blocks,
        [
            rtok(hidden), rtok(hidden), rtok(hidden), rtok(hidden),
            whole(other), whole(fother), *[whole(f) for f in backward],
            whole(gate_weight), whole(cand_weight), ORDER,
        ],
        [
            rows_of(hidden, bf16, rtok), rows_of(hidden, bf16, rtok),
            (shape((4 * R, width), bf16), fixed((4 * R, width))),
            (shape((R, hidden)), fixed((R, hidden))),
        ],
        [pltpu.VMEM((R, hidden), f32)],
        (
            scal, dh, zl, kh, hp, other, fother, *backward, gate_weight, cand_weight, order.token,
        ),
    )
    order.did(bias_part)
    after = passed_along(edge_dc[: margin * R], "seq", -1)
    send2 = gate_grads(1)
    chunk1.step()
    chunk2 = Halving(order, order.after(send2))
    chunk2.keep = gate_grads(0)
    (output,) = call(
        output_kernel, "output", blocks,
        [tok(width), tok(feed), whole(to_rm), whole(down_weight)],
        [(shape((rows, span, width), bf16), rm(clamp))],
        [],
        (far(r1), order.after(act), to_rm, far(down_weight)),
        scalars=False,
    )
    order.did(output)
    chunk2.step()
    chunk1.step()
    input_grad, sums = call(
        functools.partial(tail_kernel, blocks=blocks), "tail", 2 * blocks,
        [
            rm(late), tok(width, late), tok(hidden), tok(hidden), whole(to_pm), whole(to_rm),
            whole(edge), whole(after), whole(gain1), whole(conv_weight), whole(gate_weight),
            whole(cand_weight),
        ],
        [
            (shape((rows, span, width), bf16), rm(late)),
            (shape(((taps + 1) * R, width)), fixed(((taps + 1) * R, width))),
        ],
        [
            pltpu.VMEM((margin * R + m, width), f32),
            pltpu.VMEM((margin * R + tokens, width), f32),
        ],
        (
            far(inputs), dr1, order.after(dkz), dkh, to_pm, to_rm, edge, after, gain1, conv_weight,
            gate_weight, cand_weight,
        ),
        scalars=False,
    )
    order.did(sums)
    small = jnp.concatenate(
        [
            sums.reshape(taps + 1, R, width).sum(1),
            mg.sum(0, keepdims=True),
            bias_part.sum(0).reshape(hidden // width, width),
        ],
        0,
    )
    order.did(small)
    small_pairs = [core_pairs()] + [halving_pairs(k) for k in range(len(stage_bits()[0]))]
    coming = flat_permute(small, small_pairs[0])

    def small_step():
        nonlocal small, coming
        small = order.did(small + order.after(coming))
        small_pairs.pop(0)
        if small_pairs:
            coming = flat_permute(small, small_pairs[0])

    plan1 = ((0, feed // SLOTS, 1), (1, width // SLOTS, feed // width))
    shapes1 = ((feed, width), (width, feed))
    plan2 = (
        (0, width // SLOTS, hidden // width),
        (1, width // SLOTS, hidden // width),
        (2, hidden // SLOTS, 1),
    )
    shapes2 = ((width, hidden), (width, hidden), (hidden, width))
    held1, held2 = (), ()

    def spread1(src, mate, flip):
        nonlocal held1
        src = order.after(src)
        held1 = spread(scal, src, held1, mate, flip, PIECE1, plan1, shapes1, "spread_ffn")
        order.did(held1[0])

    def spread2(src, mate, flip):
        nonlocal held2
        src = order.after(src)
        held2 = spread(scal, src, held2, mate, flip, PIECE2, plan2, shapes2, "spread_gates")
        order.did(held2[0])

    chunk1.step()
    small_step()
    chunk2.step()
    chunk1.step()
    small_step()
    chunk2.step()
    small_step()
    chunk1.step()
    small_step()
    chunk2.step()
    while small_pairs:
        small_step()
    chunk1.step()
    chunk2.step()
    chunk2.step()
    chunk1.step()
    spread1(chunk1.total, 0, 0)
    chunk2.step()
    spread1(chunk1.theirs, 1, 0)
    chunk2.step()

    small_out = (
        small[0],
        small[1 : taps + 1],
        small[taps + 2 :].reshape(hidden),
        small[taps + 1],
    )
    small_out = order.after(*small_out)
    chunk1.step()
    spread1(chunk1.rest, 0, 1)
    spread2(chunk2.total, 0, 0)
    spread1(chunk1.their_rest, 1, 1)
    spread2(chunk2.theirs, 1, 0)
    chunk2.step()
    spread2(chunk2.rest, 0, 1)
    spread2(chunk2.their_rest, 1, 1)
    return (
        output,
        input_grad,
        small_out[0],
        small_out[1],
        held2[0],
        small_out[2],
        held2[1],
        held2[2],
        small_out[3],
        held1[1],
        held1[0],
    )


def solution(mesh):
    sharded = P("row", "seq", None)
    in_specs = (sharded, P("row")) + (P(),) * 9 + (sharded,)
    out_specs = (sharded, sharded) + (P(),) * 9
    return jax.shard_map(
        per_device, mesh=mesh, in_specs=in_specs, out_specs=out_specs, check_vma=False
    )
```

```python
import functools

import jax
import jax.numpy as jnp
import numpy as np
from jax import lax
from jax.experimental import pallas as pl
from jax.experimental.pallas import tpu as pltpu
from jax.sharding import PartitionSpec as P

epsilon = 1e-06
f32 = jnp.float32
bf16 = jnp.bfloat16
R = 8
PERM = 256
SCALARS = 4
SLOTS = 32
PIECE1 = 128
PIECE2 = 96


def nn(a, b):
    return lax.dot_general(a, b, (((1,), (0,)), ((), ())), preferred_element_type=f32)


def nt(a, b):
    return lax.dot_general(a, b, (((1,), (1,)), ((), ())), preferred_element_type=f32)


def tn(a, b):
    return lax.dot_general(a, b, (((0,), (0,)), ((), ())), preferred_element_type=f32)


def token_order():
    out = np.arange(PERM)
    source = (out % R) * (PERM // R) + out // R
    to_pm = np.zeros((PERM, PERM), np.float32)
    to_pm[out, source] = 1
    return jnp.asarray(to_pm, bf16), jnp.asarray(to_pm.T, bf16)


def position_major(perm, block):
    span = PERM // R
    parts = []
    for s in range(block.shape[1] // span):
        part = block[:, s * span : (s + 1) * span, :].reshape(PERM, block.shape[2])
        parts.append(nn(perm, part))
    return parts[0] if len(parts) == 1 else jnp.concatenate(parts, 0)


def row_major(perm, tokens):
    span = PERM // R
    parts = []
    for s in range(tokens.shape[0] // PERM):
        part = nn(perm, tokens[s * PERM : (s + 1) * PERM]).astype(bf16)
        parts.append(part.reshape(R, span, tokens.shape[1]))
    return parts[0] if len(parts) == 1 else jnp.concatenate(parts, 1)


def eight(t):
    return pl.ds(pl.multiple_of(t * R, R), R)


def sixteen(t):
    return pl.ds(pl.multiple_of(t * 2 * R, 2 * R), 2 * R)


def normed_edge(edge, gain):
    e = edge.astype(f32)
    inv = lax.rsqrt(jnp.mean(e * e, -1, keepdims=True) + epsilon)
    return (e * inv * gain).astype(bf16).astype(f32)


def set_limits(scal, limit):
    row = lax.broadcasted_iota(jnp.int32, limit.shape, 0)
    value = jnp.zeros(limit.shape, jnp.int32)
    for r in range(R):
        value = jnp.where(row == r, scal[SCALARS + r], value)
    limit[...] = value


def halves(ref, pair):
    both = ref[sixteen(pair), :].astype(f32)
    return both[:R], both[R:]


def front_kernel(scal, x, perm, edge, gain, convw, wg, bias, wc, c_out, zl_out, kh_out, ends, ext, state, limit):
    step = pl.program_id(0)
    tb = x.shape[1]
    m = tb * R
    halo = edge.shape[0]
    taps = convw.shape[0]

    @pl.when(step == 0)
    def _():
        set_limits(scal, limit)
        ext[0:halo, :] = normed_edge(edge[...], gain[...])
        state[0:R, :] = jnp.ones((R, state.shape[1]), f32)
        state[R:, :] = jnp.zeros((R, state.shape[1]), f32)

    xp = position_major(perm[...], x[...])
    inv = lax.rsqrt(jnp.mean(xp * xp, -1, keepdims=True) + epsilon)
    ext[halo:, :] = (xp * inv * gain[...]).astype(bf16).astype(f32)
    conv = convw[0:1, :] * ext[halo:, :]
    for k in range(1, taps):
        lo = halo - k * R
        conv = conv + convw[k : k + 1, :] * ext[lo : lo + m, :]
    ext[0:halo, :] = ext[m : m + halo, :]
    cb = conv.astype(bf16)
    c_out[...] = cb
    kz = nn(cb, wg[...]) + bias[...]
    zs = 1.0 / (1.0 + jnp.exp(-kz))
    width = zs.shape[1]
    zs = zs.reshape(tb, R, width)
    pos = scal[0] + step * tb + lax.broadcasted_iota(jnp.int32, (tb, R, width), 0)
    zl_out[...] = jnp.where(pos < limit[...][None], zs, 0.0).reshape(m, width).astype(bf16)
    kh_out[...] = nn(cb, wc[...]).astype(bf16)

    def body(u, carry):
        prod, h = carry
        za, zb = halves(zl_out, u)
        ka, kb = halves(kh_out, u)
        a = 1.0 - za
        b = 1.0 - zb
        return prod * (a * b), (h * a + za * ka) * b + zb * kb

    prod, h = lax.fori_loop(0, tb // 2, body, (state[0:R, :], state[R:, :]), unroll=4)
    state[0:R, :] = prod
    state[R:, :] = h
    ends[0:R, :] = prod
    ends[R:, :] = h


def gelu_parts(p):
    k0 = 0.7978845608028654
    p2 = p * p
    th = jnp.tanh(p * (k0 + (k0 * 0.044715) * p2))
    ht = 0.5 + 0.5 * th
    return p * ht, ht + (2.0 * p) * (ht - ht * ht) * (k0 + (3.0 * k0 * 0.044715) * p2)


def da_kernel(g, perm, wd, gl_out, da_out):
    gl = position_major(perm[...], g[...]).astype(bf16)
    gl_out[...] = gl
    da_out[...] = nt(gl, wd[...]).astype(bf16)


def core_kernel(scal, x, perm, gl, da, zl, kh, other, *refs, fchunk, hops):
    msgs = refs[:hops]
    wo, mgain, wu = refs[hops : hops + 3]
    r1_out, y_out, hp_out, n2_out, act_out, dp_out, dm_out, dr1_out, dh_out, back, mg = refs[hops + 3 : hops + 14]
    state, limit, run = refs[hops + 14 :]
    step = pl.program_id(0)
    tb = x.shape[1]
    m = tb * R
    width, feed = wu.shape
    hidden = wo.shape[0]

    @pl.when(step == 0)
    def _():
        set_limits(scal, limit)
        h = jnp.zeros((R, hidden), f32)
        for msg in reversed(msgs):
            both = msg[...].astype(f32)
            h = jnp.exp(both[0:R, :]) * h + both[R:, :]
        state[...] = jnp.where(scal[1] == 1, other[0:R, :] * h + other[R:, :], h)
        run[...] = jnp.ones((R, hidden), f32)
        back[...] = jnp.zeros(back.shape, f32)
        mg[...] = jnp.zeros(mg.shape, f32)

    first = scal[0] + step * tb
    lens = limit[...]

    def body(u, h):
        t = u * 2
        za, zb = halves(zl, u)
        ka, kb = halves(kh, u)
        ha = h - za * h + za * ka
        hb = ha - zb * ha + zb * kb
        hp_out[sixteen(u), :] = jnp.concatenate([h, ha], 0).astype(bf16)
        ya = jnp.where(first + t < lens, ha, 0.0)
        yb = jnp.where(first + t + 1 < lens, hb, 0.0)
        y_out[sixteen(u), :] = jnp.concatenate([ya, yb], 0).astype(bf16)
        return hb

    state[...] = lax.fori_loop(0, tb // 2, body, state[...], unroll=2)
    r1 = position_major(perm[...], x[...]) + nn(y_out[...], wo[...])
    r1_out[...] = r1
    inv = lax.rsqrt(jnp.mean(r1 * r1, -1, keepdims=True) + epsilon)
    n2 = (r1 * inv * mgain[...]).astype(bf16)
    n2_out[...] = n2
    for f in range(0, feed, fchunk):
        cols = slice(f, f + fchunk)
        a, slope = gelu_parts(nn(n2, wu[:, cols]))
        act_out[:, cols] = a.astype(bf16)
        dp_out[:, cols] = (da[:, cols].astype(f32) * slope).astype(bf16)
    dn2 = nt(dp_out[...], wu[...])
    r1 = r1_out[...]
    mg[...] += jnp.sum((dn2 * r1 * inv).reshape(tb, R, width), 0)
    s = mgain[...] * dn2
    mean = jnp.mean(s * r1, -1, keepdims=True)
    dr1 = gl[...].astype(f32) + inv * (s - r1 * (inv * inv * mean))
    dr1_out[...] = dr1
    dm = dr1.astype(bf16)
    dm_out[...] = dm
    dh = nt(dm, wo[...]).reshape(tb, R, hidden)
    pos = first + lax.broadcasted_iota(jnp.int32, (tb, R, hidden), 0)
    dh_out[...] = jnp.where(pos < lens[None], dh, 0.0).reshape(m, hidden).astype(bf16)

    def adjoint(u, carry):
        prod, total = carry
        za, zb = halves(zl, u)
        da, db = halves(dh_out, u)
        pa = prod - za * prod
        pb = pa - zb * pa
        return pb, total + (pa * da + pb * db)

    prod, total = lax.fori_loop(0, tb // 2, adjoint, (run[...], back[...]), unroll=4)
    run[...] = prod
    back[...] = total


def put_rows(dst, sel, piece, at, rows, part):
    for i in range(SLOTS // 2):
        pos = pl.multiple_of((i ^ sel) * piece + at, 16)
        dst[pl.ds(pos, rows), :] = part[i * rows : (i + 1) * rows]


def ffn_grad_kernel(scal, act, gl, n2, dp, dst, *, pick):
    step = pl.program_id(0)
    sel = scal[2 + pick]
    width = gl.shape[1]
    rows1 = act.shape[1] * 4 // SLOTS
    rows2 = n2.shape[1] * 2 // SLOTS
    part = tn(act[...], gl[...]).astype(bf16)
    per = act.shape[1] // rows1
    for i in range(per):
        pos = ((step * per + i) ^ sel) * PIECE1
        dst[pl.ds(pl.multiple_of(pos, 16), rows1), :] = part[i * rows1 : (i + 1) * rows1]
    columns = dp.shape[1] // width
    for q in range(columns):
        part = tn(n2[...], dp[:, q * width : (q + 1) * width]).astype(bf16)
        put_rows(dst, sel, PIECE1, rows1 + (step * columns + q) * rows2, rows2, part)


def gate_grad_kernel(scal, c, dkz, dkh, y, dm, dst, *, pick):
    sel = scal[2 + pick]
    width = dm.shape[1]
    rows = c.shape[1] * 2 // SLOTS
    at = 0
    for grads in (dkz, dkh):
        for q in range(grads.shape[1] // width):
            part = tn(c[...], grads[:, q * width : (q + 1) * width]).astype(bf16)
            put_rows(dst, sel, PIECE2, at, rows, part)
            at += rows
    put_rows(dst, sel, PIECE2, at, y.shape[1] * 2 // SLOTS, tn(y[...], dm[...]).astype(bf16))


def gate_kernel(scal, dh, zl, kh, hp, other, fother, *refs, blocks, hops):
    msgs = refs[:hops]
    wg, wc = refs[hops : hops + 2]
    dkz, dkh, edge_out, bias_out = refs[hops + 3 : hops + 7]
    state = refs[hops + 7]
    step = pl.program_id(0)
    m = dh.shape[0]
    tb = m // R
    block = blocks - 1 - step

    @pl.when(step == 0)
    def _():
        mm = jnp.zeros(state.shape, f32)
        for msg in reversed(msgs):
            both = msg[...].astype(f32)
            mm = jnp.exp(both[0:R, :]) * mm + both[R:, :]
        state[...] = jnp.where(scal[1] == 0, fother[...] + other[0:R, :] * mm, mm)
        bias_out[...] = jnp.zeros(bias_out.shape, f32)

    def body(u, carry):
        mm, bias = carry
        w = tb // 2 - 1 - u
        ha, hb = halves(hp, w)
        za, zb = halves(zl, w)
        da, db = halves(dh, w)
        ka, kb = halves(kh, w)
        lam = db + mm
        sb = lam * zb
        mm = lam - sb
        kb = (sb - sb * zb) * (kb - hb)
        lam = da + mm
        sa = lam * za
        mm = lam - sa
        ka = (sa - sa * za) * (ka - ha)
        kk = jnp.concatenate([ka, kb], 0).astype(bf16)
        dkz[sixteen(w), :] = kk
        dkh[sixteen(w), :] = jnp.concatenate([sa, sb], 0).astype(bf16)
        kf = kk.astype(f32)
        return mm, bias + kf[:R, :] + kf[R:, :]

    mm, bias = lax.fori_loop(0, tb // 2, body, (state[...], bias_out[...]), unroll=2)
    state[...] = mm
    bias_out[...] = bias

    @pl.when(block == 0)
    def _():
        span = edge_out.shape[0]
        edge_out[...] = (nt(dkz[0:span, :], wg[...]) + nt(dkh[0:span, :], wc[...])).astype(bf16)


def tail_kernel(x, dr1, dkz, dkh, pm, back_pm, edge, after, gain, convw, wg, wc, grad, sums, uext, dext, *, blocks):
    step = pl.program_id(0)
    tb = x.shape[1]
    m = tb * R
    halo = edge.shape[0]
    taps = convw.shape[0]
    width = gain.shape[1]

    @pl.when(step == 0)
    def _():
        uext[0:halo, :] = normed_edge(edge[...], gain[...])
        dext[blocks * m :, :] = after[...].astype(f32)
        sums[...] = jnp.zeros(sums.shape, f32)

    @pl.when(step < blocks)
    def _():
        rows = pl.ds(pl.multiple_of(step * m, m), m)
        dext[rows, :] = nt(dkz[...], wg[...]) + nt(dkh[...], wc[...])

    @pl.when(step >= blocks)
    def _():
        xp = position_major(pm[...], x[...])
        inv = lax.rsqrt(jnp.mean(xp * xp, -1, keepdims=True) + epsilon)
        xn = xp * inv
        uext[halo:, :] = (xn * gain[...]).astype(bf16).astype(f32)
        start = (step - blocks) * m
        here = dext[pl.ds(pl.multiple_of(start, R), m), :]
        du = convw[0:1, :] * here
        for k in range(taps):
            lo = halo - k * R
            part = (here * uext[lo : lo + m, :]).reshape(tb, R, width)
            sums[(k + 1) * R : (k + 2) * R, :] += jnp.sum(part, 0)
            if k:
                du = du + convw[k : k + 1, :] * dext[pl.ds(pl.multiple_of(start + k * R, R), m), :]
        uext[0:halo, :] = uext[m : m + halo, :]
        sums[0:R, :] += jnp.sum((du * xn).reshape(tb, R, width), 0)
        s1 = gain[...] * du
        mean = jnp.mean(s1 * xn, -1, keepdims=True)
        gin = dr1[...] + inv * (s1 - xn * mean)
        grad[...] = row_major(back_pm[...], gin.astype(bf16))


def output_kernel(r1, act, perm, wd, out):
    total = r1[...] + nn(act[...], wd[...])
    out[...] = row_major(perm[...], total.astype(bf16))


def spread_kernel(scal, src, *refs, piece, plan, mate):
    low = scal[2 + mate] & 7
    for a in range(8):
        base = (a ^ low) * piece
        at = 0
        for out, rows, columns in plan:
            ref = refs[len(refs) - len(plan) + out]
            for q in range(columns):
                width = src.shape[1]
                part = src[pl.ds(pl.multiple_of(base + at, 16), rows), :].astype(f32)
                ref[a * rows : (a + 1) * rows, q * width : (q + 1) * width] = part
                at += rows


def spread(scal, src, held, mate, flip, piece, plan, shapes, name):
    def block(g, s):
        return ((s[1] ^ mate) * 2 + ((s[2 + mate] >> 3) ^ flip), 0)

    count = len(held)
    return pl.pallas_call(
        functools.partial(spread_kernel, piece=piece, plan=plan, mate=mate),
        grid_spec=pltpu.PrefetchScalarGridSpec(
            num_scalar_prefetch=1,
            grid=(1,),
            in_specs=[whole(src)] + [ORDER] * count,
            out_specs=[pl.BlockSpec((dims[0] // 4, dims[1]), block) for dims in shapes],
        ),
        out_shape=[pltpu.HBM(dims, f32) for dims in shapes],
        input_output_aliases={2 + k: k for k in range(count)},
        compiler_params=params(16),
        cost_estimate=LITTLE,
        name=name,
    )(scal, src, *held)


def params(mib):
    return pltpu.CompilerParams(
        dimension_semantics=("arbitrary",), vmem_limit_bytes=mib * 1024 * 1024
    )


def shape(dims, kind=f32):
    return jax.ShapeDtypeStruct(dims, kind)


LITTLE = pl.CostEstimate(flops=1024, bytes_accessed=1024, transcendentals=0)
MUCH = pl.CostEstimate(flops=3 * 10**10, bytes_accessed=1024, transcendentals=0)
ORDER = pl.BlockSpec(memory_space=pl.ANY)


def far(array):
    return pltpu.with_memory_space_constraint(array, pltpu.HBM)


def whole(array):
    zeros = (0,) * array.ndim
    return pl.BlockSpec(array.shape, lambda *a: zeros, pipeline_mode=pl.Buffered(1))


def passed_along(value, axis, steps):
    count = lax.axis_size(axis)
    leading, last = (max(0, -steps), min(count, count - steps))
    return lax.ppermute(value, axis, [(source, source + steps) for source in range(leading, last)])


def flat_permute(value, pairs):
    return lax.ppermute(value, ("seq", "row"), pairs)


def stage_bits():
    row_bits = lax.axis_size("row").bit_length() - 1
    seq_bits = lax.axis_size("seq").bit_length() - 1
    plane = list(range(row_bits))
    line = [row_bits + 1 + z for z in range(seq_bits - 1)]
    cut = row_bits // 2
    return (plane + line, plane[cut:] + plane[:cut] + line[::-1])


def slot_of(flat, bits):
    slot = 0
    for k in range(4):
        slot = slot * 2 + ((flat >> bits[k]) & 1)
    return slot


def halving_pairs(stage):
    row_bits = lax.axis_size("row").bit_length() - 1
    orders = stage_bits()
    devices = lax.axis_size("row") * lax.axis_size("seq")
    return [(d, d ^ (1 << orders[(d >> row_bits) & 1][stage])) for d in range(devices)]


def core_pairs():
    row_bits = lax.axis_size("row").bit_length() - 1
    devices = lax.axis_size("row") * lax.axis_size("seq")
    return [(d, d ^ (1 << row_bits)) for d in range(devices)]


def added(a, b):
    return (a.astype(f32) + b.astype(f32)).astype(bf16)


class Sequence:
    def __init__(self, token):
        self.token = token

    def after(self, *arrays):
        *arrays, _ = lax.optimization_barrier((*arrays, self.token))
        return arrays[0] if len(arrays) == 1 else arrays

    def did(self, array):
        self.token = array
        return array


def split(value):
    high = lax.reduce_precision(value, 8, 7)
    return [high.astype(bf16), (value - high).astype(bf16)]


def join_kernel(mine, recv, ride, out, ride_out):
    rows = mine.shape[0] - 2 * R
    out[0:rows, :] = mine[0:rows, :]
    out[rows : 2 * rows, :] = recv[0:rows, :]
    parts = recv[rows:, :].astype(f32)
    total = ride[...] + (parts[:R] + parts[R:])
    ride_out[...] = total
    high = total.astype(bf16).astype(f32)
    out[2 * rows :, :] = jnp.concatenate([high, total - high], 0).astype(bf16)


def joined(mine, recv, ride):
    rows, width = mine.shape
    return pl.pallas_call(
        join_kernel,
        in_specs=[pl.BlockSpec(memory_space=pltpu.VMEM)] * 3,
        out_specs=[pl.BlockSpec(memory_space=pltpu.VMEM)] * 2,
        out_shape=[shape((2 * rows - 2 * R, width), bf16), shape(ride.shape)],
        compiler_params=pltpu.CompilerParams(vmem_limit_bytes=16 * 1024 * 1024),
        cost_estimate=LITTLE,
        name="join",
    )(mine, recv, ride)


class Halving:
    def __init__(self, seq, send):
        self.seq = seq
        self.recv = flat_permute(send, core_pairs())
        self.stage = 0
        self.ride = None

    def riders(self):
        return [] if self.ride is None else split(self.ride)

    def board(self, recv, rows):
        if self.ride is not None:
            low = rows + self.ride.shape[0]
            self.ride = self.ride + (recv[rows:low].astype(f32) + recv[low:].astype(f32))

    def step(self, *beside):
        k = self.stage
        self.stage += 1
        stages = len(stage_bits()[0])
        recv, *beside = self.seq.after(self.recv, *beside) if beside else (self.seq.after(self.recv),)
        if k < 4:
            half = self.keep.shape[0] // 2
            send = self.seq.did(added(self.keep[half:], recv[half:]))
            self.recv = flat_permute(send, halving_pairs(k))
            self.keep = added(self.keep[:half], recv[:half])
        elif k == 4:
            total = added(self.keep, recv)
            for extra in range(4, stages):
                total = added(total, flat_permute(total, halving_pairs(extra)))
                if self.ride is not None:
                    self.ride = self.ride + flat_permute(self.ride, halving_pairs(extra))
            self.rows = total.shape[0]
            self.total = self.seq.did(jnp.concatenate([total] + self.riders(), 0))
            self.recv = flat_permute(self.total, halving_pairs(3))
        elif k < 8:
            rows = self.rows
            self.rows = 2 * rows
            if self.ride is None:
                self.total = self.seq.did(jnp.concatenate([self.total, recv], 0))
            else:
                self.total, self.ride = joined(self.total, recv, self.ride)
                self.seq.did(self.total)
            self.recv = flat_permute(self.total, halving_pairs(7 - k))
            if k == 7:
                self.theirs = flat_permute(self.total, core_pairs())
        else:
            self.board(recv, self.rows)
            self.rest = recv
            self.their_rest = flat_permute(recv, core_pairs())
        return beside


def chip_shift(value, steps):
    return passed_along(value, "seq", 2 * steps)


def per_device(
    inputs,
    lengths,
    norm_gain,
    conv_weight,
    gate_weight,
    gate_bias,
    cand_weight,
    out_weight,
    mlp_gain,
    up_weight,
    down_weight,
    cotangent,
):
    rows, span, width = inputs.shape
    hidden = gate_weight.shape[1]
    feed = up_weight.shape[1]
    taps = conv_weight.shape[0]
    margin = taps - 1
    tokens = rows * span
    tb = 32
    blocks = span // tb
    m = tb * R
    seq = lax.axis_index("seq")
    core = seq & 1
    chips = lax.axis_size("seq") // 2
    hops = chips - 1
    flat = seq * lax.axis_size("row") + lax.axis_index("row")
    slots = [slot_of(flat, bits) for bits in stage_bits()]
    here = jnp.where(core == 0, slots[0], slots[1])
    mate = jnp.where(core == 0, slots[1], slots[0])
    scal = jnp.concatenate([jnp.stack([seq * span, core, here, mate]).astype(jnp.int32), lengths])
    gain1 = norm_gain.reshape(1, width)
    gain2 = mlp_gain.reshape(1, width)
    bias = gate_bias.reshape(1, hidden)
    to_pm, to_rm = token_order()

    edge = inputs[:, span - margin :, :].swapaxes(0, 1).reshape(margin * rows, width)
    edge = passed_along(edge, "seq", 1)

    last = blocks - 1
    clamp = lambda i: jnp.minimum(i, last)
    late = lambda i: jnp.maximum(i - blocks, 0)

    def rm(index):
        return pl.BlockSpec((rows, tb, width), lambda i, *s: (0, index(i), 0))

    def tok(w, index=clamp):
        return pl.BlockSpec((m, w), lambda i, *s: (index(i), 0))

    def rtok(w):
        return tok(w, lambda i: last - clamp(i))

    def fixed(dims):
        zeros = (0,) * len(dims)
        return pl.BlockSpec(dims, lambda i, *s: zeros)

    def call(kernel, name, grid, ins, outs, scratch, operands, scalars=True, much=False):
        spec = pltpu.PrefetchScalarGridSpec(
            num_scalar_prefetch=int(scalars),
            grid=(grid,),
            in_specs=ins,
            out_specs=[o[1] for o in outs],
            scratch_shapes=scratch,
        )
        return pl.pallas_call(
            kernel,
            grid_spec=spec,
            out_shape=[o[0] for o in outs],
            compiler_params=params(16),
            cost_estimate=MUCH if much else LITTLE,
            name=name,
        )(*operands)

    def rows_of(w, kind, spec=tok, kept=shape):
        return kept((tokens, w), kind), spec(w)

    c, zl, kh, ends = call(
        front_kernel, "front", blocks,
        [
            rm(clamp), whole(to_pm), whole(edge), whole(gain1), whole(conv_weight),
            whole(gate_weight), whole(bias), whole(cand_weight),
        ],
        [
            rows_of(width, bf16), rows_of(hidden, bf16), rows_of(hidden, bf16),
            (shape((2 * R, hidden)), fixed((2 * R, hidden))),
        ],
        [
            pltpu.VMEM((margin * R + m, width), f32),
            pltpu.VMEM((2 * R, hidden), f32),
            pltpu.VMEM((R, hidden), jnp.int32),
        ],
        (
            scal, far(inputs), far(to_pm), edge, far(gain1), far(conv_weight), far(gate_weight),
            far(bias), far(cand_weight),
        ),
    )

    other = flat_permute(ends, core_pairs())
    first = jnp.where(core == 0, ends, other)
    second = jnp.where(core == 0, other, ends)
    decay = jnp.log(jnp.maximum(ends[:R] * other[:R], 1e-37))
    message = jnp.concatenate([decay, second[:R] * first[R:] + second[R:]], 0).astype(bf16)
    forward = [chip_shift(message, k) for k in range(1, chips)]

    gl, da = call(
        da_kernel, "da", blocks,
        [rm(clamp), whole(to_pm), whole(down_weight)],
        [rows_of(width, bf16), rows_of(feed, bf16)],
        [],
        (cotangent, to_pm, down_weight),
        scalars=False,
    )

    r1, y, hp, n2, act, dp, dm, dr1, dh, back, mg = call(
        functools.partial(core_kernel, fchunk=512, hops=hops), "core", blocks,
        [
            rm(clamp), whole(to_pm), tok(width), tok(feed), tok(hidden), tok(hidden), whole(other),
            *[whole(f) for f in forward], whole(out_weight), whole(gain2), whole(up_weight),
        ],
        [
            rows_of(width, f32, kept=pltpu.HBM), rows_of(hidden, bf16), rows_of(hidden, bf16),
            rows_of(width, bf16), rows_of(feed, bf16), rows_of(feed, bf16), rows_of(width, bf16),
            rows_of(width, f32, kept=pltpu.HBM),
            rows_of(hidden, bf16),
            (shape((R, hidden)), fixed((R, hidden))), (shape((R, width)), fixed((R, width))),
        ],
        [
            pltpu.VMEM((R, hidden), f32),
            pltpu.VMEM((R, hidden), jnp.int32),
            pltpu.VMEM((R, hidden), f32),
        ],
        (scal, inputs, to_pm, gl, da, zl, kh, other, *forward, out_weight, gain2, up_weight),
    )

    order = Sequence(back)
    quarter = feed // 4

    def ffn_grads(pick, *beside):
        half = lambda s: s[1] if pick == 0 else 1 - s[1]
        a, d, *beside = order.after(act, dp, *beside)
        (piece,) = call(
            functools.partial(ffn_grad_kernel, pick=pick), "ffn_grad", 2,
            [
                pl.BlockSpec((tokens, quarter), lambda i, s: (0, half(s) * 2 + i)), whole(gl),
                pl.BlockSpec((tokens, width // 2), lambda i, s: (0, half(s))),
                pl.BlockSpec((tokens, feed // 2), lambda i, s: (0, i)),
            ],
            [(shape((SLOTS // 2 * PIECE1, width), bf16), fixed((SLOTS // 2 * PIECE1, width)))],
            [],
            (scal, a, gl, n2, d),
            much=pick == 0,
        )
        return order.did(piece), beside

    def gate_grads(pick):
        half = lambda s: s[1] if pick == 0 else 1 - s[1]
        z, h = order.after(dkz, dkh)
        (piece,) = call(
            functools.partial(gate_grad_kernel, pick=pick), "gate_grad", 1,
            [
                pl.BlockSpec((tokens, width // 2), lambda i, s: (0, half(s))),
                whole(z), whole(h),
                pl.BlockSpec((tokens, hidden // 2), lambda i, s: (0, half(s))), whole(dm),
            ],
            [(shape((SLOTS // 2 * PIECE2, width), bf16), fixed((SLOTS // 2 * PIECE2, width)))],
            [],
            (scal, c, z, h, y, dm),
            much=pick == 0,
        )
        return order.did(piece)

    fother = flat_permute(back, core_pairs())
    lower = jnp.where(core == 0, back, fother)
    upper = jnp.where(core == 0, fother, back)
    message = jnp.concatenate([decay, lower + first[:R] * upper], 0).astype(bf16)
    backward = [chip_shift(order.did(message), -k) for k in range(1, chips)]
    send1, _ = ffn_grads(1)
    chunk1 = Halving(order, send1)
    chunk1.keep, backward = ffn_grads(0, *backward)
    chunk1.step()

    dkz, dkh, edge_dc, bias_part = call(
        functools.partial(gate_kernel, blocks=blocks, hops=hops), "gates", blocks,
        [
            rtok(hidden), rtok(hidden), rtok(hidden), rtok(hidden),
            whole(other), whole(fother), *[whole(f) for f in backward],
            whole(gate_weight), whole(cand_weight), ORDER,
        ],
        [
            rows_of(hidden, bf16, rtok), rows_of(hidden, bf16, rtok),
            (shape((4 * R, width), bf16), fixed((4 * R, width))),
            (shape((R, hidden)), fixed((R, hidden))),
        ],
        [pltpu.VMEM((R, hidden), f32)],
        (
            scal, dh, zl, kh, hp, other, fother, *backward, gate_weight, cand_weight, order.token,
        ),
    )
    order.did(bias_part)
    after = passed_along(edge_dc[: margin * R], "seq", -1)
    send2 = gate_grads(1)
    chunk2 = Halving(order, send2)
    chunk1.step()
    chunk2.keep = gate_grads(0)
    chunk2.step()
    (output,) = call(
        output_kernel, "output", blocks,
        [tok(width), tok(feed), whole(to_rm), whole(down_weight)],
        [(shape((rows, span, width), bf16), rm(clamp))],
        [],
        (far(r1), order.after(act), to_rm, down_weight),
        scalars=False,
    )
    order.did(output)
    input_grad, sums = call(
        functools.partial(tail_kernel, blocks=blocks), "tail", 2 * blocks,
        [
            rm(late), tok(width, late), tok(hidden), tok(hidden), whole(to_pm), whole(to_rm),
            whole(edge), whole(after), whole(gain1), whole(conv_weight), whole(gate_weight),
            whole(cand_weight),
        ],
        [
            (shape((rows, span, width), bf16), rm(late)),
            (shape(((taps + 1) * R, width)), fixed(((taps + 1) * R, width))),
        ],
        [
            pltpu.VMEM((margin * R + m, width), f32),
            pltpu.VMEM((margin * R + tokens, width), f32),
        ],
        (
            far(inputs), far(dr1), order.after(dkz), dkh, far(to_pm), far(to_rm), edge, after,
            far(gain1), far(conv_weight), far(gate_weight), far(cand_weight),
        ),
        scalars=False,
    )
    order.did(sums)
    small = jnp.concatenate(
        [
            sums.reshape(taps + 1, R, width).sum(1),
            mg.sum(0, keepdims=True),
            bias_part.sum(0).reshape(hidden // width, width),
        ],
        0,
    )
    coming = flat_permute(small, core_pairs())

    plan1 = ((0, feed // SLOTS, 1), (1, width // SLOTS, feed // width))
    shapes1 = ((feed, width), (width, feed))
    plan2 = (
        (0, width // SLOTS, hidden // width),
        (1, width // SLOTS, hidden // width),
        (2, hidden // SLOTS, 1),
    )
    shapes2 = ((width, hidden), (width, hidden), (hidden, width))
    held1, held2 = (), ()

    def spread1(src, mate, flip):
        nonlocal held1
        src = order.after(src)
        held1 = spread(scal, src, held1, mate, flip, PIECE1, plan1, shapes1, "spread_ffn")
        order.did(held1[0])

    def spread2(src, mate, flip):
        nonlocal held2
        src = order.after(src)
        held2 = spread(scal, src, held2, mate, flip, PIECE2, plan2, shapes2, "spread_gates")
        order.did(held2[0])

    for chunk in (chunk1, chunk2, chunk1, chunk1, chunk2, chunk1, chunk2, chunk1):
        chunk.step()
    chunk2.ride = small + order.after(coming)
    chunk2.step()
    chunk2.step()
    chunk1.step()
    spread1(chunk1.total, 0, 0)
    chunk2.step()
    spread1(chunk1.theirs, 1, 0)
    chunk2.step()
    chunk1.step()
    spread1(chunk1.rest, 0, 1)
    spread2(chunk2.total, 0, 0)
    spread1(chunk1.their_rest, 1, 1)
    spread2(chunk2.theirs, 1, 0)
    chunk2.step()
    small = chunk2.ride
    small_out = order.after(
        small[0], small[1 : taps + 1], small[taps + 2 :].reshape(hidden), small[taps + 1]
    )
    spread2(chunk2.rest, 0, 1)
    spread2(chunk2.their_rest, 1, 1)
    return (
        output,
        input_grad,
        small_out[0],
        small_out[1],
        held2[0],
        small_out[2],
        held2[1],
        held2[2],
        small_out[3],
        held1[1],
        held1[0],
    )


def solution(mesh):
    sharded = P("row", "seq", None)
    in_specs = (sharded, P("row")) + (P(),) * 9 + (sharded,)
    out_specs = (sharded, sharded) + (P(),) * 9
    return jax.shard_map(
        per_device, mesh=mesh, in_specs=in_specs, out_specs=out_specs, check_vma=False
    )
```

```python
import functools

import jax
import jax.numpy as jnp
import numpy as np
from jax import lax
from jax.experimental import pallas as pl
from jax.experimental.pallas import tpu as pltpu
from jax.sharding import PartitionSpec as P

epsilon = 1e-06
f32 = jnp.float32
bf16 = jnp.bfloat16
R = 8
PERM = 256
SCALARS = 4
SLOTS = 32
PIECE1 = 128
PIECE2 = 96


def nn(a, b):
    return lax.dot_general(a, b, (((1,), (0,)), ((), ())), preferred_element_type=f32)


def nt(a, b):
    return lax.dot_general(a, b, (((1,), (1,)), ((), ())), preferred_element_type=f32)


def tn(a, b):
    return lax.dot_general(a, b, (((0,), (0,)), ((), ())), preferred_element_type=f32)


def token_order():
    out = np.arange(PERM)
    source = (out % R) * (PERM // R) + out // R
    to_pm = np.zeros((PERM, PERM), np.float32)
    to_pm[out, source] = 1
    return jnp.asarray(to_pm, bf16), jnp.asarray(to_pm.T, bf16)


def position_major(perm, block):
    span = PERM // R
    parts = []
    for s in range(block.shape[1] // span):
        part = block[:, s * span : (s + 1) * span, :].reshape(PERM, block.shape[2])
        parts.append(nn(perm, part))
    return parts[0] if len(parts) == 1 else jnp.concatenate(parts, 0)


def row_major(perm, tokens):
    span = PERM // R
    parts = []
    for s in range(tokens.shape[0] // PERM):
        part = nn(perm, tokens[s * PERM : (s + 1) * PERM]).astype(bf16)
        parts.append(part.reshape(R, span, tokens.shape[1]))
    return parts[0] if len(parts) == 1 else jnp.concatenate(parts, 1)


def eight(t):
    return pl.ds(pl.multiple_of(t * R, R), R)


def sixteen(t):
    return pl.ds(pl.multiple_of(t * 2 * R, 2 * R), 2 * R)


def normed_edge(edge, gain):
    e = edge.astype(f32)
    inv = lax.rsqrt(jnp.mean(e * e, -1, keepdims=True) + epsilon)
    return (e * inv * gain).astype(bf16).astype(f32)


def set_limits(scal, limit):
    row = lax.broadcasted_iota(jnp.int32, limit.shape, 0)
    value = jnp.zeros(limit.shape, jnp.int32)
    for r in range(R):
        value = jnp.where(row == r, scal[SCALARS + r], value)
    limit[...] = value


def halves(ref, pair):
    both = ref[sixteen(pair), :].astype(f32)
    return both[:R], both[R:]


def front_kernel(scal, x, perm, edge, gain, convw, wg, bias, wc, c_out, zl_out, kh_out, ends, ext, state, limit):
    step = pl.program_id(0)
    tb = x.shape[1]
    m = tb * R
    halo = edge.shape[0]
    taps = convw.shape[0]

    @pl.when(step == 0)
    def _():
        set_limits(scal, limit)
        ext[0:halo, :] = normed_edge(edge[...], gain[...])
        state[0:R, :] = jnp.ones((R, state.shape[1]), f32)
        state[R:, :] = jnp.zeros((R, state.shape[1]), f32)

    xp = position_major(perm[...], x[...])
    inv = lax.rsqrt(jnp.mean(xp * xp, -1, keepdims=True) + epsilon)
    ext[halo:, :] = (xp * inv * gain[...]).astype(bf16).astype(f32)
    conv = convw[0:1, :] * ext[halo:, :]
    for k in range(1, taps):
        lo = halo - k * R
        conv = conv + convw[k : k + 1, :] * ext[lo : lo + m, :]
    ext[0:halo, :] = ext[m : m + halo, :]
    cb = conv.astype(bf16)
    c_out[...] = cb
    kz = nn(cb, wg[...]) + bias[...]
    zs = 1.0 / (1.0 + jnp.exp(-kz))
    width = zs.shape[1]
    zs = zs.reshape(tb, R, width)
    pos = scal[0] + step * tb + lax.broadcasted_iota(jnp.int32, (tb, R, width), 0)
    zl_out[...] = jnp.where(pos < limit[...][None], zs, 0.0).reshape(m, width).astype(bf16)
    kh_out[...] = nn(cb, wc[...]).astype(bf16)

    def body(u, carry):
        prod, h = carry
        za, zb = halves(zl_out, u)
        ka, kb = halves(kh_out, u)
        a = 1.0 - za
        b = 1.0 - zb
        return prod * (a * b), (h * a + za * ka) * b + zb * kb

    prod, h = lax.fori_loop(0, tb // 2, body, (state[0:R, :], state[R:, :]), unroll=4)
    state[0:R, :] = prod
    state[R:, :] = h
    ends[0:R, :] = prod
    ends[R:, :] = h


def gelu_parts(p):
    k0 = 0.7978845608028654
    p2 = p * p
    th = jnp.tanh(p * (k0 + (k0 * 0.044715) * p2))
    ht = 0.5 + 0.5 * th
    return p * ht, ht + (2.0 * p) * (ht - ht * ht) * (k0 + (3.0 * k0 * 0.044715) * p2)


def da_kernel(g, perm, wd, gl_out, da_out):
    gl = position_major(perm[...], g[...]).astype(bf16)
    gl_out[...] = gl
    da_out[...] = nt(gl, wd[...]).astype(bf16)


def core_kernel(scal, x, perm, gl, da, zl, kh, other, *refs, fchunk, hops):
    msgs = refs[:hops]
    wo, mgain, wu = refs[hops : hops + 3]
    r1_out, y_out, hp_out, n2_out, act_out, dp_out, dm_out, dr1_out, dh_out, back, mg = refs[hops + 3 : hops + 14]
    state, limit, run, acc = refs[hops + 14 :]
    step = pl.program_id(0)
    tb = x.shape[1]
    m = tb * R
    width, feed = wu.shape
    hidden = wo.shape[0]

    @pl.when(step == 0)
    def _():
        set_limits(scal, limit)
        h = jnp.zeros((R, hidden), f32)
        for msg in reversed(msgs):
            both = msg[...].astype(f32)
            h = jnp.exp(both[0:R, :]) * h + both[R:, :]
        state[...] = jnp.where(scal[1] == 1, other[0:R, :] * h + other[R:, :], h)
        run[...] = jnp.ones((R, hidden), f32)
        back[...] = jnp.zeros(back.shape, f32)
        mg[...] = jnp.zeros(mg.shape, f32)

    first = scal[0] + step * tb
    lens = limit[...]

    def body(u, h):
        t = u * 2
        za, zb = halves(zl, u)
        ka, kb = halves(kh, u)
        ha = h - za * h + za * ka
        hb = ha - zb * ha + zb * kb
        hp_out[sixteen(u), :] = jnp.concatenate([h, ha], 0).astype(bf16)
        ya = jnp.where(first + t < lens, ha, 0.0)
        yb = jnp.where(first + t + 1 < lens, hb, 0.0)
        y_out[sixteen(u), :] = jnp.concatenate([ya, yb], 0).astype(bf16)
        return hb

    state[...] = lax.fori_loop(0, tb // 2, body, state[...], unroll=2)
    r1 = position_major(perm[...], x[...]) + nn(y_out[...], wo[...])
    r1_out[...] = r1
    inv = lax.rsqrt(jnp.mean(r1 * r1, -1, keepdims=True) + epsilon)
    n2 = (r1 * inv * mgain[...]).astype(bf16)
    n2_out[...] = n2
    for f in range(0, feed, fchunk):
        cols = slice(f, f + fchunk)
        a, slope = gelu_parts(nn(n2, wu[:, cols]))
        act_out[:, cols] = a.astype(bf16)
        dpb = (da[:, cols].astype(f32) * slope).astype(bf16)
        dp_out[:, cols] = dpb
        part = nt(dpb, wu[:, cols])
        acc[...] = acc[...] + part if f else part
    dn2 = acc[...]
    r1 = r1_out[...]
    mg[...] += jnp.sum((dn2 * r1 * inv).reshape(tb, R, width), 0)
    s = mgain[...] * dn2
    mean = jnp.mean(s * r1, -1, keepdims=True)
    dr1 = gl[...].astype(f32) + inv * (s - r1 * (inv * inv * mean))
    dr1_out[...] = dr1
    dm = dr1.astype(bf16)
    dm_out[...] = dm
    dh = nt(dm, wo[...]).reshape(tb, R, hidden)
    pos = first + lax.broadcasted_iota(jnp.int32, (tb, R, hidden), 0)
    dh_out[...] = jnp.where(pos < lens[None], dh, 0.0).reshape(m, hidden).astype(bf16)

    def adjoint(u, carry):
        prod, total = carry
        za, zb = halves(zl, u)
        da, db = halves(dh_out, u)
        pa = prod - za * prod
        pb = pa - zb * pa
        return pb, total + (pa * da + pb * db)

    prod, total = lax.fori_loop(0, tb // 2, adjoint, (run[...], back[...]), unroll=4)
    run[...] = prod
    back[...] = total


def put_rows(dst, sel, piece, at, rows, part):
    for i in range(SLOTS // 2):
        pos = pl.multiple_of((i ^ sel) * piece + at, 16)
        dst[pl.ds(pos, rows), :] = part[i * rows : (i + 1) * rows]


def ffn_grad_kernel(scal, act, gl, n2, dp, dst, *, pick):
    step = pl.program_id(0)
    sel = scal[2 + pick]
    width = gl.shape[1]
    rows1 = act.shape[1] * 4 // SLOTS
    rows2 = n2.shape[1] * 2 // SLOTS
    part = tn(act[...], gl[...]).astype(bf16)
    per = act.shape[1] // rows1
    for i in range(per):
        pos = ((step * per + i) ^ sel) * PIECE1
        dst[pl.ds(pl.multiple_of(pos, 16), rows1), :] = part[i * rows1 : (i + 1) * rows1]
    columns = dp.shape[1] // width
    for q in range(columns):
        part = tn(n2[...], dp[:, q * width : (q + 1) * width]).astype(bf16)
        put_rows(dst, sel, PIECE1, rows1 + (step * columns + q) * rows2, rows2, part)


def gate_grad_kernel(scal, c, dkz, dkh, y, dm, dst, *, pick):
    sel = scal[2 + pick]
    width = dm.shape[1]
    rows = c.shape[1] * 2 // SLOTS
    at = 0
    for grads in (dkz, dkh):
        for q in range(grads.shape[1] // width):
            part = tn(c[...], grads[:, q * width : (q + 1) * width]).astype(bf16)
            put_rows(dst, sel, PIECE2, at, rows, part)
            at += rows
    put_rows(dst, sel, PIECE2, at, y.shape[1] * 2 // SLOTS, tn(y[...], dm[...]).astype(bf16))


def gate_kernel(scal, dh, zl, kh, hp, other, fother, *refs, blocks, hops):
    msgs = refs[:hops]
    wg, wc = refs[hops : hops + 2]
    dkz, dkh, edge_out, bias_out = refs[hops + 3 : hops + 7]
    state = refs[hops + 7]
    step = pl.program_id(0)
    m = dh.shape[0]
    tb = m // R
    block = blocks - 1 - step

    @pl.when(step == 0)
    def _():
        mm = jnp.zeros(state.shape, f32)
        for msg in reversed(msgs):
            both = msg[...].astype(f32)
            mm = jnp.exp(both[0:R, :]) * mm + both[R:, :]
        state[...] = jnp.where(scal[1] == 0, fother[...] + other[0:R, :] * mm, mm)
        bias_out[...] = jnp.zeros(bias_out.shape, f32)

    def body(u, carry):
        mm, bias = carry
        w = tb // 2 - 1 - u
        ha, hb = halves(hp, w)
        za, zb = halves(zl, w)
        da, db = halves(dh, w)
        ka, kb = halves(kh, w)
        lam = db + mm
        sb = lam * zb
        mm = lam - sb
        kb = (sb - sb * zb) * (kb - hb)
        lam = da + mm
        sa = lam * za
        mm = lam - sa
        ka = (sa - sa * za) * (ka - ha)
        kk = jnp.concatenate([ka, kb], 0).astype(bf16)
        dkz[sixteen(w), :] = kk
        dkh[sixteen(w), :] = jnp.concatenate([sa, sb], 0).astype(bf16)
        kf = kk.astype(f32)
        return mm, bias + kf[:R, :] + kf[R:, :]

    mm, bias = lax.fori_loop(0, tb // 2, body, (state[...], bias_out[...]), unroll=2)
    state[...] = mm
    bias_out[...] = bias

    @pl.when(block == 0)
    def _():
        span = edge_out.shape[0]
        edge_out[...] = (nt(dkz[0:span, :], wg[...]) + nt(dkh[0:span, :], wc[...])).astype(bf16)


def tail_kernel(x, dr1, dkz, dkh, pm, back_pm, edge, after, gain, convw, wg, wc, grad, sums, uext, dext, *, blocks):
    step = pl.program_id(0)
    tb = x.shape[1]
    m = tb * R
    halo = edge.shape[0]
    taps = convw.shape[0]
    width = gain.shape[1]

    @pl.when(step == 0)
    def _():
        uext[0:halo, :] = normed_edge(edge[...], gain[...])
        dext[blocks * m :, :] = after[...].astype(f32)
        sums[...] = jnp.zeros(sums.shape, f32)

    @pl.when(step < blocks)
    def _():
        rows = pl.ds(pl.multiple_of(step * m, m), m)
        dext[rows, :] = nt(dkz[...], wg[...]) + nt(dkh[...], wc[...])

    @pl.when(step >= blocks)
    def _():
        xp = position_major(pm[...], x[...])
        inv = lax.rsqrt(jnp.mean(xp * xp, -1, keepdims=True) + epsilon)
        xn = xp * inv
        uext[halo:, :] = (xn * gain[...]).astype(bf16).astype(f32)
        start = (step - blocks) * m
        here = dext[pl.ds(pl.multiple_of(start, R), m), :]
        du = convw[0:1, :] * here
        for k in range(taps):
            lo = halo - k * R
            part = (here * uext[lo : lo + m, :]).reshape(tb, R, width)
            sums[(k + 1) * R : (k + 2) * R, :] += jnp.sum(part, 0)
            if k:
                du = du + convw[k : k + 1, :] * dext[pl.ds(pl.multiple_of(start + k * R, R), m), :]
        uext[0:halo, :] = uext[m : m + halo, :]
        sums[0:R, :] += jnp.sum((du * xn).reshape(tb, R, width), 0)
        s1 = gain[...] * du
        mean = jnp.mean(s1 * xn, -1, keepdims=True)
        gin = dr1[...] + inv * (s1 - xn * mean)
        grad[...] = row_major(back_pm[...], gin.astype(bf16))


def output_kernel(r1, act, perm, wd, out):
    total = r1[...] + nn(act[...], wd[...])
    out[...] = row_major(perm[...], total.astype(bf16))


def spread_kernel(scal, src, *refs, piece, plan, mate):
    low = scal[2 + mate] & 7
    for a in range(8):
        base = (a ^ low) * piece
        at = 0
        for out, rows, columns in plan:
            ref = refs[len(refs) - len(plan) + out]
            for q in range(columns):
                width = src.shape[1]
                part = src[pl.ds(pl.multiple_of(base + at, 16), rows), :].astype(f32)
                ref[a * rows : (a + 1) * rows, q * width : (q + 1) * width] = part
                at += rows


def spread(scal, src, held, mate, flip, piece, plan, shapes, name):
    def block(g, s):
        return ((s[1] ^ mate) * 2 + ((s[2 + mate] >> 3) ^ flip), 0)

    count = len(held)
    return pl.pallas_call(
        functools.partial(spread_kernel, piece=piece, plan=plan, mate=mate),
        grid_spec=pltpu.PrefetchScalarGridSpec(
            num_scalar_prefetch=1,
            grid=(1,),
            in_specs=[whole(src)] + [ORDER] * count,
            out_specs=[pl.BlockSpec((dims[0] // 4, dims[1]), block) for dims in shapes],
        ),
        out_shape=[pltpu.HBM(dims, f32) for dims in shapes],
        input_output_aliases={2 + k: k for k in range(count)},
        compiler_params=params(16),
        cost_estimate=LITTLE,
        name=name,
    )(scal, src, *held)


def params(mib):
    return pltpu.CompilerParams(
        dimension_semantics=("arbitrary",), vmem_limit_bytes=mib * 1024 * 1024
    )


def shape(dims, kind=f32):
    return jax.ShapeDtypeStruct(dims, kind)


LITTLE = pl.CostEstimate(flops=1024, bytes_accessed=1024, transcendentals=0)
MUCH = pl.CostEstimate(flops=3 * 10**10, bytes_accessed=1024, transcendentals=0)
ORDER = pl.BlockSpec(memory_space=pl.ANY)


def far(array):
    return pltpu.with_memory_space_constraint(array, pltpu.HBM)


def whole(array):
    zeros = (0,) * array.ndim
    return pl.BlockSpec(array.shape, lambda *a: zeros, pipeline_mode=pl.Buffered(1))


def passed_along(value, axis, steps):
    count = lax.axis_size(axis)
    leading, last = (max(0, -steps), min(count, count - steps))
    return lax.ppermute(value, axis, [(source, source + steps) for source in range(leading, last)])


def flat_permute(value, pairs):
    return lax.ppermute(value, ("seq", "row"), pairs)


def stage_bits():
    row_bits = lax.axis_size("row").bit_length() - 1
    seq_bits = lax.axis_size("seq").bit_length() - 1
    plane = list(range(row_bits))
    line = [row_bits + 1 + z for z in range(seq_bits - 1)]
    cut = row_bits // 2
    return (plane + line, plane[cut:] + plane[:cut] + line[::-1])


def slot_of(flat, bits):
    slot = 0
    for k in range(4):
        slot = slot * 2 + ((flat >> bits[k]) & 1)
    return slot


def halving_pairs(stage):
    row_bits = lax.axis_size("row").bit_length() - 1
    orders = stage_bits()
    devices = lax.axis_size("row") * lax.axis_size("seq")
    return [(d, d ^ (1 << orders[(d >> row_bits) & 1][stage])) for d in range(devices)]


def core_pairs():
    row_bits = lax.axis_size("row").bit_length() - 1
    devices = lax.axis_size("row") * lax.axis_size("seq")
    return [(d, d ^ (1 << row_bits)) for d in range(devices)]


def added(a, b):
    return (a.astype(f32) + b.astype(f32)).astype(bf16)


class Sequence:
    def __init__(self, token):
        self.token = token

    def after(self, *arrays):
        *arrays, _ = lax.optimization_barrier((*arrays, self.token))
        return arrays[0] if len(arrays) == 1 else arrays

    def did(self, array):
        self.token = array
        return array


def split(value):
    high = lax.reduce_precision(value, 8, 7)
    return [high.astype(bf16), (value - high).astype(bf16)]


def join_kernel(mine, recv, ride, out, ride_out):
    rows = mine.shape[0] - 2 * R
    out[0:rows, :] = mine[0:rows, :]
    out[rows : 2 * rows, :] = recv[0:rows, :]
    parts = recv[rows:, :].astype(f32)
    total = ride[...] + (parts[:R] + parts[R:])
    ride_out[...] = total
    high = total.astype(bf16).astype(f32)
    out[2 * rows :, :] = jnp.concatenate([high, total - high], 0).astype(bf16)


def joined(mine, recv, ride):
    rows, width = mine.shape
    return pl.pallas_call(
        join_kernel,
        in_specs=[pl.BlockSpec(memory_space=pltpu.VMEM)] * 3,
        out_specs=[pl.BlockSpec(memory_space=pltpu.VMEM)] * 2,
        out_shape=[shape((2 * rows - 2 * R, width), bf16), shape(ride.shape)],
        compiler_params=pltpu.CompilerParams(vmem_limit_bytes=16 * 1024 * 1024),
        cost_estimate=LITTLE,
        name="join",
    )(mine, recv, ride)


class Halving:
    def __init__(self, seq, send):
        self.seq = seq
        self.recv = flat_permute(send, core_pairs())
        self.stage = 0
        self.ride = None

    def riders(self):
        return [] if self.ride is None else split(self.ride)

    def board(self, recv, rows):
        if self.ride is not None:
            low = rows + self.ride.shape[0]
            self.ride = self.ride + (recv[rows:low].astype(f32) + recv[low:].astype(f32))

    def step(self, *beside):
        k = self.stage
        self.stage += 1
        stages = len(stage_bits()[0])
        recv, *beside = self.seq.after(self.recv, *beside) if beside else (self.seq.after(self.recv),)
        if k < 4:
            half = self.keep.shape[0] // 2
            send = self.seq.did(added(self.keep[half:], recv[half:]))
            self.recv = flat_permute(send, halving_pairs(k))
            self.keep = added(self.keep[:half], recv[:half])
        elif k == 4:
            total = added(self.keep, recv)
            for extra in range(4, stages):
                total = added(total, flat_permute(total, halving_pairs(extra)))
                if self.ride is not None:
                    self.ride = self.ride + flat_permute(self.ride, halving_pairs(extra))
            self.rows = total.shape[0]
            self.total = self.seq.did(jnp.concatenate([total] + self.riders(), 0))
            self.recv = flat_permute(self.total, halving_pairs(3))
        elif k < 8:
            rows = self.rows
            self.rows = 2 * rows
            if self.ride is None:
                self.total = self.seq.did(jnp.concatenate([self.total, recv], 0))
            else:
                self.total, self.ride = joined(self.total, recv, self.ride)
                self.seq.did(self.total)
            self.recv = flat_permute(self.total, halving_pairs(7 - k))
            if k == 7:
                self.theirs = flat_permute(self.total, core_pairs())
        else:
            self.board(recv, self.rows)
            self.rest = recv
            self.their_rest = flat_permute(recv, core_pairs())
        return beside


def chip_shift(value, steps):
    return passed_along(value, "seq", 2 * steps)


def per_device(
    inputs,
    lengths,
    norm_gain,
    conv_weight,
    gate_weight,
    gate_bias,
    cand_weight,
    out_weight,
    mlp_gain,
    up_weight,
    down_weight,
    cotangent,
):
    rows, span, width = inputs.shape
    hidden = gate_weight.shape[1]
    feed = up_weight.shape[1]
    taps = conv_weight.shape[0]
    margin = taps - 1
    tokens = rows * span
    tb = 32
    blocks = span // tb
    m = tb * R
    seq = lax.axis_index("seq")
    core = seq & 1
    chips = lax.axis_size("seq") // 2
    hops = chips - 1
    flat = seq * lax.axis_size("row") + lax.axis_index("row")
    slots = [slot_of(flat, bits) for bits in stage_bits()]
    here = jnp.where(core == 0, slots[0], slots[1])
    mate = jnp.where(core == 0, slots[1], slots[0])
    scal = jnp.concatenate([jnp.stack([seq * span, core, here, mate]).astype(jnp.int32), lengths])
    gain1 = norm_gain.reshape(1, width)
    gain2 = mlp_gain.reshape(1, width)
    bias = gate_bias.reshape(1, hidden)
    to_pm, to_rm = token_order()

    edge = inputs[:, span - margin :, :].swapaxes(0, 1).reshape(margin * rows, width)
    edge = passed_along(edge, "seq", 1)

    last = blocks - 1
    clamp = lambda i: jnp.minimum(i, last)
    late = lambda i: jnp.maximum(i - blocks, 0)

    def rm(index):
        return pl.BlockSpec((rows, tb, width), lambda i, *s: (0, index(i), 0))

    def tok(w, index=clamp):
        return pl.BlockSpec((m, w), lambda i, *s: (index(i), 0))

    def rtok(w):
        return tok(w, lambda i: last - clamp(i))

    def fixed(dims):
        zeros = (0,) * len(dims)
        return pl.BlockSpec(dims, lambda i, *s: zeros)

    def call(kernel, name, grid, ins, outs, scratch, operands, scalars=True, much=False):
        spec = pltpu.PrefetchScalarGridSpec(
            num_scalar_prefetch=int(scalars),
            grid=(grid,),
            in_specs=ins,
            out_specs=[o[1] for o in outs],
            scratch_shapes=scratch,
        )
        return pl.pallas_call(
            kernel,
            grid_spec=spec,
            out_shape=[o[0] for o in outs],
            compiler_params=params(16),
            cost_estimate=MUCH if much else LITTLE,
            name=name,
        )(*operands)

    def rows_of(w, kind, spec=tok, kept=shape):
        return kept((tokens, w), kind), spec(w)

    c, zl, kh, ends = call(
        front_kernel, "front", blocks,
        [
            rm(clamp), whole(to_pm), whole(edge), whole(gain1), whole(conv_weight),
            whole(gate_weight), whole(bias), whole(cand_weight),
        ],
        [
            rows_of(width, bf16), rows_of(hidden, bf16), rows_of(hidden, bf16),
            (shape((2 * R, hidden)), fixed((2 * R, hidden))),
        ],
        [
            pltpu.VMEM((margin * R + m, width), f32),
            pltpu.VMEM((2 * R, hidden), f32),
            pltpu.VMEM((R, hidden), jnp.int32),
        ],
        (
            scal, far(inputs), far(to_pm), edge, far(gain1), far(conv_weight), far(gate_weight),
            far(bias), far(cand_weight),
        ),
    )

    other = flat_permute(ends, core_pairs())
    first = jnp.where(core == 0, ends, other)
    second = jnp.where(core == 0, other, ends)
    decay = jnp.log(jnp.maximum(ends[:R] * other[:R], 1e-37))
    reach, ahead, forward = 1, (decay, second[:R] * first[R:] + second[R:]), []
    while reach < chips:
        message = jnp.concatenate(ahead, 0).astype(bf16)
        forward.append(chip_shift(message, reach))
        reach *= 2
        if reach < chips:
            both = forward[-1].astype(f32)
            ahead = (ahead[0] + both[:R], ahead[1] + jnp.exp(ahead[0]) * both[R:])

    gl, da = call(
        da_kernel, "da", blocks,
        [rm(clamp), whole(to_pm), whole(down_weight)],
        [rows_of(width, bf16), rows_of(feed, bf16)],
        [],
        (cotangent, to_pm, down_weight),
        scalars=False,
    )

    r1, y, hp, n2, act, dp, dm, dr1, dh, back, mg = call(
        functools.partial(core_kernel, fchunk=256, hops=len(forward)), "core", blocks,
        [
            rm(clamp), whole(to_pm), tok(width), tok(feed), tok(hidden), tok(hidden), whole(other),
            *[whole(f) for f in forward], whole(out_weight), whole(gain2), whole(up_weight),
        ],
        [
            rows_of(width, f32, kept=pltpu.HBM), rows_of(hidden, bf16), rows_of(hidden, bf16),
            rows_of(width, bf16), rows_of(feed, bf16), rows_of(feed, bf16), rows_of(width, bf16),
            rows_of(width, f32, kept=pltpu.HBM),
            rows_of(hidden, bf16),
            (shape((R, hidden)), fixed((R, hidden))), (shape((R, width)), fixed((R, width))),
        ],
        [
            pltpu.VMEM((R, hidden), f32),
            pltpu.VMEM((R, hidden), jnp.int32),
            pltpu.VMEM((R, hidden), f32),
            pltpu.VMEM((m, width), f32),
        ],
        (scal, inputs, to_pm, gl, da, zl, kh, other, *forward, out_weight, gain2, up_weight),
    )

    order = Sequence(back)
    quarter = feed // 4

    def ffn_grads(pick, *beside):
        half = lambda s: s[1] if pick == 0 else 1 - s[1]
        a, d, *beside = order.after(act, dp, *beside)
        (piece,) = call(
            functools.partial(ffn_grad_kernel, pick=pick), "ffn_grad", 2,
            [
                pl.BlockSpec((tokens, quarter), lambda i, s: (0, half(s) * 2 + i)), whole(gl),
                pl.BlockSpec((tokens, width // 2), lambda i, s: (0, half(s))),
                pl.BlockSpec((tokens, feed // 2), lambda i, s: (0, i)),
            ],
            [(shape((SLOTS // 2 * PIECE1, width), bf16), fixed((SLOTS // 2 * PIECE1, width)))],
            [],
            (scal, a, gl, n2, d),
            much=pick == 0,
        )
        return order.did(piece), beside

    def gate_grads(pick):
        half = lambda s: s[1] if pick == 0 else 1 - s[1]
        z, h = order.after(dkz, dkh)
        (piece,) = call(
            functools.partial(gate_grad_kernel, pick=pick), "gate_grad", 1,
            [
                pl.BlockSpec((tokens, width // 2), lambda i, s: (0, half(s))),
                whole(z), whole(h),
                pl.BlockSpec((tokens, hidden // 2), lambda i, s: (0, half(s))), whole(dm),
            ],
            [(shape((SLOTS // 2 * PIECE2, width), bf16), fixed((SLOTS // 2 * PIECE2, width)))],
            [],
            (scal, c, z, h, y, dm),
            much=pick == 0,
        )
        return order.did(piece)

    fother = flat_permute(back, core_pairs())
    lower = jnp.where(core == 0, back, fother)
    upper = jnp.where(core == 0, fother, back)
    message = jnp.concatenate([decay, lower + first[:R] * upper], 0).astype(bf16)
    backward = [chip_shift(order.did(message), -k) for k in range(1, chips)]
    send1, _ = ffn_grads(1)
    chunk1 = Halving(order, send1)
    chunk1.keep, backward = ffn_grads(0, *backward)
    chunk1.step()

    dkz, dkh, edge_dc, bias_part = call(
        functools.partial(gate_kernel, blocks=blocks, hops=hops), "gates", blocks,
        [
            rtok(hidden), rtok(hidden), rtok(hidden), rtok(hidden),
            whole(other), whole(fother), *[whole(f) for f in backward],
            whole(gate_weight), whole(cand_weight), ORDER,
        ],
        [
            rows_of(hidden, bf16, rtok), rows_of(hidden, bf16, rtok),
            (shape((4 * R, width), bf16), fixed((4 * R, width))),
            (shape((R, hidden)), fixed((R, hidden))),
        ],
        [pltpu.VMEM((R, hidden), f32)],
        (
            scal, dh, zl, kh, hp, other, fother, *backward, gate_weight, cand_weight, order.token,
        ),
    )
    order.did(bias_part)
    after = passed_along(edge_dc[: margin * R], "seq", -1)
    send2 = gate_grads(1)
    chunk2 = Halving(order, send2)
    (output,) = call(
        output_kernel, "output", blocks,
        [tok(width), tok(feed), whole(to_rm), whole(down_weight)],
        [(shape((rows, span, width), bf16), rm(clamp))],
        [],
        (far(r1), order.after(act), to_rm, down_weight),
        scalars=False,
    )
    order.did(output)
    chunk1.step()
    chunk2.keep = gate_grads(0)
    chunk2.step()
    input_grad, sums = call(
        functools.partial(tail_kernel, blocks=blocks), "tail", 2 * blocks,
        [
            rm(late), tok(width, late), tok(hidden), tok(hidden), whole(to_pm), whole(to_rm),
            whole(edge), whole(after), whole(gain1), whole(conv_weight), whole(gate_weight),
            whole(cand_weight),
        ],
        [
            (shape((rows, span, width), bf16), rm(late)),
            (shape(((taps + 1) * R, width)), fixed(((taps + 1) * R, width))),
        ],
        [
            pltpu.VMEM((margin * R + m, width), f32),
            pltpu.VMEM((margin * R + tokens, width), f32),
        ],
        (
            far(inputs), far(dr1), order.after(dkz), dkh, far(to_pm), far(to_rm), edge, after,
            far(gain1), far(conv_weight), far(gate_weight), far(cand_weight),
        ),
        scalars=False,
    )
    order.did(sums)
    small = jnp.concatenate(
        [
            sums.reshape(taps + 1, R, width).sum(1),
            mg.sum(0, keepdims=True),
            bias_part.sum(0).reshape(hidden // width, width),
        ],
        0,
    )
    coming = flat_permute(small, core_pairs())

    plan1 = ((0, feed // SLOTS, 1), (1, width // SLOTS, feed // width))
    shapes1 = ((feed, width), (width, feed))
    plan2 = (
        (0, width // SLOTS, hidden // width),
        (1, width // SLOTS, hidden // width),
        (2, hidden // SLOTS, 1),
    )
    shapes2 = ((width, hidden), (width, hidden), (hidden, width))
    held1, held2 = (), ()

    def spread1(src, mate, flip):
        nonlocal held1
        src = order.after(src)
        held1 = spread(scal, src, held1, mate, flip, PIECE1, plan1, shapes1, "spread_ffn")
        order.did(held1[0])

    def spread2(src, mate, flip):
        nonlocal held2
        src = order.after(src)
        held2 = spread(scal, src, held2, mate, flip, PIECE2, plan2, shapes2, "spread_gates")
        order.did(held2[0])

    for chunk in (chunk1, chunk2, chunk1, chunk1, chunk2, chunk1, chunk2, chunk1):
        chunk.step()
    chunk2.ride = small + order.after(coming)
    chunk2.step()
    chunk2.step()
    chunk1.step()
    spread1(chunk1.total, 0, 0)
    chunk2.step()
    spread1(chunk1.theirs, 1, 0)
    chunk2.step()
    chunk1.step()
    spread1(chunk1.rest, 0, 1)
    spread2(chunk2.total, 0, 0)
    spread1(chunk1.their_rest, 1, 1)
    spread2(chunk2.theirs, 1, 0)
    chunk2.step()
    small = chunk2.ride
    small_out = order.after(
        small[0], small[1 : taps + 1], small[taps + 2 :].reshape(hidden), small[taps + 1]
    )
    spread2(chunk2.rest, 0, 1)
    spread2(chunk2.their_rest, 1, 1)
    return (
        output,
        input_grad,
        small_out[0],
        small_out[1],
        held2[0],
        small_out[2],
        held2[1],
        held2[2],
        small_out[3],
        held1[1],
        held1[0],
    )


def solution(mesh):
    sharded = P("row", "seq", None)
    in_specs = (sharded, P("row")) + (P(),) * 9 + (sharded,)
    out_specs = (sharded, sharded) + (P(),) * 9
    return jax.shard_map(
        per_device, mesh=mesh, in_specs=in_specs, out_specs=out_specs, check_vma=False
    )
```

```python
import functools

import jax
import jax.numpy as jnp
import numpy as np
from jax import lax
from jax.experimental import pallas as pl
from jax.experimental.pallas import tpu as pltpu
from jax.sharding import PartitionSpec as P

epsilon = 1e-06
f32 = jnp.float32
bf16 = jnp.bfloat16
R = 8
PERM = 256
SCALARS = 4
SLOTS = 32
PIECE1 = 128
PIECE2 = 96


def nn(a, b):
    return lax.dot_general(a, b, (((1,), (0,)), ((), ())), preferred_element_type=f32)


def nt(a, b):
    return lax.dot_general(a, b, (((1,), (1,)), ((), ())), preferred_element_type=f32)


def tn(a, b):
    return lax.dot_general(a, b, (((0,), (0,)), ((), ())), preferred_element_type=f32)


def token_order():
    out = np.arange(PERM)
    source = (out % R) * (PERM // R) + out // R
    to_pm = np.zeros((PERM, PERM), np.float32)
    to_pm[out, source] = 1
    return jnp.asarray(to_pm, bf16), jnp.asarray(to_pm.T, bf16)


def position_major(perm, block):
    span = PERM // R
    parts = []
    for s in range(block.shape[1] // span):
        part = block[:, s * span : (s + 1) * span, :].reshape(PERM, block.shape[2])
        parts.append(nn(perm, part))
    return parts[0] if len(parts) == 1 else jnp.concatenate(parts, 0)


def row_major(perm, tokens):
    span = PERM // R
    parts = []
    for s in range(tokens.shape[0] // PERM):
        part = nn(perm, tokens[s * PERM : (s + 1) * PERM]).astype(bf16)
        parts.append(part.reshape(R, span, tokens.shape[1]))
    return parts[0] if len(parts) == 1 else jnp.concatenate(parts, 1)


def eight(t):
    return pl.ds(pl.multiple_of(t * R, R), R)


def sixteen(t):
    return pl.ds(pl.multiple_of(t * 2 * R, 2 * R), 2 * R)


def normed_edge(edge, gain):
    e = edge.astype(f32)
    inv = lax.rsqrt(jnp.mean(e * e, -1, keepdims=True) + epsilon)
    return (e * inv * gain).astype(bf16).astype(f32)


def set_limits(scal, limit):
    row = lax.broadcasted_iota(jnp.int32, limit.shape, 0)
    value = jnp.zeros(limit.shape, jnp.int32)
    for r in range(R):
        value = jnp.where(row == r, scal[SCALARS + r], value)
    limit[...] = value


def halves(ref, pair):
    both = ref[sixteen(pair), :].astype(f32)
    return both[:R], both[R:]


def norm_kernel(x, perm, gain, u_out):
    xp = position_major(perm[...], x[...])
    inv = lax.rsqrt(jnp.mean(xp * xp, -1, keepdims=True) + epsilon)
    u_out[...] = (xp * inv * gain[...]).astype(bf16)


def front_kernel(scal, u, edge, gain, convw, wg, bias, wc, c_out, zl_out, kh_out, ends, ext, state, limit):
    step = pl.program_id(0)
    m = u.shape[0]
    tb = m // R
    halo = edge.shape[0]
    taps = convw.shape[0]

    @pl.when(step == 0)
    def _():
        set_limits(scal, limit)
        ext[0:halo, :] = normed_edge(edge[...], gain[...])
        state[0:R, :] = jnp.ones((R, state.shape[1]), f32)
        state[R:, :] = jnp.zeros((R, state.shape[1]), f32)

    ext[halo:, :] = u[...].astype(f32)
    conv = convw[0:1, :] * ext[halo:, :]
    for k in range(1, taps):
        lo = halo - k * R
        conv = conv + convw[k : k + 1, :] * ext[lo : lo + m, :]
    ext[0:halo, :] = ext[m : m + halo, :]
    cb = conv.astype(bf16)
    c_out[...] = cb
    kz = nn(cb, wg[...]) + bias[...]
    zs = 1.0 / (1.0 + jnp.exp(-kz))
    width = zs.shape[1]
    zs = zs.reshape(tb, R, width)
    pos = scal[0] + step * tb + lax.broadcasted_iota(jnp.int32, (tb, R, width), 0)
    zl_out[...] = jnp.where(pos < limit[...][None], zs, 0.0).reshape(m, width).astype(bf16)
    kh_out[...] = nn(cb, wc[...]).astype(bf16)

    def body(u, carry):
        prod, h = carry
        za, zb = halves(zl_out, u)
        ka, kb = halves(kh_out, u)
        a = 1.0 - za
        b = 1.0 - zb
        return prod * (a * b), (h * a + za * ka) * b + zb * kb

    prod, h = lax.fori_loop(0, tb // 2, body, (state[0:R, :], state[R:, :]), unroll=4)
    state[0:R, :] = prod
    state[R:, :] = h
    ends[0:R, :] = prod
    ends[R:, :] = h


def gelu_parts(p):
    k0 = 0.7978845608028654
    p2 = p * p
    th = jnp.tanh(p * (k0 + (k0 * 0.044715) * p2))
    ht = 0.5 + 0.5 * th
    return p * ht, ht + (2.0 * p) * (ht - ht * ht) * (k0 + (3.0 * k0 * 0.044715) * p2)


def da_kernel(g, perm, wd, gl_out, da_out):
    gl = position_major(perm[...], g[...]).astype(bf16)
    gl_out[...] = gl
    da_out[...] = nt(gl, wd[...]).astype(bf16)


def core_kernel(scal, x, perm, gl, da, zl, kh, other, *refs, fchunk, hops):
    msgs = refs[:hops]
    wo, mgain, wu = refs[hops : hops + 3]
    r1_out, y_out, hp_out, n2_out, act_out, dp_out, dm_out, dr1_out, dh_out, back, mg = refs[hops + 3 : hops + 14]
    state, limit, run, acc = refs[hops + 14 :]
    step = pl.program_id(0)
    tb = x.shape[1]
    m = tb * R
    width, feed = wu.shape
    hidden = wo.shape[0]

    @pl.when(step == 0)
    def _():
        set_limits(scal, limit)
        h = jnp.zeros((R, hidden), f32)
        for msg in reversed(msgs):
            both = msg[...].astype(f32)
            h = jnp.exp(both[0:R, :]) * h + both[R:, :]
        state[...] = jnp.where(scal[1] == 1, other[0:R, :] * h + other[R:, :], h)
        run[...] = jnp.ones((R, hidden), f32)
        back[...] = jnp.zeros(back.shape, f32)
        mg[...] = jnp.zeros(mg.shape, f32)

    first = scal[0] + step * tb
    lens = limit[...]

    def body(u, h):
        t = u * 2
        za, zb = halves(zl, u)
        ka, kb = halves(kh, u)
        ha = h - za * h + za * ka
        hb = ha - zb * ha + zb * kb
        hp_out[sixteen(u), :] = jnp.concatenate([h, ha], 0).astype(bf16)
        ya = jnp.where(first + t < lens, ha, 0.0)
        yb = jnp.where(first + t + 1 < lens, hb, 0.0)
        y_out[sixteen(u), :] = jnp.concatenate([ya, yb], 0).astype(bf16)
        return hb

    state[...] = lax.fori_loop(0, tb // 2, body, state[...], unroll=2)
    r1 = position_major(perm[...], x[...]) + nn(y_out[...], wo[...])
    r1_out[...] = r1
    inv = lax.rsqrt(jnp.mean(r1 * r1, -1, keepdims=True) + epsilon)
    n2 = (r1 * inv * mgain[...]).astype(bf16)
    n2_out[...] = n2
    for f in range(0, feed, fchunk):
        cols = slice(f, f + fchunk)
        a, slope = gelu_parts(nn(n2, wu[:, cols]))
        act_out[:, cols] = a.astype(bf16)
        dpb = (da[:, cols].astype(f32) * slope).astype(bf16)
        dp_out[:, cols] = dpb
        part = nt(dpb, wu[:, cols])
        acc[...] = acc[...] + part if f else part
    dn2 = acc[...]
    r1 = r1_out[...]
    mg[...] += jnp.sum((dn2 * r1 * inv).reshape(tb, R, width), 0)
    s = mgain[...] * dn2
    mean = jnp.mean(s * r1, -1, keepdims=True)
    dr1 = gl[...].astype(f32) + inv * (s - r1 * (inv * inv * mean))
    dr1_out[...] = dr1
    dm = dr1.astype(bf16)
    dm_out[...] = dm
    dh = nt(dm, wo[...]).reshape(tb, R, hidden)
    pos = first + lax.broadcasted_iota(jnp.int32, (tb, R, hidden), 0)
    dh_out[...] = jnp.where(pos < lens[None], dh, 0.0).reshape(m, hidden).astype(bf16)

    def adjoint(u, carry):
        prod, total = carry
        za, zb = halves(zl, u)
        da, db = halves(dh_out, u)
        pa = prod - za * prod
        pb = pa - zb * pa
        return pb, total + (pa * da + pb * db)

    prod, total = lax.fori_loop(0, tb // 2, adjoint, (run[...], back[...]), unroll=4)
    run[...] = prod
    back[...] = total


def put_rows(dst, sel, piece, at, rows, part):
    for i in range(SLOTS // 2):
        pos = pl.multiple_of((i ^ sel) * piece + at, 16)
        dst[pl.ds(pos, rows), :] = part[i * rows : (i + 1) * rows]


def ffn_grad_kernel(scal, act, gl, n2, dp, dst, *, pick):
    step = pl.program_id(0)
    sel = scal[2 + pick]
    width = gl.shape[1]
    rows1 = act.shape[1] * 4 // SLOTS
    rows2 = n2.shape[1] * 2 // SLOTS
    part = tn(act[...], gl[...]).astype(bf16)
    per = act.shape[1] // rows1
    for i in range(per):
        pos = ((step * per + i) ^ sel) * PIECE1
        dst[pl.ds(pl.multiple_of(pos, 16), rows1), :] = part[i * rows1 : (i + 1) * rows1]
    columns = dp.shape[1] // width
    for q in range(columns):
        part = tn(n2[...], dp[:, q * width : (q + 1) * width]).astype(bf16)
        put_rows(dst, sel, PIECE1, rows1 + (step * columns + q) * rows2, rows2, part)


def gate_grad_kernel(scal, c, dkz, dkh, y, dm, dst, *, pick):
    sel = scal[2 + pick]
    width = dm.shape[1]
    rows = c.shape[1] * 2 // SLOTS
    at = 0
    for grads in (dkz, dkh):
        for q in range(grads.shape[1] // width):
            part = tn(c[...], grads[:, q * width : (q + 1) * width]).astype(bf16)
            put_rows(dst, sel, PIECE2, at, rows, part)
            at += rows
    put_rows(dst, sel, PIECE2, at, y.shape[1] * 2 // SLOTS, tn(y[...], dm[...]).astype(bf16))


def gate_kernel(scal, dh, zl, kh, hp, other, fother, *refs, blocks, hops):
    msgs = refs[:hops]
    wg, wc = refs[hops : hops + 2]
    dkz, dkh, edge_out, bias_out = refs[hops + 3 : hops + 7]
    state = refs[hops + 7]
    step = pl.program_id(0)
    m = dh.shape[0]
    tb = m // R
    block = blocks - 1 - step

    @pl.when(step == 0)
    def _():
        mm = jnp.zeros(state.shape, f32)
        for msg in reversed(msgs):
            both = msg[...].astype(f32)
            mm = jnp.exp(both[0:R, :]) * mm + both[R:, :]
        state[...] = jnp.where(scal[1] == 0, fother[...] + other[0:R, :] * mm, mm)
        bias_out[...] = jnp.zeros(bias_out.shape, f32)

    def body(u, carry):
        mm, bias = carry
        w = tb // 2 - 1 - u
        ha, hb = halves(hp, w)
        za, zb = halves(zl, w)
        da, db = halves(dh, w)
        ka, kb = halves(kh, w)
        lam = db + mm
        sb = lam * zb
        mm = lam - sb
        kb = (sb - sb * zb) * (kb - hb)
        lam = da + mm
        sa = lam * za
        mm = lam - sa
        ka = (sa - sa * za) * (ka - ha)
        kk = jnp.concatenate([ka, kb], 0).astype(bf16)
        dkz[sixteen(w), :] = kk
        dkh[sixteen(w), :] = jnp.concatenate([sa, sb], 0).astype(bf16)
        kf = kk.astype(f32)
        return mm, bias + kf[:R, :] + kf[R:, :]

    mm, bias = lax.fori_loop(0, tb // 2, body, (state[...], bias_out[...]), unroll=2)
    state[...] = mm
    bias_out[...] = bias

    @pl.when(block == 0)
    def _():
        span = edge_out.shape[0]
        edge_out[...] = (nt(dkz[0:span, :], wg[...]) + nt(dkh[0:span, :], wc[...])).astype(bf16)


def tail_kernel(x, dr1, dkz, dkh, pm, back_pm, edge, after, gain, convw, wg, wc, grad, sums, uext, dext, *, blocks):
    step = pl.program_id(0)
    tb = x.shape[1]
    m = tb * R
    halo = edge.shape[0]
    taps = convw.shape[0]
    width = gain.shape[1]

    @pl.when(step == 0)
    def _():
        uext[0:halo, :] = normed_edge(edge[...], gain[...])
        dext[blocks * m :, :] = after[...].astype(f32)
        sums[...] = jnp.zeros(sums.shape, f32)

    @pl.when(step < blocks)
    def _():
        rows = pl.ds(pl.multiple_of(step * m, m), m)
        dext[rows, :] = nt(dkz[...], wg[...]) + nt(dkh[...], wc[...])

    @pl.when(step >= blocks)
    def _():
        xp = position_major(pm[...], x[...])
        inv = lax.rsqrt(jnp.mean(xp * xp, -1, keepdims=True) + epsilon)
        xn = xp * inv
        uext[halo:, :] = (xn * gain[...]).astype(bf16).astype(f32)
        start = (step - blocks) * m
        here = dext[pl.ds(pl.multiple_of(start, R), m), :]
        du = convw[0:1, :] * here
        for k in range(taps):
            lo = halo - k * R
            part = (here * uext[lo : lo + m, :]).reshape(tb, R, width)
            sums[(k + 1) * R : (k + 2) * R, :] += jnp.sum(part, 0)
            if k:
                du = du + convw[k : k + 1, :] * dext[pl.ds(pl.multiple_of(start + k * R, R), m), :]
        uext[0:halo, :] = uext[m : m + halo, :]
        sums[0:R, :] += jnp.sum((du * xn).reshape(tb, R, width), 0)
        s1 = gain[...] * du
        mean = jnp.mean(s1 * xn, -1, keepdims=True)
        gin = dr1[...] + inv * (s1 - xn * mean)
        grad[...] = row_major(back_pm[...], gin.astype(bf16))


def output_kernel(r1, act, perm, wd, out):
    total = r1[...] + nn(act[...], wd[...])
    out[...] = row_major(perm[...], total.astype(bf16))


def spread_kernel(scal, src, *refs, piece, plan, mate):
    low = scal[2 + mate] & 7
    for a in range(8):
        base = (a ^ low) * piece
        at = 0
        for out, rows, columns in plan:
            ref = refs[len(refs) - len(plan) + out]
            for q in range(columns):
                width = src.shape[1]
                part = src[pl.ds(pl.multiple_of(base + at, 16), rows), :].astype(f32)
                ref[a * rows : (a + 1) * rows, q * width : (q + 1) * width] = part
                at += rows


def spread(scal, src, held, mate, flip, piece, plan, shapes, name):
    def block(g, s):
        return ((s[1] ^ mate) * 2 + ((s[2 + mate] >> 3) ^ flip), 0)

    count = len(held)
    return pl.pallas_call(
        functools.partial(spread_kernel, piece=piece, plan=plan, mate=mate),
        grid_spec=pltpu.PrefetchScalarGridSpec(
            num_scalar_prefetch=1,
            grid=(1,),
            in_specs=[whole(src)] + [ORDER] * count,
            out_specs=[pl.BlockSpec((dims[0] // 4, dims[1]), block) for dims in shapes],
        ),
        out_shape=[pltpu.HBM(dims, f32) for dims in shapes],
        input_output_aliases={2 + k: k for k in range(count)},
        compiler_params=params(16),
        cost_estimate=LITTLE,
        name=name,
    )(scal, src, *held)


def params(mib):
    return pltpu.CompilerParams(
        dimension_semantics=("arbitrary",), vmem_limit_bytes=mib * 1024 * 1024
    )


def shape(dims, kind=f32):
    return jax.ShapeDtypeStruct(dims, kind)


LITTLE = pl.CostEstimate(flops=1024, bytes_accessed=1024, transcendentals=0)
MUCH = pl.CostEstimate(flops=3 * 10**10, bytes_accessed=1024, transcendentals=0)
ORDER = pl.BlockSpec(memory_space=pl.ANY)


def far(array):
    return pltpu.with_memory_space_constraint(array, pltpu.HBM)


def whole(array):
    zeros = (0,) * array.ndim
    return pl.BlockSpec(array.shape, lambda *a: zeros, pipeline_mode=pl.Buffered(1))


def passed_along(value, axis, steps):
    count = lax.axis_size(axis)
    leading, last = (max(0, -steps), min(count, count - steps))
    return lax.ppermute(value, axis, [(source, source + steps) for source in range(leading, last)])


def flat_permute(value, pairs):
    return lax.ppermute(value, ("seq", "row"), pairs)


def stage_bits():
    row_bits = lax.axis_size("row").bit_length() - 1
    seq_bits = lax.axis_size("seq").bit_length() - 1
    plane = list(range(row_bits))
    line = [row_bits + 1 + z for z in range(seq_bits - 1)]
    cut = row_bits // 2
    return (plane + line, plane[cut:] + plane[:cut] + line[::-1])


def slot_of(flat, bits):
    slot = 0
    for k in range(4):
        slot = slot * 2 + ((flat >> bits[k]) & 1)
    return slot


def halving_pairs(stage):
    row_bits = lax.axis_size("row").bit_length() - 1
    orders = stage_bits()
    devices = lax.axis_size("row") * lax.axis_size("seq")
    return [(d, d ^ (1 << orders[(d >> row_bits) & 1][stage])) for d in range(devices)]


def core_pairs():
    row_bits = lax.axis_size("row").bit_length() - 1
    devices = lax.axis_size("row") * lax.axis_size("seq")
    return [(d, d ^ (1 << row_bits)) for d in range(devices)]


def added(a, b):
    return (a.astype(f32) + b.astype(f32)).astype(bf16)


class Sequence:
    def __init__(self, token):
        self.token = token

    def after(self, *arrays):
        *arrays, _ = lax.optimization_barrier((*arrays, self.token))
        return arrays[0] if len(arrays) == 1 else arrays

    def did(self, array):
        self.token = array
        return array


def split(value):
    high = lax.reduce_precision(value, 8, 7)
    return [high.astype(bf16), (value - high).astype(bf16)]


def join_kernel(mine, recv, ride, out, ride_out):
    rows = mine.shape[0] - 2 * R
    out[0:rows, :] = mine[0:rows, :]
    out[rows : 2 * rows, :] = recv[0:rows, :]
    parts = recv[rows:, :].astype(f32)
    total = ride[...] + (parts[:R] + parts[R:])
    ride_out[...] = total
    high = total.astype(bf16).astype(f32)
    out[2 * rows :, :] = jnp.concatenate([high, total - high], 0).astype(bf16)


def joined(mine, recv, ride):
    rows, width = mine.shape
    return pl.pallas_call(
        join_kernel,
        in_specs=[pl.BlockSpec(memory_space=pltpu.VMEM)] * 3,
        out_specs=[pl.BlockSpec(memory_space=pltpu.VMEM)] * 2,
        out_shape=[shape((2 * rows - 2 * R, width), bf16), shape(ride.shape)],
        compiler_params=pltpu.CompilerParams(vmem_limit_bytes=16 * 1024 * 1024),
        cost_estimate=LITTLE,
        name="join",
    )(mine, recv, ride)


class Halving:
    def __init__(self, seq, send):
        self.seq = seq
        self.recv = flat_permute(send, core_pairs())
        self.stage = 0
        self.ride = None

    def riders(self):
        return [] if self.ride is None else split(self.ride)

    def board(self, recv, rows):
        if self.ride is not None:
            low = rows + self.ride.shape[0]
            self.ride = self.ride + (recv[rows:low].astype(f32) + recv[low:].astype(f32))

    def step(self, *beside):
        k = self.stage
        self.stage += 1
        stages = len(stage_bits()[0])
        recv, *beside = self.seq.after(self.recv, *beside) if beside else (self.seq.after(self.recv),)
        if k < 4:
            half = self.keep.shape[0] // 2
            send = self.seq.did(added(self.keep[half:], recv[half:]))
            self.recv = flat_permute(send, halving_pairs(k))
            self.keep = added(self.keep[:half], recv[:half])
        elif k == 4:
            total = added(self.keep, recv)
            for extra in range(4, stages):
                total = added(total, flat_permute(total, halving_pairs(extra)))
                if self.ride is not None:
                    self.ride = self.ride + flat_permute(self.ride, halving_pairs(extra))
            self.rows = total.shape[0]
            self.total = self.seq.did(jnp.concatenate([total] + self.riders(), 0))
            self.recv = flat_permute(self.total, halving_pairs(3))
        elif k < 8:
            rows = self.rows
            self.rows = 2 * rows
            if self.ride is None:
                self.total = self.seq.did(jnp.concatenate([self.total, recv], 0))
            else:
                self.total, self.ride = joined(self.total, recv, self.ride)
                self.seq.did(self.total)
            self.recv = flat_permute(self.total, halving_pairs(7 - k))
            if k == 7:
                self.theirs = flat_permute(self.total, core_pairs())
        else:
            self.board(recv, self.rows)
            self.rest = recv
            self.their_rest = flat_permute(recv, core_pairs())
        return beside


def chip_shift(value, steps):
    return passed_along(value, "seq", 2 * steps)


def per_device(
    inputs,
    lengths,
    norm_gain,
    conv_weight,
    gate_weight,
    gate_bias,
    cand_weight,
    out_weight,
    mlp_gain,
    up_weight,
    down_weight,
    cotangent,
):
    rows, span, width = inputs.shape
    hidden = gate_weight.shape[1]
    feed = up_weight.shape[1]
    taps = conv_weight.shape[0]
    margin = taps - 1
    tokens = rows * span
    tb = 32
    blocks = span // tb
    m = tb * R
    seq = lax.axis_index("seq")
    core = seq & 1
    chips = lax.axis_size("seq") // 2
    hops = chips - 1
    flat = seq * lax.axis_size("row") + lax.axis_index("row")
    slots = [slot_of(flat, bits) for bits in stage_bits()]
    here = jnp.where(core == 0, slots[0], slots[1])
    mate = jnp.where(core == 0, slots[1], slots[0])
    scal = jnp.concatenate([jnp.stack([seq * span, core, here, mate]).astype(jnp.int32), lengths])
    gain1 = norm_gain.reshape(1, width)
    gain2 = mlp_gain.reshape(1, width)
    bias = gate_bias.reshape(1, hidden)
    to_pm, to_rm = token_order()

    edge = inputs[:, span - margin :, :].swapaxes(0, 1).reshape(margin * rows, width)
    edge = passed_along(edge, "seq", 1)

    last = blocks - 1
    clamp = lambda i: jnp.minimum(i, last)
    late = lambda i: jnp.maximum(i - blocks, 0)

    def rm(index):
        return pl.BlockSpec((rows, tb, width), lambda i, *s: (0, index(i), 0))

    def tok(w, index=clamp):
        return pl.BlockSpec((m, w), lambda i, *s: (index(i), 0))

    def rtok(w):
        return tok(w, lambda i: last - clamp(i))

    def fixed(dims):
        zeros = (0,) * len(dims)
        return pl.BlockSpec(dims, lambda i, *s: zeros)

    def call(kernel, name, grid, ins, outs, scratch, operands, scalars=True, much=False):
        spec = pltpu.PrefetchScalarGridSpec(
            num_scalar_prefetch=int(scalars),
            grid=(grid,),
            in_specs=ins,
            out_specs=[o[1] for o in outs],
            scratch_shapes=scratch,
        )
        return pl.pallas_call(
            kernel,
            grid_spec=spec,
            out_shape=[o[0] for o in outs],
            compiler_params=params(16),
            cost_estimate=MUCH if much else LITTLE,
            name=name,
        )(*operands)

    def rows_of(w, kind, spec=tok, kept=shape):
        return kept((tokens, w), kind), spec(w)

    (normed,) = call(
        norm_kernel, "norm", blocks,
        [rm(clamp), whole(to_pm), whole(gain1)],
        [rows_of(width, bf16)],
        [],
        (far(inputs), far(to_pm), far(gain1)),
        scalars=False,
    )
    edge, normed = lax.optimization_barrier((edge, normed))
    c, zl, kh, ends = call(
        front_kernel, "front", blocks,
        [
            tok(width), whole(edge), whole(gain1), whole(conv_weight),
            whole(gate_weight), whole(bias), whole(cand_weight),
        ],
        [
            rows_of(width, bf16), rows_of(hidden, bf16), rows_of(hidden, bf16),
            (shape((2 * R, hidden)), fixed((2 * R, hidden))),
        ],
        [
            pltpu.VMEM((margin * R + m, width), f32),
            pltpu.VMEM((2 * R, hidden), f32),
            pltpu.VMEM((R, hidden), jnp.int32),
        ],
        (
            scal, normed, edge, far(gain1), far(conv_weight), gate_weight, far(bias),
            cand_weight,
        ),
    )

    other = flat_permute(ends, core_pairs())
    first = jnp.where(core == 0, ends, other)
    second = jnp.where(core == 0, other, ends)
    decay = jnp.log(jnp.maximum(ends[:R] * other[:R], 1e-37))
    reach, ahead, forward = 1, (decay, second[:R] * first[R:] + second[R:]), []
    while reach < chips:
        message = jnp.concatenate(ahead, 0).astype(bf16)
        forward.append(chip_shift(message, reach))
        reach *= 2
        if reach < chips:
            both = forward[-1].astype(f32)
            ahead = (ahead[0] + both[:R], ahead[1] + jnp.exp(ahead[0]) * both[R:])

    gl, da = call(
        da_kernel, "da", blocks,
        [rm(clamp), whole(to_pm), whole(down_weight)],
        [rows_of(width, bf16), rows_of(feed, bf16)],
        [],
        (far(cotangent), far(to_pm), far(down_weight)),
        scalars=False,
    )

    r1, y, hp, n2, act, dp, dm, dr1, dh, back, mg = call(
        functools.partial(core_kernel, fchunk=256, hops=len(forward)), "core", blocks,
        [
            rm(clamp), whole(to_pm), tok(width), tok(feed), tok(hidden), tok(hidden), whole(other),
            *[whole(f) for f in forward], whole(out_weight), whole(gain2), whole(up_weight),
        ],
        [
            rows_of(width, f32, kept=pltpu.HBM), rows_of(hidden, bf16), rows_of(hidden, bf16),
            rows_of(width, bf16), rows_of(feed, bf16), rows_of(feed, bf16), rows_of(width, bf16),
            rows_of(width, f32, kept=pltpu.HBM),
            rows_of(hidden, bf16),
            (shape((R, hidden)), fixed((R, hidden))), (shape((R, width)), fixed((R, width))),
        ],
        [
            pltpu.VMEM((R, hidden), f32),
            pltpu.VMEM((R, hidden), jnp.int32),
            pltpu.VMEM((R, hidden), f32),
            pltpu.VMEM((m, width), f32),
        ],
        (
            scal, far(inputs), far(to_pm), gl, da, zl, kh, other, *forward, far(out_weight), far(gain2),
            far(up_weight),
        ),
    )

    order = Sequence(back)
    quarter = feed // 4

    def ffn_grads(pick, *beside):
        half = lambda s: s[1] if pick == 0 else 1 - s[1]
        a, d, *beside = order.after(act, dp, *beside)
        (piece,) = call(
            functools.partial(ffn_grad_kernel, pick=pick), "ffn_grad", 2,
            [
                pl.BlockSpec((tokens, quarter), lambda i, s: (0, half(s) * 2 + i)), whole(gl),
                pl.BlockSpec((tokens, width // 2), lambda i, s: (0, half(s))),
                pl.BlockSpec((tokens, feed // 2), lambda i, s: (0, i)),
            ],
            [(shape((SLOTS // 2 * PIECE1, width), bf16), fixed((SLOTS // 2 * PIECE1, width)))],
            [],
            (scal, a, gl, n2, d),
            much=pick == 0,
        )
        return order.did(piece), beside

    def gate_grads(pick):
        half = lambda s: s[1] if pick == 0 else 1 - s[1]
        z, h = order.after(dkz, dkh)
        (piece,) = call(
            functools.partial(gate_grad_kernel, pick=pick), "gate_grad", 1,
            [
                pl.BlockSpec((tokens, width // 2), lambda i, s: (0, half(s))),
                whole(z), whole(h),
                pl.BlockSpec((tokens, hidden // 2), lambda i, s: (0, half(s))), whole(dm),
            ],
            [(shape((SLOTS // 2 * PIECE2, width), bf16), fixed((SLOTS // 2 * PIECE2, width)))],
            [],
            (scal, c, z, h, y, dm),
            much=pick == 0,
        )
        return order.did(piece)

    fother = flat_permute(back, core_pairs())
    lower = jnp.where(core == 0, back, fother)
    upper = jnp.where(core == 0, fother, back)
    message = jnp.concatenate([decay, lower + first[:R] * upper], 0).astype(bf16)
    backward = [chip_shift(order.did(message), -k) for k in range(1, chips)]
    send1, _ = ffn_grads(1)
    chunk1 = Halving(order, send1)
    chunk1.keep, backward = ffn_grads(0, *backward)
    chunk1.step()

    dkz, dkh, edge_dc, bias_part = call(
        functools.partial(gate_kernel, blocks=blocks, hops=hops), "gates", blocks,
        [
            rtok(hidden), rtok(hidden), rtok(hidden), rtok(hidden),
            whole(other), whole(fother), *[whole(f) for f in backward],
            whole(gate_weight), whole(cand_weight), ORDER,
        ],
        [
            rows_of(hidden, bf16, rtok), rows_of(hidden, bf16, rtok),
            (shape((4 * R, width), bf16), fixed((4 * R, width))),
            (shape((R, hidden)), fixed((R, hidden))),
        ],
        [pltpu.VMEM((R, hidden), f32)],
        (
            scal, dh, zl, kh, hp, other, fother, *backward, gate_weight, cand_weight, order.token,
        ),
    )
    order.did(bias_part)
    after = passed_along(edge_dc[: margin * R], "seq", -1)
    send2 = gate_grads(1)
    chunk2 = Halving(order, send2)
    (output,) = call(
        output_kernel, "output", blocks,
        [tok(width), tok(feed), whole(to_rm), whole(down_weight)],
        [(shape((rows, span, width), bf16), rm(clamp))],
        [],
        (far(r1), order.after(act), to_rm, down_weight),
        scalars=False,
    )
    order.did(output)
    chunk1.step()
    chunk2.keep = gate_grads(0)
    chunk2.step()
    input_grad, sums = call(
        functools.partial(tail_kernel, blocks=blocks), "tail", 2 * blocks,
        [
            rm(late), tok(width, late), tok(hidden), tok(hidden), whole(to_pm), whole(to_rm),
            whole(edge), whole(after), whole(gain1), whole(conv_weight), whole(gate_weight),
            whole(cand_weight),
        ],
        [
            (shape((rows, span, width), bf16), rm(late)),
            (shape(((taps + 1) * R, width)), fixed(((taps + 1) * R, width))),
        ],
        [
            pltpu.VMEM((margin * R + m, width), f32),
            pltpu.VMEM((margin * R + tokens, width), f32),
        ],
        (
            far(inputs), far(dr1), order.after(dkz), dkh, far(to_pm), far(to_rm), edge, after,
            far(gain1), far(conv_weight), far(gate_weight), far(cand_weight),
        ),
        scalars=False,
    )
    order.did(sums)
    small = jnp.concatenate(
        [
            sums.reshape(taps + 1, R, width).sum(1),
            mg.sum(0, keepdims=True),
            bias_part.sum(0).reshape(hidden // width, width),
        ],
        0,
    )
    coming = flat_permute(small, core_pairs())

    plan1 = ((0, feed // SLOTS, 1), (1, width // SLOTS, feed // width))
    shapes1 = ((feed, width), (width, feed))
    plan2 = (
        (0, width // SLOTS, hidden // width),
        (1, width // SLOTS, hidden // width),
        (2, hidden // SLOTS, 1),
    )
    shapes2 = ((width, hidden), (width, hidden), (hidden, width))
    held1, held2 = (), ()

    def spread1(src, mate, flip):
        nonlocal held1
        src = order.after(src)
        held1 = spread(scal, src, held1, mate, flip, PIECE1, plan1, shapes1, "spread_ffn")
        order.did(held1[0])

    def spread2(src, mate, flip):
        nonlocal held2
        src = order.after(src)
        held2 = spread(scal, src, held2, mate, flip, PIECE2, plan2, shapes2, "spread_gates")
        order.did(held2[0])

    for chunk in (chunk1, chunk2, chunk1, chunk1, chunk2, chunk1, chunk2, chunk1):
        chunk.step()
    chunk2.ride = small + order.after(coming)
    chunk2.step()
    chunk2.step()
    chunk1.step()
    spread1(chunk1.total, 0, 0)
    chunk2.step()
    spread1(chunk1.theirs, 1, 0)
    chunk2.step()
    chunk1.step()
    spread1(chunk1.rest, 0, 1)
    spread2(chunk2.total, 0, 0)
    spread1(chunk1.their_rest, 1, 1)
    spread2(chunk2.theirs, 1, 0)
    chunk2.step()
    small = chunk2.ride
    small_out = order.after(
        small[0], small[1 : taps + 1], small[taps + 2 :].reshape(hidden), small[taps + 1]
    )
    spread2(chunk2.rest, 0, 1)
    spread2(chunk2.their_rest, 1, 1)
    return (
        output,
        input_grad,
        small_out[0],
        small_out[1],
        held2[0],
        small_out[2],
        held2[1],
        held2[2],
        small_out[3],
        held1[1],
        held1[0],
    )


def solution(mesh):
    sharded = P("row", "seq", None)
    in_specs = (sharded, P("row")) + (P(),) * 9 + (sharded,)
    out_specs = (sharded, sharded) + (P(),) * 9
    return jax.shard_map(
        per_device, mesh=mesh, in_specs=in_specs, out_specs=out_specs, check_vma=False
    )
```

```python
import functools

import jax
import jax.numpy as jnp
import numpy as np
from jax import lax
from jax.experimental import pallas as pl
from jax.experimental.pallas import tpu as pltpu
from jax.sharding import PartitionSpec as P

epsilon = 1e-06
f32 = jnp.float32
bf16 = jnp.bfloat16
R = 8
PERM = 256
SCALARS = 4
SLOTS = 32
PIECE1 = 128
PIECE2 = 96


def nn(a, b):
    return lax.dot_general(a, b, (((1,), (0,)), ((), ())), preferred_element_type=f32)


def nt(a, b):
    return lax.dot_general(a, b, (((1,), (1,)), ((), ())), preferred_element_type=f32)


def tn(a, b):
    return lax.dot_general(a, b, (((0,), (0,)), ((), ())), preferred_element_type=f32)


def token_order():
    out = np.arange(PERM)
    source = (out % R) * (PERM // R) + out // R
    to_pm = np.zeros((PERM, PERM), np.float32)
    to_pm[out, source] = 1
    return jnp.asarray(to_pm, bf16), jnp.asarray(to_pm.T, bf16)


def position_major(perm, block):
    span = PERM // R
    parts = []
    for s in range(block.shape[1] // span):
        part = block[:, s * span : (s + 1) * span, :].reshape(PERM, block.shape[2])
        parts.append(nn(perm, part))
    return parts[0] if len(parts) == 1 else jnp.concatenate(parts, 0)


def row_major(perm, tokens):
    span = PERM // R
    parts = []
    for s in range(tokens.shape[0] // PERM):
        part = nn(perm, tokens[s * PERM : (s + 1) * PERM]).astype(bf16)
        parts.append(part.reshape(R, span, tokens.shape[1]))
    return parts[0] if len(parts) == 1 else jnp.concatenate(parts, 1)


def eight(t):
    return pl.ds(pl.multiple_of(t * R, R), R)


def sixteen(t):
    return pl.ds(pl.multiple_of(t * 2 * R, 2 * R), 2 * R)


def normed_edge(edge, gain):
    e = edge.astype(f32)
    inv = lax.rsqrt(jnp.mean(e * e, -1, keepdims=True) + epsilon)
    return (e * inv * gain).astype(bf16).astype(f32)


def set_limits(scal, limit):
    row = lax.broadcasted_iota(jnp.int32, limit.shape, 0)
    value = jnp.zeros(limit.shape, jnp.int32)
    for r in range(R):
        value = jnp.where(row == r, scal[SCALARS + r], value)
    limit[...] = value


def halves(ref, pair):
    both = ref[sixteen(pair), :].astype(f32)
    return both[:R], both[R:]


def norm_kernel(x, perm, gain, u_out):
    xp = position_major(perm[...], x[...])
    inv = lax.rsqrt(jnp.mean(xp * xp, -1, keepdims=True) + epsilon)
    u_out[...] = (xp * inv * gain[...]).astype(bf16)


def front_kernel(scal, u, edge, gain, convw, wg, bias, wc, c_out, zl_out, kh_out, ends, ext, state, limit):
    step = pl.program_id(0)
    m = u.shape[0]
    tb = m // R
    halo = edge.shape[0]
    taps = convw.shape[0]

    @pl.when(step == 0)
    def _():
        set_limits(scal, limit)
        ext[0:halo, :] = normed_edge(edge[...], gain[...])
        state[0:R, :] = jnp.ones((R, state.shape[1]), f32)
        state[R:, :] = jnp.zeros((R, state.shape[1]), f32)

    ext[halo:, :] = u[...].astype(f32)
    conv = convw[0:1, :] * ext[halo:, :]
    for k in range(1, taps):
        lo = halo - k * R
        conv = conv + convw[k : k + 1, :] * ext[lo : lo + m, :]
    ext[0:halo, :] = ext[m : m + halo, :]
    cb = conv.astype(bf16)
    c_out[...] = cb
    kz = nn(cb, wg[...]) + bias[...]
    zs = 1.0 / (1.0 + jnp.exp(-kz))
    width = zs.shape[1]
    zs = zs.reshape(tb, R, width)
    pos = scal[0] + step * tb + lax.broadcasted_iota(jnp.int32, (tb, R, width), 0)
    zl_out[...] = jnp.where(pos < limit[...][None], zs, 0.0).reshape(m, width).astype(bf16)
    kh_out[...] = nn(cb, wc[...]).astype(bf16)

    def body(u, carry):
        prod, h = carry
        za, zb = halves(zl_out, u)
        ka, kb = halves(kh_out, u)
        a = 1.0 - za
        b = 1.0 - zb
        return prod * (a * b), (h * a + za * ka) * b + zb * kb

    prod, h = lax.fori_loop(0, tb // 2, body, (state[0:R, :], state[R:, :]), unroll=4)
    state[0:R, :] = prod
    state[R:, :] = h
    ends[0:R, :] = prod
    ends[R:, :] = h


def gelu_parts(p):
    k0 = 0.7978845608028654
    p2 = p * p
    th = jnp.tanh(p * (k0 + (k0 * 0.044715) * p2))
    ht = 0.5 + 0.5 * th
    return p * ht, ht + (2.0 * p) * (ht - ht * ht) * (k0 + (3.0 * k0 * 0.044715) * p2)


def da_kernel(g, perm, wd, gl_out, da_out):
    gl = position_major(perm[...], g[...]).astype(bf16)
    gl_out[...] = gl
    da_out[...] = nt(gl, wd[...]).astype(bf16)


def core_kernel(scal, x, perm, gl, da, zl, zl_next, kh, kh_next, zl_before, other, *refs, fchunk, hops, blocks):
    msgs = refs[:hops]
    wo, mgain, wu = refs[hops : hops + 3]
    r1_out, y_out, hp_out, n2_out, act_out, dp_out, dm_out, dr1_out, dh_out, back, mg = refs[hops + 3 : hops + 14]
    state, limit, run, acc, ys, hps, dhs = refs[hops + 14 :]
    step = pl.program_id(0)
    tb = x.shape[1]
    m = tb * R
    width, feed = wu.shape
    hidden = wo.shape[0]
    first = scal[0] + step * tb

    def scan_pair(zs, ks, start, u, h):
        t = u * 2
        za, zb = halves(zs, u)
        ka, kb = halves(ks, u)
        ha = h - za * h + za * ka
        hb = ha - zb * ha + zb * kb
        hps[sixteen(u), :] = jnp.concatenate([h, ha], 0).astype(bf16)
        ya = jnp.where(start + t < limit[...], ha, 0.0)
        yb = jnp.where(start + t + 1 < limit[...], hb, 0.0)
        ys[sixteen(u), :] = jnp.concatenate([ya, yb], 0).astype(bf16)
        return hb

    def adjoint_pair(zs, ds, u, prod, total):
        za, zb = halves(zs, u)
        da, db = halves(ds, u)
        pa = prod - za * prod
        pb = pa - zb * pa
        return pb, total + (pa * da + pb * db)

    @pl.when(step == 0)
    def _():
        set_limits(scal, limit)
        h = jnp.zeros((R, hidden), f32)
        for msg in reversed(msgs):
            both = msg[...].astype(f32)
            h = jnp.exp(both[0:R, :]) * h + both[R:, :]
        h = jnp.where(scal[1] == 1, other[0:R, :] * h + other[R:, :], h)
        run[...] = jnp.ones((R, hidden), f32)
        back[...] = jnp.zeros(back.shape, f32)
        mg[...] = jnp.zeros(mg.shape, f32)
        dhs[...] = jnp.zeros(dhs.shape, bf16)
        state[...] = lax.fori_loop(0, tb // 2, lambda u, h: scan_pair(zl, kh, scal[0], u, h), h, unroll=2)

    hp_out[...] = hps[...]
    y = ys[...]
    y_out[...] = y
    r1 = position_major(perm[...], x[...]) + nn(y, wo[...])
    r1_out[...] = r1
    inv = lax.rsqrt(jnp.mean(r1 * r1, -1, keepdims=True) + epsilon)
    n2 = (r1 * inv * mgain[...]).astype(bf16)
    n2_out[...] = n2
    chunks = feed // fchunk
    pairs = tb // 2 // chunks
    for f in range(chunks):
        cols = slice(f * fchunk, (f + 1) * fchunk)
        a, slope = gelu_parts(nn(n2, wu[:, cols]))
        act_out[:, cols] = a.astype(bf16)
        dpb = (da[:, cols].astype(f32) * slope).astype(bf16)
        dp_out[:, cols] = dpb
        part = nt(dpb, wu[:, cols])
        acc[...] = acc[...] + part if f else part
        h, prod, total = state[...], run[...], back[...]
        for u in range(f * pairs, (f + 1) * pairs):
            h = scan_pair(zl_next, kh_next, first + tb, u, h)
            prod, total = adjoint_pair(zl_before, dhs, u, prod, total)
        state[...] = h
        run[...] = jnp.where(step == 0, 1.0, prod)
        back[...] = total
    dn2 = acc[...]
    r1 = r1_out[...]
    mg[...] += jnp.sum((dn2 * r1 * inv).reshape(tb, R, width), 0)
    s = mgain[...] * dn2
    mean = jnp.mean(s * r1, -1, keepdims=True)
    dr1 = gl[...].astype(f32) + inv * (s - r1 * (inv * inv * mean))
    dr1_out[...] = dr1
    dm = dr1.astype(bf16)
    dm_out[...] = dm
    dh = nt(dm, wo[...]).reshape(tb, R, hidden)
    pos = first + lax.broadcasted_iota(jnp.int32, (tb, R, hidden), 0)
    dh = jnp.where(pos < limit[...][None], dh, 0.0).reshape(m, hidden).astype(bf16)
    dh_out[...] = dh
    dhs[...] = dh

    @pl.when(step == blocks - 1)
    def _():
        carry = lax.fori_loop(
            0, tb // 2, lambda u, carry: adjoint_pair(zl, dhs, u, *carry), (run[...], back[...]), unroll=4
        )
        back[...] = carry[1]


def put_rows(dst, sel, piece, at, rows, part):
    for i in range(SLOTS // 2):
        pos = pl.multiple_of((i ^ sel) * piece + at, 16)
        dst[pl.ds(pos, rows), :] = part[i * rows : (i + 1) * rows]


def ffn_grad_kernel(scal, act, gl, n2, dp, dst, *, pick):
    step = pl.program_id(0)
    sel = scal[2 + pick]
    width = gl.shape[1]
    rows1 = act.shape[1] * 4 // SLOTS
    rows2 = n2.shape[1] * 2 // SLOTS
    part = tn(act[...], gl[...]).astype(bf16)
    per = act.shape[1] // rows1
    for i in range(per):
        pos = ((step * per + i) ^ sel) * PIECE1
        dst[pl.ds(pl.multiple_of(pos, 16), rows1), :] = part[i * rows1 : (i + 1) * rows1]
    columns = dp.shape[1] // width
    for q in range(columns):
        part = tn(n2[...], dp[:, q * width : (q + 1) * width]).astype(bf16)
        put_rows(dst, sel, PIECE1, rows1 + (step * columns + q) * rows2, rows2, part)


def gate_grad_kernel(scal, c, dkz, dkh, y, dm, dst, *, pick):
    sel = scal[2 + pick]
    width = dm.shape[1]
    rows = c.shape[1] * 2 // SLOTS
    at = 0
    for grads in (dkz, dkh):
        for q in range(grads.shape[1] // width):
            part = tn(c[...], grads[:, q * width : (q + 1) * width]).astype(bf16)
            put_rows(dst, sel, PIECE2, at, rows, part)
            at += rows
    put_rows(dst, sel, PIECE2, at, y.shape[1] * 2 // SLOTS, tn(y[...], dm[...]).astype(bf16))


def gate_kernel(scal, dh, zl, kh, hp, other, fother, *refs, blocks, hops):
    msgs = refs[:hops]
    wg, wc = refs[hops : hops + 2]
    dkz, dkh, edge_out, bias_out = refs[hops + 3 : hops + 7]
    state = refs[hops + 7]
    step = pl.program_id(0)
    m = dh.shape[0]
    tb = m // R
    block = blocks - 1 - step

    @pl.when(step == 0)
    def _():
        mm = jnp.zeros(state.shape, f32)
        for msg in reversed(msgs):
            both = msg[...].astype(f32)
            mm = jnp.exp(both[0:R, :]) * mm + both[R:, :]
        state[...] = jnp.where(scal[1] == 0, fother[...] + other[0:R, :] * mm, mm)
        bias_out[...] = jnp.zeros(bias_out.shape, f32)

    def body(u, carry):
        mm, bias = carry
        w = tb // 2 - 1 - u
        ha, hb = halves(hp, w)
        za, zb = halves(zl, w)
        da, db = halves(dh, w)
        ka, kb = halves(kh, w)
        lam = db + mm
        sb = lam * zb
        mm = lam - sb
        kb = (sb - sb * zb) * (kb - hb)
        lam = da + mm
        sa = lam * za
        mm = lam - sa
        ka = (sa - sa * za) * (ka - ha)
        kk = jnp.concatenate([ka, kb], 0).astype(bf16)
        dkz[sixteen(w), :] = kk
        dkh[sixteen(w), :] = jnp.concatenate([sa, sb], 0).astype(bf16)
        kf = kk.astype(f32)
        return mm, bias + kf[:R, :] + kf[R:, :]

    mm, bias = lax.fori_loop(0, tb // 2, body, (state[...], bias_out[...]), unroll=2)
    state[...] = mm
    bias_out[...] = bias

    @pl.when(block == 0)
    def _():
        span = edge_out.shape[0]
        edge_out[...] = (nt(dkz[0:span, :], wg[...]) + nt(dkh[0:span, :], wc[...])).astype(bf16)


def tail_kernel(x, dr1, dkz, dkh, pm, back_pm, edge, after, gain, convw, wg, wc, grad, sums, uext, dext, *, blocks):
    step = pl.program_id(0)
    tb = x.shape[1]
    m = tb * R
    halo = edge.shape[0]
    taps = convw.shape[0]
    width = gain.shape[1]

    @pl.when(step == 0)
    def _():
        uext[0:halo, :] = normed_edge(edge[...], gain[...])
        dext[blocks * m :, :] = after[...].astype(f32)
        sums[...] = jnp.zeros(sums.shape, f32)

    @pl.when(step < blocks)
    def _():
        rows = pl.ds(pl.multiple_of(step * m, m), m)
        dext[rows, :] = nt(dkz[...], wg[...]) + nt(dkh[...], wc[...])

    @pl.when(step >= blocks)
    def _():
        xp = position_major(pm[...], x[...])
        inv = lax.rsqrt(jnp.mean(xp * xp, -1, keepdims=True) + epsilon)
        xn = xp * inv
        uext[halo:, :] = (xn * gain[...]).astype(bf16).astype(f32)
        start = (step - blocks) * m
        here = dext[pl.ds(pl.multiple_of(start, R), m), :]
        du = convw[0:1, :] * here
        for k in range(taps):
            lo = halo - k * R
            part = (here * uext[lo : lo + m, :]).reshape(tb, R, width)
            sums[(k + 1) * R : (k + 2) * R, :] += jnp.sum(part, 0)
            if k:
                du = du + convw[k : k + 1, :] * dext[pl.ds(pl.multiple_of(start + k * R, R), m), :]
        uext[0:halo, :] = uext[m : m + halo, :]
        sums[0:R, :] += jnp.sum((du * xn).reshape(tb, R, width), 0)
        s1 = gain[...] * du
        mean = jnp.mean(s1 * xn, -1, keepdims=True)
        gin = dr1[...] + inv * (s1 - xn * mean)
        grad[...] = row_major(back_pm[...], gin.astype(bf16))


def output_kernel(r1, act, perm, wd, out):
    total = r1[...] + nn(act[...], wd[...])
    out[...] = row_major(perm[...], total.astype(bf16))


def spread_kernel(scal, src, *refs, piece, plan, mate):
    low = scal[2 + mate] & 7
    for a in range(8):
        base = (a ^ low) * piece
        at = 0
        for out, rows, columns in plan:
            ref = refs[len(refs) - len(plan) + out]
            for q in range(columns):
                width = src.shape[1]
                part = src[pl.ds(pl.multiple_of(base + at, 16), rows), :].astype(f32)
                ref[a * rows : (a + 1) * rows, q * width : (q + 1) * width] = part
                at += rows


def spread(scal, src, held, mate, flip, piece, plan, shapes, name):
    def block(g, s):
        return ((s[1] ^ mate) * 2 + ((s[2 + mate] >> 3) ^ flip), 0)

    count = len(held)
    return pl.pallas_call(
        functools.partial(spread_kernel, piece=piece, plan=plan, mate=mate),
        grid_spec=pltpu.PrefetchScalarGridSpec(
            num_scalar_prefetch=1,
            grid=(1,),
            in_specs=[whole(src)] + [ORDER] * count,
            out_specs=[pl.BlockSpec((dims[0] // 4, dims[1]), block) for dims in shapes],
        ),
        out_shape=[pltpu.HBM(dims, f32) for dims in shapes],
        input_output_aliases={2 + k: k for k in range(count)},
        compiler_params=params(16),
        cost_estimate=LITTLE,
        name=name,
    )(scal, src, *held)


def params(mib):
    return pltpu.CompilerParams(
        dimension_semantics=("arbitrary",), vmem_limit_bytes=mib * 1024 * 1024
    )


def shape(dims, kind=f32):
    return jax.ShapeDtypeStruct(dims, kind)


LITTLE = pl.CostEstimate(flops=1024, bytes_accessed=1024, transcendentals=0)
MUCH = pl.CostEstimate(flops=3 * 10**10, bytes_accessed=1024, transcendentals=0)
ORDER = pl.BlockSpec(memory_space=pl.ANY)


def far(array):
    return pltpu.with_memory_space_constraint(array, pltpu.HBM)


def whole(array):
    zeros = (0,) * array.ndim
    return pl.BlockSpec(array.shape, lambda *a: zeros, pipeline_mode=pl.Buffered(1))


def passed_along(value, axis, steps):
    count = lax.axis_size(axis)
    leading, last = (max(0, -steps), min(count, count - steps))
    return lax.ppermute(value, axis, [(source, source + steps) for source in range(leading, last)])


def flat_permute(value, pairs):
    return lax.ppermute(value, ("seq", "row"), pairs)


def stage_bits():
    row_bits = lax.axis_size("row").bit_length() - 1
    seq_bits = lax.axis_size("seq").bit_length() - 1
    plane = list(range(row_bits))
    line = [row_bits + 1 + z for z in range(seq_bits - 1)]
    cut = row_bits // 2
    return (plane + line, plane[cut:] + plane[:cut] + line[::-1])


def slot_of(flat, bits):
    slot = 0
    for k in range(4):
        slot = slot * 2 + ((flat >> bits[k]) & 1)
    return slot


def halving_pairs(stage):
    row_bits = lax.axis_size("row").bit_length() - 1
    orders = stage_bits()
    devices = lax.axis_size("row") * lax.axis_size("seq")
    return [(d, d ^ (1 << orders[(d >> row_bits) & 1][stage])) for d in range(devices)]


def core_pairs():
    row_bits = lax.axis_size("row").bit_length() - 1
    devices = lax.axis_size("row") * lax.axis_size("seq")
    return [(d, d ^ (1 << row_bits)) for d in range(devices)]


def added(a, b):
    return (a.astype(f32) + b.astype(f32)).astype(bf16)


class Sequence:
    def __init__(self, token):
        self.token = token

    def after(self, *arrays):
        *arrays, _ = lax.optimization_barrier((*arrays, self.token))
        return arrays[0] if len(arrays) == 1 else arrays

    def did(self, array):
        self.token = array
        return array


def split(value):
    high = lax.reduce_precision(value, 8, 7)
    return [high.astype(bf16), (value - high).astype(bf16)]


def join_kernel(mine, recv, ride, out, ride_out):
    rows = mine.shape[0] - 2 * R
    out[0:rows, :] = mine[0:rows, :]
    out[rows : 2 * rows, :] = recv[0:rows, :]
    parts = recv[rows:, :].astype(f32)
    total = ride[...] + (parts[:R] + parts[R:])
    ride_out[...] = total
    high = total.astype(bf16).astype(f32)
    out[2 * rows :, :] = jnp.concatenate([high, total - high], 0).astype(bf16)


def joined(mine, recv, ride):
    rows, width = mine.shape
    return pl.pallas_call(
        join_kernel,
        in_specs=[pl.BlockSpec(memory_space=pltpu.VMEM)] * 3,
        out_specs=[pl.BlockSpec(memory_space=pltpu.VMEM)] * 2,
        out_shape=[shape((2 * rows - 2 * R, width), bf16), shape(ride.shape)],
        compiler_params=pltpu.CompilerParams(vmem_limit_bytes=16 * 1024 * 1024),
        cost_estimate=LITTLE,
        name="join",
    )(mine, recv, ride)


class Halving:
    def __init__(self, seq, send):
        self.seq = seq
        self.recv = flat_permute(send, core_pairs())
        self.stage = 0
        self.ride = None

    def riders(self):
        return [] if self.ride is None else split(self.ride)

    def board(self, recv, rows):
        if self.ride is not None:
            low = rows + self.ride.shape[0]
            self.ride = self.ride + (recv[rows:low].astype(f32) + recv[low:].astype(f32))

    def step(self, *beside):
        k = self.stage
        self.stage += 1
        stages = len(stage_bits()[0])
        recv, *beside = self.seq.after(self.recv, *beside) if beside else (self.seq.after(self.recv),)
        if k < 4:
            half = self.keep.shape[0] // 2
            send = self.seq.did(added(self.keep[half:], recv[half:]))
            self.recv = flat_permute(send, halving_pairs(k))
            self.keep = added(self.keep[:half], recv[:half])
        elif k == 4:
            total = added(self.keep, recv)
            for extra in range(4, stages):
                total = added(total, flat_permute(total, halving_pairs(extra)))
                if self.ride is not None:
                    self.ride = self.ride + flat_permute(self.ride, halving_pairs(extra))
            self.rows = total.shape[0]
            self.total = self.seq.did(jnp.concatenate([total] + self.riders(), 0))
            self.recv = flat_permute(self.total, halving_pairs(3))
        elif k < 8:
            rows = self.rows
            self.rows = 2 * rows
            if self.ride is None:
                self.total = self.seq.did(jnp.concatenate([self.total, recv], 0))
            else:
                self.total, self.ride = joined(self.total, recv, self.ride)
                self.seq.did(self.total)
            self.recv = flat_permute(self.total, halving_pairs(7 - k))
            if k == 7:
                self.theirs = flat_permute(self.total, core_pairs())
        else:
            self.board(recv, self.rows)
            self.rest = recv
            self.their_rest = flat_permute(recv, core_pairs())
        return beside


def chip_shift(value, steps):
    return passed_along(value, "seq", 2 * steps)


def per_device(
    inputs,
    lengths,
    norm_gain,
    conv_weight,
    gate_weight,
    gate_bias,
    cand_weight,
    out_weight,
    mlp_gain,
    up_weight,
    down_weight,
    cotangent,
):
    rows, span, width = inputs.shape
    hidden = gate_weight.shape[1]
    feed = up_weight.shape[1]
    taps = conv_weight.shape[0]
    margin = taps - 1
    tokens = rows * span
    tb = 32
    blocks = span // tb
    m = tb * R
    seq = lax.axis_index("seq")
    core = seq & 1
    chips = lax.axis_size("seq") // 2
    hops = chips - 1
    flat = seq * lax.axis_size("row") + lax.axis_index("row")
    slots = [slot_of(flat, bits) for bits in stage_bits()]
    here = jnp.where(core == 0, slots[0], slots[1])
    mate = jnp.where(core == 0, slots[1], slots[0])
    scal = jnp.concatenate([jnp.stack([seq * span, core, here, mate]).astype(jnp.int32), lengths])
    gain1 = norm_gain.reshape(1, width)
    gain2 = mlp_gain.reshape(1, width)
    bias = gate_bias.reshape(1, hidden)
    to_pm, to_rm = token_order()

    edge = inputs[:, span - margin :, :].swapaxes(0, 1).reshape(margin * rows, width)
    edge = passed_along(edge, "seq", 1)

    last = blocks - 1
    clamp = lambda i: jnp.minimum(i, last)
    late = lambda i: jnp.maximum(i - blocks, 0)
    later = lambda i: jnp.minimum(i + 1, last)
    before = lambda i: jnp.maximum(i - 1, 0)

    def rm(index):
        return pl.BlockSpec((rows, tb, width), lambda i, *s: (0, index(i), 0))

    def tok(w, index=clamp):
        return pl.BlockSpec((m, w), lambda i, *s: (index(i), 0))

    def rtok(w):
        return tok(w, lambda i: last - clamp(i))

    def fixed(dims):
        zeros = (0,) * len(dims)
        return pl.BlockSpec(dims, lambda i, *s: zeros)

    def call(kernel, name, grid, ins, outs, scratch, operands, scalars=True, much=False):
        spec = pltpu.PrefetchScalarGridSpec(
            num_scalar_prefetch=int(scalars),
            grid=(grid,),
            in_specs=ins,
            out_specs=[o[1] for o in outs],
            scratch_shapes=scratch,
        )
        return pl.pallas_call(
            kernel,
            grid_spec=spec,
            out_shape=[o[0] for o in outs],
            compiler_params=params(16),
            cost_estimate=MUCH if much else LITTLE,
            name=name,
        )(*operands)

    def rows_of(w, kind, spec=tok, kept=shape):
        return kept((tokens, w), kind), spec(w)

    (normed,) = call(
        norm_kernel, "norm", blocks,
        [rm(clamp), whole(to_pm), whole(gain1)],
        [rows_of(width, bf16)],
        [],
        (far(inputs), far(to_pm), far(gain1)),
        scalars=False,
    )
    edge, normed = lax.optimization_barrier((edge, normed))
    c, zl, kh, ends = call(
        front_kernel, "front", blocks,
        [
            tok(width), whole(edge), whole(gain1), whole(conv_weight),
            whole(gate_weight), whole(bias), whole(cand_weight),
        ],
        [
            rows_of(width, bf16), rows_of(hidden, bf16), rows_of(hidden, bf16),
            (shape((2 * R, hidden)), fixed((2 * R, hidden))),
        ],
        [
            pltpu.VMEM((margin * R + m, width), f32),
            pltpu.VMEM((2 * R, hidden), f32),
            pltpu.VMEM((R, hidden), jnp.int32),
        ],
        (
            scal, normed, edge, far(gain1), far(conv_weight), gate_weight, far(bias),
            cand_weight,
        ),
    )

    other = flat_permute(ends, core_pairs())
    first = jnp.where(core == 0, ends, other)
    second = jnp.where(core == 0, other, ends)
    decay = jnp.log(jnp.maximum(ends[:R] * other[:R], 1e-37))
    message = jnp.concatenate([decay, second[:R] * first[R:] + second[R:]], 0).astype(bf16)
    forward = [chip_shift(message, k) for k in range(1, chips)]

    gl, da = call(
        da_kernel, "da", blocks,
        [rm(clamp), whole(to_pm), whole(down_weight)],
        [rows_of(width, bf16), rows_of(feed, bf16)],
        [],
        (cotangent, to_pm, down_weight),
        scalars=False,
    )

    r1, y, hp, n2, act, dp, dm, dr1, dh, back, mg = call(
        functools.partial(core_kernel, fchunk=256, hops=hops, blocks=blocks), "core", blocks,
        [
            rm(clamp), whole(to_pm), tok(width), tok(feed), tok(hidden), tok(hidden, later), tok(hidden),
            tok(hidden, later), tok(hidden, before), whole(other),
            *[whole(f) for f in forward], whole(out_weight), whole(gain2), whole(up_weight),
        ],
        [
            rows_of(width, f32, kept=pltpu.HBM), rows_of(hidden, bf16), rows_of(hidden, bf16),
            rows_of(width, bf16), rows_of(feed, bf16), rows_of(feed, bf16), rows_of(width, bf16),
            rows_of(width, f32, kept=pltpu.HBM),
            rows_of(hidden, bf16),
            (shape((R, hidden)), fixed((R, hidden))), (shape((R, width)), fixed((R, width))),
        ],
        [
            pltpu.VMEM((R, hidden), f32),
            pltpu.VMEM((R, hidden), jnp.int32),
            pltpu.VMEM((R, hidden), f32),
            pltpu.VMEM((m, width), f32),
            pltpu.VMEM((m, hidden), bf16),
            pltpu.VMEM((m, hidden), bf16),
            pltpu.VMEM((m, hidden), bf16),
        ],
        (
            scal, inputs, to_pm, gl, da, zl, zl, kh, kh, zl, other, *forward, far(out_weight), gain2, up_weight,
        ),
    )

    order = Sequence(back)
    quarter = feed // 4

    def ffn_grads(pick, *beside):
        half = lambda s: s[1] if pick == 0 else 1 - s[1]
        a, d, *beside = order.after(act, dp, *beside)
        (piece,) = call(
            functools.partial(ffn_grad_kernel, pick=pick), "ffn_grad", 2,
            [
                pl.BlockSpec((tokens, quarter), lambda i, s: (0, half(s) * 2 + i)), whole(gl),
                pl.BlockSpec((tokens, width // 2), lambda i, s: (0, half(s))),
                pl.BlockSpec((tokens, feed // 2), lambda i, s: (0, i)),
            ],
            [(shape((SLOTS // 2 * PIECE1, width), bf16), fixed((SLOTS // 2 * PIECE1, width)))],
            [],
            (scal, a, gl, n2, d),
            much=pick == 0,
        )
        return order.did(piece), beside

    def gate_grads(pick):
        half = lambda s: s[1] if pick == 0 else 1 - s[1]
        z, h = order.after(dkz, dkh)
        (piece,) = call(
            functools.partial(gate_grad_kernel, pick=pick), "gate_grad", 1,
            [
                pl.BlockSpec((tokens, width // 2), lambda i, s: (0, half(s))),
                whole(z), whole(h),
                pl.BlockSpec((tokens, hidden // 2), lambda i, s: (0, half(s))), whole(dm),
            ],
            [(shape((SLOTS // 2 * PIECE2, width), bf16), fixed((SLOTS // 2 * PIECE2, width)))],
            [],
            (scal, c, z, h, y, dm),
            much=pick == 0,
        )
        return order.did(piece)

    fother = flat_permute(back, core_pairs())
    lower = jnp.where(core == 0, back, fother)
    upper = jnp.where(core == 0, fother, back)
    message = jnp.concatenate([decay, lower + first[:R] * upper], 0).astype(bf16)
    backward = [chip_shift(order.did(message), -k) for k in range(1, chips)]
    send1, _ = ffn_grads(1)
    chunk1 = Halving(order, send1)
    chunk1.keep, backward = ffn_grads(0, *backward)
    chunk1.step()

    dkz, dkh, edge_dc, bias_part = call(
        functools.partial(gate_kernel, blocks=blocks, hops=hops), "gates", blocks,
        [
            rtok(hidden), rtok(hidden), rtok(hidden), rtok(hidden),
            whole(other), whole(fother), *[whole(f) for f in backward],
            whole(gate_weight), whole(cand_weight), ORDER,
        ],
        [
            rows_of(hidden, bf16, rtok), rows_of(hidden, bf16, rtok),
            (shape((4 * R, width), bf16), fixed((4 * R, width))),
            (shape((R, hidden)), fixed((R, hidden))),
        ],
        [pltpu.VMEM((R, hidden), f32)],
        (
            scal, dh, zl, kh, hp, other, fother, *backward, gate_weight, cand_weight, order.token,
        ),
    )
    order.did(bias_part)
    after = passed_along(edge_dc[: margin * R], "seq", -1)
    send2 = gate_grads(1)
    chunk2 = Halving(order, send2)
    (output,) = call(
        output_kernel, "output", blocks,
        [tok(width), tok(feed), whole(to_rm), whole(down_weight)],
        [(shape((rows, span, width), bf16), rm(clamp))],
        [],
        (far(r1), order.after(act), to_rm, down_weight),
        scalars=False,
    )
    order.did(output)
    chunk1.step()
    chunk2.keep = gate_grads(0)
    chunk2.step()
    input_grad, sums = call(
        functools.partial(tail_kernel, blocks=blocks), "tail", 2 * blocks,
        [
            rm(late), tok(width, late), tok(hidden), tok(hidden), whole(to_pm), whole(to_rm),
            whole(edge), whole(after), whole(gain1), whole(conv_weight), whole(gate_weight),
            whole(cand_weight),
        ],
        [
            (shape((rows, span, width), bf16), rm(late)),
            (shape(((taps + 1) * R, width)), fixed(((taps + 1) * R, width))),
        ],
        [
            pltpu.VMEM((margin * R + m, width), f32),
            pltpu.VMEM((margin * R + tokens, width), f32),
        ],
        (
            far(inputs), far(dr1), order.after(dkz), dkh, far(to_pm), far(to_rm), edge, after,
            far(gain1), far(conv_weight), far(gate_weight), far(cand_weight),
        ),
        scalars=False,
    )
    order.did(sums)
    small = jnp.concatenate(
        [
            sums.reshape(taps + 1, R, width).sum(1),
            mg.sum(0, keepdims=True),
            bias_part.sum(0).reshape(hidden // width, width),
        ],
        0,
    )
    coming = flat_permute(small, core_pairs())

    plan1 = ((0, feed // SLOTS, 1), (1, width // SLOTS, feed // width))
    shapes1 = ((feed, width), (width, feed))
    plan2 = (
        (0, width // SLOTS, hidden // width),
        (1, width // SLOTS, hidden // width),
        (2, hidden // SLOTS, 1),
    )
    shapes2 = ((width, hidden), (width, hidden), (hidden, width))
    held1, held2 = (), ()

    def spread1(src, mate, flip):
        nonlocal held1
        src = order.after(src)
        held1 = spread(scal, src, held1, mate, flip, PIECE1, plan1, shapes1, "spread_ffn")
        order.did(held1[0])

    def spread2(src, mate, flip):
        nonlocal held2
        src = order.after(src)
        held2 = spread(scal, src, held2, mate, flip, PIECE2, plan2, shapes2, "spread_gates")
        order.did(held2[0])

    for chunk in (chunk1, chunk2, chunk1, chunk1, chunk2, chunk1, chunk2, chunk1):
        chunk.step()
    chunk2.ride = small + order.after(coming)
    chunk2.step()
    chunk2.step()
    chunk1.step()
    spread1(chunk1.total, 0, 0)
    chunk2.step()
    spread1(chunk1.theirs, 1, 0)
    chunk2.step()
    chunk1.step()
    spread1(chunk1.rest, 0, 1)
    spread2(chunk2.total, 0, 0)
    spread1(chunk1.their_rest, 1, 1)
    spread2(chunk2.theirs, 1, 0)
    chunk2.step()
    small = chunk2.ride
    small_out = order.after(
        small[0], small[1 : taps + 1], small[taps + 2 :].reshape(hidden), small[taps + 1]
    )
    spread2(chunk2.rest, 0, 1)
    spread2(chunk2.their_rest, 1, 1)
    return (
        output,
        input_grad,
        small_out[0],
        small_out[1],
        held2[0],
        small_out[2],
        held2[1],
        held2[2],
        small_out[3],
        held1[1],
        held1[0],
    )


def solution(mesh):
    sharded = P("row", "seq", None)
    in_specs = (sharded, P("row")) + (P(),) * 9 + (sharded,)
    out_specs = (sharded, sharded) + (P(),) * 9
    return jax.shard_map(
        per_device, mesh=mesh, in_specs=in_specs, out_specs=out_specs, check_vma=False
    )
```

```python
import functools

import jax
import jax.numpy as jnp
import numpy as np
from jax import lax
from jax.experimental import pallas as pl
from jax.experimental.pallas import tpu as pltpu
from jax.sharding import PartitionSpec as P

epsilon = 1e-06
f32 = jnp.float32
bf16 = jnp.bfloat16
R = 8
PERM = 256
SCALARS = 4
SLOTS = 32
PIECE1 = 128
PIECE2 = 96


def nn(a, b):
    return lax.dot_general(a, b, (((1,), (0,)), ((), ())), preferred_element_type=f32)


def nt(a, b):
    return lax.dot_general(a, b, (((1,), (1,)), ((), ())), preferred_element_type=f32)


def tn(a, b):
    return lax.dot_general(a, b, (((0,), (0,)), ((), ())), preferred_element_type=f32)


def token_order():
    out = np.arange(PERM)
    source = (out % R) * (PERM // R) + out // R
    to_pm = np.zeros((PERM, PERM), np.float32)
    to_pm[out, source] = 1
    return jnp.asarray(to_pm, bf16), jnp.asarray(to_pm.T, bf16)


def position_major(perm, block):
    span = PERM // R
    parts = []
    for s in range(block.shape[1] // span):
        part = block[:, s * span : (s + 1) * span, :].reshape(PERM, block.shape[2])
        parts.append(nn(perm, part))
    return parts[0] if len(parts) == 1 else jnp.concatenate(parts, 0)


def row_major(perm, tokens):
    span = PERM // R
    parts = []
    for s in range(tokens.shape[0] // PERM):
        part = nn(perm, tokens[s * PERM : (s + 1) * PERM]).astype(bf16)
        parts.append(part.reshape(R, span, tokens.shape[1]))
    return parts[0] if len(parts) == 1 else jnp.concatenate(parts, 1)


def eight(t):
    return pl.ds(pl.multiple_of(t * R, R), R)


def sixteen(t):
    return pl.ds(pl.multiple_of(t * 2 * R, 2 * R), 2 * R)


def normed_edge(edge, gain):
    e = edge.astype(f32)
    inv = lax.rsqrt(jnp.mean(e * e, -1, keepdims=True) + epsilon)
    return (e * inv * gain).astype(bf16).astype(f32)


def set_limits(scal, limit):
    row = lax.broadcasted_iota(jnp.int32, limit.shape, 0)
    value = jnp.zeros(limit.shape, jnp.int32)
    for r in range(R):
        value = jnp.where(row == r, scal[SCALARS + r], value)
    limit[...] = value


def halves(ref, pair):
    both = ref[sixteen(pair), :].astype(f32)
    return both[:R], both[R:]


def norm_kernel(x, perm, gain, u_out):
    xp = position_major(perm[...], x[...])
    inv = lax.rsqrt(jnp.mean(xp * xp, -1, keepdims=True) + epsilon)
    u_out[...] = (xp * inv * gain[...]).astype(bf16)


def front_kernel(scal, u, edge, gain, convw, wg, bias, wc, c_out, zl_out, kh_out, ends, ext, state, limit):
    step = pl.program_id(0)
    m = u.shape[0]
    tb = m // R
    halo = edge.shape[0]
    taps = convw.shape[0]

    @pl.when(step == 0)
    def _():
        set_limits(scal, limit)
        ext[0:halo, :] = normed_edge(edge[...], gain[...])
        state[0:R, :] = jnp.ones((R, state.shape[1]), f32)
        state[R:, :] = jnp.zeros((R, state.shape[1]), f32)

    ext[halo:, :] = u[...].astype(f32)
    conv = convw[0:1, :] * ext[halo:, :]
    for k in range(1, taps):
        lo = halo - k * R
        conv = conv + convw[k : k + 1, :] * ext[lo : lo + m, :]
    ext[0:halo, :] = ext[m : m + halo, :]
    cb = conv.astype(bf16)
    c_out[...] = cb
    kz = nn(cb, wg[...]) + bias[...]
    zs = 1.0 / (1.0 + jnp.exp(-kz))
    width = zs.shape[1]
    zs = zs.reshape(tb, R, width)
    pos = scal[0] + step * tb + lax.broadcasted_iota(jnp.int32, (tb, R, width), 0)
    zl_out[...] = jnp.where(pos < limit[...][None], zs, 0.0).reshape(m, width).astype(bf16)
    kh_out[...] = nn(cb, wc[...]).astype(bf16)

    def body(u, carry):
        prod, h = carry
        za, zb = halves(zl_out, u)
        ka, kb = halves(kh_out, u)
        a = 1.0 - za
        b = 1.0 - zb
        return prod * (a * b), (h * a + za * ka) * b + zb * kb

    prod, h = lax.fori_loop(0, tb // 2, body, (state[0:R, :], state[R:, :]), unroll=4)
    state[0:R, :] = prod
    state[R:, :] = h
    ends[0:R, :] = prod
    ends[R:, :] = h


def gelu_parts(p):
    k0 = 0.7978845608028654
    inner = p * (k0 + (k0 * 0.044715) * (p * p))
    th = jnp.tanh(inner)
    ht = 0.5 + 0.5 * th
    return p * ht, ht + (1.0 - th * th) * (1.5 * inner - k0 * p)


def da_kernel(g, perm, wd, gl_out, da_out):
    gl = position_major(perm[...], g[...]).astype(bf16)
    gl_out[...] = gl
    da_out[...] = nt(gl, wd[...]).astype(bf16)


def core_kernel(scal, x, perm, gl, da, zl, zl_next, kh, kh_next, zl_before, other, *refs, fchunk, hops, blocks):
    msgs = refs[:hops]
    wo, mgain, wu = refs[hops : hops + 3]
    r1_out, y_out, hp_out, n2_out, act_out, dp_out, dm_out, dr1_out, dh_out, back, mg = refs[hops + 3 : hops + 14]
    state, limit, run, acc, ys, hps, dhs = refs[hops + 14 :]
    step = pl.program_id(0)
    tb = x.shape[1]
    m = tb * R
    width, feed = wu.shape
    hidden = wo.shape[0]
    first = scal[0] + step * tb

    def scan_pair(zs, ks, start, u, h):
        t = u * 2
        za, zb = halves(zs, u)
        ka, kb = halves(ks, u)
        ha = h - za * h + za * ka
        hb = ha - zb * ha + zb * kb
        hps[sixteen(u), :] = jnp.concatenate([h, ha], 0).astype(bf16)
        ya = jnp.where(start + t < limit[...], ha, 0.0)
        yb = jnp.where(start + t + 1 < limit[...], hb, 0.0)
        ys[sixteen(u), :] = jnp.concatenate([ya, yb], 0).astype(bf16)
        return hb

    def adjoint_pair(zs, ds, u, prod, total):
        za, zb = halves(zs, u)
        da, db = halves(ds, u)
        pa = prod - za * prod
        pb = pa - zb * pa
        return pb, total + (pa * da + pb * db)

    @pl.when(step == 0)
    def _():
        set_limits(scal, limit)
        h = jnp.zeros((R, hidden), f32)
        for msg in reversed(msgs):
            both = msg[...].astype(f32)
            h = jnp.exp(both[0:R, :]) * h + both[R:, :]
        h = jnp.where(scal[1] == 1, other[0:R, :] * h + other[R:, :], h)
        run[...] = jnp.ones((R, hidden), f32)
        back[...] = jnp.zeros(back.shape, f32)
        mg[...] = jnp.zeros(mg.shape, f32)
        dhs[...] = jnp.zeros(dhs.shape, bf16)
        state[...] = lax.fori_loop(0, tb // 2, lambda u, h: scan_pair(zl, kh, scal[0], u, h), h, unroll=2)

    hp_out[...] = hps[...]
    y = ys[...]
    y_out[...] = y
    r1 = position_major(perm[...], x[...]) + nn(y, wo[...])
    r1_out[...] = r1
    inv = lax.rsqrt(jnp.mean(r1 * r1, -1, keepdims=True) + epsilon)
    n2 = (r1 * inv * mgain[...]).astype(bf16)
    n2_out[...] = n2
    chunks = feed // fchunk
    pairs = tb // 2 // chunks
    for f in range(chunks):
        cols = slice(f * fchunk, (f + 1) * fchunk)
        a, slope = gelu_parts(nn(n2, wu[:, cols]).astype(bf16))
        act_out[:, cols] = a
        dpb = da[:, cols] * slope
        dp_out[:, cols] = dpb
        part = nt(dpb, wu[:, cols])
        acc[...] = acc[...] + part if f else part
        h, prod, total = state[...], run[...], back[...]
        for u in range(f * pairs, (f + 1) * pairs):
            h = scan_pair(zl_next, kh_next, first + tb, u, h)
            prod, total = adjoint_pair(zl_before, dhs, u, prod, total)
        state[...] = h
        run[...] = jnp.where(step == 0, 1.0, prod)
        back[...] = total
    dn2 = acc[...]
    r1 = r1_out[...]
    mg[...] += jnp.sum((dn2 * r1 * inv).reshape(tb, R, width), 0)
    s = mgain[...] * dn2
    mean = jnp.mean(s * r1, -1, keepdims=True)
    dr1 = gl[...].astype(f32) + inv * (s - r1 * (inv * inv * mean))
    dr1_out[...] = dr1
    dm = dr1.astype(bf16)
    dm_out[...] = dm
    dh = nt(dm, wo[...]).reshape(tb, R, hidden)
    pos = first + lax.broadcasted_iota(jnp.int32, (tb, R, hidden), 0)
    dh = jnp.where(pos < limit[...][None], dh, 0.0).reshape(m, hidden).astype(bf16)
    dh_out[...] = dh
    dhs[...] = dh

    @pl.when(step == blocks - 1)
    def _():
        carry = lax.fori_loop(
            0, tb // 2, lambda u, carry: adjoint_pair(zl, dhs, u, *carry), (run[...], back[...]), unroll=4
        )
        back[...] = carry[1]


def put_rows(dst, sel, piece, at, rows, part):
    for i in range(SLOTS // 2):
        pos = pl.multiple_of((i ^ sel) * piece + at, 16)
        dst[pl.ds(pos, rows), :] = part[i * rows : (i + 1) * rows]


def ffn_grad_kernel(scal, act, gl, n2, dp, dst, *, pick):
    step = pl.program_id(0)
    sel = scal[2 + pick]
    width = gl.shape[1]
    rows1 = act.shape[1] * 4 // SLOTS
    rows2 = n2.shape[1] * 2 // SLOTS
    part = tn(act[...], gl[...]).astype(bf16)
    per = act.shape[1] // rows1
    for i in range(per):
        pos = ((step * per + i) ^ sel) * PIECE1
        dst[pl.ds(pl.multiple_of(pos, 16), rows1), :] = part[i * rows1 : (i + 1) * rows1]
    columns = dp.shape[1] // width
    for q in range(columns):
        part = tn(n2[...], dp[:, q * width : (q + 1) * width]).astype(bf16)
        put_rows(dst, sel, PIECE1, rows1 + (step * columns + q) * rows2, rows2, part)


def gate_grad_kernel(scal, c, dkz, dkh, y, dm, dst, *, pick):
    sel = scal[2 + pick]
    width = dm.shape[1]
    rows = c.shape[1] * 2 // SLOTS
    at = 0
    for grads in (dkz, dkh):
        for q in range(grads.shape[1] // width):
            part = tn(c[...], grads[:, q * width : (q + 1) * width]).astype(bf16)
            put_rows(dst, sel, PIECE2, at, rows, part)
            at += rows
    put_rows(dst, sel, PIECE2, at, y.shape[1] * 2 // SLOTS, tn(y[...], dm[...]).astype(bf16))


def gate_kernel(scal, dh, zl, kh, hp, other, fother, *refs, blocks, hops):
    msgs = refs[:hops]
    wg, wc = refs[hops : hops + 2]
    dkz, dkh, edge_out, bias_out = refs[hops + 3 : hops + 7]
    state = refs[hops + 7]
    step = pl.program_id(0)
    m = dh.shape[0]
    tb = m // R
    block = blocks - 1 - step

    @pl.when(step == 0)
    def _():
        mm = jnp.zeros(state.shape, f32)
        for msg in reversed(msgs):
            both = msg[...].astype(f32)
            mm = jnp.exp(both[0:R, :]) * mm + both[R:, :]
        state[...] = jnp.where(scal[1] == 0, fother[...] + other[0:R, :] * mm, mm)
        bias_out[...] = jnp.zeros(bias_out.shape, f32)

    def body(u, carry):
        mm, bias = carry
        w = tb // 2 - 1 - u
        ha, hb = halves(hp, w)
        za, zb = halves(zl, w)
        da, db = halves(dh, w)
        ka, kb = halves(kh, w)
        lam = db + mm
        sb = lam * zb
        mm = lam - sb
        kb = (sb - sb * zb) * (kb - hb)
        lam = da + mm
        sa = lam * za
        mm = lam - sa
        ka = (sa - sa * za) * (ka - ha)
        kk = jnp.concatenate([ka, kb], 0).astype(bf16)
        dkz[sixteen(w), :] = kk
        dkh[sixteen(w), :] = jnp.concatenate([sa, sb], 0).astype(bf16)
        kf = kk.astype(f32)
        return mm, bias + kf[:R, :] + kf[R:, :]

    mm, bias = lax.fori_loop(0, tb // 2, body, (state[...], bias_out[...]), unroll=2)
    state[...] = mm
    bias_out[...] = bias

    @pl.when(block == 0)
    def _():
        span = edge_out.shape[0]
        edge_out[...] = (nt(dkz[0:span, :], wg[...]) + nt(dkh[0:span, :], wc[...])).astype(bf16)


def tail_kernel(x, dr1, dkz, dkh, pm, back_pm, edge, after, gain, convw, wg, wc, grad, sums, uext, dext, *, blocks):
    step = pl.program_id(0)
    tb = x.shape[1]
    m = tb * R
    halo = edge.shape[0]
    taps = convw.shape[0]
    width = gain.shape[1]

    @pl.when(step == 0)
    def _():
        uext[0:halo, :] = normed_edge(edge[...], gain[...])
        dext[blocks * m :, :] = after[...].astype(f32)
        sums[...] = jnp.zeros(sums.shape, f32)

    @pl.when(step < blocks)
    def _():
        rows = pl.ds(pl.multiple_of(step * m, m), m)
        dext[rows, :] = nt(dkz[...], wg[...]) + nt(dkh[...], wc[...])

    @pl.when(step >= blocks)
    def _():
        xp = position_major(pm[...], x[...])
        inv = lax.rsqrt(jnp.mean(xp * xp, -1, keepdims=True) + epsilon)
        xn = xp * inv
        uext[halo:, :] = (xn * gain[...]).astype(bf16).astype(f32)
        start = (step - blocks) * m
        here = dext[pl.ds(pl.multiple_of(start, R), m), :]
        du = convw[0:1, :] * here
        for k in range(taps):
            lo = halo - k * R
            part = (here * uext[lo : lo + m, :]).reshape(tb, R, width)
            sums[(k + 1) * R : (k + 2) * R, :] += jnp.sum(part, 0)
            if k:
                du = du + convw[k : k + 1, :] * dext[pl.ds(pl.multiple_of(start + k * R, R), m), :]
        uext[0:halo, :] = uext[m : m + halo, :]
        sums[0:R, :] += jnp.sum((du * xn).reshape(tb, R, width), 0)
        s1 = gain[...] * du
        mean = jnp.mean(s1 * xn, -1, keepdims=True)
        gin = dr1[...] + inv * (s1 - xn * mean)
        grad[...] = row_major(back_pm[...], gin.astype(bf16))


def output_kernel(r1, act, perm, wd, out):
    total = r1[...] + nn(act[...], wd[...])
    out[...] = row_major(perm[...], total.astype(bf16))


def spread_kernel(scal, src, *refs, piece, plan, mate):
    low = scal[2 + mate] & 7
    for a in range(8):
        base = (a ^ low) * piece
        at = 0
        for out, rows, columns in plan:
            ref = refs[len(refs) - len(plan) + out]
            for q in range(columns):
                width = src.shape[1]
                part = src[pl.ds(pl.multiple_of(base + at, 16), rows), :].astype(f32)
                ref[a * rows : (a + 1) * rows, q * width : (q + 1) * width] = part
                at += rows


def spread(scal, src, held, mate, flip, piece, plan, shapes, name):
    def block(g, s):
        return ((s[1] ^ mate) * 2 + ((s[2 + mate] >> 3) ^ flip), 0)

    count = len(held)
    return pl.pallas_call(
        functools.partial(spread_kernel, piece=piece, plan=plan, mate=mate),
        grid_spec=pltpu.PrefetchScalarGridSpec(
            num_scalar_prefetch=1,
            grid=(1,),
            in_specs=[whole(src)] + [ORDER] * count,
            out_specs=[pl.BlockSpec((dims[0] // 4, dims[1]), block) for dims in shapes],
        ),
        out_shape=[pltpu.HBM(dims, f32) for dims in shapes],
        input_output_aliases={2 + k: k for k in range(count)},
        compiler_params=params(16),
        cost_estimate=LITTLE,
        name=name,
    )(scal, src, *held)


def params(mib):
    return pltpu.CompilerParams(
        dimension_semantics=("arbitrary",), vmem_limit_bytes=mib * 1024 * 1024
    )


def shape(dims, kind=f32):
    return jax.ShapeDtypeStruct(dims, kind)


LITTLE = pl.CostEstimate(flops=1024, bytes_accessed=1024, transcendentals=0)
MUCH = pl.CostEstimate(flops=3 * 10**10, bytes_accessed=1024, transcendentals=0)
ORDER = pl.BlockSpec(memory_space=pl.ANY)


def far(array):
    return pltpu.with_memory_space_constraint(array, pltpu.HBM)


def whole(array):
    zeros = (0,) * array.ndim
    return pl.BlockSpec(array.shape, lambda *a: zeros, pipeline_mode=pl.Buffered(1))


def passed_along(value, axis, steps):
    count = lax.axis_size(axis)
    leading, last = (max(0, -steps), min(count, count - steps))
    return lax.ppermute(value, axis, [(source, source + steps) for source in range(leading, last)])


def flat_permute(value, pairs):
    return lax.ppermute(value, ("seq", "row"), pairs)


def stage_bits():
    row_bits = lax.axis_size("row").bit_length() - 1
    seq_bits = lax.axis_size("seq").bit_length() - 1
    plane = list(range(row_bits))
    line = [row_bits + 1 + z for z in range(seq_bits - 1)]
    cut = row_bits // 2
    return (plane + line, plane[cut:] + plane[:cut] + line[::-1])


def slot_of(flat, bits):
    slot = 0
    for k in range(4):
        slot = slot * 2 + ((flat >> bits[k]) & 1)
    return slot


def halving_pairs(stage):
    row_bits = lax.axis_size("row").bit_length() - 1
    orders = stage_bits()
    devices = lax.axis_size("row") * lax.axis_size("seq")
    return [(d, d ^ (1 << orders[(d >> row_bits) & 1][stage])) for d in range(devices)]


def core_pairs():
    row_bits = lax.axis_size("row").bit_length() - 1
    devices = lax.axis_size("row") * lax.axis_size("seq")
    return [(d, d ^ (1 << row_bits)) for d in range(devices)]


def added(a, b):
    return (a.astype(f32) + b.astype(f32)).astype(bf16)


class Sequence:
    def __init__(self, token):
        self.token = token

    def after(self, *arrays):
        *arrays, _ = lax.optimization_barrier((*arrays, self.token))
        return arrays[0] if len(arrays) == 1 else arrays

    def did(self, array):
        self.token = array
        return array


def split(value):
    high = lax.reduce_precision(value, 8, 7)
    return [high.astype(bf16), (value - high).astype(bf16)]


def join_kernel(mine, recv, ride, out, ride_out):
    rows = mine.shape[0] - 2 * R
    out[0:rows, :] = mine[0:rows, :]
    out[rows : 2 * rows, :] = recv[0:rows, :]
    parts = recv[rows:, :].astype(f32)
    total = ride[...] + (parts[:R] + parts[R:])
    ride_out[...] = total
    high = total.astype(bf16).astype(f32)
    out[2 * rows :, :] = jnp.concatenate([high, total - high], 0).astype(bf16)


def joined(mine, recv, ride):
    rows, width = mine.shape
    return pl.pallas_call(
        join_kernel,
        in_specs=[pl.BlockSpec(memory_space=pltpu.VMEM)] * 3,
        out_specs=[pl.BlockSpec(memory_space=pltpu.VMEM)] * 2,
        out_shape=[shape((2 * rows - 2 * R, width), bf16), shape(ride.shape)],
        compiler_params=pltpu.CompilerParams(vmem_limit_bytes=16 * 1024 * 1024),
        cost_estimate=LITTLE,
        name="join",
    )(mine, recv, ride)


class Halving:
    def __init__(self, seq, send):
        self.seq = seq
        self.recv = flat_permute(send, core_pairs())
        self.stage = 0
        self.ride = None

    def riders(self):
        return [] if self.ride is None else split(self.ride)

    def board(self, recv, rows):
        if self.ride is not None:
            low = rows + self.ride.shape[0]
            self.ride = self.ride + (recv[rows:low].astype(f32) + recv[low:].astype(f32))

    def step(self, *beside):
        k = self.stage
        self.stage += 1
        stages = len(stage_bits()[0])
        recv, *beside = self.seq.after(self.recv, *beside) if beside else (self.seq.after(self.recv),)
        if k < 4:
            half = self.keep.shape[0] // 2
            send = self.seq.did(added(self.keep[half:], recv[half:]))
            self.recv = flat_permute(send, halving_pairs(k))
            self.keep = added(self.keep[:half], recv[:half])
        elif k == 4:
            total = added(self.keep, recv)
            for extra in range(4, stages):
                total = added(total, flat_permute(total, halving_pairs(extra)))
                if self.ride is not None:
                    self.ride = self.ride + flat_permute(self.ride, halving_pairs(extra))
            self.rows = total.shape[0]
            self.total = self.seq.did(jnp.concatenate([total] + self.riders(), 0))
            self.recv = flat_permute(self.total, halving_pairs(3))
        elif k < 8:
            rows = self.rows
            self.rows = 2 * rows
            if self.ride is None:
                self.total = self.seq.did(jnp.concatenate([self.total, recv], 0))
            else:
                self.total, self.ride = joined(self.total, recv, self.ride)
                self.seq.did(self.total)
            self.recv = flat_permute(self.total, halving_pairs(7 - k))
            if k == 7:
                self.theirs = flat_permute(self.total, core_pairs())
        else:
            self.board(recv, self.rows)
            self.rest = recv
            self.their_rest = flat_permute(recv, core_pairs())
        return beside


def chip_shift(value, steps):
    return passed_along(value, "seq", 2 * steps)


def per_device(
    inputs,
    lengths,
    norm_gain,
    conv_weight,
    gate_weight,
    gate_bias,
    cand_weight,
    out_weight,
    mlp_gain,
    up_weight,
    down_weight,
    cotangent,
):
    rows, span, width = inputs.shape
    hidden = gate_weight.shape[1]
    feed = up_weight.shape[1]
    taps = conv_weight.shape[0]
    margin = taps - 1
    tokens = rows * span
    tb = 32
    blocks = span // tb
    m = tb * R
    seq = lax.axis_index("seq")
    core = seq & 1
    chips = lax.axis_size("seq") // 2
    hops = chips - 1
    flat = seq * lax.axis_size("row") + lax.axis_index("row")
    slots = [slot_of(flat, bits) for bits in stage_bits()]
    here = jnp.where(core == 0, slots[0], slots[1])
    mate = jnp.where(core == 0, slots[1], slots[0])
    scal = jnp.concatenate([jnp.stack([seq * span, core, here, mate]).astype(jnp.int32), lengths])
    gain1 = norm_gain.reshape(1, width)
    gain2 = mlp_gain.reshape(1, width)
    bias = gate_bias.reshape(1, hidden)
    to_pm, to_rm = token_order()

    edge = inputs[:, span - margin :, :].swapaxes(0, 1).reshape(margin * rows, width)
    edge = passed_along(edge, "seq", 1)

    last = blocks - 1
    clamp = lambda i: jnp.minimum(i, last)
    late = lambda i: jnp.maximum(i - blocks, 0)
    later = lambda i: jnp.minimum(i + 1, last)
    before = lambda i: jnp.maximum(i - 1, 0)

    def rm(index):
        return pl.BlockSpec((rows, tb, width), lambda i, *s: (0, index(i), 0))

    def tok(w, index=clamp):
        return pl.BlockSpec((m, w), lambda i, *s: (index(i), 0))

    def rtok(w):
        return tok(w, lambda i: last - clamp(i))

    def fixed(dims):
        zeros = (0,) * len(dims)
        return pl.BlockSpec(dims, lambda i, *s: zeros)

    def call(kernel, name, grid, ins, outs, scratch, operands, scalars=True, much=False):
        spec = pltpu.PrefetchScalarGridSpec(
            num_scalar_prefetch=int(scalars),
            grid=(grid,),
            in_specs=ins,
            out_specs=[o[1] for o in outs],
            scratch_shapes=scratch,
        )
        return pl.pallas_call(
            kernel,
            grid_spec=spec,
            out_shape=[o[0] for o in outs],
            compiler_params=params(16),
            cost_estimate=MUCH if much else LITTLE,
            name=name,
        )(*operands)

    def rows_of(w, kind, spec=tok, kept=shape):
        return kept((tokens, w), kind), spec(w)

    (normed,) = call(
        norm_kernel, "norm", blocks,
        [rm(clamp), whole(to_pm), whole(gain1)],
        [rows_of(width, bf16)],
        [],
        (far(inputs), far(to_pm), far(gain1)),
        scalars=False,
    )
    edge, normed = lax.optimization_barrier((edge, normed))
    c, zl, kh, ends = call(
        front_kernel, "front", blocks,
        [
            tok(width), whole(edge), whole(gain1), whole(conv_weight),
            whole(gate_weight), whole(bias), whole(cand_weight),
        ],
        [
            rows_of(width, bf16), rows_of(hidden, bf16), rows_of(hidden, bf16),
            (shape((2 * R, hidden)), fixed((2 * R, hidden))),
        ],
        [
            pltpu.VMEM((margin * R + m, width), f32),
            pltpu.VMEM((2 * R, hidden), f32),
            pltpu.VMEM((R, hidden), jnp.int32),
        ],
        (
            scal, normed, edge, far(gain1), far(conv_weight), gate_weight, far(bias),
            cand_weight,
        ),
    )

    other = flat_permute(ends, core_pairs())
    first = jnp.where(core == 0, ends, other)
    second = jnp.where(core == 0, other, ends)
    decay = jnp.log(jnp.maximum(ends[:R] * other[:R], 1e-37))
    message = jnp.concatenate([decay, second[:R] * first[R:] + second[R:]], 0).astype(bf16)
    forward = [chip_shift(message, k) for k in range(1, chips)]

    gl, da = call(
        da_kernel, "da", blocks,
        [rm(clamp), whole(to_pm), whole(down_weight)],
        [rows_of(width, bf16), rows_of(feed, bf16)],
        [],
        (cotangent, to_pm, down_weight),
        scalars=False,
    )

    r1, y, hp, n2, act, dp, dm, dr1, dh, back, mg = call(
        functools.partial(core_kernel, fchunk=256, hops=hops, blocks=blocks), "core", blocks,
        [
            rm(clamp), whole(to_pm), tok(width), tok(feed), tok(hidden), tok(hidden, later), tok(hidden),
            tok(hidden, later), tok(hidden, before), whole(other),
            *[whole(f) for f in forward], whole(out_weight), whole(gain2), whole(up_weight),
        ],
        [
            rows_of(width, f32, kept=pltpu.HBM), rows_of(hidden, bf16), rows_of(hidden, bf16),
            rows_of(width, bf16), rows_of(feed, bf16), rows_of(feed, bf16), rows_of(width, bf16),
            rows_of(width, f32, kept=pltpu.HBM),
            rows_of(hidden, bf16),
            (shape((R, hidden)), fixed((R, hidden))), (shape((R, width)), fixed((R, width))),
        ],
        [
            pltpu.VMEM((R, hidden), f32),
            pltpu.VMEM((R, hidden), jnp.int32),
            pltpu.VMEM((R, hidden), f32),
            pltpu.VMEM((m, width), f32),
            pltpu.VMEM((m, hidden), bf16),
            pltpu.VMEM((m, hidden), bf16),
            pltpu.VMEM((m, hidden), bf16),
        ],
        (
            scal, inputs, to_pm, gl, da, zl, zl, kh, kh, zl, other, *forward, far(out_weight), gain2, up_weight,
        ),
    )

    order = Sequence(back)
    quarter = feed // 4

    def ffn_grads(pick, *beside):
        half = lambda s: s[1] if pick == 0 else 1 - s[1]
        a, d, *beside = order.after(act, dp, *beside)
        (piece,) = call(
            functools.partial(ffn_grad_kernel, pick=pick), "ffn_grad", 2,
            [
                pl.BlockSpec((tokens, quarter), lambda i, s: (0, half(s) * 2 + i)), whole(gl),
                pl.BlockSpec((tokens, width // 2), lambda i, s: (0, half(s))),
                pl.BlockSpec((tokens, feed // 2), lambda i, s: (0, i)),
            ],
            [(shape((SLOTS // 2 * PIECE1, width), bf16), fixed((SLOTS // 2 * PIECE1, width)))],
            [],
            (scal, a, gl, n2, d),
            much=pick == 0,
        )
        return order.did(piece), beside

    def gate_grads(pick):
        half = lambda s: s[1] if pick == 0 else 1 - s[1]
        z, h = order.after(dkz, dkh)
        (piece,) = call(
            functools.partial(gate_grad_kernel, pick=pick), "gate_grad", 1,
            [
                pl.BlockSpec((tokens, width // 2), lambda i, s: (0, half(s))),
                whole(z), whole(h),
                pl.BlockSpec((tokens, hidden // 2), lambda i, s: (0, half(s))), whole(dm),
            ],
            [(shape((SLOTS // 2 * PIECE2, width), bf16), fixed((SLOTS // 2 * PIECE2, width)))],
            [],
            (scal, c, z, h, y, dm),
            much=pick == 0,
        )
        return order.did(piece)

    fother = flat_permute(back, core_pairs())
    lower = jnp.where(core == 0, back, fother)
    upper = jnp.where(core == 0, fother, back)
    message = jnp.concatenate([decay, lower + first[:R] * upper], 0).astype(bf16)
    backward = [chip_shift(order.did(message), -k) for k in range(1, chips)]
    send1, _ = ffn_grads(1)
    chunk1 = Halving(order, send1)
    chunk1.keep, backward = ffn_grads(0, *backward)
    chunk1.step()

    dkz, dkh, edge_dc, bias_part = call(
        functools.partial(gate_kernel, blocks=blocks, hops=hops), "gates", blocks,
        [
            rtok(hidden), rtok(hidden), rtok(hidden), rtok(hidden),
            whole(other), whole(fother), *[whole(f) for f in backward],
            whole(gate_weight), whole(cand_weight), ORDER,
        ],
        [
            rows_of(hidden, bf16, rtok), rows_of(hidden, bf16, rtok),
            (shape((4 * R, width), bf16), fixed((4 * R, width))),
            (shape((R, hidden)), fixed((R, hidden))),
        ],
        [pltpu.VMEM((R, hidden), f32)],
        (
            scal, dh, zl, kh, hp, other, fother, *backward, gate_weight, cand_weight, order.token,
        ),
    )
    order.did(bias_part)
    after = passed_along(edge_dc[: margin * R], "seq", -1)
    send2 = gate_grads(1)
    chunk2 = Halving(order, send2)
    (output,) = call(
        output_kernel, "output", blocks,
        [tok(width), tok(feed), whole(to_rm), whole(down_weight)],
        [(shape((rows, span, width), bf16), rm(clamp))],
        [],
        (far(r1), order.after(act), to_rm, down_weight),
        scalars=False,
    )
    order.did(output)
    chunk1.step()
    chunk2.keep = gate_grads(0)
    chunk2.step()
    input_grad, sums = call(
        functools.partial(tail_kernel, blocks=blocks), "tail", 2 * blocks,
        [
            rm(late), tok(width, late), tok(hidden), tok(hidden), whole(to_pm), whole(to_rm),
            whole(edge), whole(after), whole(gain1), whole(conv_weight), whole(gate_weight),
            whole(cand_weight),
        ],
        [
            (shape((rows, span, width), bf16), rm(late)),
            (shape(((taps + 1) * R, width)), fixed(((taps + 1) * R, width))),
        ],
        [
            pltpu.VMEM((margin * R + m, width), f32),
            pltpu.VMEM((margin * R + tokens, width), f32),
        ],
        (
            far(inputs), far(dr1), order.after(dkz), dkh, far(to_pm), far(to_rm), edge, after,
            far(gain1), far(conv_weight), far(gate_weight), far(cand_weight),
        ),
        scalars=False,
    )
    order.did(sums)
    small = jnp.concatenate(
        [
            sums.reshape(taps + 1, R, width).sum(1),
            mg.sum(0, keepdims=True),
            bias_part.sum(0).reshape(hidden // width, width),
        ],
        0,
    )
    coming = flat_permute(small, core_pairs())

    plan1 = ((0, feed // SLOTS, 1), (1, width // SLOTS, feed // width))
    shapes1 = ((feed, width), (width, feed))
    plan2 = (
        (0, width // SLOTS, hidden // width),
        (1, width // SLOTS, hidden // width),
        (2, hidden // SLOTS, 1),
    )
    shapes2 = ((width, hidden), (width, hidden), (hidden, width))
    held1, held2 = (), ()

    def spread1(src, mate, flip):
        nonlocal held1
        src = order.after(src)
        held1 = spread(scal, src, held1, mate, flip, PIECE1, plan1, shapes1, "spread_ffn")
        order.did(held1[0])

    def spread2(src, mate, flip):
        nonlocal held2
        src = order.after(src)
        held2 = spread(scal, src, held2, mate, flip, PIECE2, plan2, shapes2, "spread_gates")
        order.did(held2[0])

    for chunk in (chunk1, chunk2, chunk1, chunk1, chunk2, chunk1, chunk2, chunk1):
        chunk.step()
    chunk2.ride = small + order.after(coming)
    chunk2.step()
    chunk2.step()
    chunk1.step()
    spread1(chunk1.total, 0, 0)
    chunk2.step()
    spread1(chunk1.theirs, 1, 0)
    chunk2.step()
    chunk1.step()
    spread1(chunk1.rest, 0, 1)
    spread2(chunk2.total, 0, 0)
    spread1(chunk1.their_rest, 1, 1)
    spread2(chunk2.theirs, 1, 0)
    chunk2.step()
    small = chunk2.ride
    small_out = order.after(
        small[0], small[1 : taps + 1], small[taps + 2 :].reshape(hidden), small[taps + 1]
    )
    spread2(chunk2.rest, 0, 1)
    spread2(chunk2.their_rest, 1, 1)
    return (
        output,
        input_grad,
        small_out[0],
        small_out[1],
        held2[0],
        small_out[2],
        held2[1],
        held2[2],
        small_out[3],
        held1[1],
        held1[0],
    )


def solution(mesh):
    sharded = P("row", "seq", None)
    in_specs = (sharded, P("row")) + (P(),) * 9 + (sharded,)
    out_specs = (sharded, sharded) + (P(),) * 9
    return jax.shard_map(
        per_device, mesh=mesh, in_specs=in_specs, out_specs=out_specs, check_vma=False
    )
```

```python
import functools

import jax
import jax.numpy as jnp
import numpy as np
from jax import lax
from jax.experimental import pallas as pl
from jax.experimental.pallas import tpu as pltpu
from jax.sharding import PartitionSpec as P

epsilon = 1e-06
f32 = jnp.float32
bf16 = jnp.bfloat16
R = 8
PERM = 256
SCALARS = 4
SLOTS = 32
PIECES = (64, 96, 64)


def nn(a, b):
    return lax.dot_general(a, b, (((1,), (0,)), ((), ())), preferred_element_type=f32)


def nt(a, b):
    return lax.dot_general(a, b, (((1,), (1,)), ((), ())), preferred_element_type=f32)


def tn(a, b):
    return lax.dot_general(a, b, (((0,), (0,)), ((), ())), preferred_element_type=f32)


def token_order():
    out = np.arange(PERM)
    source = (out % R) * (PERM // R) + out // R
    to_pm = np.zeros((PERM, PERM), np.float32)
    to_pm[out, source] = 1
    return jnp.asarray(to_pm, bf16), jnp.asarray(to_pm.T, bf16)


def position_major(perm, block):
    span = PERM // R
    parts = []
    for s in range(block.shape[1] // span):
        part = block[:, s * span : (s + 1) * span, :].reshape(PERM, block.shape[2])
        parts.append(nn(perm, part))
    return parts[0] if len(parts) == 1 else jnp.concatenate(parts, 0)


def row_major(perm, tokens):
    span = PERM // R
    parts = []
    for s in range(tokens.shape[0] // PERM):
        part = nn(perm, tokens[s * PERM : (s + 1) * PERM]).astype(bf16)
        parts.append(part.reshape(R, span, tokens.shape[1]))
    return parts[0] if len(parts) == 1 else jnp.concatenate(parts, 1)


def eight(t):
    return pl.ds(pl.multiple_of(t * R, R), R)


def sixteen(t):
    return pl.ds(pl.multiple_of(t * 2 * R, 2 * R), 2 * R)


def normed_edge(edge, gain):
    e = edge.astype(f32)
    inv = lax.rsqrt(jnp.mean(e * e, -1, keepdims=True) + epsilon)
    return (e * inv * gain).astype(bf16).astype(f32)


def set_limits(scal, limit):
    row = lax.broadcasted_iota(jnp.int32, limit.shape, 0)
    value = jnp.zeros(limit.shape, jnp.int32)
    for r in range(R):
        value = jnp.where(row == r, scal[SCALARS + r], value)
    limit[...] = value


def halves(ref, pair):
    both = ref[sixteen(pair), :].astype(f32)
    return both[:R], both[R:]


def norm_kernel(x, perm, gain, u_out):
    xp = position_major(perm[...], x[...])
    inv = lax.rsqrt(jnp.mean(xp * xp, -1, keepdims=True) + epsilon)
    u_out[...] = (xp * inv * gain[...]).astype(bf16)


def front_kernel(scal, u, edge, gain, convw, wg, bias, wc, c_out, zl_out, kh_out, ends, ext, state, limit):
    step = pl.program_id(0)
    m = u.shape[0]
    tb = m // R
    halo = edge.shape[0]
    taps = convw.shape[0]

    @pl.when(step == 0)
    def _():
        set_limits(scal, limit)
        ext[0:halo, :] = normed_edge(edge[...], gain[...])
        state[0:R, :] = jnp.ones((R, state.shape[1]), f32)
        state[R:, :] = jnp.zeros((R, state.shape[1]), f32)

    ext[halo:, :] = u[...].astype(f32)
    conv = convw[0:1, :] * ext[halo:, :]
    for k in range(1, taps):
        lo = halo - k * R
        conv = conv + convw[k : k + 1, :] * ext[lo : lo + m, :]
    ext[0:halo, :] = ext[m : m + halo, :]
    cb = conv.astype(bf16)
    c_out[...] = cb
    kz = nn(cb, wg[...]) + bias[...]
    zs = 1.0 / (1.0 + jnp.exp(-kz))
    width = zs.shape[1]
    zs = zs.reshape(tb, R, width)
    pos = scal[0] + step * tb + lax.broadcasted_iota(jnp.int32, (tb, R, width), 0)
    zl_out[...] = jnp.where(pos < limit[...][None], zs, 0.0).reshape(m, width).astype(bf16)
    kh_out[...] = nn(cb, wc[...]).astype(bf16)

    def body(u, carry):
        prod, h = carry
        za, zb = halves(zl_out, u)
        ka, kb = halves(kh_out, u)
        a = 1.0 - za
        b = 1.0 - zb
        return prod * (a * b), (h * a + za * ka) * b + zb * kb

    prod, h = lax.fori_loop(0, tb // 2, body, (state[0:R, :], state[R:, :]), unroll=4)
    state[0:R, :] = prod
    state[R:, :] = h
    ends[0:R, :] = prod
    ends[R:, :] = h


def gelu_parts(p):
    k0 = 0.7978845608028654
    inner = p * (k0 + (k0 * 0.044715) * (p * p))
    th = jnp.tanh(inner)
    ht = 0.5 + 0.5 * th
    return p * ht, ht + (1.0 - th * th) * (1.5 * inner - k0 * p)


def da_kernel(g, perm, wd, gl_out, da_out):
    gl = position_major(perm[...], g[...]).astype(bf16)
    gl_out[...] = gl
    da_out[...] = nt(gl, wd[...]).astype(bf16)


def core_kernel(scal, x, perm, gl, da, zl, zl_next, kh, kh_next, zl_before, other, *refs, fchunk, hops, blocks):
    msgs = refs[:hops]
    wo, mgain, wu = refs[hops : hops + 3]
    r1_out, y_out, hp_out, n2_out, act_out, dp_out, dm_out, dr1_out, dh_out, back, mg = refs[hops + 3 : hops + 14]
    state, limit, run, acc, ys, hps, dhs = refs[hops + 14 :]
    step = pl.program_id(0)
    tb = x.shape[1]
    m = tb * R
    width, feed = wu.shape
    hidden = wo.shape[0]
    first = scal[0] + step * tb

    def scan_pair(zs, ks, start, u, h):
        t = u * 2
        za, zb = halves(zs, u)
        ka, kb = halves(ks, u)
        ha = h - za * h + za * ka
        hb = ha - zb * ha + zb * kb
        hps[sixteen(u), :] = jnp.concatenate([h, ha], 0).astype(bf16)
        ya = jnp.where(start + t < limit[...], ha, 0.0)
        yb = jnp.where(start + t + 1 < limit[...], hb, 0.0)
        ys[sixteen(u), :] = jnp.concatenate([ya, yb], 0).astype(bf16)
        return hb

    def adjoint_pair(zs, ds, u, prod, total):
        za, zb = halves(zs, u)
        da, db = halves(ds, u)
        pa = prod - za * prod
        pb = pa - zb * pa
        return pb, total + (pa * da + pb * db)

    @pl.when(step == 0)
    def _():
        set_limits(scal, limit)
        h = jnp.zeros((R, hidden), f32)
        for msg in reversed(msgs):
            both = msg[...].astype(f32)
            h = jnp.exp(both[0:R, :]) * h + both[R:, :]
        h = jnp.where(scal[1] == 1, other[0:R, :] * h + other[R:, :], h)
        run[...] = jnp.ones((R, hidden), f32)
        back[...] = jnp.zeros(back.shape, f32)
        mg[...] = jnp.zeros(mg.shape, f32)
        dhs[...] = jnp.zeros(dhs.shape, bf16)
        state[...] = lax.fori_loop(0, tb // 2, lambda u, h: scan_pair(zl, kh, scal[0], u, h), h, unroll=2)

    hp_out[...] = hps[...]
    y = ys[...]
    y_out[...] = y
    r1 = position_major(perm[...], x[...]) + nn(y, wo[...])
    r1_out[...] = r1
    inv = lax.rsqrt(jnp.mean(r1 * r1, -1, keepdims=True) + epsilon)
    n2 = (r1 * inv * mgain[...]).astype(bf16)
    n2_out[...] = n2
    chunks = feed // fchunk
    pairs = tb // 2 // chunks
    for f in range(chunks):
        cols = slice(f * fchunk, (f + 1) * fchunk)
        a, slope = gelu_parts(nn(n2, wu[:, cols]).astype(bf16))
        act_out[:, cols] = a
        dpb = da[:, cols] * slope
        dp_out[:, cols] = dpb
        part = nt(dpb, wu[:, cols])
        acc[...] = acc[...] + part if f else part
        h, prod, total = state[...], run[...], back[...]
        for u in range(f * pairs, (f + 1) * pairs):
            h = scan_pair(zl_next, kh_next, first + tb, u, h)
            prod, total = adjoint_pair(zl_before, dhs, u, prod, total)
        state[...] = h
        run[...] = jnp.where(step == 0, 1.0, prod)
        back[...] = total
    dn2 = acc[...]
    r1 = r1_out[...]
    mg[...] += jnp.sum((dn2 * r1 * inv).reshape(tb, R, width), 0)
    s = mgain[...] * dn2
    mean = jnp.mean(s * r1, -1, keepdims=True)
    dr1 = gl[...].astype(f32) + inv * (s - r1 * (inv * inv * mean))
    dr1_out[...] = dr1
    dm = dr1.astype(bf16)
    dm_out[...] = dm
    dh = nt(dm, wo[...]).reshape(tb, R, hidden)
    pos = first + lax.broadcasted_iota(jnp.int32, (tb, R, hidden), 0)
    dh = jnp.where(pos < limit[...][None], dh, 0.0).reshape(m, hidden).astype(bf16)
    dh_out[...] = dh
    dhs[...] = dh

    @pl.when(step == blocks - 1)
    def _():
        carry = lax.fori_loop(
            0, tb // 2, lambda u, carry: adjoint_pair(zl, dhs, u, *carry), (run[...], back[...]), unroll=4
        )
        back[...] = carry[1]


def put_rows(dst, sel, piece, at, rows, part):
    for i in range(SLOTS // 2):
        pos = pl.multiple_of((i ^ sel) * piece + at, 16)
        dst[pl.ds(pos, rows), :] = part[i * rows : (i + 1) * rows]


def some_rows(dst, sel, piece, at, step, rows, part):
    per = part.shape[0] // rows
    for i in range(per):
        pos = ((step * per + i) ^ sel) * piece + at
        dst[pl.ds(pl.multiple_of(pos, 16), rows), :] = part[i * rows : (i + 1) * rows]


def down_grad_kernel(scal, act, gl, dst, *, pick):
    part = tn(act[...], gl[...]).astype(bf16)
    some_rows(dst, scal[2 + pick], PIECES[0], 0, pl.program_id(0), act.shape[1] * 4 // SLOTS, part)


def up_out_grad_kernel(scal, n2, dp, y, dm, dst, *, pick):
    step = pl.program_id(0)
    sel = scal[2 + pick]
    width = dm.shape[1]
    rows = n2.shape[1] * 2 // SLOTS
    columns = dp.shape[1] // width
    for q in range(columns):
        part = tn(n2[...], dp[:, q * width : (q + 1) * width]).astype(bf16)
        put_rows(dst, sel, PIECES[1], (step * columns + q) * rows, rows, part)
    part = tn(y[...], dm[...]).astype(bf16)
    some_rows(dst, sel, PIECES[1], 2 * columns * rows, step, y.shape[1] * 4 // SLOTS, part)


def gate_grad_kernel(scal, c, dkz, dkh, dst, *, pick):
    sel = scal[2 + pick]
    width = c.shape[1] * 2
    rows = width // SLOTS
    at = 0
    for grads in (dkz, dkh):
        for q in range(grads.shape[1] // width):
            part = tn(c[...], grads[:, q * width : (q + 1) * width]).astype(bf16)
            put_rows(dst, sel, PIECES[2], at, rows, part)
            at += rows


def gate_kernel(scal, dh, zl, kh, hp, other, fother, *refs, blocks, hops):
    msgs = refs[:hops]
    wg, wc = refs[hops : hops + 2]
    dkz, dkh, edge_out, bias_out = refs[hops + 3 : hops + 7]
    state = refs[hops + 7]
    step = pl.program_id(0)
    m = dh.shape[0]
    tb = m // R
    block = blocks - 1 - step

    @pl.when(step == 0)
    def _():
        mm = jnp.zeros(state.shape, f32)
        for msg in reversed(msgs):
            both = msg[...].astype(f32)
            mm = jnp.exp(both[0:R, :]) * mm + both[R:, :]
        state[...] = jnp.where(scal[1] == 0, fother[...] + other[0:R, :] * mm, mm)
        bias_out[...] = jnp.zeros(bias_out.shape, f32)

    def body(u, carry):
        mm, bias = carry
        w = tb // 2 - 1 - u
        ha, hb = halves(hp, w)
        za, zb = halves(zl, w)
        da, db = halves(dh, w)
        ka, kb = halves(kh, w)
        lam = db + mm
        sb = lam * zb
        mm = lam - sb
        kb = (sb - sb * zb) * (kb - hb)
        lam = da + mm
        sa = lam * za
        mm = lam - sa
        ka = (sa - sa * za) * (ka - ha)
        kk = jnp.concatenate([ka, kb], 0).astype(bf16)
        dkz[sixteen(w), :] = kk
        dkh[sixteen(w), :] = jnp.concatenate([sa, sb], 0).astype(bf16)
        kf = kk.astype(f32)
        return mm, bias + kf[:R, :] + kf[R:, :]

    mm, bias = lax.fori_loop(0, tb // 2, body, (state[...], bias_out[...]), unroll=2)
    state[...] = mm
    bias_out[...] = bias

    @pl.when(block == 0)
    def _():
        span = edge_out.shape[0]
        edge_out[...] = (nt(dkz[0:span, :], wg[...]) + nt(dkh[0:span, :], wc[...])).astype(bf16)


def tail_kernel(x, dr1, dkz, dkh, pm, back_pm, edge, after, gain, convw, wg, wc, grad, sums, uext, dext, *, blocks):
    step = pl.program_id(0)
    tb = x.shape[1]
    m = tb * R
    halo = edge.shape[0]
    taps = convw.shape[0]
    width = gain.shape[1]

    @pl.when(step == 0)
    def _():
        uext[0:halo, :] = normed_edge(edge[...], gain[...])
        dext[blocks * m :, :] = after[...].astype(f32)
        sums[...] = jnp.zeros(sums.shape, f32)

    @pl.when(step < blocks)
    def _():
        rows = pl.ds(pl.multiple_of(step * m, m), m)
        dext[rows, :] = nt(dkz[...], wg[...]) + nt(dkh[...], wc[...])

    @pl.when(step >= blocks)
    def _():
        xp = position_major(pm[...], x[...])
        inv = lax.rsqrt(jnp.mean(xp * xp, -1, keepdims=True) + epsilon)
        xn = xp * inv
        uext[halo:, :] = (xn * gain[...]).astype(bf16).astype(f32)
        start = (step - blocks) * m
        here = dext[pl.ds(pl.multiple_of(start, R), m), :]
        du = convw[0:1, :] * here
        for k in range(taps):
            lo = halo - k * R
            part = (here * uext[lo : lo + m, :]).reshape(tb, R, width)
            sums[(k + 1) * R : (k + 2) * R, :] += jnp.sum(part, 0)
            if k:
                du = du + convw[k : k + 1, :] * dext[pl.ds(pl.multiple_of(start + k * R, R), m), :]
        uext[0:halo, :] = uext[m : m + halo, :]
        sums[0:R, :] += jnp.sum((du * xn).reshape(tb, R, width), 0)
        s1 = gain[...] * du
        mean = jnp.mean(s1 * xn, -1, keepdims=True)
        gin = dr1[...] + inv * (s1 - xn * mean)
        grad[...] = row_major(back_pm[...], gin.astype(bf16))


def output_kernel(r1, act, perm, wd, out):
    total = r1[...] + nn(act[...], wd[...])
    out[...] = row_major(perm[...], total.astype(bf16))


def spread_kernel(scal, src, *refs, piece, plan, mate):
    low = scal[2 + mate] & 7
    for a in range(8):
        base = (a ^ low) * piece
        at = 0
        for out, rows, columns in plan:
            ref = refs[len(refs) - len(plan) + out]
            for q in range(columns):
                width = src.shape[1]
                part = src[pl.ds(pl.multiple_of(base + at, 16), rows), :].astype(f32)
                ref[a * rows : (a + 1) * rows, q * width : (q + 1) * width] = part
                at += rows


def spread(scal, src, held, mate, flip, piece, plan, shapes, name):
    def block(g, s):
        return ((s[1] ^ mate) * 2 + ((s[2 + mate] >> 3) ^ flip), 0)

    count = len(held)
    return pl.pallas_call(
        functools.partial(spread_kernel, piece=piece, plan=plan, mate=mate),
        grid_spec=pltpu.PrefetchScalarGridSpec(
            num_scalar_prefetch=1,
            grid=(1,),
            in_specs=[whole(src)] + [ORDER] * count,
            out_specs=[pl.BlockSpec((dims[0] // 4, dims[1]), block) for dims in shapes],
        ),
        out_shape=[pltpu.HBM(dims, f32) for dims in shapes],
        input_output_aliases={2 + k: k for k in range(count)},
        compiler_params=params(16),
        cost_estimate=LITTLE,
        name=name,
    )(scal, src, *held)


def params(mib):
    return pltpu.CompilerParams(
        dimension_semantics=("arbitrary",), vmem_limit_bytes=mib * 1024 * 1024
    )


def shape(dims, kind=f32):
    return jax.ShapeDtypeStruct(dims, kind)


LITTLE = pl.CostEstimate(flops=1024, bytes_accessed=1024, transcendentals=0)
MUCH = pl.CostEstimate(flops=3 * 10**10, bytes_accessed=1024, transcendentals=0)
ORDER = pl.BlockSpec(memory_space=pl.ANY)


def far(array):
    return pltpu.with_memory_space_constraint(array, pltpu.HBM)


def whole(array):
    zeros = (0,) * array.ndim
    return pl.BlockSpec(array.shape, lambda *a: zeros, pipeline_mode=pl.Buffered(1))


def passed_along(value, axis, steps):
    count = lax.axis_size(axis)
    leading, last = (max(0, -steps), min(count, count - steps))
    return lax.ppermute(value, axis, [(source, source + steps) for source in range(leading, last)])


def flat_permute(value, pairs):
    return lax.ppermute(value, ("seq", "row"), pairs)


def stage_bits():
    row_bits = lax.axis_size("row").bit_length() - 1
    seq_bits = lax.axis_size("seq").bit_length() - 1
    plane = list(range(row_bits))
    line = [row_bits + 1 + z for z in range(seq_bits - 1)]
    cut = row_bits // 2
    return (plane + line, plane[cut:] + plane[:cut] + line[::-1])


def slot_of(flat, bits):
    slot = 0
    for k in range(4):
        slot = slot * 2 + ((flat >> bits[k]) & 1)
    return slot


def halving_pairs(stage):
    row_bits = lax.axis_size("row").bit_length() - 1
    orders = stage_bits()
    devices = lax.axis_size("row") * lax.axis_size("seq")
    return [(d, d ^ (1 << orders[(d >> row_bits) & 1][stage])) for d in range(devices)]


def quarter_pairs(piece):
    row_bits = lax.axis_size("row").bit_length() - 1
    devices = lax.axis_size("row") * lax.axis_size("seq")
    pairs = []
    for d in range(devices):
        bits = stage_bits()[(d >> row_bits) & 1]
        pairs.append((d, d ^ ((piece >> 1) << bits[2]) ^ ((piece & 1) << bits[3])))
    return pairs


def core_pairs():
    row_bits = lax.axis_size("row").bit_length() - 1
    devices = lax.axis_size("row") * lax.axis_size("seq")
    return [(d, d ^ (1 << row_bits)) for d in range(devices)]


def added(a, b):
    return (a.astype(f32) + b.astype(f32)).astype(bf16)


class Sequence:
    def __init__(self, token):
        self.token = token

    def after(self, *arrays):
        *arrays, _ = lax.optimization_barrier((*arrays, self.token))
        return arrays[0] if len(arrays) == 1 else arrays

    def did(self, array):
        self.token = array
        return array


def split(value):
    high = lax.reduce_precision(value, 8, 7)
    return [high.astype(bf16), (value - high).astype(bf16)]


def join_kernel(*refs):
    parts, ride, out, ride_out = refs[:-3], refs[-3], refs[-2], refs[-1]
    rows = parts[0].shape[0] - 2 * R
    total = ride[...]
    for i, part in enumerate(parts):
        out[i * rows : (i + 1) * rows, :] = part[0:rows, :]
        if i:
            both = part[rows:, :].astype(f32)
            total = total + (both[:R] + both[R:])
    ride_out[...] = total
    high = total.astype(bf16).astype(f32)
    out[len(parts) * rows :, :] = jnp.concatenate([high, total - high], 0).astype(bf16)


def chain_kernel(*refs):
    parts, out = refs[:-1], refs[-1]
    rows = parts[0].shape[0]
    for i, part in enumerate(parts):
        out[i * rows : (i + 1) * rows, :] = part[...]


def chained(parts):
    rows, width = parts[0].shape
    return pl.pallas_call(
        chain_kernel,
        in_specs=[pl.BlockSpec(memory_space=pltpu.VMEM)] * len(parts),
        out_specs=pl.BlockSpec(memory_space=pltpu.VMEM),
        out_shape=shape((len(parts) * rows, width), bf16),
        compiler_params=pltpu.CompilerParams(vmem_limit_bytes=16 * 1024 * 1024),
        cost_estimate=LITTLE,
        name="chain",
    )(*parts)


def joined(parts, ride):
    rows, width = parts[0].shape
    return pl.pallas_call(
        join_kernel,
        in_specs=[pl.BlockSpec(memory_space=pltpu.VMEM)] * (len(parts) + 1),
        out_specs=[pl.BlockSpec(memory_space=pltpu.VMEM)] * 2,
        out_shape=[shape((len(parts) * (rows - 2 * R) + 2 * R, width), bf16), shape(ride.shape)],
        compiler_params=pltpu.CompilerParams(vmem_limit_bytes=16 * 1024 * 1024),
        cost_estimate=LITTLE,
        name="join",
    )(*parts, ride)


class Halving:
    def __init__(self, seq, send):
        self.seq = seq
        self.recv = [flat_permute(send, core_pairs())]
        self.stage = 0
        self.ride = None

    def gather(self, parts):
        if self.ride is None:
            return chained(parts)
        message, self.ride = joined(parts, self.ride)
        return message

    def step(self, *beside):
        k = self.stage
        self.stage += 1
        stages = len(stage_bits()[0])
        arrived = self.seq.after(*self.recv, *beside)
        arrived = arrived if isinstance(arrived, list) else [arrived]
        recv, beside = arrived[: len(self.recv)], arrived[len(self.recv) :]
        if k < 2:
            half = self.keep.shape[0] // 2
            send = self.seq.did(added(self.keep[half:], recv[0][half:]))
            self.recv = [flat_permute(send, halving_pairs(k))]
            self.keep = added(self.keep[:half], recv[0][:half])
        elif k == 2:
            rows = self.keep.shape[0] // 4
            cut = [slice(j * rows, (j + 1) * rows) for j in range(4)]
            parts = [added(self.keep[c], recv[0][c]) for c in cut]
            self.seq.did(parts[3])
            self.recv = [flat_permute(parts[j], quarter_pairs(j)) for j in (1, 2, 3)]
            self.keep = parts[0]
        elif k == 3:
            total = sum((r.astype(f32) for r in recv), self.keep.astype(f32)).astype(bf16)
            for extra in range(4, stages):
                total = added(total, flat_permute(total, halving_pairs(extra)))
                if self.ride is not None:
                    self.ride = self.ride + flat_permute(self.ride, halving_pairs(extra))
            self.rows = total.shape[0]
            riders = [] if self.ride is None else split(self.ride)
            self.total = self.seq.did(jnp.concatenate([total] + riders, 0))
            self.recv = [flat_permute(self.total, quarter_pairs(j)) for j in (1, 2, 3)]
        elif k < 6:
            self.total = self.seq.did(self.gather([self.total] + recv))
            self.rows *= 1 + len(recv)
            self.recv = [flat_permute(self.total, halving_pairs(5 - k))]
            if k == 5:
                self.theirs = flat_permute(self.total, core_pairs())
        else:
            (self.rest,) = recv
            if self.ride is not None:
                low = self.rows + R
                extra = self.rest[self.rows : low].astype(f32) + self.rest[low:].astype(f32)
                self.ride = self.ride + extra
            self.their_rest = flat_permute(self.rest, core_pairs())
        return beside


def chip_shift(value, steps):
    return passed_along(value, "seq", 2 * steps)


def per_device(
    inputs,
    lengths,
    norm_gain,
    conv_weight,
    gate_weight,
    gate_bias,
    cand_weight,
    out_weight,
    mlp_gain,
    up_weight,
    down_weight,
    cotangent,
):
    rows, span, width = inputs.shape
    hidden = gate_weight.shape[1]
    feed = up_weight.shape[1]
    taps = conv_weight.shape[0]
    margin = taps - 1
    tokens = rows * span
    tb = 32
    blocks = span // tb
    m = tb * R
    seq = lax.axis_index("seq")
    core = seq & 1
    chips = lax.axis_size("seq") // 2
    hops = chips - 1
    flat = seq * lax.axis_size("row") + lax.axis_index("row")
    slots = [slot_of(flat, bits) for bits in stage_bits()]
    here = jnp.where(core == 0, slots[0], slots[1])
    mate = jnp.where(core == 0, slots[1], slots[0])
    scal = jnp.concatenate([jnp.stack([seq * span, core, here, mate]).astype(jnp.int32), lengths])
    gain1 = norm_gain.reshape(1, width)
    gain2 = mlp_gain.reshape(1, width)
    bias = gate_bias.reshape(1, hidden)
    to_pm, to_rm = token_order()

    edge = inputs[:, span - margin :, :].swapaxes(0, 1).reshape(margin * rows, width)
    edge = passed_along(edge, "seq", 1)

    last = blocks - 1
    clamp = lambda i: jnp.minimum(i, last)
    late = lambda i: jnp.maximum(i - blocks, 0)
    later = lambda i: jnp.minimum(i + 1, last)
    before = lambda i: jnp.maximum(i - 1, 0)

    def rm(index):
        return pl.BlockSpec((rows, tb, width), lambda i, *s: (0, index(i), 0))

    def tok(w, index=clamp):
        return pl.BlockSpec((m, w), lambda i, *s: (index(i), 0))

    def rtok(w):
        return tok(w, lambda i: last - clamp(i))

    def fixed(dims):
        zeros = (0,) * len(dims)
        return pl.BlockSpec(dims, lambda i, *s: zeros)

    def call(kernel, name, grid, ins, outs, scratch, operands, scalars=True, much=False):
        spec = pltpu.PrefetchScalarGridSpec(
            num_scalar_prefetch=int(scalars),
            grid=(grid,),
            in_specs=ins,
            out_specs=[o[1] for o in outs],
            scratch_shapes=scratch,
        )
        return pl.pallas_call(
            kernel,
            grid_spec=spec,
            out_shape=[o[0] for o in outs],
            compiler_params=params(16),
            cost_estimate=MUCH if much else LITTLE,
            name=name,
        )(*operands)

    def rows_of(w, kind, spec=tok, kept=shape):
        return kept((tokens, w), kind), spec(w)

    (normed,) = call(
        norm_kernel, "norm", blocks,
        [rm(clamp), whole(to_pm), whole(gain1)],
        [rows_of(width, bf16)],
        [],
        (far(inputs), far(to_pm), far(gain1)),
        scalars=False,
    )
    edge, normed = lax.optimization_barrier((edge, normed))
    c, zl, kh, ends = call(
        front_kernel, "front", blocks,
        [
            tok(width), whole(edge), whole(gain1), whole(conv_weight),
            whole(gate_weight), whole(bias), whole(cand_weight),
        ],
        [
            rows_of(width, bf16), rows_of(hidden, bf16), rows_of(hidden, bf16),
            (shape((2 * R, hidden)), fixed((2 * R, hidden))),
        ],
        [
            pltpu.VMEM((margin * R + m, width), f32),
            pltpu.VMEM((2 * R, hidden), f32),
            pltpu.VMEM((R, hidden), jnp.int32),
        ],
        (
            scal, normed, edge, far(gain1), far(conv_weight), gate_weight, far(bias),
            cand_weight,
        ),
    )

    other = flat_permute(ends, core_pairs())
    first = jnp.where(core == 0, ends, other)
    second = jnp.where(core == 0, other, ends)
    decay = jnp.log(jnp.maximum(ends[:R] * other[:R], 1e-37))
    message = jnp.concatenate([decay, second[:R] * first[R:] + second[R:]], 0).astype(bf16)
    forward = [chip_shift(message, k) for k in range(1, chips)]

    gl, da = call(
        da_kernel, "da", blocks,
        [rm(clamp), whole(to_pm), whole(down_weight)],
        [rows_of(width, bf16), rows_of(feed, bf16)],
        [],
        (cotangent, to_pm, down_weight),
        scalars=False,
    )

    r1, y, hp, n2, act, dp, dm, dr1, dh, back, mg = call(
        functools.partial(core_kernel, fchunk=256, hops=hops, blocks=blocks), "core", blocks,
        [
            rm(clamp), whole(to_pm), tok(width), tok(feed), tok(hidden), tok(hidden, later), tok(hidden),
            tok(hidden, later), tok(hidden, before), whole(other),
            *[whole(f) for f in forward], whole(out_weight), whole(gain2), whole(up_weight),
        ],
        [
            rows_of(width, f32, kept=pltpu.HBM), rows_of(hidden, bf16), rows_of(hidden, bf16),
            rows_of(width, bf16), rows_of(feed, bf16), rows_of(feed, bf16), rows_of(width, bf16),
            rows_of(width, f32, kept=pltpu.HBM),
            rows_of(hidden, bf16),
            (shape((R, hidden)), fixed((R, hidden))), (shape((R, width)), fixed((R, width))),
        ],
        [
            pltpu.VMEM((R, hidden), f32),
            pltpu.VMEM((R, hidden), jnp.int32),
            pltpu.VMEM((R, hidden), f32),
            pltpu.VMEM((m, width), f32),
            pltpu.VMEM((m, hidden), bf16),
            pltpu.VMEM((m, hidden), bf16),
            pltpu.VMEM((m, hidden), bf16),
        ],
        (
            scal, inputs, to_pm, gl, da, zl, zl, kh, kh, zl, other, *forward, far(out_weight), gain2, up_weight,
        ),
    )

    order = Sequence(back)
    quarter = feed // 4
    half = lambda pick, s: s[1] if pick == 0 else 1 - s[1]

    def grads(kernel, name, number, pick, steps, specs, operands, beside=()):
        first_two = order.after(*operands[:2], *beside)
        dims = (SLOTS // 2 * PIECES[number], width)
        (piece,) = call(
            functools.partial(kernel, pick=pick), name, steps, specs,
            [(shape(dims, bf16), fixed(dims))], [],
            (scal, *first_two[:2], *operands[2:]),
            much=pick == 0 and number != 2,
        )
        return order.did(piece), first_two[2:]

    def down_grads(pick):
        return grads(
            down_grad_kernel, "down_grad", 0, pick, 2,
            [pl.BlockSpec((tokens, quarter), lambda i, s: (0, half(pick, s) * 2 + i)), whole(gl)],
            (act, gl),
        )[0]

    def up_out_grads(pick, *beside):
        return grads(
            up_out_grad_kernel, "up_grad", 1, pick, 2,
            [
                pl.BlockSpec((tokens, width // 2), lambda i, s: (0, half(pick, s))),
                pl.BlockSpec((tokens, feed // 2), lambda i, s: (0, i)),
                pl.BlockSpec((tokens, hidden // 4), lambda i, s: (0, half(pick, s) * 2 + i)),
                whole(dm),
            ],
            (n2, dp, y, dm), beside,
        )

    def gate_grads(pick):
        return grads(
            gate_grad_kernel, "gate_grad", 2, pick, 1,
            [
                pl.BlockSpec((tokens, width // 2), lambda i, s: (0, half(pick, s))),
                whole(dkz), whole(dkh),
            ],
            (c, dkz, dkh),
        )[0]

    fother = flat_permute(back, core_pairs())
    lower = jnp.where(core == 0, back, fother)
    upper = jnp.where(core == 0, fother, back)
    message = jnp.concatenate([decay, lower + first[:R] * upper], 0).astype(bf16)
    backward = [chip_shift(order.did(message), -k) for k in range(1, chips)]
    send1, _ = up_out_grads(1)
    chunk1 = Halving(order, send1)
    chunk1.keep, backward = up_out_grads(0, *backward)
    chunk1.step()

    dkz, dkh, edge_dc, bias_part = call(
        functools.partial(gate_kernel, blocks=blocks, hops=hops), "gates", blocks,
        [
            rtok(hidden), rtok(hidden), rtok(hidden), rtok(hidden),
            whole(other), whole(fother), *[whole(f) for f in backward],
            whole(gate_weight), whole(cand_weight), ORDER,
        ],
        [
            rows_of(hidden, bf16, rtok), rows_of(hidden, bf16, rtok),
            (shape((4 * R, width), bf16), fixed((4 * R, width))),
            (shape((R, hidden)), fixed((R, hidden))),
        ],
        [pltpu.VMEM((R, hidden), f32)],
        (
            scal, dh, zl, kh, hp, other, fother, *backward, gate_weight, cand_weight, order.token,
        ),
    )
    order.did(bias_part)
    after = passed_along(edge_dc[: margin * R], "seq", -1)
    chunk2 = Halving(order, gate_grads(1))
    chunk0 = Halving(order, down_grads(1))
    chunk1.step()
    chunk0.keep = down_grads(0)
    chunk2.keep = gate_grads(0)
    chunk2.step()
    chunk0.step()
    chunk1.step()
    input_grad, sums = call(
        functools.partial(tail_kernel, blocks=blocks), "tail", 2 * blocks,
        [
            rm(late), tok(width, late), tok(hidden), tok(hidden), whole(to_pm), whole(to_rm),
            whole(edge), whole(after), whole(gain1), whole(conv_weight), whole(gate_weight),
            whole(cand_weight),
        ],
        [
            (shape((rows, span, width), bf16), rm(late)),
            (shape(((taps + 1) * R, width)), fixed(((taps + 1) * R, width))),
        ],
        [
            pltpu.VMEM((margin * R + m, width), f32),
            pltpu.VMEM((margin * R + tokens, width), f32),
        ],
        (
            far(inputs), far(dr1), order.after(dkz), dkh, far(to_pm), far(to_rm), edge, after,
            far(gain1), far(conv_weight), far(gate_weight), far(cand_weight),
        ),
        scalars=False,
    )
    order.did(sums)
    small = jnp.concatenate(
        [
            sums.reshape(taps + 1, R, width).sum(1),
            mg.sum(0, keepdims=True),
            bias_part.sum(0).reshape(hidden // width, width),
        ],
        0,
    )
    coming = flat_permute(small, core_pairs())

    plans = (
        ((0, feed // SLOTS, 1),),
        ((0, width // SLOTS, feed // width), (1, hidden // SLOTS, 1)),
        ((0, width // SLOTS, hidden // width), (1, width // SLOTS, hidden // width)),
    )
    shapes = (
        ((feed, width),),
        ((width, feed), (hidden, width)),
        ((width, hidden), (width, hidden)),
    )
    names = ("spread_down", "spread_up", "spread_gate")
    held = [(), (), ()]

    def put(number, src, mate, flip):
        src = order.after(src)
        held[number] = spread(
            scal, src, held[number], mate, flip, PIECES[number], plans[number], shapes[number],
            names[number],
        )
        order.did(held[number][0])

    chunk2.step()
    chunk1.step()
    chunk2.ride = small + order.after(coming)
    chunk0.step()
    chunk2.step()
    (output,) = call(
        output_kernel, "output", blocks,
        [tok(width), tok(feed), whole(to_rm), whole(down_weight)],
        [(shape((rows, span, width), bf16), rm(clamp))],
        [],
        (far(r1), order.after(act), to_rm, down_weight),
        scalars=False,
    )
    order.did(output)
    chunk1.step()
    chunk0.step()
    chunk2.step()
    chunk1.step()
    chunk0.step()
    chunk2.step()
    put(1, chunk1.total, 0, 0)
    put(1, chunk1.theirs, 1, 0)
    chunk0.step()
    chunk1.step()
    chunk2.step()
    put(1, chunk1.rest, 0, 1)
    put(2, chunk2.total, 0, 0)
    chunk0.step()
    put(1, chunk1.their_rest, 1, 1)
    put(2, chunk2.theirs, 1, 0)
    put(0, chunk0.total, 0, 0)
    chunk2.step()
    small = chunk2.ride
    small_out = order.after(
        small[0], small[1 : taps + 1], small[taps + 2 :].reshape(hidden), small[taps + 1]
    )
    put(2, chunk2.rest, 0, 1)
    put(0, chunk0.theirs, 1, 0)
    put(2, chunk2.their_rest, 1, 1)
    chunk0.step()
    put(0, chunk0.rest, 0, 1)
    put(0, chunk0.their_rest, 1, 1)
    return (
        output,
        input_grad,
        small_out[0],
        small_out[1],
        held[2][0],
        small_out[2],
        held[2][1],
        held[1][1],
        small_out[3],
        held[1][0],
        held[0][0],
    )


def solution(mesh):
    sharded = P("row", "seq", None)
    in_specs = (sharded, P("row")) + (P(),) * 9 + (sharded,)
    out_specs = (sharded, sharded) + (P(),) * 9
    return jax.shard_map(
        per_device, mesh=mesh, in_specs=in_specs, out_specs=out_specs, check_vma=False
    )
```

```python
import functools

import jax
import jax.numpy as jnp
import numpy as np
from jax import lax
from jax.experimental import pallas as pl
from jax.experimental.pallas import tpu as pltpu
from jax.sharding import PartitionSpec as P

epsilon = 1e-06
f32 = jnp.float32
bf16 = jnp.bfloat16
R = 8
PERM = 256
SCALARS = 4
SLOTS = 32
PIECE1 = 128
PIECE2 = 96


def nn(a, b):
    return lax.dot_general(a, b, (((1,), (0,)), ((), ())), preferred_element_type=f32)


def nt(a, b):
    return lax.dot_general(a, b, (((1,), (1,)), ((), ())), preferred_element_type=f32)


def tn(a, b):
    return lax.dot_general(a, b, (((0,), (0,)), ((), ())), preferred_element_type=f32)


def token_order():
    out = np.arange(PERM)
    source = (out % R) * (PERM // R) + out // R
    to_pm = np.zeros((PERM, PERM), np.float32)
    to_pm[out, source] = 1
    return jnp.asarray(to_pm, bf16), jnp.asarray(to_pm.T, bf16)


def position_major(perm, block):
    span = PERM // R
    parts = []
    for s in range(block.shape[1] // span):
        part = block[:, s * span : (s + 1) * span, :].reshape(PERM, block.shape[2])
        parts.append(nn(perm, part))
    return parts[0] if len(parts) == 1 else jnp.concatenate(parts, 0)


def row_major(perm, tokens):
    span = PERM // R
    parts = []
    for s in range(tokens.shape[0] // PERM):
        part = nn(perm, tokens[s * PERM : (s + 1) * PERM]).astype(bf16)
        parts.append(part.reshape(R, span, tokens.shape[1]))
    return parts[0] if len(parts) == 1 else jnp.concatenate(parts, 1)


def eight(t):
    return pl.ds(pl.multiple_of(t * R, R), R)


def sixteen(t):
    return pl.ds(pl.multiple_of(t * 2 * R, 2 * R), 2 * R)


def normed_edge(edge, gain):
    e = edge.astype(f32)
    inv = lax.rsqrt(jnp.mean(e * e, -1, keepdims=True) + epsilon)
    return (e * inv * gain).astype(bf16).astype(f32)


def set_limits(scal, limit):
    row = lax.broadcasted_iota(jnp.int32, limit.shape, 0)
    value = jnp.zeros(limit.shape, jnp.int32)
    for r in range(R):
        value = jnp.where(row == r, scal[SCALARS + r], value)
    limit[...] = value


def halves(ref, pair):
    both = ref[sixteen(pair), :].astype(f32)
    return both[:R], both[R:]


def norm_kernel(x, perm, gain, u_out):
    xp = position_major(perm[...], x[...])
    inv = lax.rsqrt(jnp.mean(xp * xp, -1, keepdims=True) + epsilon)
    u_out[...] = (xp * inv * gain[...]).astype(bf16)


def front_kernel(scal, u, edge, gain, convw, wg, bias, wc, c_out, zl_out, kh_out, ends, ext, state, limit):
    step = pl.program_id(0)
    m = u.shape[0]
    tb = m // R
    halo = edge.shape[0]
    taps = convw.shape[0]

    @pl.when(step == 0)
    def _():
        set_limits(scal, limit)
        ext[0:halo, :] = normed_edge(edge[...], gain[...])
        state[0:R, :] = jnp.ones((R, state.shape[1]), f32)
        state[R:, :] = jnp.zeros((R, state.shape[1]), f32)

    ext[halo:, :] = u[...].astype(f32)
    conv = convw[0:1, :] * ext[halo:, :]
    for k in range(1, taps):
        lo = halo - k * R
        conv = conv + convw[k : k + 1, :] * ext[lo : lo + m, :]
    ext[0:halo, :] = ext[m : m + halo, :]
    cb = conv.astype(bf16)
    c_out[...] = cb
    kz = nn(cb, wg[...]) + bias[...]
    zs = 1.0 / (1.0 + jnp.exp(-kz))
    width = zs.shape[1]
    zs = zs.reshape(tb, R, width)
    pos = scal[0] + step * tb + lax.broadcasted_iota(jnp.int32, (tb, R, width), 0)
    zl_out[...] = jnp.where(pos < limit[...][None], zs, 0.0).reshape(m, width).astype(bf16)
    kh_out[...] = nn(cb, wc[...]).astype(bf16)

    def body(u, carry):
        prod, h = carry
        za, zb = halves(zl_out, u)
        ka, kb = halves(kh_out, u)
        a = 1.0 - za
        b = 1.0 - zb
        return prod * (a * b), (h * a + za * ka) * b + zb * kb

    prod, h = lax.fori_loop(0, tb // 2, body, (state[0:R, :], state[R:, :]), unroll=4)
    state[0:R, :] = prod
    state[R:, :] = h
    ends[0:R, :] = prod
    ends[R:, :] = h


def gelu_parts(p):
    k0 = 0.7978845608028654
    inner = p * (k0 + (k0 * 0.044715) * (p * p))
    th = jnp.tanh(inner)
    ht = 0.5 + 0.5 * th
    return p * ht, ht + (1.0 - th * th) * (1.5 * inner - k0 * p)


def da_kernel(g, perm, wd, gl_out, da_out):
    gl = position_major(perm[...], g[...]).astype(bf16)
    gl_out[...] = gl
    da_out[...] = nt(gl, wd[...]).astype(bf16)


def core_kernel(scal, x, perm, gl, da, zl, zl_next, kh, kh_next, zl_before, other, *refs, fchunk, hops, blocks):
    msgs = refs[:hops]
    wo, mgain, wu = refs[hops : hops + 3]
    r1_out, y_out, hp_out, n2_out, act_out, dp_out, dm_out, dr1_out, dh_out, back, mg = refs[hops + 3 : hops + 14]
    state, limit, run, acc, ys, hps, dhs = refs[hops + 14 :]
    step = pl.program_id(0)
    tb = x.shape[1]
    m = tb * R
    width, feed = wu.shape
    hidden = wo.shape[0]
    first = scal[0] + step * tb

    def scan_pair(zs, ks, start, u, h):
        t = u * 2
        za, zb = halves(zs, u)
        ka, kb = halves(ks, u)
        ha = h - za * h + za * ka
        hb = ha - zb * ha + zb * kb
        hps[sixteen(u), :] = jnp.concatenate([h, ha], 0).astype(bf16)
        ya = jnp.where(start + t < limit[...], ha, 0.0)
        yb = jnp.where(start + t + 1 < limit[...], hb, 0.0)
        ys[sixteen(u), :] = jnp.concatenate([ya, yb], 0).astype(bf16)
        return hb

    def adjoint_pair(zs, ds, u, prod, total):
        za, zb = halves(zs, u)
        da, db = halves(ds, u)
        pa = prod - za * prod
        pb = pa - zb * pa
        return pb, total + (pa * da + pb * db)

    @pl.when(step == 0)
    def _():
        set_limits(scal, limit)
        h = jnp.zeros((R, hidden), f32)
        for msg in reversed(msgs):
            both = msg[...].astype(f32)
            h = jnp.exp(both[0:R, :]) * h + both[R:, :]
        h = jnp.where(scal[1] == 1, other[0:R, :] * h + other[R:, :], h)
        run[...] = jnp.ones((R, hidden), f32)
        back[...] = jnp.zeros(back.shape, f32)
        mg[...] = jnp.zeros(mg.shape, f32)
        dhs[...] = jnp.zeros(dhs.shape, bf16)
        state[...] = lax.fori_loop(0, tb // 2, lambda u, h: scan_pair(zl, kh, scal[0], u, h), h, unroll=2)

    hp_out[...] = hps[...]
    y = ys[...]
    y_out[...] = y
    r1 = position_major(perm[...], x[...]) + nn(y, wo[...])
    r1_out[...] = r1
    inv = lax.rsqrt(jnp.mean(r1 * r1, -1, keepdims=True) + epsilon)
    n2 = (r1 * inv * mgain[...]).astype(bf16)
    n2_out[...] = n2
    chunks = feed // fchunk
    pairs = tb // 2 // chunks
    for f in range(chunks):
        cols = slice(f * fchunk, (f + 1) * fchunk)
        a, slope = gelu_parts(nn(n2, wu[:, cols]).astype(bf16))
        act_out[:, cols] = a
        dpb = da[:, cols] * slope
        dp_out[:, cols] = dpb
        part = nt(dpb, wu[:, cols])
        acc[...] = acc[...] + part if f else part
        h, prod, total = state[...], run[...], back[...]
        for u in range(f * pairs, (f + 1) * pairs):
            h = scan_pair(zl_next, kh_next, first + tb, u, h)
            prod, total = adjoint_pair(zl_before, dhs, u, prod, total)
        state[...] = h
        run[...] = jnp.where(step == 0, 1.0, prod)
        back[...] = total
    dn2 = acc[...]
    r1 = r1_out[...]
    mg[...] += jnp.sum((dn2 * r1 * inv).reshape(tb, R, width), 0)
    s = mgain[...] * dn2
    mean = jnp.mean(s * r1, -1, keepdims=True)
    dr1 = gl[...].astype(f32) + inv * (s - r1 * (inv * inv * mean))
    dr1_out[...] = dr1
    dm = dr1.astype(bf16)
    dm_out[...] = dm
    dh = nt(dm, wo[...]).reshape(tb, R, hidden)
    pos = first + lax.broadcasted_iota(jnp.int32, (tb, R, hidden), 0)
    dh = jnp.where(pos < limit[...][None], dh, 0.0).reshape(m, hidden).astype(bf16)
    dh_out[...] = dh
    dhs[...] = dh

    @pl.when(step == blocks - 1)
    def _():
        carry = lax.fori_loop(
            0, tb // 2, lambda u, carry: adjoint_pair(zl, dhs, u, *carry), (run[...], back[...]), unroll=4
        )
        back[...] = carry[1]


def put_rows(dst, sel, piece, at, rows, part):
    for i in range(SLOTS // 2):
        pos = pl.multiple_of((i ^ sel) * piece + at, 16)
        dst[pl.ds(pos, rows), :] = part[i * rows : (i + 1) * rows]


def ffn_grad_kernel(scal, act, gl, n2, dp, dst, *, pick):
    step = pl.program_id(0)
    sel = scal[2 + pick]
    width = gl.shape[1]
    rows1 = act.shape[1] * 4 // SLOTS
    rows2 = n2.shape[1] * 2 // SLOTS
    part = tn(act[...], gl[...]).astype(bf16)
    per = act.shape[1] // rows1
    for i in range(per):
        pos = ((step * per + i) ^ sel) * PIECE1
        dst[pl.ds(pl.multiple_of(pos, 16), rows1), :] = part[i * rows1 : (i + 1) * rows1]
    columns = dp.shape[1] // width
    for q in range(columns):
        part = tn(n2[...], dp[:, q * width : (q + 1) * width]).astype(bf16)
        put_rows(dst, sel, PIECE1, rows1 + (step * columns + q) * rows2, rows2, part)


def gate_grad_kernel(scal, c, dkz, dkh, y, dm, dst, *, pick):
    sel = scal[2 + pick]
    width = dm.shape[1]
    rows = c.shape[1] * 2 // SLOTS
    at = 0
    for grads in (dkz, dkh):
        for q in range(grads.shape[1] // width):
            part = tn(c[...], grads[:, q * width : (q + 1) * width]).astype(bf16)
            put_rows(dst, sel, PIECE2, at, rows, part)
            at += rows
    put_rows(dst, sel, PIECE2, at, y.shape[1] * 2 // SLOTS, tn(y[...], dm[...]).astype(bf16))


def gate_kernel(scal, dh, zl, kh, hp, other, fother, *refs, blocks, hops):
    msgs = refs[:hops]
    wg, wc = refs[hops : hops + 2]
    dkz, dkh, edge_out, bias_out = refs[hops + 3 : hops + 7]
    state = refs[hops + 7]
    step = pl.program_id(0)
    m = dh.shape[0]
    tb = m // R
    block = blocks - 1 - step

    @pl.when(step == 0)
    def _():
        mm = jnp.zeros(state.shape, f32)
        for msg in reversed(msgs):
            both = msg[...].astype(f32)
            mm = jnp.exp(both[0:R, :]) * mm + both[R:, :]
        state[...] = jnp.where(scal[1] == 0, fother[...] + other[0:R, :] * mm, mm)
        bias_out[...] = jnp.zeros(bias_out.shape, f32)

    def body(u, carry):
        mm, bias = carry
        w = tb // 2 - 1 - u
        ha, hb = halves(hp, w)
        za, zb = halves(zl, w)
        da, db = halves(dh, w)
        ka, kb = halves(kh, w)
        lam = db + mm
        sb = lam * zb
        mm = lam - sb
        kb = (sb - sb * zb) * (kb - hb)
        lam = da + mm
        sa = lam * za
        mm = lam - sa
        ka = (sa - sa * za) * (ka - ha)
        kk = jnp.concatenate([ka, kb], 0).astype(bf16)
        dkz[sixteen(w), :] = kk
        dkh[sixteen(w), :] = jnp.concatenate([sa, sb], 0).astype(bf16)
        kf = kk.astype(f32)
        return mm, bias + kf[:R, :] + kf[R:, :]

    mm, bias = lax.fori_loop(0, tb // 2, body, (state[...], bias_out[...]), unroll=2)
    state[...] = mm
    bias_out[...] = bias

    @pl.when(block == 0)
    def _():
        span = edge_out.shape[0]
        edge_out[...] = (nt(dkz[0:span, :], wg[...]) + nt(dkh[0:span, :], wc[...])).astype(bf16)


def tail_kernel(x, dr1, dkz, dkh, pm, back_pm, edge, after, gain, convw, wg, wc, grad, sums, uext, dext, *, blocks):
    step = pl.program_id(0)
    tb = x.shape[1]
    m = tb * R
    halo = edge.shape[0]
    taps = convw.shape[0]
    width = gain.shape[1]

    @pl.when(step == 0)
    def _():
        uext[0:halo, :] = normed_edge(edge[...], gain[...])
        dext[blocks * m :, :] = after[...].astype(f32)
        sums[...] = jnp.zeros(sums.shape, f32)

    @pl.when(step < blocks)
    def _():
        rows = pl.ds(pl.multiple_of(step * m, m), m)
        dext[rows, :] = nt(dkz[...], wg[...]) + nt(dkh[...], wc[...])

    @pl.when(step >= blocks)
    def _():
        xp = position_major(pm[...], x[...])
        inv = lax.rsqrt(jnp.mean(xp * xp, -1, keepdims=True) + epsilon)
        xn = xp * inv
        uext[halo:, :] = (xn * gain[...]).astype(bf16).astype(f32)
        start = (step - blocks) * m
        here = dext[pl.ds(pl.multiple_of(start, R), m), :]
        du = convw[0:1, :] * here
        for k in range(taps):
            lo = halo - k * R
            part = (here * uext[lo : lo + m, :]).reshape(tb, R, width)
            sums[(k + 1) * R : (k + 2) * R, :] += jnp.sum(part, 0)
            if k:
                du = du + convw[k : k + 1, :] * dext[pl.ds(pl.multiple_of(start + k * R, R), m), :]
        uext[0:halo, :] = uext[m : m + halo, :]
        sums[0:R, :] += jnp.sum((du * xn).reshape(tb, R, width), 0)
        s1 = gain[...] * du
        mean = jnp.mean(s1 * xn, -1, keepdims=True)
        gin = dr1[...] + inv * (s1 - xn * mean)
        grad[...] = row_major(back_pm[...], gin.astype(bf16))


def output_kernel(r1, act, perm, wd, out):
    total = r1[...] + nn(act[...], wd[...])
    out[...] = row_major(perm[...], total.astype(bf16))


def spread_kernel(scal, src, *refs, piece, plan, mate):
    low = scal[2 + mate] & 7
    for a in range(8):
        base = (a ^ low) * piece
        at = 0
        for out, rows, columns in plan:
            ref = refs[len(refs) - len(plan) + out]
            for q in range(columns):
                width = src.shape[1]
                part = src[pl.ds(pl.multiple_of(base + at, 16), rows), :].astype(f32)
                ref[a * rows : (a + 1) * rows, q * width : (q + 1) * width] = part
                at += rows


def last_spread_kernel(scal, src, ride, rest, theirs, *refs, piece, plan, taps):
    norm, conv, mlp, bias = refs[-4:]
    spread_kernel(scal, src, *refs[:-4], piece=piece, plan=plan, mate=1)
    tail = src.shape[0] - 2 * R
    total = ride[...]
    for rows in (rest[...], theirs[...], src[tail:, :]):
        both = rows.astype(f32)
        total = total + (both[:R] + both[R:])
    norm[...] = total[0:1]
    conv[...] = total[1 : taps + 1]
    mlp[...] = total[taps + 1 : taps + 2]
    width = total.shape[1]
    for i in range(bias.shape[1] // width):
        bias[:, i * width : (i + 1) * width] = total[taps + 2 + i : taps + 3 + i]


def last_spread(scal, chunk, held, piece, plan, shapes, taps, hidden):
    src = chunk.their_rest
    width = src.shape[1]
    rows = 2 * R
    tail = pl.BlockSpec((rows, width), lambda g, s: (src.shape[0] // rows - 1, 0))
    small = ((1, width), (taps, width), (1, width), (1, hidden))

    def block(g, s):
        return ((s[1] ^ 1) * 2 + ((s[3] >> 3) ^ 1), 0)

    return pl.pallas_call(
        functools.partial(last_spread_kernel, piece=piece, plan=plan, taps=taps),
        grid_spec=pltpu.PrefetchScalarGridSpec(
            num_scalar_prefetch=1,
            grid=(1,),
            in_specs=[whole(src), whole(chunk.ride), tail, tail] + [ORDER] * len(held),
            out_specs=[pl.BlockSpec((dims[0] // 4, dims[1]), block) for dims in shapes]
            + [pl.BlockSpec(dims, lambda g, s: (0, 0)) for dims in small],
        ),
        out_shape=[pltpu.HBM(dims, f32) for dims in shapes] + [shape(dims) for dims in small],
        input_output_aliases={5 + k: k for k in range(len(held))},
        compiler_params=params(16),
        cost_estimate=LITTLE,
        name="spread_last",
    )(scal, src, chunk.ride, chunk.rest, chunk.theirs, *held)


def spread(scal, src, held, mate, flip, piece, plan, shapes, name):
    def block(g, s):
        return ((s[1] ^ mate) * 2 + ((s[2 + mate] >> 3) ^ flip), 0)

    count = len(held)
    return pl.pallas_call(
        functools.partial(spread_kernel, piece=piece, plan=plan, mate=mate),
        grid_spec=pltpu.PrefetchScalarGridSpec(
            num_scalar_prefetch=1,
            grid=(1,),
            in_specs=[whole(src)] + [ORDER] * count,
            out_specs=[pl.BlockSpec((dims[0] // 4, dims[1]), block) for dims in shapes],
        ),
        out_shape=[pltpu.HBM(dims, f32) for dims in shapes],
        input_output_aliases={2 + k: k for k in range(count)},
        compiler_params=params(16),
        cost_estimate=LITTLE,
        name=name,
    )(scal, src, *held)


def params(mib):
    return pltpu.CompilerParams(
        dimension_semantics=("arbitrary",), vmem_limit_bytes=mib * 1024 * 1024
    )


def shape(dims, kind=f32):
    return jax.ShapeDtypeStruct(dims, kind)


LITTLE = pl.CostEstimate(flops=1024, bytes_accessed=1024, transcendentals=0)
MUCH = pl.CostEstimate(flops=3 * 10**10, bytes_accessed=1024, transcendentals=0)
ORDER = pl.BlockSpec(memory_space=pl.ANY)


def far(array):
    return pltpu.with_memory_space_constraint(array, pltpu.HBM)


def whole(array):
    zeros = (0,) * array.ndim
    return pl.BlockSpec(array.shape, lambda *a: zeros, pipeline_mode=pl.Buffered(1))


def passed_along(value, axis, steps):
    count = lax.axis_size(axis)
    leading, last = (max(0, -steps), min(count, count - steps))
    return lax.ppermute(value, axis, [(source, source + steps) for source in range(leading, last)])


def flat_permute(value, pairs):
    return lax.ppermute(value, ("seq", "row"), pairs)


def stage_bits():
    row_bits = lax.axis_size("row").bit_length() - 1
    seq_bits = lax.axis_size("seq").bit_length() - 1
    plane = list(range(row_bits))
    line = [row_bits + 1 + z for z in range(seq_bits - 1)]
    cut = row_bits // 2
    return (plane + line, plane[cut:] + plane[:cut] + line[::-1])


def slot_of(flat, bits):
    slot = 0
    for k in range(4):
        slot = slot * 2 + ((flat >> bits[k]) & 1)
    return slot


def halving_pairs(stage):
    row_bits = lax.axis_size("row").bit_length() - 1
    orders = stage_bits()
    devices = lax.axis_size("row") * lax.axis_size("seq")
    return [(d, d ^ (1 << orders[(d >> row_bits) & 1][stage])) for d in range(devices)]


def core_pairs():
    row_bits = lax.axis_size("row").bit_length() - 1
    devices = lax.axis_size("row") * lax.axis_size("seq")
    return [(d, d ^ (1 << row_bits)) for d in range(devices)]


def added(a, b):
    return (a.astype(f32) + b.astype(f32)).astype(bf16)


class Sequence:
    def __init__(self, token):
        self.token = token

    def after(self, *arrays):
        *arrays, _ = lax.optimization_barrier((*arrays, self.token))
        return arrays[0] if len(arrays) == 1 else arrays

    def did(self, array):
        self.token = array
        return array


def split(value):
    high = lax.reduce_precision(value, 8, 7)
    return [high.astype(bf16), (value - high).astype(bf16)]


def join_kernel(mine, recv, ride, out, ride_out):
    rows = mine.shape[0] - 2 * R
    out[0:rows, :] = mine[0:rows, :]
    out[rows : 2 * rows, :] = recv[0:rows, :]
    parts = recv[rows:, :].astype(f32)
    total = ride[...] + (parts[:R] + parts[R:])
    ride_out[...] = total
    high = total.astype(bf16).astype(f32)
    out[2 * rows :, :] = jnp.concatenate([high, total - high], 0).astype(bf16)


def joined(mine, recv, ride):
    rows, width = mine.shape
    return pl.pallas_call(
        join_kernel,
        in_specs=[pl.BlockSpec(memory_space=pltpu.VMEM)] * 3,
        out_specs=[pl.BlockSpec(memory_space=pltpu.VMEM)] * 2,
        out_shape=[shape((2 * rows - 2 * R, width), bf16), shape(ride.shape)],
        compiler_params=pltpu.CompilerParams(vmem_limit_bytes=16 * 1024 * 1024),
        cost_estimate=LITTLE,
        name="join",
    )(mine, recv, ride)


class Halving:
    def __init__(self, seq, send):
        self.seq = seq
        self.recv = flat_permute(send, core_pairs())
        self.stage = 0
        self.ride = None

    def riders(self):
        return [] if self.ride is None else split(self.ride)

    def step(self, *beside):
        k = self.stage
        self.stage += 1
        stages = len(stage_bits()[0])
        recv, *beside = self.seq.after(self.recv, *beside) if beside else (self.seq.after(self.recv),)
        if k < 4:
            half = self.keep.shape[0] // 2
            send = self.seq.did(added(self.keep[half:], recv[half:]))
            self.recv = flat_permute(send, halving_pairs(k))
            self.keep = added(self.keep[:half], recv[:half])
        elif k == 4:
            total = added(self.keep, recv)
            for extra in range(4, stages):
                total = added(total, flat_permute(total, halving_pairs(extra)))
                if self.ride is not None:
                    self.ride = self.ride + flat_permute(self.ride, halving_pairs(extra))
            self.rows = total.shape[0]
            self.total = self.seq.did(jnp.concatenate([total] + self.riders(), 0))
            self.recv = flat_permute(self.total, halving_pairs(3))
        elif k < 8:
            rows = self.rows
            self.rows = 2 * rows
            if self.ride is None:
                self.total = self.seq.did(jnp.concatenate([self.total, recv], 0))
            else:
                self.total, self.ride = joined(self.total, recv, self.ride)
                self.seq.did(self.total)
            self.recv = flat_permute(self.total, halving_pairs(7 - k))
            if k == 7:
                self.theirs = flat_permute(self.total, core_pairs())
        else:
            self.rest = recv
            self.their_rest = flat_permute(recv, core_pairs())
        return beside


def chip_shift(value, steps):
    return passed_along(value, "seq", 2 * steps)


def per_device(
    inputs,
    lengths,
    norm_gain,
    conv_weight,
    gate_weight,
    gate_bias,
    cand_weight,
    out_weight,
    mlp_gain,
    up_weight,
    down_weight,
    cotangent,
):
    rows, span, width = inputs.shape
    hidden = gate_weight.shape[1]
    feed = up_weight.shape[1]
    taps = conv_weight.shape[0]
    margin = taps - 1
    tokens = rows * span
    tb = 32
    blocks = span // tb
    m = tb * R
    seq = lax.axis_index("seq")
    core = seq & 1
    chips = lax.axis_size("seq") // 2
    hops = chips - 1
    flat = seq * lax.axis_size("row") + lax.axis_index("row")
    slots = [slot_of(flat, bits) for bits in stage_bits()]
    here = jnp.where(core == 0, slots[0], slots[1])
    mate = jnp.where(core == 0, slots[1], slots[0])
    scal = jnp.concatenate([jnp.stack([seq * span, core, here, mate]).astype(jnp.int32), lengths])
    gain1 = norm_gain.reshape(1, width)
    gain2 = mlp_gain.reshape(1, width)
    bias = gate_bias.reshape(1, hidden)
    to_pm, to_rm = token_order()

    edge = inputs[:, span - margin :, :].swapaxes(0, 1).reshape(margin * rows, width)
    edge = passed_along(edge, "seq", 1)

    last = blocks - 1
    clamp = lambda i: jnp.minimum(i, last)
    late = lambda i: jnp.maximum(i - blocks, 0)
    later = lambda i: jnp.minimum(i + 1, last)
    before = lambda i: jnp.maximum(i - 1, 0)

    def rm(index):
        return pl.BlockSpec((rows, tb, width), lambda i, *s: (0, index(i), 0))

    def tok(w, index=clamp):
        return pl.BlockSpec((m, w), lambda i, *s: (index(i), 0))

    def rtok(w):
        return tok(w, lambda i: last - clamp(i))

    def fixed(dims):
        zeros = (0,) * len(dims)
        return pl.BlockSpec(dims, lambda i, *s: zeros)

    def call(kernel, name, grid, ins, outs, scratch, operands, scalars=True, much=False):
        spec = pltpu.PrefetchScalarGridSpec(
            num_scalar_prefetch=int(scalars),
            grid=(grid,),
            in_specs=ins,
            out_specs=[o[1] for o in outs],
            scratch_shapes=scratch,
        )
        return pl.pallas_call(
            kernel,
            grid_spec=spec,
            out_shape=[o[0] for o in outs],
            compiler_params=params(16),
            cost_estimate=MUCH if much else LITTLE,
            name=name,
        )(*operands)

    def rows_of(w, kind, spec=tok, kept=shape):
        return kept((tokens, w), kind), spec(w)

    (normed,) = call(
        norm_kernel, "norm", blocks,
        [rm(clamp), whole(to_pm), whole(gain1)],
        [rows_of(width, bf16)],
        [],
        (far(inputs), far(to_pm), far(gain1)),
        scalars=False,
    )
    edge, normed = lax.optimization_barrier((edge, normed))
    c, zl, kh, ends = call(
        front_kernel, "front", blocks,
        [
            tok(width), whole(edge), whole(gain1), whole(conv_weight),
            whole(gate_weight), whole(bias), whole(cand_weight),
        ],
        [
            rows_of(width, bf16), rows_of(hidden, bf16), rows_of(hidden, bf16),
            (shape((2 * R, hidden)), fixed((2 * R, hidden))),
        ],
        [
            pltpu.VMEM((margin * R + m, width), f32),
            pltpu.VMEM((2 * R, hidden), f32),
            pltpu.VMEM((R, hidden), jnp.int32),
        ],
        (
            scal, normed, edge, far(gain1), far(conv_weight), gate_weight, far(bias),
            cand_weight,
        ),
    )

    other = flat_permute(ends, core_pairs())
    first = jnp.where(core == 0, ends, other)
    second = jnp.where(core == 0, other, ends)
    decay = jnp.log(jnp.maximum(ends[:R] * other[:R], 1e-37))
    message = jnp.concatenate([decay, second[:R] * first[R:] + second[R:]], 0).astype(bf16)
    forward = [chip_shift(message, k) for k in range(1, chips)]

    gl, da = call(
        da_kernel, "da", blocks,
        [rm(clamp), whole(to_pm), whole(down_weight)],
        [rows_of(width, bf16), rows_of(feed, bf16)],
        [],
        (cotangent, to_pm, down_weight),
        scalars=False,
    )

    r1, y, hp, n2, act, dp, dm, dr1, dh, back, mg = call(
        functools.partial(core_kernel, fchunk=256, hops=hops, blocks=blocks), "core", blocks,
        [
            rm(clamp), whole(to_pm), tok(width), tok(feed), tok(hidden), tok(hidden, later), tok(hidden),
            tok(hidden, later), tok(hidden, before), whole(other),
            *[whole(f) for f in forward], whole(out_weight), whole(gain2), whole(up_weight),
        ],
        [
            rows_of(width, f32, kept=pltpu.HBM), rows_of(hidden, bf16), rows_of(hidden, bf16),
            rows_of(width, bf16), rows_of(feed, bf16), rows_of(feed, bf16), rows_of(width, bf16),
            rows_of(width, f32, kept=pltpu.HBM),
            rows_of(hidden, bf16),
            (shape((R, hidden)), fixed((R, hidden))), (shape((R, width)), fixed((R, width))),
        ],
        [
            pltpu.VMEM((R, hidden), f32),
            pltpu.VMEM((R, hidden), jnp.int32),
            pltpu.VMEM((R, hidden), f32),
            pltpu.VMEM((m, width), f32),
            pltpu.VMEM((m, hidden), bf16),
            pltpu.VMEM((m, hidden), bf16),
            pltpu.VMEM((m, hidden), bf16),
        ],
        (
            scal, inputs, to_pm, gl, da, zl, zl, kh, kh, zl, other, *forward, far(out_weight), gain2, up_weight,
        ),
    )

    order = Sequence(back)
    quarter = feed // 4

    def ffn_grads(pick, *beside):
        half = lambda s: s[1] if pick == 0 else 1 - s[1]
        a, d, *beside = order.after(act, dp, *beside)
        (piece,) = call(
            functools.partial(ffn_grad_kernel, pick=pick), "ffn_grad", 2,
            [
                pl.BlockSpec((tokens, quarter), lambda i, s: (0, half(s) * 2 + i)), whole(gl),
                pl.BlockSpec((tokens, width // 2), lambda i, s: (0, half(s))),
                pl.BlockSpec((tokens, feed // 2), lambda i, s: (0, i)),
            ],
            [(shape((SLOTS // 2 * PIECE1, width), bf16), fixed((SLOTS // 2 * PIECE1, width)))],
            [],
            (scal, a, gl, n2, d),
            much=pick == 0,
        )
        return order.did(piece), beside

    def gate_grads(pick):
        half = lambda s: s[1] if pick == 0 else 1 - s[1]
        z, h = order.after(dkz, dkh)
        (piece,) = call(
            functools.partial(gate_grad_kernel, pick=pick), "gate_grad", 1,
            [
                pl.BlockSpec((tokens, width // 2), lambda i, s: (0, half(s))),
                whole(z), whole(h),
                pl.BlockSpec((tokens, hidden // 2), lambda i, s: (0, half(s))), whole(dm),
            ],
            [(shape((SLOTS // 2 * PIECE2, width), bf16), fixed((SLOTS // 2 * PIECE2, width)))],
            [],
            (scal, c, z, h, y, dm),
            much=pick == 0,
        )
        return order.did(piece)

    fother = flat_permute(back, core_pairs())
    lower = jnp.where(core == 0, back, fother)
    upper = jnp.where(core == 0, fother, back)
    message = jnp.concatenate([decay, lower + first[:R] * upper], 0).astype(bf16)
    backward = [chip_shift(order.did(message), -k) for k in range(1, chips)]
    send1, _ = ffn_grads(1)
    chunk1 = Halving(order, send1)
    chunk1.keep, backward = ffn_grads(0, *backward)
    chunk1.step()

    dkz, dkh, edge_dc, bias_part = call(
        functools.partial(gate_kernel, blocks=blocks, hops=hops), "gates", blocks,
        [
            rtok(hidden), rtok(hidden), rtok(hidden), rtok(hidden),
            whole(other), whole(fother), *[whole(f) for f in backward],
            whole(gate_weight), whole(cand_weight), ORDER,
        ],
        [
            rows_of(hidden, bf16, rtok), rows_of(hidden, bf16, rtok),
            (shape((4 * R, width), bf16), fixed((4 * R, width))),
            (shape((R, hidden)), fixed((R, hidden))),
        ],
        [pltpu.VMEM((R, hidden), f32)],
        (
            scal, dh, zl, kh, hp, other, fother, *backward, gate_weight, cand_weight, order.token,
        ),
    )
    order.did(bias_part)
    after = passed_along(edge_dc[: margin * R], "seq", -1)
    send2 = gate_grads(1)
    chunk2 = Halving(order, send2)
    (output,) = call(
        output_kernel, "output", blocks,
        [tok(width), tok(feed), whole(to_rm), whole(down_weight)],
        [(shape((rows, span, width), bf16), rm(clamp))],
        [],
        (far(r1), order.after(act), to_rm, down_weight),
        scalars=False,
    )
    order.did(output)
    chunk1.step()
    chunk2.keep = gate_grads(0)
    (after,) = chunk2.step(after)
    input_grad, sums = call(
        functools.partial(tail_kernel, blocks=blocks), "tail", 2 * blocks,
        [
            rm(late), tok(width, late), tok(hidden), tok(hidden), whole(to_pm), whole(to_rm),
            whole(edge), whole(after), whole(gain1), whole(conv_weight), whole(gate_weight),
            whole(cand_weight),
        ],
        [
            (shape((rows, span, width), bf16), rm(late)),
            (shape(((taps + 1) * R, width)), fixed(((taps + 1) * R, width))),
        ],
        [
            pltpu.VMEM((margin * R + m, width), f32),
            pltpu.VMEM((margin * R + tokens, width), f32),
        ],
        (
            far(inputs), far(dr1), order.after(dkz), dkh, far(to_pm), far(to_rm), edge, after,
            far(gain1), far(conv_weight), far(gate_weight), far(cand_weight),
        ),
        scalars=False,
    )
    order.did(sums)
    small = jnp.concatenate(
        [
            sums.reshape(taps + 1, R, width).sum(1),
            mg.sum(0, keepdims=True),
            bias_part.sum(0).reshape(hidden // width, width),
        ],
        0,
    )

    plan1 = ((0, feed // SLOTS, 1), (1, width // SLOTS, feed // width))
    shapes1 = ((feed, width), (width, feed))
    plan2 = (
        (0, width // SLOTS, hidden // width),
        (1, width // SLOTS, hidden // width),
        (2, hidden // SLOTS, 1),
    )
    shapes2 = ((width, hidden), (width, hidden), (hidden, width))
    held1, held2 = (), ()

    def spread1(src, mate, flip):
        nonlocal held1
        src = order.after(src)
        held1 = spread(scal, src, held1, mate, flip, PIECE1, plan1, shapes1, "spread_ffn")
        order.did(held1[0])

    def spread2(src, mate, flip):
        nonlocal held2
        src = order.after(src)
        held2 = spread(scal, src, held2, mate, flip, PIECE2, plan2, shapes2, "spread_gates")
        order.did(held2[0])

    for chunk in (chunk1, chunk2, chunk1, chunk1, chunk2, chunk1, chunk2, chunk1):
        chunk.step()
    chunk2.ride = small
    chunk2.step()
    chunk2.step()
    chunk1.step()
    spread1(chunk1.total, 0, 0)
    chunk2.step()
    spread1(chunk1.theirs, 1, 0)
    chunk2.step()
    chunk1.step()
    spread1(chunk1.rest, 0, 1)
    spread2(chunk2.total, 0, 0)
    spread1(chunk1.their_rest, 1, 1)
    spread2(chunk2.theirs, 1, 0)
    chunk2.step()
    spread2(chunk2.rest, 0, 1)
    chunk2.their_rest = order.after(chunk2.their_rest)
    *held2, norm_sum, conv_sum, mlp_sum, bias_sum = last_spread(
        scal, chunk2, held2, PIECE2, plan2, shapes2, taps, hidden
    )
    return (
        output,
        input_grad,
        norm_sum.reshape(width),
        conv_sum,
        held2[0],
        bias_sum.reshape(hidden),
        held2[1],
        held2[2],
        mlp_sum.reshape(width),
        held1[1],
        held1[0],
    )


def solution(mesh):
    sharded = P("row", "seq", None)
    in_specs = (sharded, P("row")) + (P(),) * 9 + (sharded,)
    out_specs = (sharded, sharded) + (P(),) * 9
    return jax.shard_map(
        per_device, mesh=mesh, in_specs=in_specs, out_specs=out_specs, check_vma=False
    )
```

```python
import functools

import jax
import jax.numpy as jnp
import numpy as np
from jax import lax
from jax.experimental import pallas as pl
from jax.experimental.pallas import tpu as pltpu
from jax.sharding import PartitionSpec as P

epsilon = 1e-06
f32 = jnp.float32
bf16 = jnp.bfloat16
R = 8
PERM = 256
SCALARS = 4
SLOTS = 32
PIECE1 = 128
PIECE2 = 96


def nn(a, b):
    return lax.dot_general(a, b, (((1,), (0,)), ((), ())), preferred_element_type=f32)


def nt(a, b):
    return lax.dot_general(a, b, (((1,), (1,)), ((), ())), preferred_element_type=f32)


def tn(a, b):
    return lax.dot_general(a, b, (((0,), (0,)), ((), ())), preferred_element_type=f32)


def token_order():
    out = np.arange(PERM)
    source = (out % R) * (PERM // R) + out // R
    to_pm = np.zeros((PERM, PERM), np.float32)
    to_pm[out, source] = 1
    return jnp.asarray(to_pm, bf16), jnp.asarray(to_pm.T, bf16)


def position_major(perm, block):
    span = PERM // R
    parts = []
    for s in range(block.shape[1] // span):
        part = block[:, s * span : (s + 1) * span, :].reshape(PERM, block.shape[2])
        parts.append(nn(perm, part))
    return parts[0] if len(parts) == 1 else jnp.concatenate(parts, 0)


def row_major(perm, tokens):
    span = PERM // R
    parts = []
    for s in range(tokens.shape[0] // PERM):
        part = nn(perm, tokens[s * PERM : (s + 1) * PERM]).astype(bf16)
        parts.append(part.reshape(R, span, tokens.shape[1]))
    return parts[0] if len(parts) == 1 else jnp.concatenate(parts, 1)


def eight(t):
    return pl.ds(pl.multiple_of(t * R, R), R)


def sixteen(t):
    return pl.ds(pl.multiple_of(t * 2 * R, 2 * R), 2 * R)


def normed_edge(edge, gain):
    e = edge.astype(f32)
    inv = lax.rsqrt(jnp.mean(e * e, -1, keepdims=True) + epsilon)
    return (e * inv * gain).astype(bf16).astype(f32)


def set_limits(scal, limit):
    row = lax.broadcasted_iota(jnp.int32, limit.shape, 0)
    value = jnp.zeros(limit.shape, jnp.int32)
    for r in range(R):
        value = jnp.where(row == r, scal[SCALARS + r], value)
    limit[...] = value


def halves(ref, pair):
    both = ref[sixteen(pair), :].astype(f32)
    return both[:R], both[R:]


def norm_kernel(x, perm, gain, u_out):
    xp = position_major(perm[...], x[...])
    inv = lax.rsqrt(jnp.mean(xp * xp, -1, keepdims=True) + epsilon)
    u_out[...] = (xp * inv * gain[...]).astype(bf16)


def front_kernel(scal, u, edge, gain, convw, wg, bias, wc, c_out, zl_out, kh_out, ends, ext, state, limit):
    step = pl.program_id(0)
    m = u.shape[0]
    tb = m // R
    halo = edge.shape[0]
    taps = convw.shape[0]

    @pl.when(step == 0)
    def _():
        set_limits(scal, limit)
        ext[0:halo, :] = normed_edge(edge[...], gain[...])
        state[0:R, :] = jnp.ones((R, state.shape[1]), f32)
        state[R:, :] = jnp.zeros((R, state.shape[1]), f32)

    ext[halo:, :] = u[...].astype(f32)
    conv = convw[0:1, :] * ext[halo:, :]
    for k in range(1, taps):
        lo = halo - k * R
        conv = conv + convw[k : k + 1, :] * ext[lo : lo + m, :]
    ext[0:halo, :] = ext[m : m + halo, :]
    cb = conv.astype(bf16)
    c_out[...] = cb
    kz = nn(cb, wg[...]) + bias[...]
    zs = 1.0 / (1.0 + jnp.exp(-kz))
    width = zs.shape[1]
    zs = zs.reshape(tb, R, width)
    pos = scal[0] + step * tb + lax.broadcasted_iota(jnp.int32, (tb, R, width), 0)
    zl_out[...] = jnp.where(pos < limit[...][None], zs, 0.0).reshape(m, width).astype(bf16)
    kh_out[...] = nn(cb, wc[...]).astype(bf16)

    def body(u, carry):
        prod, h = carry
        za, zb = halves(zl_out, u)
        ka, kb = halves(kh_out, u)
        a = 1.0 - za
        b = 1.0 - zb
        return prod * (a * b), (h * a + za * ka) * b + zb * kb

    prod, h = lax.fori_loop(0, tb // 2, body, (state[0:R, :], state[R:, :]), unroll=4)
    state[0:R, :] = prod
    state[R:, :] = h
    ends[0:R, :] = prod
    ends[R:, :] = h


def gelu_parts(p):
    k0 = 0.7978845608028654
    inner = p * (k0 + (k0 * 0.044715) * (p * p))
    th = jnp.tanh(inner)
    ht = 0.5 + 0.5 * th
    return p * ht, ht + (1.0 - th * th) * (1.5 * inner - k0 * p)


def da_kernel(g, perm, wd, gl_out, da_out):
    gl = position_major(perm[...], g[...]).astype(bf16)
    gl_out[...] = gl
    da_out[...] = nt(gl, wd[...]).astype(bf16)


def core_kernel(scal, x, perm, gl, da, zl, zl_next, kh, kh_next, zl_before, other, *refs, fchunk, hops, blocks):
    msgs = refs[:hops]
    wo, mgain, wu = refs[hops : hops + 3]
    r1_out, y_out, hp_out, n2_out, act_out, dp_out, dm_out, dr1_out, dh_out, back, mg = refs[hops + 3 : hops + 14]
    state, limit, run, acc, ys, hps, dhs = refs[hops + 14 :]
    step = pl.program_id(0)
    tb = x.shape[1]
    m = tb * R
    width, feed = wu.shape
    hidden = wo.shape[0]
    first = scal[0] + step * tb

    def scan_pair(zs, ks, start, u, h):
        t = u * 2
        za, zb = halves(zs, u)
        ka, kb = halves(ks, u)
        ha = h - za * h + za * ka
        hb = ha - zb * ha + zb * kb
        hps[sixteen(u), :] = jnp.concatenate([h, ha], 0).astype(bf16)
        ya = jnp.where(start + t < limit[...], ha, 0.0)
        yb = jnp.where(start + t + 1 < limit[...], hb, 0.0)
        ys[sixteen(u), :] = jnp.concatenate([ya, yb], 0).astype(bf16)
        return hb

    def adjoint_pair(zs, ds, u, prod, total):
        za, zb = halves(zs, u)
        da, db = halves(ds, u)
        pa = prod - za * prod
        pb = pa - zb * pa
        return pb, total + (pa * da + pb * db)

    @pl.when(step == 0)
    def _():
        set_limits(scal, limit)
        h = jnp.zeros((R, hidden), f32)
        for msg in reversed(msgs):
            both = msg[...].astype(f32)
            h = jnp.exp(both[0:R, :]) * h + both[R:, :]
        h = jnp.where(scal[1] == 1, other[0:R, :] * h + other[R:, :], h)
        run[...] = jnp.ones((R, hidden), f32)
        back[...] = jnp.zeros(back.shape, f32)
        mg[...] = jnp.zeros(mg.shape, f32)
        dhs[...] = jnp.zeros(dhs.shape, bf16)
        state[...] = lax.fori_loop(0, tb // 2, lambda u, h: scan_pair(zl, kh, scal[0], u, h), h, unroll=2)

    hp_out[...] = hps[...]
    y = ys[...]
    y_out[...] = y
    r1 = position_major(perm[...], x[...]) + nn(y, wo[...])
    r1_out[...] = r1
    inv = lax.rsqrt(jnp.mean(r1 * r1, -1, keepdims=True) + epsilon)
    n2 = (r1 * inv * mgain[...]).astype(bf16)
    n2_out[...] = n2
    chunks = feed // fchunk
    pairs = tb // 2 // chunks
    for f in range(chunks):
        cols = slice(f * fchunk, (f + 1) * fchunk)
        a, slope = gelu_parts(nn(n2, wu[:, cols]).astype(bf16))
        act_out[:, cols] = a
        dpb = da[:, cols] * slope
        dp_out[:, cols] = dpb
        part = nt(dpb, wu[:, cols])
        acc[...] = acc[...] + part if f else part
        h, prod, total = state[...], run[...], back[...]
        for u in range(f * pairs, (f + 1) * pairs):
            h = scan_pair(zl_next, kh_next, first + tb, u, h)
            prod, total = adjoint_pair(zl_before, dhs, u, prod, total)
        state[...] = h
        run[...] = jnp.where(step == 0, 1.0, prod)
        back[...] = total
    dn2 = acc[...]
    r1 = r1_out[...]
    mg[...] += jnp.sum((dn2 * r1 * inv).reshape(tb, R, width), 0)
    s = mgain[...] * dn2
    mean = jnp.mean(s * r1, -1, keepdims=True)
    dr1 = gl[...].astype(f32) + inv * (s - r1 * (inv * inv * mean))
    dr1_out[...] = dr1
    dm = dr1.astype(bf16)
    dm_out[...] = dm
    dh = nt(dm, wo[...]).reshape(tb, R, hidden)
    pos = first + lax.broadcasted_iota(jnp.int32, (tb, R, hidden), 0)
    dh = jnp.where(pos < limit[...][None], dh, 0.0).reshape(m, hidden).astype(bf16)
    dh_out[...] = dh
    dhs[...] = dh

    @pl.when(step == blocks - 1)
    def _():
        carry = lax.fori_loop(
            0, tb // 2, lambda u, carry: adjoint_pair(zl, dhs, u, *carry), (run[...], back[...]), unroll=4
        )
        back[...] = carry[1]


def put_rows(dst, sel, piece, at, rows, part):
    for i in range(SLOTS // 2):
        pos = pl.multiple_of((i ^ sel) * piece + at, 16)
        dst[pl.ds(pos, rows), :] = part[i * rows : (i + 1) * rows]


def ffn_grad_kernel(scal, act, gl, n2, dp, dst, *, pick):
    step = pl.program_id(0)
    sel = scal[2 + pick]
    width = gl.shape[1]
    rows1 = act.shape[1] * 4 // SLOTS
    rows2 = n2.shape[1] * 2 // SLOTS
    part = tn(act[...], gl[...]).astype(bf16)
    per = act.shape[1] // rows1
    for i in range(per):
        pos = ((step * per + i) ^ sel) * PIECE1
        dst[pl.ds(pl.multiple_of(pos, 16), rows1), :] = part[i * rows1 : (i + 1) * rows1]
    columns = dp.shape[1] // width
    for q in range(columns):
        part = tn(n2[...], dp[:, q * width : (q + 1) * width]).astype(bf16)
        put_rows(dst, sel, PIECE1, rows1 + (step * columns + q) * rows2, rows2, part)


def gate_grad_kernel(scal, c, dkz, dkh, y, dm, dst, *, pick):
    sel = scal[2 + pick]
    width = dm.shape[1]
    rows = c.shape[1] * 2 // SLOTS
    at = 0
    for grads in (dkz, dkh):
        for q in range(grads.shape[1] // width):
            part = tn(c[...], grads[:, q * width : (q + 1) * width]).astype(bf16)
            put_rows(dst, sel, PIECE2, at, rows, part)
            at += rows
    put_rows(dst, sel, PIECE2, at, y.shape[1] * 2 // SLOTS, tn(y[...], dm[...]).astype(bf16))


def gate_kernel(scal, dh, zl, kh, hp, other, fother, *refs, blocks, hops):
    msgs = refs[:hops]
    wg, wc = refs[hops : hops + 2]
    dkz, dkh, edge_out, bias_out = refs[hops + 3 : hops + 7]
    state = refs[hops + 7]
    step = pl.program_id(0)
    m = dh.shape[0]
    tb = m // R
    block = blocks - 1 - step

    @pl.when(step == 0)
    def _():
        mm = jnp.zeros(state.shape, f32)
        for msg in reversed(msgs):
            both = msg[...].astype(f32)
            mm = jnp.exp(both[0:R, :]) * mm + both[R:, :]
        state[...] = jnp.where(scal[1] == 0, fother[...] + other[0:R, :] * mm, mm)
        bias_out[...] = jnp.zeros(bias_out.shape, f32)

    def body(u, carry):
        mm, bias = carry
        w = tb // 2 - 1 - u
        ha, hb = halves(hp, w)
        za, zb = halves(zl, w)
        da, db = halves(dh, w)
        ka, kb = halves(kh, w)
        lam = db + mm
        sb = lam * zb
        mm = lam - sb
        kb = (sb - sb * zb) * (kb - hb)
        lam = da + mm
        sa = lam * za
        mm = lam - sa
        ka = (sa - sa * za) * (ka - ha)
        kk = jnp.concatenate([ka, kb], 0).astype(bf16)
        dkz[sixteen(w), :] = kk
        dkh[sixteen(w), :] = jnp.concatenate([sa, sb], 0).astype(bf16)
        kf = kk.astype(f32)
        return mm, bias + kf[:R, :] + kf[R:, :]

    mm, bias = lax.fori_loop(0, tb // 2, body, (state[...], bias_out[...]), unroll=2)
    state[...] = mm
    bias_out[...] = bias

    @pl.when(block == 0)
    def _():
        span = edge_out.shape[0]
        edge_out[...] = (nt(dkz[0:span, :], wg[...]) + nt(dkh[0:span, :], wc[...])).astype(bf16)


def tail_kernel(x, dr1, dkz, dkh, pm, back_pm, edge, after, gain, convw, wg, wc, grad, sums, uext, dext, *, blocks):
    step = pl.program_id(0)
    tb = x.shape[1]
    m = tb * R
    halo = edge.shape[0]
    taps = convw.shape[0]
    width = gain.shape[1]

    @pl.when(step == 0)
    def _():
        uext[0:halo, :] = normed_edge(edge[...], gain[...])
        dext[blocks * m :, :] = after[...].astype(f32)
        sums[...] = jnp.zeros(sums.shape, f32)

    @pl.when(step < blocks)
    def _():
        rows = pl.ds(pl.multiple_of(step * m, m), m)
        dext[rows, :] = nt(dkz[...], wg[...]) + nt(dkh[...], wc[...])

    @pl.when(step >= blocks)
    def _():
        xp = position_major(pm[...], x[...])
        inv = lax.rsqrt(jnp.mean(xp * xp, -1, keepdims=True) + epsilon)
        xn = xp * inv
        uext[halo:, :] = (xn * gain[...]).astype(bf16).astype(f32)
        start = (step - blocks) * m
        here = dext[pl.ds(pl.multiple_of(start, R), m), :]
        du = convw[0:1, :] * here
        for k in range(taps):
            lo = halo - k * R
            part = (here * uext[lo : lo + m, :]).reshape(tb, R, width)
            sums[(k + 1) * R : (k + 2) * R, :] += jnp.sum(part, 0)
            if k:
                du = du + convw[k : k + 1, :] * dext[pl.ds(pl.multiple_of(start + k * R, R), m), :]
        uext[0:halo, :] = uext[m : m + halo, :]
        sums[0:R, :] += jnp.sum((du * xn).reshape(tb, R, width), 0)
        s1 = gain[...] * du
        mean = jnp.mean(s1 * xn, -1, keepdims=True)
        gin = dr1[...] + inv * (s1 - xn * mean)
        grad[...] = row_major(back_pm[...], gin.astype(bf16))


def output_kernel(r1, act, perm, wd, out):
    total = r1[...] + nn(act[...], wd[...])
    out[...] = row_major(perm[...], total.astype(bf16))


def spread_kernel(scal, src, *refs, piece, plan, mate):
    low = scal[2 + mate] & 7
    for a in range(8):
        base = (a ^ low) * piece
        at = 0
        for out, rows, columns in plan:
            ref = refs[len(refs) - len(plan) + out]
            for q in range(columns):
                width = src.shape[1]
                part = src[pl.ds(pl.multiple_of(base + at, 16), rows), :].astype(f32)
                ref[a * rows : (a + 1) * rows, q * width : (q + 1) * width] = part
                at += rows


def last_spread_kernel(scal, src, ride, rest, theirs, *refs, piece, plan, taps):
    norm, conv, mlp, bias = refs[-4:]
    spread_kernel(scal, src, *refs[:-4], piece=piece, plan=plan, mate=1)
    tail = src.shape[0] - 2 * R
    total = ride[...]
    for rows in (rest[...], theirs[...], src[tail:, :]):
        both = rows.astype(f32)
        total = total + (both[:R] + both[R:])
    norm[...] = total[0:1]
    conv[...] = total[1 : taps + 1]
    mlp[...] = total[taps + 1 : taps + 2]
    width = total.shape[1]
    for i in range(bias.shape[1] // width):
        bias[:, i * width : (i + 1) * width] = total[taps + 2 + i : taps + 3 + i]


def last_spread(scal, chunk, held, piece, plan, shapes, taps, hidden):
    src = chunk.their_rest
    width = src.shape[1]
    rows = 2 * R
    tail = pl.BlockSpec((rows, width), lambda g, s: (src.shape[0] // rows - 1, 0))
    small = ((1, width), (taps, width), (1, width), (1, hidden))

    def block(g, s):
        return ((s[1] ^ 1) * 2 + ((s[3] >> 3) ^ 1), 0)

    return pl.pallas_call(
        functools.partial(last_spread_kernel, piece=piece, plan=plan, taps=taps),
        grid_spec=pltpu.PrefetchScalarGridSpec(
            num_scalar_prefetch=1,
            grid=(1,),
            in_specs=[whole(src), whole(chunk.ride), tail, tail] + [ORDER] * len(held),
            out_specs=[pl.BlockSpec((dims[0] // 4, dims[1]), block) for dims in shapes]
            + [pl.BlockSpec(dims, lambda g, s: (0, 0)) for dims in small],
        ),
        out_shape=[pltpu.HBM(dims, f32) for dims in shapes] + [shape(dims) for dims in small],
        input_output_aliases={5 + k: k for k in range(len(held))},
        compiler_params=params(16),
        cost_estimate=MUCH,
        name="spread_last",
    )(scal, src, chunk.ride, chunk.rest, chunk.theirs, *held)


def spread(scal, src, held, mate, flip, piece, plan, shapes, name):
    def block(g, s):
        return ((s[1] ^ mate) * 2 + ((s[2 + mate] >> 3) ^ flip), 0)

    count = len(held)
    return pl.pallas_call(
        functools.partial(spread_kernel, piece=piece, plan=plan, mate=mate),
        grid_spec=pltpu.PrefetchScalarGridSpec(
            num_scalar_prefetch=1,
            grid=(1,),
            in_specs=[whole(src)] + [ORDER] * count,
            out_specs=[pl.BlockSpec((dims[0] // 4, dims[1]), block) for dims in shapes],
        ),
        out_shape=[pltpu.HBM(dims, f32) for dims in shapes],
        input_output_aliases={2 + k: k for k in range(count)},
        compiler_params=params(16),
        cost_estimate=MUCH,
        name=name,
    )(scal, src, *held)


def params(mib):
    return pltpu.CompilerParams(
        dimension_semantics=("arbitrary",), vmem_limit_bytes=mib * 1024 * 1024
    )


def shape(dims, kind=f32):
    return jax.ShapeDtypeStruct(dims, kind)


LITTLE = pl.CostEstimate(flops=1024, bytes_accessed=1024, transcendentals=0)
MUCH = pl.CostEstimate(flops=3 * 10**10, bytes_accessed=1024, transcendentals=0)
ORDER = pl.BlockSpec(memory_space=pl.ANY)


def far(array):
    return pltpu.with_memory_space_constraint(array, pltpu.HBM)


def whole(array):
    zeros = (0,) * array.ndim
    return pl.BlockSpec(array.shape, lambda *a: zeros, pipeline_mode=pl.Buffered(1))


def passed_along(value, axis, steps):
    count = lax.axis_size(axis)
    leading, last = (max(0, -steps), min(count, count - steps))
    return lax.ppermute(value, axis, [(source, source + steps) for source in range(leading, last)])


def flat_permute(value, pairs):
    return lax.ppermute(value, ("seq", "row"), pairs)


def stage_bits():
    row_bits = lax.axis_size("row").bit_length() - 1
    seq_bits = lax.axis_size("seq").bit_length() - 1
    plane = list(range(row_bits))
    line = [row_bits + 1 + z for z in range(seq_bits - 1)]
    cut = row_bits // 2
    return (plane + line, plane[cut:] + plane[:cut] + line[::-1])


def slot_of(flat, bits):
    slot = 0
    for k in range(4):
        slot = slot * 2 + ((flat >> bits[k]) & 1)
    return slot


def halving_pairs(stage):
    row_bits = lax.axis_size("row").bit_length() - 1
    orders = stage_bits()
    devices = lax.axis_size("row") * lax.axis_size("seq")
    return [(d, d ^ (1 << orders[(d >> row_bits) & 1][stage])) for d in range(devices)]


def core_pairs():
    row_bits = lax.axis_size("row").bit_length() - 1
    devices = lax.axis_size("row") * lax.axis_size("seq")
    return [(d, d ^ (1 << row_bits)) for d in range(devices)]


def added(a, b):
    return (a.astype(f32) + b.astype(f32)).astype(bf16)


class Sequence:
    def __init__(self, token):
        self.token = token

    def after(self, *arrays):
        *arrays, _ = lax.optimization_barrier((*arrays, self.token))
        return arrays[0] if len(arrays) == 1 else arrays

    def did(self, array):
        self.token = array
        return array


def split(value):
    high = lax.reduce_precision(value, 8, 7)
    return [high.astype(bf16), (value - high).astype(bf16)]


def join_kernel(mine, recv, ride, out, ride_out):
    rows = mine.shape[0] - 2 * R
    out[0:rows, :] = mine[0:rows, :]
    out[rows : 2 * rows, :] = recv[0:rows, :]
    parts = recv[rows:, :].astype(f32)
    total = ride[...] + (parts[:R] + parts[R:])
    ride_out[...] = total
    high = total.astype(bf16).astype(f32)
    out[2 * rows :, :] = jnp.concatenate([high, total - high], 0).astype(bf16)


def chain_kernel(mine, recv, out):
    rows = mine.shape[0]
    out[0:rows, :] = mine[...]
    out[rows:, :] = recv[...]


def chained(mine, recv):
    rows, width = mine.shape
    return pl.pallas_call(
        chain_kernel,
        in_specs=[pl.BlockSpec(memory_space=pltpu.VMEM)] * 2,
        out_specs=pl.BlockSpec(memory_space=pltpu.VMEM),
        out_shape=shape((2 * rows, width), bf16),
        compiler_params=pltpu.CompilerParams(vmem_limit_bytes=16 * 1024 * 1024),
        cost_estimate=MUCH,
        name="chain",
    )(mine, recv)


def joined(mine, recv, ride, estimate):
    rows, width = mine.shape
    return pl.pallas_call(
        join_kernel,
        in_specs=[pl.BlockSpec(memory_space=pltpu.VMEM)] * 3,
        out_specs=[pl.BlockSpec(memory_space=pltpu.VMEM)] * 2,
        out_shape=[shape((2 * rows - 2 * R, width), bf16), shape(ride.shape)],
        compiler_params=pltpu.CompilerParams(vmem_limit_bytes=16 * 1024 * 1024),
        cost_estimate=estimate,
        name="join",
    )(mine, recv, ride)


class Halving:
    def __init__(self, seq, send):
        self.seq = seq
        self.recv = flat_permute(send, core_pairs())
        self.stage = 0
        self.ride = None

    def riders(self):
        return [] if self.ride is None else split(self.ride)

    def step(self, *beside):
        k = self.stage
        self.stage += 1
        stages = len(stage_bits()[0])
        recv, *beside = self.seq.after(self.recv, *beside) if beside else (self.seq.after(self.recv),)
        if k < 4:
            half = self.keep.shape[0] // 2
            send = self.seq.did(added(self.keep[half:], recv[half:]))
            self.recv = flat_permute(send, halving_pairs(k))
            self.keep = added(self.keep[:half], recv[:half])
        elif k == 4:
            total = added(self.keep, recv)
            for extra in range(4, stages):
                total = added(total, flat_permute(total, halving_pairs(extra)))
                if self.ride is not None:
                    self.ride = self.ride + flat_permute(self.ride, halving_pairs(extra))
            self.rows = total.shape[0]
            self.total = self.seq.did(jnp.concatenate([total] + self.riders(), 0))
            self.recv = flat_permute(self.total, halving_pairs(3))
        elif k < 8:
            rows = self.rows
            self.rows = 2 * rows
            if self.ride is None:
                self.total = self.seq.did(chained(self.total, recv))
            else:
                self.total, self.ride = joined(
                    self.total, recv, self.ride, LITTLE if k == 5 else MUCH
                )
                self.seq.did(self.total)
            self.recv = flat_permute(self.total, halving_pairs(7 - k))
            if k == 7:
                self.theirs = flat_permute(self.total, core_pairs())
        else:
            self.rest = recv
            self.their_rest = flat_permute(recv, core_pairs())
        return beside


def chip_shift(value, steps):
    return passed_along(value, "seq", 2 * steps)


def per_device(
    inputs,
    lengths,
    norm_gain,
    conv_weight,
    gate_weight,
    gate_bias,
    cand_weight,
    out_weight,
    mlp_gain,
    up_weight,
    down_weight,
    cotangent,
):
    rows, span, width = inputs.shape
    hidden = gate_weight.shape[1]
    feed = up_weight.shape[1]
    taps = conv_weight.shape[0]
    margin = taps - 1
    tokens = rows * span
    tb = 32
    blocks = span // tb
    m = tb * R
    seq = lax.axis_index("seq")
    core = seq & 1
    chips = lax.axis_size("seq") // 2
    hops = chips - 1
    flat = seq * lax.axis_size("row") + lax.axis_index("row")
    slots = [slot_of(flat, bits) for bits in stage_bits()]
    here = jnp.where(core == 0, slots[0], slots[1])
    mate = jnp.where(core == 0, slots[1], slots[0])
    scal = jnp.concatenate([jnp.stack([seq * span, core, here, mate]).astype(jnp.int32), lengths])
    gain1 = norm_gain.reshape(1, width)
    gain2 = mlp_gain.reshape(1, width)
    bias = gate_bias.reshape(1, hidden)
    to_pm, to_rm = token_order()

    edge = inputs[:, span - margin :, :].swapaxes(0, 1).reshape(margin * rows, width)
    edge = passed_along(edge, "seq", 1)

    last = blocks - 1
    clamp = lambda i: jnp.minimum(i, last)
    late = lambda i: jnp.maximum(i - blocks, 0)
    later = lambda i: jnp.minimum(i + 1, last)
    before = lambda i: jnp.maximum(i - 1, 0)

    def rm(index):
        return pl.BlockSpec((rows, tb, width), lambda i, *s: (0, index(i), 0))

    def tok(w, index=clamp):
        return pl.BlockSpec((m, w), lambda i, *s: (index(i), 0))

    def rtok(w):
        return tok(w, lambda i: last - clamp(i))

    def fixed(dims):
        zeros = (0,) * len(dims)
        return pl.BlockSpec(dims, lambda i, *s: zeros)

    def call(kernel, name, grid, ins, outs, scratch, operands, scalars=True, much=False):
        spec = pltpu.PrefetchScalarGridSpec(
            num_scalar_prefetch=int(scalars),
            grid=(grid,),
            in_specs=ins,
            out_specs=[o[1] for o in outs],
            scratch_shapes=scratch,
        )
        return pl.pallas_call(
            kernel,
            grid_spec=spec,
            out_shape=[o[0] for o in outs],
            compiler_params=params(16),
            cost_estimate=MUCH if much else LITTLE,
            name=name,
        )(*operands)

    def rows_of(w, kind, spec=tok, kept=shape):
        return kept((tokens, w), kind), spec(w)

    (normed,) = call(
        norm_kernel, "norm", blocks,
        [rm(clamp), whole(to_pm), whole(gain1)],
        [rows_of(width, bf16)],
        [],
        (far(inputs), far(to_pm), far(gain1)),
        scalars=False,
    )
    edge, normed = lax.optimization_barrier((edge, normed))
    c, zl, kh, ends = call(
        front_kernel, "front", blocks,
        [
            tok(width), whole(edge), whole(gain1), whole(conv_weight),
            whole(gate_weight), whole(bias), whole(cand_weight),
        ],
        [
            rows_of(width, bf16), rows_of(hidden, bf16), rows_of(hidden, bf16),
            (shape((2 * R, hidden)), fixed((2 * R, hidden))),
        ],
        [
            pltpu.VMEM((margin * R + m, width), f32),
            pltpu.VMEM((2 * R, hidden), f32),
            pltpu.VMEM((R, hidden), jnp.int32),
        ],
        (
            scal, normed, edge, far(gain1), far(conv_weight), gate_weight, far(bias),
            cand_weight,
        ),
    )

    other = flat_permute(ends, core_pairs())
    first = jnp.where(core == 0, ends, other)
    second = jnp.where(core == 0, other, ends)
    decay = jnp.log(jnp.maximum(ends[:R] * other[:R], 1e-37))
    message = jnp.concatenate([decay, second[:R] * first[R:] + second[R:]], 0).astype(bf16)
    forward = [chip_shift(message, k) for k in range(1, chips)]

    gl, da = call(
        da_kernel, "da", blocks,
        [rm(clamp), whole(to_pm), whole(down_weight)],
        [rows_of(width, bf16), rows_of(feed, bf16)],
        [],
        (cotangent, to_pm, down_weight),
        scalars=False,
    )

    r1, y, hp, n2, act, dp, dm, dr1, dh, back, mg = call(
        functools.partial(core_kernel, fchunk=256, hops=hops, blocks=blocks), "core", blocks,
        [
            rm(clamp), whole(to_pm), tok(width), tok(feed), tok(hidden), tok(hidden, later), tok(hidden),
            tok(hidden, later), tok(hidden, before), whole(other),
            *[whole(f) for f in forward], whole(out_weight), whole(gain2), whole(up_weight),
        ],
        [
            rows_of(width, f32, kept=pltpu.HBM), rows_of(hidden, bf16), rows_of(hidden, bf16),
            rows_of(width, bf16), rows_of(feed, bf16), rows_of(feed, bf16), rows_of(width, bf16),
            rows_of(width, f32, kept=pltpu.HBM),
            rows_of(hidden, bf16),
            (shape((R, hidden)), fixed((R, hidden))), (shape((R, width)), fixed((R, width))),
        ],
        [
            pltpu.VMEM((R, hidden), f32),
            pltpu.VMEM((R, hidden), jnp.int32),
            pltpu.VMEM((R, hidden), f32),
            pltpu.VMEM((m, width), f32),
            pltpu.VMEM((m, hidden), bf16),
            pltpu.VMEM((m, hidden), bf16),
            pltpu.VMEM((m, hidden), bf16),
        ],
        (
            scal, inputs, to_pm, gl, da, zl, zl, kh, kh, zl, other, *forward, far(out_weight), gain2, up_weight,
        ),
    )

    order = Sequence(back)
    quarter = feed // 4

    def ffn_grads(pick, *beside):
        half = lambda s: s[1] if pick == 0 else 1 - s[1]
        a, d, *beside = order.after(act, dp, *beside)
        (piece,) = call(
            functools.partial(ffn_grad_kernel, pick=pick), "ffn_grad", 2,
            [
                pl.BlockSpec((tokens, quarter), lambda i, s: (0, half(s) * 2 + i)), whole(gl),
                pl.BlockSpec((tokens, width // 2), lambda i, s: (0, half(s))),
                pl.BlockSpec((tokens, feed // 2), lambda i, s: (0, i)),
            ],
            [(shape((SLOTS // 2 * PIECE1, width), bf16), fixed((SLOTS // 2 * PIECE1, width)))],
            [],
            (scal, a, gl, n2, d),
            much=pick == 0,
        )
        return order.did(piece), beside

    def gate_grads(pick):
        half = lambda s: s[1] if pick == 0 else 1 - s[1]
        z, h = order.after(dkz, dkh)
        (piece,) = call(
            functools.partial(gate_grad_kernel, pick=pick), "gate_grad", 1,
            [
                pl.BlockSpec((tokens, width // 2), lambda i, s: (0, half(s))),
                whole(z), whole(h),
                pl.BlockSpec((tokens, hidden // 2), lambda i, s: (0, half(s))), whole(dm),
            ],
            [(shape((SLOTS // 2 * PIECE2, width), bf16), fixed((SLOTS // 2 * PIECE2, width)))],
            [],
            (scal, c, z, h, y, dm),
            much=pick == 0,
        )
        return order.did(piece)

    fother = flat_permute(back, core_pairs())
    lower = jnp.where(core == 0, back, fother)
    upper = jnp.where(core == 0, fother, back)
    message = jnp.concatenate([decay, lower + first[:R] * upper], 0).astype(bf16)
    backward = [chip_shift(order.did(message), -k) for k in range(1, chips)]
    send1, _ = ffn_grads(1)
    chunk1 = Halving(order, send1)
    chunk1.keep, backward = ffn_grads(0, *backward)
    chunk1.step()

    dkz, dkh, edge_dc, bias_part = call(
        functools.partial(gate_kernel, blocks=blocks, hops=hops), "gates", blocks,
        [
            rtok(hidden), rtok(hidden), rtok(hidden), rtok(hidden),
            whole(other), whole(fother), *[whole(f) for f in backward],
            whole(gate_weight), whole(cand_weight), ORDER,
        ],
        [
            rows_of(hidden, bf16, rtok), rows_of(hidden, bf16, rtok),
            (shape((4 * R, width), bf16), fixed((4 * R, width))),
            (shape((R, hidden)), fixed((R, hidden))),
        ],
        [pltpu.VMEM((R, hidden), f32)],
        (
            scal, dh, zl, kh, hp, other, fother, *backward, gate_weight, cand_weight, order.token,
        ),
    )
    order.did(bias_part)
    after = passed_along(edge_dc[: margin * R], "seq", -1)
    send2 = gate_grads(1)
    chunk2 = Halving(order, send2)
    (output,) = call(
        output_kernel, "output", blocks,
        [tok(width), tok(feed), whole(to_rm), whole(down_weight)],
        [(shape((rows, span, width), bf16), rm(clamp))],
        [],
        (far(r1), order.after(act), to_rm, down_weight),
        scalars=False,
    )
    order.did(output)
    chunk1.step()
    chunk2.keep = gate_grads(0)
    (after,) = chunk2.step(after)
    input_grad, sums = call(
        functools.partial(tail_kernel, blocks=blocks), "tail", 2 * blocks,
        [
            rm(late), tok(width, late), tok(hidden), tok(hidden), whole(to_pm), whole(to_rm),
            whole(edge), whole(after), whole(gain1), whole(conv_weight), whole(gate_weight),
            whole(cand_weight),
        ],
        [
            (shape((rows, span, width), bf16), rm(late)),
            (shape(((taps + 1) * R, width)), fixed(((taps + 1) * R, width))),
        ],
        [
            pltpu.VMEM((margin * R + m, width), f32),
            pltpu.VMEM((margin * R + tokens, width), f32),
        ],
        (
            far(inputs), far(dr1), order.after(dkz), dkh, far(to_pm), far(to_rm), edge, after,
            far(gain1), far(conv_weight), far(gate_weight), far(cand_weight),
        ),
        scalars=False,
    )
    order.did(sums)
    small = jnp.concatenate(
        [
            sums.reshape(taps + 1, R, width).sum(1),
            mg.sum(0, keepdims=True),
            bias_part.sum(0).reshape(hidden // width, width),
        ],
        0,
    )

    plan1 = ((0, feed // SLOTS, 1), (1, width // SLOTS, feed // width))
    shapes1 = ((feed, width), (width, feed))
    plan2 = (
        (0, width // SLOTS, hidden // width),
        (1, width // SLOTS, hidden // width),
        (2, hidden // SLOTS, 1),
    )
    shapes2 = ((width, hidden), (width, hidden), (hidden, width))
    held1, held2 = (), ()

    def spread1(src, mate, flip):
        nonlocal held1
        src = order.after(src)
        held1 = spread(scal, src, held1, mate, flip, PIECE1, plan1, shapes1, "spread_ffn")
        order.did(held1[0])

    def spread2(src, mate, flip):
        nonlocal held2
        src = order.after(src)
        held2 = spread(scal, src, held2, mate, flip, PIECE2, plan2, shapes2, "spread_gates")
        order.did(held2[0])

    chunk2.ride = small
    for chunk in (chunk1, chunk2, chunk1, chunk2, chunk1, chunk2, chunk1, chunk2):
        chunk.step()
    chunk2.step()
    chunk1.step()
    chunk2.step()
    chunk1.step()
    chunk2.step()
    spread1(chunk1.total, 0, 0)
    spread1(chunk1.theirs, 1, 0)
    chunk1.step()
    spread1(chunk1.rest, 0, 1)
    spread2(chunk2.total, 0, 0)
    spread1(chunk1.their_rest, 1, 1)
    spread2(chunk2.theirs, 1, 0)
    chunk2.step()
    spread2(chunk2.rest, 0, 1)
    chunk2.their_rest = order.after(chunk2.their_rest)
    *held2, norm_sum, conv_sum, mlp_sum, bias_sum = last_spread(
        scal, chunk2, held2, PIECE2, plan2, shapes2, taps, hidden
    )
    return (
        output,
        input_grad,
        norm_sum.reshape(width),
        conv_sum,
        held2[0],
        bias_sum.reshape(hidden),
        held2[1],
        held2[2],
        mlp_sum.reshape(width),
        held1[1],
        held1[0],
    )


def solution(mesh):
    sharded = P("row", "seq", None)
    in_specs = (sharded, P("row")) + (P(),) * 9 + (sharded,)
    out_specs = (sharded, sharded) + (P(),) * 9
    return jax.shard_map(
        per_device, mesh=mesh, in_specs=in_specs, out_specs=out_specs, check_vma=False
    )
```

```python
import functools

import jax
import jax.numpy as jnp
import numpy as np
from jax import lax
from jax.experimental import pallas as pl
from jax.experimental.pallas import tpu as pltpu
from jax.sharding import PartitionSpec as P

epsilon = 1e-06
f32 = jnp.float32
bf16 = jnp.bfloat16
R = 8
PERM = 256
SCALARS = 4
SLOTS = 32
PIECE1 = 128
PIECE2 = 96


def nn(a, b):
    return lax.dot_general(a, b, (((1,), (0,)), ((), ())), preferred_element_type=f32)


def nt(a, b):
    return lax.dot_general(a, b, (((1,), (1,)), ((), ())), preferred_element_type=f32)


def tn(a, b):
    return lax.dot_general(a, b, (((0,), (0,)), ((), ())), preferred_element_type=f32)


def token_order():
    out = np.arange(PERM)
    source = (out % R) * (PERM // R) + out // R
    to_pm = np.zeros((PERM, PERM), np.float32)
    to_pm[out, source] = 1
    return jnp.asarray(to_pm, bf16), jnp.asarray(to_pm.T, bf16)


def position_major(perm, block):
    span = PERM // R
    parts = []
    for s in range(block.shape[1] // span):
        part = block[:, s * span : (s + 1) * span, :].reshape(PERM, block.shape[2])
        parts.append(nn(perm, part))
    return parts[0] if len(parts) == 1 else jnp.concatenate(parts, 0)


def row_major(perm, tokens):
    span = PERM // R
    parts = []
    for s in range(tokens.shape[0] // PERM):
        part = nn(perm, tokens[s * PERM : (s + 1) * PERM]).astype(bf16)
        parts.append(part.reshape(R, span, tokens.shape[1]))
    return parts[0] if len(parts) == 1 else jnp.concatenate(parts, 1)


def eight(t):
    return pl.ds(pl.multiple_of(t * R, R), R)


def sixteen(t):
    return pl.ds(pl.multiple_of(t * 2 * R, 2 * R), 2 * R)


def normed_edge(edge, gain):
    e = edge.astype(f32)
    inv = lax.rsqrt(jnp.mean(e * e, -1, keepdims=True) + epsilon)
    return (e * inv * gain).astype(bf16).astype(f32)


def set_limits(scal, limit):
    row = lax.broadcasted_iota(jnp.int32, limit.shape, 0)
    value = jnp.zeros(limit.shape, jnp.int32)
    for r in range(R):
        value = jnp.where(row == r, scal[SCALARS + r], value)
    limit[...] = value


def halves(ref, pair):
    both = ref[sixteen(pair), :].astype(f32)
    return both[:R], both[R:]


def norm_kernel(x, perm, gain, u_out):
    xp = position_major(perm[...], x[...])
    inv = lax.rsqrt(jnp.mean(xp * xp, -1, keepdims=True) + epsilon)
    u_out[...] = (xp * inv * gain[...]).astype(bf16)


def front_kernel(scal, u, edge, gain, convw, wg, bias, wc, c_out, zl_out, kh_out, ends, ext, state, limit):
    step = pl.program_id(0)
    m = u.shape[0]
    tb = m // R
    halo = edge.shape[0]
    taps = convw.shape[0]

    @pl.when(step == 0)
    def _():
        set_limits(scal, limit)
        ext[0:halo, :] = normed_edge(edge[...], gain[...])
        state[0:R, :] = jnp.ones((R, state.shape[1]), f32)
        state[R:, :] = jnp.zeros((R, state.shape[1]), f32)

    ext[halo:, :] = u[...].astype(f32)
    conv = convw[0:1, :] * ext[halo:, :]
    for k in range(1, taps):
        lo = halo - k * R
        conv = conv + convw[k : k + 1, :] * ext[lo : lo + m, :]
    ext[0:halo, :] = ext[m : m + halo, :]
    cb = conv.astype(bf16)
    c_out[...] = cb
    kz = nn(cb, wg[...]) + bias[...]
    zs = 1.0 / (1.0 + jnp.exp(-kz))
    width = zs.shape[1]
    zs = zs.reshape(tb, R, width)
    pos = scal[0] + step * tb + lax.broadcasted_iota(jnp.int32, (tb, R, width), 0)
    zl_out[...] = jnp.where(pos < limit[...][None], zs, 0.0).reshape(m, width).astype(bf16)
    kh_out[...] = nn(cb, wc[...]).astype(bf16)

    def body(u, carry):
        prod, h = carry
        za, zb = halves(zl_out, u)
        ka, kb = halves(kh_out, u)
        a = 1.0 - za
        b = 1.0 - zb
        return prod * (a * b), (h * a + za * ka) * b + zb * kb

    prod, h = lax.fori_loop(0, tb // 2, body, (state[0:R, :], state[R:, :]), unroll=4)
    state[0:R, :] = prod
    state[R:, :] = h
    ends[0:R, :] = prod
    ends[R:, :] = h


def gelu_parts(p):
    k0 = 0.7978845608028654
    inner = p * (k0 + (k0 * 0.044715) * (p * p))
    th = jnp.tanh(inner)
    ht = 0.5 + 0.5 * th
    return p * ht, ht + (1.0 - th * th) * (1.5 * inner - k0 * p)


def da_kernel(g, perm, wd, gl_out, da_out):
    gl = position_major(perm[...], g[...]).astype(bf16)
    gl_out[...] = gl
    da_out[...] = nt(gl, wd[...]).astype(bf16)


def core_kernel(scal, x, perm, gl, da, zl, zl_next, kh, kh_next, zl_before, other, *refs, fchunk, hops, blocks):
    msgs = refs[:hops]
    wo, mgain, wu = refs[hops : hops + 3]
    r1_out, y_out, hp_out, n2_out, act_out, dp_out, dm_out, dr1_out, dh_out, back, mg = refs[hops + 3 : hops + 14]
    state, limit, run, acc, ys, hps, dhs = refs[hops + 14 :]
    step = pl.program_id(0)
    tb = x.shape[1]
    m = tb * R
    width, feed = wu.shape
    hidden = wo.shape[0]
    first = scal[0] + step * tb

    def scan_pair(zs, ks, start, u, h):
        t = u * 2
        za, zb = halves(zs, u)
        ka, kb = halves(ks, u)
        ha = h - za * h + za * ka
        hb = ha - zb * ha + zb * kb
        hps[sixteen(u), :] = jnp.concatenate([h, ha], 0).astype(bf16)
        ya = jnp.where(start + t < limit[...], ha, 0.0)
        yb = jnp.where(start + t + 1 < limit[...], hb, 0.0)
        ys[sixteen(u), :] = jnp.concatenate([ya, yb], 0).astype(bf16)
        return hb

    def adjoint_pair(zs, ds, u, prod, total):
        za, zb = halves(zs, u)
        da, db = halves(ds, u)
        pa = prod - za * prod
        pb = pa - zb * pa
        return pb, total + (pa * da + pb * db)

    @pl.when(step == 0)
    def _():
        set_limits(scal, limit)
        h = jnp.zeros((R, hidden), f32)
        for msg in reversed(msgs):
            both = msg[...].astype(f32)
            h = jnp.exp(both[0:R, :]) * h + both[R:, :]
        h = jnp.where(scal[1] == 1, other[0:R, :] * h + other[R:, :], h)
        run[...] = jnp.ones((R, hidden), f32)
        back[...] = jnp.zeros(back.shape, f32)
        mg[...] = jnp.zeros(mg.shape, f32)
        dhs[...] = jnp.zeros(dhs.shape, bf16)
        state[...] = lax.fori_loop(0, tb // 2, lambda u, h: scan_pair(zl, kh, scal[0], u, h), h, unroll=2)

    hp_out[...] = hps[...]
    y = ys[...]
    y_out[...] = y
    r1 = position_major(perm[...], x[...]) + nn(y, wo[...])
    r1_out[...] = r1
    inv = lax.rsqrt(jnp.mean(r1 * r1, -1, keepdims=True) + epsilon)
    n2 = (r1 * inv * mgain[...]).astype(bf16)
    n2_out[...] = n2
    chunks = feed // fchunk
    pairs = tb // 2 // chunks
    for f in range(chunks):
        cols = slice(f * fchunk, (f + 1) * fchunk)
        a, slope = gelu_parts(nn(n2, wu[:, cols]).astype(bf16))
        act_out[:, cols] = a
        dpb = da[:, cols] * slope
        dp_out[:, cols] = dpb
        part = nt(dpb, wu[:, cols])
        acc[...] = acc[...] + part if f else part
        h, prod, total = state[...], run[...], back[...]
        for u in range(f * pairs, (f + 1) * pairs):
            h = scan_pair(zl_next, kh_next, first + tb, u, h)
            prod, total = adjoint_pair(zl_before, dhs, u, prod, total)
        state[...] = h
        run[...] = jnp.where(step == 0, 1.0, prod)
        back[...] = total
    dn2 = acc[...]
    r1 = r1_out[...]
    mg[...] += jnp.sum((dn2 * r1 * inv).reshape(tb, R, width), 0)
    s = mgain[...] * dn2
    mean = jnp.mean(s * r1, -1, keepdims=True)
    dr1 = gl[...].astype(f32) + inv * (s - r1 * (inv * inv * mean))
    dr1_out[...] = dr1
    dm = dr1.astype(bf16)
    dm_out[...] = dm
    dh = nt(dm, wo[...]).reshape(tb, R, hidden)
    pos = first + lax.broadcasted_iota(jnp.int32, (tb, R, hidden), 0)
    dh = jnp.where(pos < limit[...][None], dh, 0.0).reshape(m, hidden).astype(bf16)
    dh_out[...] = dh
    dhs[...] = dh

    @pl.when(step == blocks - 1)
    def _():
        carry = lax.fori_loop(
            0, tb // 2, lambda u, carry: adjoint_pair(zl, dhs, u, *carry), (run[...], back[...]), unroll=4
        )
        back[...] = carry[1]


def put_rows(dst, sel, piece, at, rows, part):
    for i in range(SLOTS // 2):
        pos = pl.multiple_of((i ^ sel) * piece + at, 16)
        dst[pl.ds(pos, rows), :] = part[i * rows : (i + 1) * rows]


def ffn_grad_kernel(scal, act, gl, n2, dp, dst, *, pick):
    step = pl.program_id(0)
    sel = scal[2 + pick]
    width = gl.shape[1]
    rows1 = act.shape[1] * 4 // SLOTS
    rows2 = n2.shape[1] * 2 // SLOTS
    part = tn(act[...], gl[...]).astype(bf16)
    per = act.shape[1] // rows1
    for i in range(per):
        pos = ((step * per + i) ^ sel) * PIECE1
        dst[pl.ds(pl.multiple_of(pos, 16), rows1), :] = part[i * rows1 : (i + 1) * rows1]
    columns = dp.shape[1] // width
    for q in range(columns):
        part = tn(n2[...], dp[:, q * width : (q + 1) * width]).astype(bf16)
        put_rows(dst, sel, PIECE1, rows1 + (step * columns + q) * rows2, rows2, part)


def gate_grad_kernel(scal, c, dkz, dkh, y, dm, dst, *, pick):
    sel = scal[2 + pick]
    width = dm.shape[1]
    rows = c.shape[1] * 2 // SLOTS
    at = 0
    for grads in (dkz, dkh):
        for q in range(grads.shape[1] // width):
            part = tn(c[...], grads[:, q * width : (q + 1) * width]).astype(bf16)
            put_rows(dst, sel, PIECE2, at, rows, part)
            at += rows
    put_rows(dst, sel, PIECE2, at, y.shape[1] * 2 // SLOTS, tn(y[...], dm[...]).astype(bf16))


def gate_kernel(scal, dh, zl, kh, hp, other, fother, *refs, blocks, hops):
    msgs = refs[:hops]
    wg, wc = refs[hops : hops + 2]
    dkz, dkh, edge_out, bias_out = refs[hops + 3 : hops + 7]
    state = refs[hops + 7]
    step = pl.program_id(0)
    m = dh.shape[0]
    tb = m // R
    block = blocks - 1 - step

    @pl.when(step == 0)
    def _():
        mm = jnp.zeros(state.shape, f32)
        for msg in reversed(msgs):
            both = msg[...].astype(f32)
            mm = jnp.exp(both[0:R, :]) * mm + both[R:, :]
        state[...] = jnp.where(scal[1] == 0, fother[...] + other[0:R, :] * mm, mm)
        bias_out[...] = jnp.zeros(bias_out.shape, f32)

    def body(u, carry):
        mm, bias = carry
        w = tb // 2 - 1 - u
        ha, hb = halves(hp, w)
        za, zb = halves(zl, w)
        da, db = halves(dh, w)
        ka, kb = halves(kh, w)
        lam = db + mm
        sb = lam * zb
        mm = lam - sb
        kb = (sb - sb * zb) * (kb - hb)
        lam = da + mm
        sa = lam * za
        mm = lam - sa
        ka = (sa - sa * za) * (ka - ha)
        kk = jnp.concatenate([ka, kb], 0).astype(bf16)
        dkz[sixteen(w), :] = kk
        dkh[sixteen(w), :] = jnp.concatenate([sa, sb], 0).astype(bf16)
        kf = kk.astype(f32)
        return mm, bias + kf[:R, :] + kf[R:, :]

    mm, bias = lax.fori_loop(0, tb // 2, body, (state[...], bias_out[...]), unroll=2)
    state[...] = mm
    bias_out[...] = bias

    @pl.when(block == 0)
    def _():
        span = edge_out.shape[0]
        edge_out[...] = (nt(dkz[0:span, :], wg[...]) + nt(dkh[0:span, :], wc[...])).astype(bf16)


def tail_kernel(x, dr1, dkz, dkh, pm, back_pm, edge, after, gain, convw, wg, wc, grad, sums, uext, dext, *, blocks):
    step = pl.program_id(0)
    tb = x.shape[1]
    m = tb * R
    halo = edge.shape[0]
    taps = convw.shape[0]
    width = gain.shape[1]

    @pl.when(step == 0)
    def _():
        uext[0:halo, :] = normed_edge(edge[...], gain[...])
        dext[blocks * m :, :] = after[...].astype(f32)
        sums[...] = jnp.zeros(sums.shape, f32)

    @pl.when(step < blocks)
    def _():
        rows = pl.ds(pl.multiple_of(step * m, m), m)
        dext[rows, :] = nt(dkz[...], wg[...]) + nt(dkh[...], wc[...])

    @pl.when(step >= blocks)
    def _():
        xp = position_major(pm[...], x[...])
        inv = lax.rsqrt(jnp.mean(xp * xp, -1, keepdims=True) + epsilon)
        xn = xp * inv
        uext[halo:, :] = (xn * gain[...]).astype(bf16).astype(f32)
        start = (step - blocks) * m
        here = dext[pl.ds(pl.multiple_of(start, R), m), :]
        du = convw[0:1, :] * here
        for k in range(taps):
            lo = halo - k * R
            part = (here * uext[lo : lo + m, :]).reshape(tb, R, width)
            sums[(k + 1) * R : (k + 2) * R, :] += jnp.sum(part, 0)
            if k:
                du = du + convw[k : k + 1, :] * dext[pl.ds(pl.multiple_of(start + k * R, R), m), :]
        uext[0:halo, :] = uext[m : m + halo, :]
        sums[0:R, :] += jnp.sum((du * xn).reshape(tb, R, width), 0)
        s1 = gain[...] * du
        mean = jnp.mean(s1 * xn, -1, keepdims=True)
        gin = dr1[...] + inv * (s1 - xn * mean)
        grad[...] = row_major(back_pm[...], gin.astype(bf16))


def output_kernel(r1, act, perm, wd, out):
    total = r1[...] + nn(act[...], wd[...])
    out[...] = row_major(perm[...], total.astype(bf16))


def spread_kernel(scal, src, *refs, piece, plan, mate):
    low = scal[2 + mate] & 7
    for a in range(8):
        base = (a ^ low) * piece
        at = 0
        for out, rows, columns in plan:
            ref = refs[len(refs) - len(plan) + out]
            for q in range(columns):
                width = src.shape[1]
                part = src[pl.ds(pl.multiple_of(base + at, 16), rows), :].astype(f32)
                ref[a * rows : (a + 1) * rows, q * width : (q + 1) * width] = part
                at += rows


def last_spread_kernel(scal, src, ride, rest, theirs, *refs, piece, plan, taps):
    norm, conv, mlp, bias = refs[-4:]
    spread_kernel(scal, src, *refs[:-4], piece=piece, plan=plan, mate=1)
    tail = src.shape[0] - 2 * R
    total = ride[...]
    for rows in (rest[...], theirs[...], src[tail:, :]):
        both = rows.astype(f32)
        total = total + (both[:R] + both[R:])
    norm[...] = total[0:1]
    conv[...] = total[1 : taps + 1]
    mlp[...] = total[taps + 1 : taps + 2]
    width = total.shape[1]
    for i in range(bias.shape[1] // width):
        bias[:, i * width : (i + 1) * width] = total[taps + 2 + i : taps + 3 + i]


def last_spread(scal, chunk, held, piece, plan, shapes, taps, hidden):
    src = chunk.their_rest
    width = src.shape[1]
    rows = 2 * R
    tail = pl.BlockSpec((rows, width), lambda g, s: (src.shape[0] // rows - 1, 0))
    small = ((1, width), (taps, width), (1, width), (1, hidden))

    def block(g, s):
        return ((s[1] ^ 1) * 2 + ((s[3] >> 3) ^ 1), 0)

    return pl.pallas_call(
        functools.partial(last_spread_kernel, piece=piece, plan=plan, taps=taps),
        grid_spec=pltpu.PrefetchScalarGridSpec(
            num_scalar_prefetch=1,
            grid=(1,),
            in_specs=[whole(src), whole(chunk.ride), tail, tail] + [ORDER] * len(held),
            out_specs=[pl.BlockSpec((dims[0] // 4, dims[1]), block) for dims in shapes]
            + [pl.BlockSpec(dims, lambda g, s: (0, 0)) for dims in small],
        ),
        out_shape=[pltpu.HBM(dims, f32) for dims in shapes] + [shape(dims) for dims in small],
        input_output_aliases={5 + k: k for k in range(len(held))},
        compiler_params=params(16),
        cost_estimate=SOME,
        name="spread_last",
    )(scal, src, chunk.ride, chunk.rest, chunk.theirs, *held)


def spread(scal, src, held, mate, flip, piece, plan, shapes, name):
    def block(g, s):
        return ((s[1] ^ mate) * 2 + ((s[2 + mate] >> 3) ^ flip), 0)

    count = len(held)
    return pl.pallas_call(
        functools.partial(spread_kernel, piece=piece, plan=plan, mate=mate),
        grid_spec=pltpu.PrefetchScalarGridSpec(
            num_scalar_prefetch=1,
            grid=(1,),
            in_specs=[whole(src)] + [ORDER] * count,
            out_specs=[pl.BlockSpec((dims[0] // 4, dims[1]), block) for dims in shapes],
        ),
        out_shape=[pltpu.HBM(dims, f32) for dims in shapes],
        input_output_aliases={2 + k: k for k in range(count)},
        compiler_params=params(16),
        cost_estimate=SOME,
        name=name,
    )(scal, src, *held)


def params(mib):
    return pltpu.CompilerParams(
        dimension_semantics=("arbitrary",), vmem_limit_bytes=mib * 1024 * 1024
    )


def shape(dims, kind=f32):
    return jax.ShapeDtypeStruct(dims, kind)


LITTLE = pl.CostEstimate(flops=1024, bytes_accessed=1024, transcendentals=0)
MUCH = pl.CostEstimate(flops=3 * 10**10, bytes_accessed=1024, transcendentals=0)
SOME = pl.CostEstimate(flops=10**10, bytes_accessed=1024, transcendentals=0)
ORDER = pl.BlockSpec(memory_space=pl.ANY)


def far(array):
    return pltpu.with_memory_space_constraint(array, pltpu.HBM)


def whole(array):
    zeros = (0,) * array.ndim
    return pl.BlockSpec(array.shape, lambda *a: zeros, pipeline_mode=pl.Buffered(1))


def passed_along(value, axis, steps):
    count = lax.axis_size(axis)
    leading, last = (max(0, -steps), min(count, count - steps))
    return lax.ppermute(value, axis, [(source, source + steps) for source in range(leading, last)])


def flat_permute(value, pairs):
    return lax.ppermute(value, ("seq", "row"), pairs)


def stage_bits():
    row_bits = lax.axis_size("row").bit_length() - 1
    seq_bits = lax.axis_size("seq").bit_length() - 1
    plane = list(range(row_bits))
    line = [row_bits + 1 + z for z in range(seq_bits - 1)]
    cut = row_bits // 2
    return (plane + line, plane[cut:] + plane[:cut] + line[::-1])


def slot_of(flat, bits):
    slot = 0
    for k in range(4):
        slot = slot * 2 + ((flat >> bits[k]) & 1)
    return slot


def halving_pairs(stage):
    row_bits = lax.axis_size("row").bit_length() - 1
    orders = stage_bits()
    devices = lax.axis_size("row") * lax.axis_size("seq")
    return [(d, d ^ (1 << orders[(d >> row_bits) & 1][stage])) for d in range(devices)]


def core_pairs():
    row_bits = lax.axis_size("row").bit_length() - 1
    devices = lax.axis_size("row") * lax.axis_size("seq")
    return [(d, d ^ (1 << row_bits)) for d in range(devices)]


def added(a, b):
    return (a.astype(f32) + b.astype(f32)).astype(bf16)


class Sequence:
    def __init__(self, token):
        self.token = token

    def after(self, *arrays):
        *arrays, _ = lax.optimization_barrier((*arrays, self.token))
        return arrays[0] if len(arrays) == 1 else arrays

    def did(self, array):
        self.token = array
        return array


def split(value):
    high = lax.reduce_precision(value, 8, 7)
    return [high.astype(bf16), (value - high).astype(bf16)]


def join_kernel(mine, recv, ride, out, ride_out):
    rows = mine.shape[0] - 2 * R
    out[0:rows, :] = mine[0:rows, :]
    out[rows : 2 * rows, :] = recv[0:rows, :]
    parts = recv[rows:, :].astype(f32)
    total = ride[...] + (parts[:R] + parts[R:])
    ride_out[...] = total
    high = total.astype(bf16).astype(f32)
    out[2 * rows :, :] = jnp.concatenate([high, total - high], 0).astype(bf16)


def chain_kernel(mine, recv, out):
    rows = mine.shape[0]
    out[0:rows, :] = mine[...]
    out[rows:, :] = recv[...]


def chained(mine, recv):
    rows, width = mine.shape
    return pl.pallas_call(
        chain_kernel,
        in_specs=[pl.BlockSpec(memory_space=pltpu.VMEM)] * 2,
        out_specs=pl.BlockSpec(memory_space=pltpu.VMEM),
        out_shape=shape((2 * rows, width), bf16),
        compiler_params=pltpu.CompilerParams(vmem_limit_bytes=16 * 1024 * 1024),
        cost_estimate=SOME,
        name="chain",
    )(mine, recv)


def joined(mine, recv, ride, estimate):
    rows, width = mine.shape
    return pl.pallas_call(
        join_kernel,
        in_specs=[pl.BlockSpec(memory_space=pltpu.VMEM)] * 3,
        out_specs=[pl.BlockSpec(memory_space=pltpu.VMEM)] * 2,
        out_shape=[shape((2 * rows - 2 * R, width), bf16), shape(ride.shape)],
        compiler_params=pltpu.CompilerParams(vmem_limit_bytes=16 * 1024 * 1024),
        cost_estimate=estimate,
        name="join",
    )(mine, recv, ride)


class Halving:
    def __init__(self, seq, send):
        self.seq = seq
        self.recv = flat_permute(send, core_pairs())
        self.stage = 0
        self.ride = None

    def riders(self):
        return [] if self.ride is None else split(self.ride)

    def step(self, *beside):
        k = self.stage
        self.stage += 1
        stages = len(stage_bits()[0])
        recv, *beside = self.seq.after(self.recv, *beside) if beside else (self.seq.after(self.recv),)
        if k < 4:
            half = self.keep.shape[0] // 2
            send = self.seq.did(added(self.keep[half:], recv[half:]))
            self.recv = flat_permute(send, halving_pairs(k))
            self.keep = added(self.keep[:half], recv[:half])
        elif k == 4:
            total = added(self.keep, recv)
            for extra in range(4, stages):
                total = added(total, flat_permute(total, halving_pairs(extra)))
                if self.ride is not None:
                    self.ride = self.ride + flat_permute(self.ride, halving_pairs(extra))
            self.rows = total.shape[0]
            self.total = self.seq.did(jnp.concatenate([total] + self.riders(), 0))
            self.recv = flat_permute(self.total, halving_pairs(3))
        elif k < 8:
            rows = self.rows
            self.rows = 2 * rows
            if self.ride is None:
                self.total = self.seq.did(chained(self.total, recv))
            else:
                self.total, self.ride = joined(
                    self.total, recv, self.ride, LITTLE if k == 5 else SOME
                )
                self.seq.did(self.total)
            self.recv = flat_permute(self.total, halving_pairs(7 - k))
            if k == 7:
                self.theirs = flat_permute(self.total, core_pairs())
        else:
            self.rest = recv
            self.their_rest = flat_permute(recv, core_pairs())
        return beside


def chip_shift(value, steps):
    return passed_along(value, "seq", 2 * steps)


def per_device(
    inputs,
    lengths,
    norm_gain,
    conv_weight,
    gate_weight,
    gate_bias,
    cand_weight,
    out_weight,
    mlp_gain,
    up_weight,
    down_weight,
    cotangent,
):
    rows, span, width = inputs.shape
    hidden = gate_weight.shape[1]
    feed = up_weight.shape[1]
    taps = conv_weight.shape[0]
    margin = taps - 1
    tokens = rows * span
    tb = 32
    blocks = span // tb
    m = tb * R
    seq = lax.axis_index("seq")
    core = seq & 1
    chips = lax.axis_size("seq") // 2
    hops = chips - 1
    flat = seq * lax.axis_size("row") + lax.axis_index("row")
    slots = [slot_of(flat, bits) for bits in stage_bits()]
    here = jnp.where(core == 0, slots[0], slots[1])
    mate = jnp.where(core == 0, slots[1], slots[0])
    scal = jnp.concatenate([jnp.stack([seq * span, core, here, mate]).astype(jnp.int32), lengths])
    gain1 = norm_gain.reshape(1, width)
    gain2 = mlp_gain.reshape(1, width)
    bias = gate_bias.reshape(1, hidden)
    to_pm, to_rm = token_order()

    edge = inputs[:, span - margin :, :].swapaxes(0, 1).reshape(margin * rows, width)
    edge = passed_along(edge, "seq", 1)

    last = blocks - 1
    clamp = lambda i: jnp.minimum(i, last)
    late = lambda i: jnp.maximum(i - blocks, 0)
    later = lambda i: jnp.minimum(i + 1, last)
    before = lambda i: jnp.maximum(i - 1, 0)

    def rm(index):
        return pl.BlockSpec((rows, tb, width), lambda i, *s: (0, index(i), 0))

    def tok(w, index=clamp):
        return pl.BlockSpec((m, w), lambda i, *s: (index(i), 0))

    def rtok(w):
        return tok(w, lambda i: last - clamp(i))

    def fixed(dims):
        zeros = (0,) * len(dims)
        return pl.BlockSpec(dims, lambda i, *s: zeros)

    def call(kernel, name, grid, ins, outs, scratch, operands, scalars=True, much=False):
        spec = pltpu.PrefetchScalarGridSpec(
            num_scalar_prefetch=int(scalars),
            grid=(grid,),
            in_specs=ins,
            out_specs=[o[1] for o in outs],
            scratch_shapes=scratch,
        )
        return pl.pallas_call(
            kernel,
            grid_spec=spec,
            out_shape=[o[0] for o in outs],
            compiler_params=params(16),
            cost_estimate=MUCH if much else LITTLE,
            name=name,
        )(*operands)

    def rows_of(w, kind, spec=tok, kept=shape):
        return kept((tokens, w), kind), spec(w)

    (normed,) = call(
        norm_kernel, "norm", blocks,
        [rm(clamp), whole(to_pm), whole(gain1)],
        [rows_of(width, bf16)],
        [],
        (far(inputs), far(to_pm), far(gain1)),
        scalars=False,
    )
    edge, normed = lax.optimization_barrier((edge, normed))
    c, zl, kh, ends = call(
        front_kernel, "front", blocks,
        [
            tok(width), whole(edge), whole(gain1), whole(conv_weight),
            whole(gate_weight), whole(bias), whole(cand_weight),
        ],
        [
            rows_of(width, bf16), rows_of(hidden, bf16), rows_of(hidden, bf16),
            (shape((2 * R, hidden)), fixed((2 * R, hidden))),
        ],
        [
            pltpu.VMEM((margin * R + m, width), f32),
            pltpu.VMEM((2 * R, hidden), f32),
            pltpu.VMEM((R, hidden), jnp.int32),
        ],
        (
            scal, normed, edge, far(gain1), far(conv_weight), gate_weight, far(bias),
            cand_weight,
        ),
    )

    other = flat_permute(ends, core_pairs())
    first = jnp.where(core == 0, ends, other)
    second = jnp.where(core == 0, other, ends)
    decay = jnp.log(jnp.maximum(ends[:R] * other[:R], 1e-37))
    message = jnp.concatenate([decay, second[:R] * first[R:] + second[R:]], 0).astype(bf16)
    forward = [chip_shift(message, k) for k in range(1, chips)]

    gl, da = call(
        da_kernel, "da", blocks,
        [rm(clamp), whole(to_pm), whole(down_weight)],
        [rows_of(width, bf16), rows_of(feed, bf16)],
        [],
        (cotangent, to_pm, down_weight),
        scalars=False,
    )

    r1, y, hp, n2, act, dp, dm, dr1, dh, back, mg = call(
        functools.partial(core_kernel, fchunk=256, hops=hops, blocks=blocks), "core", blocks,
        [
            rm(clamp), whole(to_pm), tok(width), tok(feed), tok(hidden), tok(hidden, later), tok(hidden),
            tok(hidden, later), tok(hidden, before), whole(other),
            *[whole(f) for f in forward], whole(out_weight), whole(gain2), whole(up_weight),
        ],
        [
            rows_of(width, f32, kept=pltpu.HBM), rows_of(hidden, bf16), rows_of(hidden, bf16),
            rows_of(width, bf16), rows_of(feed, bf16), rows_of(feed, bf16), rows_of(width, bf16),
            rows_of(width, f32, kept=pltpu.HBM),
            rows_of(hidden, bf16),
            (shape((R, hidden)), fixed((R, hidden))), (shape((R, width)), fixed((R, width))),
        ],
        [
            pltpu.VMEM((R, hidden), f32),
            pltpu.VMEM((R, hidden), jnp.int32),
            pltpu.VMEM((R, hidden), f32),
            pltpu.VMEM((m, width), f32),
            pltpu.VMEM((m, hidden), bf16),
            pltpu.VMEM((m, hidden), bf16),
            pltpu.VMEM((m, hidden), bf16),
        ],
        (
            scal, inputs, to_pm, gl, da, zl, zl, kh, kh, zl, other, *forward, far(out_weight), gain2, up_weight,
        ),
    )

    order = Sequence(back)
    quarter = feed // 4

    def ffn_grads(pick, *beside):
        half = lambda s: s[1] if pick == 0 else 1 - s[1]
        a, d, *beside = order.after(act, dp, *beside)
        (piece,) = call(
            functools.partial(ffn_grad_kernel, pick=pick), "ffn_grad", 2,
            [
                pl.BlockSpec((tokens, quarter), lambda i, s: (0, half(s) * 2 + i)), whole(gl),
                pl.BlockSpec((tokens, width // 2), lambda i, s: (0, half(s))),
                pl.BlockSpec((tokens, feed // 2), lambda i, s: (0, i)),
            ],
            [(shape((SLOTS // 2 * PIECE1, width), bf16), fixed((SLOTS // 2 * PIECE1, width)))],
            [],
            (scal, a, gl, n2, d),
            much=pick == 0,
        )
        return order.did(piece), beside

    def gate_grads(pick):
        half = lambda s: s[1] if pick == 0 else 1 - s[1]
        z, h = order.after(dkz, dkh)
        (piece,) = call(
            functools.partial(gate_grad_kernel, pick=pick), "gate_grad", 1,
            [
                pl.BlockSpec((tokens, width // 2), lambda i, s: (0, half(s))),
                whole(z), whole(h),
                pl.BlockSpec((tokens, hidden // 2), lambda i, s: (0, half(s))), whole(dm),
            ],
            [(shape((SLOTS // 2 * PIECE2, width), bf16), fixed((SLOTS // 2 * PIECE2, width)))],
            [],
            (scal, c, z, h, y, dm),
            much=pick == 0,
        )
        return order.did(piece)

    fother = flat_permute(back, core_pairs())
    lower = jnp.where(core == 0, back, fother)
    upper = jnp.where(core == 0, fother, back)
    message = jnp.concatenate([decay, lower + first[:R] * upper], 0).astype(bf16)
    backward = [chip_shift(order.did(message), -k) for k in range(1, chips)]
    send1, _ = ffn_grads(1)
    chunk1 = Halving(order, send1)
    chunk1.keep, backward = ffn_grads(0, *backward)
    chunk1.step()

    dkz, dkh, edge_dc, bias_part = call(
        functools.partial(gate_kernel, blocks=blocks, hops=hops), "gates", blocks,
        [
            rtok(hidden), rtok(hidden), rtok(hidden), rtok(hidden),
            whole(other), whole(fother), *[whole(f) for f in backward],
            whole(gate_weight), whole(cand_weight), ORDER,
        ],
        [
            rows_of(hidden, bf16, rtok), rows_of(hidden, bf16, rtok),
            (shape((4 * R, width), bf16), fixed((4 * R, width))),
            (shape((R, hidden)), fixed((R, hidden))),
        ],
        [pltpu.VMEM((R, hidden), f32)],
        (
            scal, dh, zl, kh, hp, other, fother, *backward, gate_weight, cand_weight, order.token,
        ),
    )
    order.did(bias_part)
    after = passed_along(edge_dc[: margin * R], "seq", -1)
    send2 = gate_grads(1)
    chunk2 = Halving(order, send2)
    (output,) = call(
        output_kernel, "output", blocks,
        [tok(width), tok(feed), whole(to_rm), whole(down_weight)],
        [(shape((rows, span, width), bf16), rm(clamp))],
        [],
        (far(r1), order.after(act), to_rm, down_weight),
        scalars=False,
    )
    order.did(output)
    chunk1.step()
    chunk2.keep = gate_grads(0)
    (after,) = chunk2.step(after)
    input_grad, sums = call(
        functools.partial(tail_kernel, blocks=blocks), "tail", 2 * blocks,
        [
            rm(late), tok(width, late), tok(hidden), tok(hidden), whole(to_pm), whole(to_rm),
            whole(edge), whole(after), whole(gain1), whole(conv_weight), whole(gate_weight),
            whole(cand_weight),
        ],
        [
            (shape((rows, span, width), bf16), rm(late)),
            (shape(((taps + 1) * R, width)), fixed(((taps + 1) * R, width))),
        ],
        [
            pltpu.VMEM((margin * R + m, width), f32),
            pltpu.VMEM((margin * R + tokens, width), f32),
        ],
        (
            far(inputs), far(dr1), order.after(dkz), dkh, far(to_pm), far(to_rm), edge, after,
            far(gain1), far(conv_weight), far(gate_weight), far(cand_weight),
        ),
        scalars=False,
    )
    order.did(sums)
    small = jnp.concatenate(
        [
            sums.reshape(taps + 1, R, width).sum(1),
            mg.sum(0, keepdims=True),
            bias_part.sum(0).reshape(hidden // width, width),
        ],
        0,
    )

    plan1 = ((0, feed // SLOTS, 1), (1, width // SLOTS, feed // width))
    shapes1 = ((feed, width), (width, feed))
    plan2 = (
        (0, width // SLOTS, hidden // width),
        (1, width // SLOTS, hidden // width),
        (2, hidden // SLOTS, 1),
    )
    shapes2 = ((width, hidden), (width, hidden), (hidden, width))
    held1, held2 = (), ()

    def spread1(src, mate, flip):
        nonlocal held1
        src = order.after(src)
        held1 = spread(scal, src, held1, mate, flip, PIECE1, plan1, shapes1, "spread_ffn")
        order.did(held1[0])

    def spread2(src, mate, flip):
        nonlocal held2
        src = order.after(src)
        held2 = spread(scal, src, held2, mate, flip, PIECE2, plan2, shapes2, "spread_gates")
        order.did(held2[0])

    chunk2.ride = small
    for chunk in (chunk1, chunk2, chunk1, chunk2, chunk1, chunk2, chunk1, chunk2):
        chunk.step()
    chunk2.step()
    chunk1.step()
    chunk2.step()
    chunk1.step()
    chunk2.step()
    spread1(chunk1.total, 0, 0)
    spread1(chunk1.theirs, 1, 0)
    chunk1.step()
    spread1(chunk1.rest, 0, 1)
    spread2(chunk2.total, 0, 0)
    spread1(chunk1.their_rest, 1, 1)
    spread2(chunk2.theirs, 1, 0)
    chunk2.step()
    spread2(chunk2.rest, 0, 1)
    chunk2.their_rest = order.after(chunk2.their_rest)
    *held2, norm_sum, conv_sum, mlp_sum, bias_sum = last_spread(
        scal, chunk2, held2, PIECE2, plan2, shapes2, taps, hidden
    )
    return (
        output,
        input_grad,
        norm_sum.reshape(width),
        conv_sum,
        held2[0],
        bias_sum.reshape(hidden),
        held2[1],
        held2[2],
        mlp_sum.reshape(width),
        held1[1],
        held1[0],
    )


def solution(mesh):
    sharded = P("row", "seq", None)
    in_specs = (sharded, P("row")) + (P(),) * 9 + (sharded,)
    out_specs = (sharded, sharded) + (P(),) * 9
    return jax.shard_map(
        per_device, mesh=mesh, in_specs=in_specs, out_specs=out_specs, check_vma=False
    )
```

```python
import functools

import jax
import jax.numpy as jnp
import numpy as np
from jax import lax
from jax.experimental import pallas as pl
from jax.experimental.pallas import tpu as pltpu
from jax.sharding import PartitionSpec as P

epsilon = 1e-06
f32 = jnp.float32
bf16 = jnp.bfloat16
R = 8
PERM = 256
SCALARS = 4
SLOTS = 32
PIECE1 = 128
PIECE2 = 96


def nn(a, b):
    return lax.dot_general(a, b, (((1,), (0,)), ((), ())), preferred_element_type=f32)


def nt(a, b):
    return lax.dot_general(a, b, (((1,), (1,)), ((), ())), preferred_element_type=f32)


def tn(a, b):
    return lax.dot_general(a, b, (((0,), (0,)), ((), ())), preferred_element_type=f32)


def token_order():
    out = np.arange(PERM)
    source = (out % R) * (PERM // R) + out // R
    to_pm = np.zeros((PERM, PERM), np.float32)
    to_pm[out, source] = 1
    return jnp.asarray(to_pm, bf16), jnp.asarray(to_pm.T, bf16)


def position_major(perm, block):
    span = PERM // R
    parts = []
    for s in range(block.shape[1] // span):
        part = block[:, s * span : (s + 1) * span, :].reshape(PERM, block.shape[2])
        parts.append(nn(perm, part))
    return parts[0] if len(parts) == 1 else jnp.concatenate(parts, 0)


def row_major(perm, tokens):
    span = PERM // R
    parts = []
    for s in range(tokens.shape[0] // PERM):
        part = nn(perm, tokens[s * PERM : (s + 1) * PERM]).astype(bf16)
        parts.append(part.reshape(R, span, tokens.shape[1]))
    return parts[0] if len(parts) == 1 else jnp.concatenate(parts, 1)


def eight(t):
    return pl.ds(pl.multiple_of(t * R, R), R)


def sixteen(t):
    return pl.ds(pl.multiple_of(t * 2 * R, 2 * R), 2 * R)


def normed_edge(edge, gain):
    e = edge.astype(f32)
    inv = lax.rsqrt(jnp.mean(e * e, -1, keepdims=True) + epsilon)
    return (e * inv * gain).astype(bf16).astype(f32)


def set_limits(scal, limit):
    row = lax.broadcasted_iota(jnp.int32, limit.shape, 0)
    value = jnp.zeros(limit.shape, jnp.int32)
    for r in range(R):
        value = jnp.where(row == r, scal[SCALARS + r], value)
    limit[...] = value


def halves(ref, pair):
    both = ref[sixteen(pair), :].astype(f32)
    return both[:R], both[R:]


def norm_kernel(x, perm, gain, u_out):
    xp = position_major(perm[...], x[...])
    inv = lax.rsqrt(jnp.mean(xp * xp, -1, keepdims=True) + epsilon)
    u_out[...] = (xp * inv * gain[...]).astype(bf16)


def front_kernel(scal, u, edge, gain, convw, wg, bias, wc, c_out, zl_out, kh_out, ends, ext, state, limit):
    step = pl.program_id(0)
    m = u.shape[0]
    tb = m // R
    halo = edge.shape[0]
    taps = convw.shape[0]

    @pl.when(step == 0)
    def _():
        set_limits(scal, limit)
        ext[0:halo, :] = normed_edge(edge[...], gain[...])
        state[0:R, :] = jnp.ones((R, state.shape[1]), f32)
        state[R:, :] = jnp.zeros((R, state.shape[1]), f32)

    ext[halo:, :] = u[...].astype(f32)
    conv = convw[0:1, :] * ext[halo:, :]
    for k in range(1, taps):
        lo = halo - k * R
        conv = conv + convw[k : k + 1, :] * ext[lo : lo + m, :]
    ext[0:halo, :] = ext[m : m + halo, :]
    cb = conv.astype(bf16)
    c_out[...] = cb
    kz = nn(cb, wg[...]) + bias[...]
    zs = 1.0 / (1.0 + jnp.exp(-kz))
    width = zs.shape[1]
    zs = zs.reshape(tb, R, width)
    pos = scal[0] + step * tb + lax.broadcasted_iota(jnp.int32, (tb, R, width), 0)
    zl_out[...] = jnp.where(pos < limit[...][None], zs, 0.0).reshape(m, width).astype(bf16)
    kh_out[...] = nn(cb, wc[...]).astype(bf16)

    def body(u, carry):
        prod, h = carry
        za, zb = halves(zl_out, u)
        ka, kb = halves(kh_out, u)
        a = 1.0 - za
        b = 1.0 - zb
        return prod * (a * b), (h * a + za * ka) * b + zb * kb

    prod, h = lax.fori_loop(0, tb // 2, body, (state[0:R, :], state[R:, :]), unroll=4)
    state[0:R, :] = prod
    state[R:, :] = h
    ends[0:R, :] = prod
    ends[R:, :] = h


def gelu_parts(p):
    k0 = 0.7978845608028654
    inner = p * (k0 + (k0 * 0.044715) * (p * p))
    th = jnp.tanh(inner)
    ht = 0.5 + 0.5 * th
    return p * ht, ht + (1.0 - th * th) * (1.5 * inner - k0 * p)


def da_kernel(g, perm, wd, gl_out, da_out):
    gl = position_major(perm[...], g[...]).astype(bf16)
    gl_out[...] = gl
    da_out[...] = nt(gl, wd[...]).astype(bf16)


def core_kernel(scal, x, perm, gl, da, zl, zl_next, kh, kh_next, zl_before, other, *refs, fchunk, hops, blocks):
    msgs = refs[:hops]
    wo, mgain, wu = refs[hops : hops + 3]
    r1_out, y_out, hp_out, n2_out, act_out, dp_out, dm_out, dr1_out, dh_out, back, mg = refs[hops + 3 : hops + 14]
    state, limit, run, acc, ys, hps, dhs = refs[hops + 14 :]
    step = pl.program_id(0)
    tb = x.shape[1]
    m = tb * R
    width, feed = wu.shape
    hidden = wo.shape[0]
    first = scal[0] + step * tb

    def scan_pair(zs, ks, start, u, h):
        t = u * 2
        za, zb = halves(zs, u)
        ka, kb = halves(ks, u)
        ha = h - za * h + za * ka
        hb = ha - zb * ha + zb * kb
        hps[sixteen(u), :] = jnp.concatenate([h, ha], 0).astype(bf16)
        ya = jnp.where(start + t < limit[...], ha, 0.0)
        yb = jnp.where(start + t + 1 < limit[...], hb, 0.0)
        ys[sixteen(u), :] = jnp.concatenate([ya, yb], 0).astype(bf16)
        return hb

    def adjoint_pair(zs, ds, u, prod, total):
        za, zb = halves(zs, u)
        da, db = halves(ds, u)
        pa = prod - za * prod
        pb = pa - zb * pa
        return pb, total + (pa * da + pb * db)

    @pl.when(step == 0)
    def _():
        set_limits(scal, limit)
        h = jnp.zeros((R, hidden), f32)
        for msg in reversed(msgs):
            both = msg[...].astype(f32)
            h = jnp.exp(both[0:R, :]) * h + both[R:, :]
        h = jnp.where(scal[1] == 1, other[0:R, :] * h + other[R:, :], h)
        run[...] = jnp.ones((R, hidden), f32)
        back[...] = jnp.zeros(back.shape, f32)
        mg[...] = jnp.zeros(mg.shape, f32)
        dhs[...] = jnp.zeros(dhs.shape, bf16)
        state[...] = lax.fori_loop(0, tb // 2, lambda u, h: scan_pair(zl, kh, scal[0], u, h), h, unroll=2)

    hp_out[...] = hps[...]
    y = ys[...]
    y_out[...] = y
    r1 = position_major(perm[...], x[...]) + nn(y, wo[...])
    r1_out[...] = r1
    inv = lax.rsqrt(jnp.mean(r1 * r1, -1, keepdims=True) + epsilon)
    n2 = (r1 * inv * mgain[...]).astype(bf16)
    n2_out[...] = n2
    chunks = feed // fchunk
    pairs = tb // 2 // chunks
    for f in range(chunks):
        cols = slice(f * fchunk, (f + 1) * fchunk)
        a, slope = gelu_parts(nn(n2, wu[:, cols]).astype(bf16))
        act_out[:, cols] = a
        dpb = da[:, cols] * slope
        dp_out[:, cols] = dpb
        part = nt(dpb, wu[:, cols])
        acc[...] = acc[...] + part if f else part
        h, prod, total = state[...], run[...], back[...]
        for u in range(f * pairs, (f + 1) * pairs):
            h = scan_pair(zl_next, kh_next, first + tb, u, h)
            prod, total = adjoint_pair(zl_before, dhs, u, prod, total)
        state[...] = h
        run[...] = jnp.where(step == 0, 1.0, prod)
        back[...] = total
    dn2 = acc[...]
    r1 = r1_out[...]
    mg[...] += jnp.sum((dn2 * r1 * inv).reshape(tb, R, width), 0)
    s = mgain[...] * dn2
    mean = jnp.mean(s * r1, -1, keepdims=True)
    dr1 = gl[...].astype(f32) + inv * (s - r1 * (inv * inv * mean))
    dr1_out[...] = dr1
    dm = dr1.astype(bf16)
    dm_out[...] = dm
    dh = nt(dm, wo[...]).reshape(tb, R, hidden)
    pos = first + lax.broadcasted_iota(jnp.int32, (tb, R, hidden), 0)
    dh = jnp.where(pos < limit[...][None], dh, 0.0).reshape(m, hidden).astype(bf16)
    dh_out[...] = dh
    dhs[...] = dh

    @pl.when(step == blocks - 1)
    def _():
        carry = lax.fori_loop(
            0, tb // 2, lambda u, carry: adjoint_pair(zl, dhs, u, *carry), (run[...], back[...]), unroll=4
        )
        back[...] = carry[1]


def put_rows(dst, sel, piece, at, rows, part):
    for i in range(SLOTS // 2):
        pos = pl.multiple_of((i ^ sel) * piece + at, 16)
        dst[pl.ds(pos, rows), :] = part[i * rows : (i + 1) * rows]


def ffn_grad_kernel(scal, act, gl, n2, dp, dst, *, pick):
    step = pl.program_id(0)
    sel = scal[2 + pick]
    width = gl.shape[1]
    rows1 = act.shape[1] * 4 // SLOTS
    rows2 = n2.shape[1] * 2 // SLOTS
    part = tn(act[...], gl[...]).astype(bf16)
    per = act.shape[1] // rows1
    for i in range(per):
        pos = ((step * per + i) ^ sel) * PIECE1
        dst[pl.ds(pl.multiple_of(pos, 16), rows1), :] = part[i * rows1 : (i + 1) * rows1]
    columns = dp.shape[1] // width
    for q in range(columns):
        part = tn(n2[...], dp[:, q * width : (q + 1) * width]).astype(bf16)
        put_rows(dst, sel, PIECE1, rows1 + (step * columns + q) * rows2, rows2, part)


def gate_grad_kernel(scal, c, dkz, dkh, y, dm, dst, *, pick):
    sel = scal[2 + pick]
    width = dm.shape[1]
    rows = c.shape[1] * 2 // SLOTS
    at = 0
    for grads in (dkz, dkh):
        for q in range(grads.shape[1] // width):
            part = tn(c[...], grads[:, q * width : (q + 1) * width]).astype(bf16)
            put_rows(dst, sel, PIECE2, at, rows, part)
            at += rows
    put_rows(dst, sel, PIECE2, at, y.shape[1] * 2 // SLOTS, tn(y[...], dm[...]).astype(bf16))


def gate_kernel(scal, dh, zl, kh, hp, other, fother, *refs, blocks, hops):
    msgs = refs[:hops]
    wg, wc = refs[hops : hops + 2]
    dkz, dkh, edge_out, bias_out = refs[hops + 3 : hops + 7]
    state = refs[hops + 7]
    step = pl.program_id(0)
    m = dh.shape[0]
    tb = m // R
    block = blocks - 1 - step

    @pl.when(step == 0)
    def _():
        mm = jnp.zeros(state.shape, f32)
        for msg in reversed(msgs):
            both = msg[...].astype(f32)
            mm = jnp.exp(both[0:R, :]) * mm + both[R:, :]
        state[...] = jnp.where(scal[1] == 0, fother[...] + other[0:R, :] * mm, mm)
        bias_out[...] = jnp.zeros(bias_out.shape, f32)

    def body(u, carry):
        mm, bias = carry
        w = tb // 2 - 1 - u
        ha, hb = halves(hp, w)
        za, zb = halves(zl, w)
        da, db = halves(dh, w)
        ka, kb = halves(kh, w)
        lam = db + mm
        sb = lam * zb
        mm = lam - sb
        kb = (sb - sb * zb) * (kb - hb)
        lam = da + mm
        sa = lam * za
        mm = lam - sa
        ka = (sa - sa * za) * (ka - ha)
        kk = jnp.concatenate([ka, kb], 0).astype(bf16)
        dkz[sixteen(w), :] = kk
        dkh[sixteen(w), :] = jnp.concatenate([sa, sb], 0).astype(bf16)
        kf = kk.astype(f32)
        return mm, bias + kf[:R, :] + kf[R:, :]

    mm, bias = lax.fori_loop(0, tb // 2, body, (state[...], bias_out[...]), unroll=2)
    state[...] = mm
    bias_out[...] = bias

    @pl.when(block == 0)
    def _():
        span = edge_out.shape[0]
        edge_out[...] = (nt(dkz[0:span, :], wg[...]) + nt(dkh[0:span, :], wc[...])).astype(bf16)


def tail_kernel(x, dr1, dkz, dkh, pm, back_pm, edge, after, gain, convw, wg, wc, grad, sums, uext, dext, *, blocks):
    step = pl.program_id(0)
    tb = x.shape[1]
    m = tb * R
    halo = edge.shape[0]
    taps = convw.shape[0]
    width = gain.shape[1]

    @pl.when(step == 0)
    def _():
        uext[0:halo, :] = normed_edge(edge[...], gain[...])
        dext[blocks * m :, :] = after[...].astype(f32)
        sums[...] = jnp.zeros(sums.shape, f32)

    @pl.when(step < blocks)
    def _():
        rows = pl.ds(pl.multiple_of(step * m, m), m)
        dext[rows, :] = nt(dkz[...], wg[...]) + nt(dkh[...], wc[...])

    @pl.when(step >= blocks)
    def _():
        xp = position_major(pm[...], x[...])
        inv = lax.rsqrt(jnp.mean(xp * xp, -1, keepdims=True) + epsilon)
        xn = xp * inv
        uext[halo:, :] = (xn * gain[...]).astype(bf16).astype(f32)
        start = (step - blocks) * m
        here = dext[pl.ds(pl.multiple_of(start, R), m), :]
        du = convw[0:1, :] * here
        for k in range(taps):
            lo = halo - k * R
            part = (here * uext[lo : lo + m, :]).reshape(tb, R, width)
            sums[(k + 1) * R : (k + 2) * R, :] += jnp.sum(part, 0)
            if k:
                du = du + convw[k : k + 1, :] * dext[pl.ds(pl.multiple_of(start + k * R, R), m), :]
        uext[0:halo, :] = uext[m : m + halo, :]
        sums[0:R, :] += jnp.sum((du * xn).reshape(tb, R, width), 0)
        s1 = gain[...] * du
        mean = jnp.mean(s1 * xn, -1, keepdims=True)
        gin = dr1[...] + inv * (s1 - xn * mean)
        grad[...] = row_major(back_pm[...], gin.astype(bf16))


def output_kernel(r1, act, perm, wd, out):
    total = r1[...] + nn(act[...], wd[...])
    out[...] = row_major(perm[...], total.astype(bf16))


def spread_kernel(scal, src, *refs, piece, plan, mate):
    low = scal[2 + mate] & 7
    for a in range(8):
        base = (a ^ low) * piece
        at = 0
        for out, rows, columns in plan:
            ref = refs[len(refs) - len(plan) + out]
            for q in range(columns):
                width = src.shape[1]
                part = src[pl.ds(pl.multiple_of(base + at, 16), rows), :].astype(f32)
                ref[a * rows : (a + 1) * rows, q * width : (q + 1) * width] = part
                at += rows


def last_spread_kernel(scal, src, ride, rest, theirs, *refs, piece, plan, taps):
    norm, conv, mlp, bias = refs[-4:]
    spread_kernel(scal, src, *refs[:-4], piece=piece, plan=plan, mate=1)
    tail = src.shape[0] - 2 * R
    total = ride[...]
    for rows in (rest[...], theirs[...], src[tail:, :]):
        both = rows.astype(f32)
        total = total + (both[:R] + both[R:])
    norm[...] = total[0:1]
    conv[...] = total[1 : taps + 1]
    mlp[...] = total[taps + 1 : taps + 2]
    width = total.shape[1]
    for i in range(bias.shape[1] // width):
        bias[:, i * width : (i + 1) * width] = total[taps + 2 + i : taps + 3 + i]


def last_spread(scal, chunk, held, piece, plan, shapes, taps, hidden):
    src = chunk.their_rest
    width = src.shape[1]
    rows = 2 * R
    tail = pl.BlockSpec((rows, width), lambda g, s: (src.shape[0] // rows - 1, 0))
    small = ((1, width), (taps, width), (1, width), (1, hidden))

    def block(g, s):
        return ((s[1] ^ 1) * 2 + ((s[3] >> 3) ^ 1), 0)

    return pl.pallas_call(
        functools.partial(last_spread_kernel, piece=piece, plan=plan, taps=taps),
        grid_spec=pltpu.PrefetchScalarGridSpec(
            num_scalar_prefetch=1,
            grid=(1,),
            in_specs=[whole(src), whole(chunk.ride), tail, tail] + [ORDER] * len(held),
            out_specs=[pl.BlockSpec((dims[0] // 4, dims[1]), block) for dims in shapes]
            + [pl.BlockSpec(dims, lambda g, s: (0, 0)) for dims in small],
        ),
        out_shape=[pltpu.HBM(dims, f32) for dims in shapes] + [shape(dims) for dims in small],
        input_output_aliases={5 + k: k for k in range(len(held))},
        compiler_params=params(16),
        cost_estimate=SOME,
        name="spread_last",
    )(scal, src, chunk.ride, chunk.rest, chunk.theirs, *held)


def spread(scal, src, held, mate, flip, piece, plan, shapes, name):
    def block(g, s):
        return ((s[1] ^ mate) * 2 + ((s[2 + mate] >> 3) ^ flip), 0)

    count = len(held)
    return pl.pallas_call(
        functools.partial(spread_kernel, piece=piece, plan=plan, mate=mate),
        grid_spec=pltpu.PrefetchScalarGridSpec(
            num_scalar_prefetch=1,
            grid=(1,),
            in_specs=[whole(src)] + [ORDER] * count,
            out_specs=[pl.BlockSpec((dims[0] // 4, dims[1]), block) for dims in shapes],
        ),
        out_shape=[pltpu.HBM(dims, f32) for dims in shapes],
        input_output_aliases={2 + k: k for k in range(count)},
        compiler_params=params(16),
        cost_estimate=SOME,
        name=name,
    )(scal, src, *held)


def params(mib):
    return pltpu.CompilerParams(
        dimension_semantics=("arbitrary",), vmem_limit_bytes=mib * 1024 * 1024
    )


def shape(dims, kind=f32):
    return jax.ShapeDtypeStruct(dims, kind)


LITTLE = pl.CostEstimate(flops=1024, bytes_accessed=1024, transcendentals=0)
MUCH = pl.CostEstimate(flops=3 * 10**10, bytes_accessed=1024, transcendentals=0)
SOME = pl.CostEstimate(flops=8 * 10**9, bytes_accessed=1024, transcendentals=0)
ORDER = pl.BlockSpec(memory_space=pl.ANY)


def far(array):
    return pltpu.with_memory_space_constraint(array, pltpu.HBM)


def whole(array):
    zeros = (0,) * array.ndim
    return pl.BlockSpec(array.shape, lambda *a: zeros, pipeline_mode=pl.Buffered(1))


def passed_along(value, axis, steps):
    count = lax.axis_size(axis)
    leading, last = (max(0, -steps), min(count, count - steps))
    return lax.ppermute(value, axis, [(source, source + steps) for source in range(leading, last)])


def flat_permute(value, pairs):
    return lax.ppermute(value, ("seq", "row"), pairs)


def stage_bits():
    row_bits = lax.axis_size("row").bit_length() - 1
    seq_bits = lax.axis_size("seq").bit_length() - 1
    plane = list(range(row_bits))
    line = [row_bits + 1 + z for z in range(seq_bits - 1)]
    cut = row_bits // 2
    return (plane + line, plane[cut:] + plane[:cut] + line[::-1])


def slot_of(flat, bits):
    slot = 0
    for k in range(4):
        slot = slot * 2 + ((flat >> bits[k]) & 1)
    return slot


def halving_pairs(stage):
    row_bits = lax.axis_size("row").bit_length() - 1
    orders = stage_bits()
    devices = lax.axis_size("row") * lax.axis_size("seq")
    return [(d, d ^ (1 << orders[(d >> row_bits) & 1][stage])) for d in range(devices)]


def core_pairs():
    row_bits = lax.axis_size("row").bit_length() - 1
    devices = lax.axis_size("row") * lax.axis_size("seq")
    return [(d, d ^ (1 << row_bits)) for d in range(devices)]


def added(a, b):
    return (a.astype(f32) + b.astype(f32)).astype(bf16)


class Sequence:
    def __init__(self, token):
        self.token = token

    def after(self, *arrays):
        *arrays, _ = lax.optimization_barrier((*arrays, self.token))
        return arrays[0] if len(arrays) == 1 else arrays

    def did(self, array):
        self.token = array
        return array


def split(value):
    high = lax.reduce_precision(value, 8, 7)
    return [high.astype(bf16), (value - high).astype(bf16)]


def join_kernel(mine, recv, ride, out, ride_out):
    rows = mine.shape[0] - 2 * R
    out[0:rows, :] = mine[0:rows, :]
    out[rows : 2 * rows, :] = recv[0:rows, :]
    parts = recv[rows:, :].astype(f32)
    total = ride[...] + (parts[:R] + parts[R:])
    ride_out[...] = total
    high = total.astype(bf16).astype(f32)
    out[2 * rows :, :] = jnp.concatenate([high, total - high], 0).astype(bf16)


def chain_kernel(mine, recv, out):
    rows = mine.shape[0]
    out[0:rows, :] = mine[...]
    out[rows:, :] = recv[...]


def chained(mine, recv):
    rows, width = mine.shape
    return pl.pallas_call(
        chain_kernel,
        in_specs=[pl.BlockSpec(memory_space=pltpu.VMEM)] * 2,
        out_specs=pl.BlockSpec(memory_space=pltpu.VMEM),
        out_shape=shape((2 * rows, width), bf16),
        compiler_params=pltpu.CompilerParams(vmem_limit_bytes=16 * 1024 * 1024),
        cost_estimate=SOME,
        name="chain",
    )(mine, recv)


def joined(mine, recv, ride, estimate):
    rows, width = mine.shape
    return pl.pallas_call(
        join_kernel,
        in_specs=[pl.BlockSpec(memory_space=pltpu.VMEM)] * 3,
        out_specs=[pl.BlockSpec(memory_space=pltpu.VMEM)] * 2,
        out_shape=[shape((2 * rows - 2 * R, width), bf16), shape(ride.shape)],
        compiler_params=pltpu.CompilerParams(vmem_limit_bytes=16 * 1024 * 1024),
        cost_estimate=estimate,
        name="join",
    )(mine, recv, ride)


class Halving:
    def __init__(self, seq, send):
        self.seq = seq
        self.recv = flat_permute(send, core_pairs())
        self.stage = 0
        self.ride = None

    def riders(self):
        return [] if self.ride is None else split(self.ride)

    def step(self, *beside):
        k = self.stage
        self.stage += 1
        stages = len(stage_bits()[0])
        recv, *beside = self.seq.after(self.recv, *beside) if beside else (self.seq.after(self.recv),)
        if k < 4:
            half = self.keep.shape[0] // 2
            send = self.seq.did(added(self.keep[half:], recv[half:]))
            self.recv = flat_permute(send, halving_pairs(k))
            self.keep = added(self.keep[:half], recv[:half])
        elif k == 4:
            total = added(self.keep, recv)
            for extra in range(4, stages):
                total = added(total, flat_permute(total, halving_pairs(extra)))
                if self.ride is not None:
                    self.ride = self.ride + flat_permute(self.ride, halving_pairs(extra))
            self.rows = total.shape[0]
            self.total = self.seq.did(jnp.concatenate([total] + self.riders(), 0))
            self.recv = flat_permute(self.total, halving_pairs(3))
        elif k < 8:
            rows = self.rows
            self.rows = 2 * rows
            if self.ride is None:
                self.total = self.seq.did(chained(self.total, recv))
            else:
                self.total, self.ride = joined(
                    self.total, recv, self.ride, LITTLE if k == 5 else SOME
                )
                self.seq.did(self.total)
            self.recv = flat_permute(self.total, halving_pairs(7 - k))
            if k == 7:
                self.theirs = flat_permute(self.total, core_pairs())
        else:
            self.rest = recv
            self.their_rest = flat_permute(recv, core_pairs())
        return beside


def chip_shift(value, steps):
    return passed_along(value, "seq", 2 * steps)


def per_device(
    inputs,
    lengths,
    norm_gain,
    conv_weight,
    gate_weight,
    gate_bias,
    cand_weight,
    out_weight,
    mlp_gain,
    up_weight,
    down_weight,
    cotangent,
):
    rows, span, width = inputs.shape
    hidden = gate_weight.shape[1]
    feed = up_weight.shape[1]
    taps = conv_weight.shape[0]
    margin = taps - 1
    tokens = rows * span
    tb = 32
    blocks = span // tb
    m = tb * R
    seq = lax.axis_index("seq")
    core = seq & 1
    chips = lax.axis_size("seq") // 2
    hops = chips - 1
    flat = seq * lax.axis_size("row") + lax.axis_index("row")
    slots = [slot_of(flat, bits) for bits in stage_bits()]
    here = jnp.where(core == 0, slots[0], slots[1])
    mate = jnp.where(core == 0, slots[1], slots[0])
    scal = jnp.concatenate([jnp.stack([seq * span, core, here, mate]).astype(jnp.int32), lengths])
    gain1 = norm_gain.reshape(1, width)
    gain2 = mlp_gain.reshape(1, width)
    bias = gate_bias.reshape(1, hidden)
    to_pm, to_rm = token_order()

    edge = inputs[:, span - margin :, :].swapaxes(0, 1).reshape(margin * rows, width)
    edge = passed_along(edge, "seq", 1)

    last = blocks - 1
    clamp = lambda i: jnp.minimum(i, last)
    late = lambda i: jnp.maximum(i - blocks, 0)
    later = lambda i: jnp.minimum(i + 1, last)
    before = lambda i: jnp.maximum(i - 1, 0)

    def rm(index):
        return pl.BlockSpec((rows, tb, width), lambda i, *s: (0, index(i), 0))

    def tok(w, index=clamp):
        return pl.BlockSpec((m, w), lambda i, *s: (index(i), 0))

    def rtok(w):
        return tok(w, lambda i: last - clamp(i))

    def fixed(dims):
        zeros = (0,) * len(dims)
        return pl.BlockSpec(dims, lambda i, *s: zeros)

    def call(kernel, name, grid, ins, outs, scratch, operands, scalars=True, estimate=None):
        estimate = LITTLE if estimate is None else estimate
        spec = pltpu.PrefetchScalarGridSpec(
            num_scalar_prefetch=int(scalars),
            grid=(grid,),
            in_specs=ins,
            out_specs=[o[1] for o in outs],
            scratch_shapes=scratch,
        )
        return pl.pallas_call(
            kernel,
            grid_spec=spec,
            out_shape=[o[0] for o in outs],
            compiler_params=params(16),
            cost_estimate=estimate,
            name=name,
        )(*operands)

    def rows_of(w, kind, spec=tok, kept=shape):
        return kept((tokens, w), kind), spec(w)

    (normed,) = call(
        norm_kernel, "norm", blocks,
        [rm(clamp), whole(to_pm), whole(gain1)],
        [rows_of(width, bf16)],
        [],
        (far(inputs), far(to_pm), far(gain1)),
        scalars=False,
    )
    edge, normed = lax.optimization_barrier((edge, normed))
    c, zl, kh, ends = call(
        front_kernel, "front", blocks,
        [
            tok(width), whole(edge), whole(gain1), whole(conv_weight),
            whole(gate_weight), whole(bias), whole(cand_weight),
        ],
        [
            rows_of(width, bf16), rows_of(hidden, bf16), rows_of(hidden, bf16),
            (shape((2 * R, hidden)), fixed((2 * R, hidden))),
        ],
        [
            pltpu.VMEM((margin * R + m, width), f32),
            pltpu.VMEM((2 * R, hidden), f32),
            pltpu.VMEM((R, hidden), jnp.int32),
        ],
        (
            scal, normed, edge, far(gain1), far(conv_weight), gate_weight, far(bias),
            cand_weight,
        ),
    )

    other = flat_permute(ends, core_pairs())
    first = jnp.where(core == 0, ends, other)
    second = jnp.where(core == 0, other, ends)
    decay = jnp.log(jnp.maximum(ends[:R] * other[:R], 1e-37))
    message = jnp.concatenate([decay, second[:R] * first[R:] + second[R:]], 0).astype(bf16)
    forward = [chip_shift(message, k) for k in range(1, chips)]

    gl, da = call(
        da_kernel, "da", blocks,
        [rm(clamp), whole(to_pm), whole(down_weight)],
        [rows_of(width, bf16), rows_of(feed, bf16)],
        [],
        (cotangent, to_pm, down_weight),
        scalars=False,
    )

    r1, y, hp, n2, act, dp, dm, dr1, dh, back, mg = call(
        functools.partial(core_kernel, fchunk=256, hops=hops, blocks=blocks), "core", blocks,
        [
            rm(clamp), whole(to_pm), tok(width), tok(feed), tok(hidden), tok(hidden, later), tok(hidden),
            tok(hidden, later), tok(hidden, before), whole(other),
            *[whole(f) for f in forward], whole(out_weight), whole(gain2), whole(up_weight),
        ],
        [
            rows_of(width, f32, kept=pltpu.HBM), rows_of(hidden, bf16), rows_of(hidden, bf16),
            rows_of(width, bf16), rows_of(feed, bf16), rows_of(feed, bf16), rows_of(width, bf16),
            rows_of(width, f32, kept=pltpu.HBM),
            rows_of(hidden, bf16),
            (shape((R, hidden)), fixed((R, hidden))), (shape((R, width)), fixed((R, width))),
        ],
        [
            pltpu.VMEM((R, hidden), f32),
            pltpu.VMEM((R, hidden), jnp.int32),
            pltpu.VMEM((R, hidden), f32),
            pltpu.VMEM((m, width), f32),
            pltpu.VMEM((m, hidden), bf16),
            pltpu.VMEM((m, hidden), bf16),
            pltpu.VMEM((m, hidden), bf16),
        ],
        (
            scal, inputs, to_pm, gl, da, zl, zl, kh, kh, zl, other, *forward, far(out_weight), gain2, up_weight,
        ),
    )

    order = Sequence(back)
    quarter = feed // 4

    def ffn_grads(pick, *beside):
        half = lambda s: s[1] if pick == 0 else 1 - s[1]
        a, d, *beside = order.after(act, dp, *beside)
        (piece,) = call(
            functools.partial(ffn_grad_kernel, pick=pick), "ffn_grad", 2,
            [
                pl.BlockSpec((tokens, quarter), lambda i, s: (0, half(s) * 2 + i)), whole(gl),
                pl.BlockSpec((tokens, width // 2), lambda i, s: (0, half(s))),
                pl.BlockSpec((tokens, feed // 2), lambda i, s: (0, i)),
            ],
            [(shape((SLOTS // 2 * PIECE1, width), bf16), fixed((SLOTS // 2 * PIECE1, width)))],
            [],
            (scal, a, gl, n2, d),
            estimate=MUCH if pick == 0 else LITTLE,
        )
        return order.did(piece), beside

    def gate_grads(pick):
        half = lambda s: s[1] if pick == 0 else 1 - s[1]
        z, h = order.after(dkz, dkh)
        (piece,) = call(
            functools.partial(gate_grad_kernel, pick=pick), "gate_grad", 1,
            [
                pl.BlockSpec((tokens, width // 2), lambda i, s: (0, half(s))),
                whole(z), whole(h),
                pl.BlockSpec((tokens, hidden // 2), lambda i, s: (0, half(s))), whole(dm),
            ],
            [(shape((SLOTS // 2 * PIECE2, width), bf16), fixed((SLOTS // 2 * PIECE2, width)))],
            [],
            (scal, c, z, h, y, dm),
            estimate=SOME if pick == 0 else LITTLE,
        )
        return order.did(piece)

    fother = flat_permute(back, core_pairs())
    lower = jnp.where(core == 0, back, fother)
    upper = jnp.where(core == 0, fother, back)
    message = jnp.concatenate([decay, lower + first[:R] * upper], 0).astype(bf16)
    backward = [chip_shift(order.did(message), -k) for k in range(1, chips)]
    send1, _ = ffn_grads(1)
    chunk1 = Halving(order, send1)
    chunk1.keep, backward = ffn_grads(0, *backward)
    chunk1.step()

    dkz, dkh, edge_dc, bias_part = call(
        functools.partial(gate_kernel, blocks=blocks, hops=hops), "gates", blocks,
        [
            rtok(hidden), rtok(hidden), rtok(hidden), rtok(hidden),
            whole(other), whole(fother), *[whole(f) for f in backward],
            whole(gate_weight), whole(cand_weight), ORDER,
        ],
        [
            rows_of(hidden, bf16, rtok), rows_of(hidden, bf16, rtok),
            (shape((4 * R, width), bf16), fixed((4 * R, width))),
            (shape((R, hidden)), fixed((R, hidden))),
        ],
        [pltpu.VMEM((R, hidden), f32)],
        (
            scal, dh, zl, kh, hp, other, fother, *backward, gate_weight, cand_weight, order.token,
        ),
    )
    order.did(bias_part)
    after = passed_along(edge_dc[: margin * R], "seq", -1)
    send2 = gate_grads(1)
    chunk2 = Halving(order, send2)
    (output,) = call(
        output_kernel, "output", blocks,
        [tok(width), tok(feed), whole(to_rm), whole(down_weight)],
        [(shape((rows, span, width), bf16), rm(clamp))],
        [],
        (far(r1), order.after(act), to_rm, down_weight),
        scalars=False,
    )
    order.did(output)
    chunk1.step()
    chunk2.keep = gate_grads(0)
    (after,) = chunk2.step(after)
    input_grad, sums = call(
        functools.partial(tail_kernel, blocks=blocks), "tail", 2 * blocks,
        [
            rm(late), tok(width, late), tok(hidden), tok(hidden), whole(to_pm), whole(to_rm),
            whole(edge), whole(after), whole(gain1), whole(conv_weight), whole(gate_weight),
            whole(cand_weight),
        ],
        [
            (shape((rows, span, width), bf16), rm(late)),
            (shape(((taps + 1) * R, width)), fixed(((taps + 1) * R, width))),
        ],
        [
            pltpu.VMEM((margin * R + m, width), f32),
            pltpu.VMEM((margin * R + tokens, width), f32),
        ],
        (
            far(inputs), far(dr1), order.after(dkz), dkh, far(to_pm), far(to_rm), edge, after,
            far(gain1), far(conv_weight), far(gate_weight), far(cand_weight),
        ),
        scalars=False,
    )
    order.did(sums)
    small = jnp.concatenate(
        [
            sums.reshape(taps + 1, R, width).sum(1),
            mg.sum(0, keepdims=True),
            bias_part.sum(0).reshape(hidden // width, width),
        ],
        0,
    )

    plan1 = ((0, feed // SLOTS, 1), (1, width // SLOTS, feed // width))
    shapes1 = ((feed, width), (width, feed))
    plan2 = (
        (0, width // SLOTS, hidden // width),
        (1, width // SLOTS, hidden // width),
        (2, hidden // SLOTS, 1),
    )
    shapes2 = ((width, hidden), (width, hidden), (hidden, width))
    held1, held2 = (), ()

    def spread1(src, mate, flip):
        nonlocal held1
        src = order.after(src)
        held1 = spread(scal, src, held1, mate, flip, PIECE1, plan1, shapes1, "spread_ffn")
        order.did(held1[0])

    def spread2(src, mate, flip):
        nonlocal held2
        src = order.after(src)
        held2 = spread(scal, src, held2, mate, flip, PIECE2, plan2, shapes2, "spread_gates")
        order.did(held2[0])

    chunk2.ride = small
    for chunk in (chunk1, chunk2, chunk1, chunk2, chunk1, chunk2, chunk1, chunk2):
        chunk.step()
    chunk2.step()
    chunk1.step()
    chunk2.step()
    chunk1.step()
    chunk2.step()
    spread1(chunk1.total, 0, 0)
    spread1(chunk1.theirs, 1, 0)
    chunk1.step()
    spread1(chunk1.rest, 0, 1)
    spread2(chunk2.total, 0, 0)
    spread1(chunk1.their_rest, 1, 1)
    spread2(chunk2.theirs, 1, 0)
    chunk2.step()
    spread2(chunk2.rest, 0, 1)
    chunk2.their_rest = order.after(chunk2.their_rest)
    *held2, norm_sum, conv_sum, mlp_sum, bias_sum = last_spread(
        scal, chunk2, held2, PIECE2, plan2, shapes2, taps, hidden
    )
    return (
        output,
        input_grad,
        norm_sum.reshape(width),
        conv_sum,
        held2[0],
        bias_sum.reshape(hidden),
        held2[1],
        held2[2],
        mlp_sum.reshape(width),
        held1[1],
        held1[0],
    )


def solution(mesh):
    sharded = P("row", "seq", None)
    in_specs = (sharded, P("row")) + (P(),) * 9 + (sharded,)
    out_specs = (sharded, sharded) + (P(),) * 9
    return jax.shard_map(
        per_device, mesh=mesh, in_specs=in_specs, out_specs=out_specs, check_vma=False
    )
```

```python
import functools

import jax
import jax.numpy as jnp
import numpy as np
from jax import lax
from jax.experimental import pallas as pl
from jax.experimental.pallas import tpu as pltpu
from jax.sharding import PartitionSpec as P

epsilon = 1e-06
f32 = jnp.float32
bf16 = jnp.bfloat16
R = 8
PERM = 256
SCALARS = 4
SLOTS = 32
PIECE1 = 128
PIECE2 = 96


def nn(a, b):
    return lax.dot_general(a, b, (((1,), (0,)), ((), ())), preferred_element_type=f32)


def nt(a, b):
    return lax.dot_general(a, b, (((1,), (1,)), ((), ())), preferred_element_type=f32)


def tn(a, b):
    return lax.dot_general(a, b, (((0,), (0,)), ((), ())), preferred_element_type=f32)


def token_order():
    out = np.arange(PERM)
    source = (out % R) * (PERM // R) + out // R
    to_pm = np.zeros((PERM, PERM), np.float32)
    to_pm[out, source] = 1
    return jnp.asarray(to_pm, bf16), jnp.asarray(to_pm.T, bf16)


def position_major(perm, block):
    span = PERM // R
    parts = []
    for s in range(block.shape[1] // span):
        part = block[:, s * span : (s + 1) * span, :].reshape(PERM, block.shape[2])
        parts.append(nn(perm, part))
    return parts[0] if len(parts) == 1 else jnp.concatenate(parts, 0)


def row_major(perm, tokens):
    span = PERM // R
    parts = []
    for s in range(tokens.shape[0] // PERM):
        part = nn(perm, tokens[s * PERM : (s + 1) * PERM]).astype(bf16)
        parts.append(part.reshape(R, span, tokens.shape[1]))
    return parts[0] if len(parts) == 1 else jnp.concatenate(parts, 1)


def eight(t):
    return pl.ds(pl.multiple_of(t * R, R), R)


def sixteen(t):
    return pl.ds(pl.multiple_of(t * 2 * R, 2 * R), 2 * R)


def normed_edge(edge, gain):
    e = edge.astype(f32)
    inv = lax.rsqrt(jnp.mean(e * e, -1, keepdims=True) + epsilon)
    return (e * inv * gain).astype(bf16).astype(f32)


def set_limits(scal, limit):
    row = lax.broadcasted_iota(jnp.int32, limit.shape, 0)
    value = jnp.zeros(limit.shape, jnp.int32)
    for r in range(R):
        value = jnp.where(row == r, scal[SCALARS + r], value)
    limit[...] = value


def halves(ref, pair):
    both = ref[sixteen(pair), :].astype(f32)
    return both[:R], both[R:]


def norm_kernel(x, perm, gain, u_out):
    xp = position_major(perm[...], x[...])
    inv = lax.rsqrt(jnp.mean(xp * xp, -1, keepdims=True) + epsilon)
    u_out[...] = (xp * inv * gain[...]).astype(bf16)


def front_kernel(scal, u, edge, gain, convw, wg, bias, wc, c_out, zl_out, kh_out, ends, ext, state, limit):
    step = pl.program_id(0)
    m = u.shape[0]
    tb = m // R
    halo = edge.shape[0]
    taps = convw.shape[0]

    @pl.when(step == 0)
    def _():
        set_limits(scal, limit)
        ext[0:halo, :] = normed_edge(edge[...], gain[...])
        state[0:R, :] = jnp.ones((R, state.shape[1]), f32)
        state[R:, :] = jnp.zeros((R, state.shape[1]), f32)

    ext[halo:, :] = u[...].astype(f32)
    conv = convw[0:1, :] * ext[halo:, :]
    for k in range(1, taps):
        lo = halo - k * R
        conv = conv + convw[k : k + 1, :] * ext[lo : lo + m, :]
    ext[0:halo, :] = ext[m : m + halo, :]
    cb = conv.astype(bf16)
    c_out[...] = cb
    kz = nn(cb, wg[...]) + bias[...]
    zs = 1.0 / (1.0 + jnp.exp(-kz))
    width = zs.shape[1]
    zs = zs.reshape(tb, R, width)
    pos = scal[0] + step * tb + lax.broadcasted_iota(jnp.int32, (tb, R, width), 0)
    zl_out[...] = jnp.where(pos < limit[...][None], zs, 0.0).reshape(m, width).astype(bf16)
    kh_out[...] = nn(cb, wc[...]).astype(bf16)

    def body(u, carry):
        prod, h = carry
        za, zb = halves(zl_out, u)
        ka, kb = halves(kh_out, u)
        a = 1.0 - za
        b = 1.0 - zb
        return prod * (a * b), (h * a + za * ka) * b + zb * kb

    prod, h = lax.fori_loop(0, tb // 2, body, (state[0:R, :], state[R:, :]), unroll=4)
    state[0:R, :] = prod
    state[R:, :] = h
    ends[0:R, :] = prod
    ends[R:, :] = h


def gelu_parts(p):
    k0 = 0.7978845608028654
    inner = p * (k0 + (k0 * 0.044715) * (p * p))
    th = jnp.tanh(inner)
    ht = 0.5 + 0.5 * th
    return p * ht, ht + (1.0 - th * th) * (1.5 * inner - k0 * p)


def da_kernel(g, perm, wd, gl_out, da_out):
    gl = position_major(perm[...], g[...]).astype(bf16)
    gl_out[...] = gl
    da_out[...] = nt(gl, wd[...]).astype(bf16)


def core_kernel(scal, x, perm, gl, da, zl, zl_next, kh, kh_next, zl_before, other, *refs, fchunk, hops, blocks):
    msgs = refs[:hops]
    wo, mgain, wu = refs[hops : hops + 3]
    r1_out, y_out, hp_out, n2_out, act_out, dp_out, dm_out, dr1_out, dh_out, back, mg = refs[hops + 3 : hops + 14]
    state, limit, run, acc, ys, hps, dhs = refs[hops + 14 :]
    step = pl.program_id(0)
    tb = x.shape[1]
    m = tb * R
    width, feed = wu.shape
    hidden = wo.shape[0]
    first = scal[0] + step * tb

    def scan_pair(zs, ks, start, u, h):
        t = u * 2
        za, zb = halves(zs, u)
        ka, kb = halves(ks, u)
        ha = h - za * h + za * ka
        hb = ha - zb * ha + zb * kb
        hps[sixteen(u), :] = jnp.concatenate([h, ha], 0).astype(bf16)
        ya = jnp.where(start + t < limit[...], ha, 0.0)
        yb = jnp.where(start + t + 1 < limit[...], hb, 0.0)
        ys[sixteen(u), :] = jnp.concatenate([ya, yb], 0).astype(bf16)
        return hb

    def adjoint_pair(zs, ds, u, prod, total):
        za, zb = halves(zs, u)
        da, db = halves(ds, u)
        pa = prod - za * prod
        pb = pa - zb * pa
        return pb, total + (pa * da + pb * db)

    @pl.when(step == 0)
    def _():
        set_limits(scal, limit)
        h = jnp.zeros((R, hidden), f32)
        for msg in reversed(msgs):
            both = msg[...].astype(f32)
            h = jnp.exp(both[0:R, :]) * h + both[R:, :]
        h = jnp.where(scal[1] == 1, other[0:R, :] * h + other[R:, :], h)
        run[...] = jnp.ones((R, hidden), f32)
        back[...] = jnp.zeros(back.shape, f32)
        mg[...] = jnp.zeros(mg.shape, f32)
        dhs[...] = jnp.zeros(dhs.shape, bf16)
        state[...] = lax.fori_loop(0, tb // 2, lambda u, h: scan_pair(zl, kh, scal[0], u, h), h, unroll=2)

    hp_out[...] = hps[...]
    y = ys[...]
    y_out[...] = y
    r1 = position_major(perm[...], x[...]) + nn(y, wo[...])
    r1_out[...] = r1
    inv = lax.rsqrt(jnp.mean(r1 * r1, -1, keepdims=True) + epsilon)
    n2 = (r1 * inv * mgain[...]).astype(bf16)
    n2_out[...] = n2
    chunks = feed // fchunk
    pairs = tb // 2 // chunks
    for f in range(chunks):
        cols = slice(f * fchunk, (f + 1) * fchunk)
        a, slope = gelu_parts(nn(n2, wu[:, cols]).astype(bf16))
        act_out[:, cols] = a
        dpb = da[:, cols] * slope
        dp_out[:, cols] = dpb
        part = nt(dpb, wu[:, cols])
        acc[...] = acc[...] + part if f else part
        h, prod, total = state[...], run[...], back[...]
        for u in range(f * pairs, (f + 1) * pairs):
            h = scan_pair(zl_next, kh_next, first + tb, u, h)
            prod, total = adjoint_pair(zl_before, dhs, u, prod, total)
        state[...] = h
        run[...] = jnp.where(step == 0, 1.0, prod)
        back[...] = total
    dn2 = acc[...]
    r1 = r1_out[...]
    mg[...] += jnp.sum((dn2 * r1 * inv).reshape(tb, R, width), 0)
    s = mgain[...] * dn2
    mean = jnp.mean(s * r1, -1, keepdims=True)
    dr1 = gl[...].astype(f32) + inv * (s - r1 * (inv * inv * mean))
    dr1_out[...] = dr1
    dm = dr1.astype(bf16)
    dm_out[...] = dm
    dh = nt(dm, wo[...]).reshape(tb, R, hidden)
    pos = first + lax.broadcasted_iota(jnp.int32, (tb, R, hidden), 0)
    dh = jnp.where(pos < limit[...][None], dh, 0.0).reshape(m, hidden).astype(bf16)
    dh_out[...] = dh
    dhs[...] = dh

    @pl.when(step == blocks - 1)
    def _():
        carry = lax.fori_loop(
            0, tb // 2, lambda u, carry: adjoint_pair(zl, dhs, u, *carry), (run[...], back[...]), unroll=4
        )
        back[...] = carry[1]


def put_rows(dst, sel, piece, at, rows, part):
    for i in range(SLOTS // 2):
        pos = pl.multiple_of((i ^ sel) * piece + at, 16)
        dst[pl.ds(pos, rows), :] = part[i * rows : (i + 1) * rows]


def ffn_grad_kernel(scal, act, gl, n2, dp, dst, *, pick):
    step = pl.program_id(0)
    sel = scal[2 + pick]
    width = gl.shape[1]
    rows1 = act.shape[1] * 4 // SLOTS
    rows2 = n2.shape[1] * 2 // SLOTS
    part = tn(act[...], gl[...]).astype(bf16)
    per = act.shape[1] // rows1
    for i in range(per):
        pos = ((step * per + i) ^ sel) * PIECE1
        dst[pl.ds(pl.multiple_of(pos, 16), rows1), :] = part[i * rows1 : (i + 1) * rows1]
    columns = dp.shape[1] // width
    for q in range(columns):
        part = tn(n2[...], dp[:, q * width : (q + 1) * width]).astype(bf16)
        put_rows(dst, sel, PIECE1, rows1 + (step * columns + q) * rows2, rows2, part)


def gate_grad_kernel(scal, c, dkz, dkh, y, dm, dst, *, pick):
    sel = scal[2 + pick]
    width = dm.shape[1]
    rows = c.shape[1] * 2 // SLOTS
    at = 0
    for grads in (dkz, dkh):
        for q in range(grads.shape[1] // width):
            part = tn(c[...], grads[:, q * width : (q + 1) * width]).astype(bf16)
            put_rows(dst, sel, PIECE2, at, rows, part)
            at += rows
    put_rows(dst, sel, PIECE2, at, y.shape[1] * 2 // SLOTS, tn(y[...], dm[...]).astype(bf16))


def gate_kernel(scal, dh, zl, kh, hp, other, fother, *refs, blocks, hops):
    msgs = refs[:hops]
    wg, wc = refs[hops : hops + 2]
    dkz, dkh, edge_out, bias_out = refs[hops + 3 : hops + 7]
    state = refs[hops + 7]
    step = pl.program_id(0)
    m = dh.shape[0]
    tb = m // R
    block = blocks - 1 - step

    @pl.when(step == 0)
    def _():
        mm = jnp.zeros(state.shape, f32)
        for msg in reversed(msgs):
            both = msg[...].astype(f32)
            mm = jnp.exp(both[0:R, :]) * mm + both[R:, :]
        state[...] = jnp.where(scal[1] == 0, fother[...] + other[0:R, :] * mm, mm)
        bias_out[...] = jnp.zeros(bias_out.shape, f32)

    def body(u, carry):
        mm, bias = carry
        w = tb // 2 - 1 - u
        ha, hb = halves(hp, w)
        za, zb = halves(zl, w)
        da, db = halves(dh, w)
        ka, kb = halves(kh, w)
        lam = db + mm
        sb = lam * zb
        mm = lam - sb
        kb = (sb - sb * zb) * (kb - hb)
        lam = da + mm
        sa = lam * za
        mm = lam - sa
        ka = (sa - sa * za) * (ka - ha)
        kk = jnp.concatenate([ka, kb], 0).astype(bf16)
        dkz[sixteen(w), :] = kk
        dkh[sixteen(w), :] = jnp.concatenate([sa, sb], 0).astype(bf16)
        kf = kk.astype(f32)
        return mm, bias + kf[:R, :] + kf[R:, :]

    mm, bias = lax.fori_loop(0, tb // 2, body, (state[...], bias_out[...]), unroll=2)
    state[...] = mm
    bias_out[...] = bias

    @pl.when(block == 0)
    def _():
        span = edge_out.shape[0]
        edge_out[...] = (nt(dkz[0:span, :], wg[...]) + nt(dkh[0:span, :], wc[...])).astype(bf16)


def tail_kernel(x, dr1, dkz, dkh, pm, back_pm, edge, after, gain, convw, wg, wc, grad, sums, uext, dext, *, blocks):
    step = pl.program_id(0)
    tb = x.shape[1]
    m = tb * R
    halo = edge.shape[0]
    taps = convw.shape[0]
    width = gain.shape[1]

    @pl.when(step == 0)
    def _():
        uext[0:halo, :] = normed_edge(edge[...], gain[...])
        dext[blocks * m :, :] = after[...].astype(f32)
        sums[...] = jnp.zeros(sums.shape, f32)

    @pl.when(step < blocks)
    def _():
        rows = pl.ds(pl.multiple_of(step * m, m), m)
        dext[rows, :] = nt(dkz[...], wg[...]) + nt(dkh[...], wc[...])

    @pl.when(step >= blocks)
    def _():
        xp = position_major(pm[...], x[...])
        inv = lax.rsqrt(jnp.mean(xp * xp, -1, keepdims=True) + epsilon)
        xn = xp * inv
        uext[halo:, :] = (xn * gain[...]).astype(bf16).astype(f32)
        start = (step - blocks) * m
        here = dext[pl.ds(pl.multiple_of(start, R), m), :]
        du = convw[0:1, :] * here
        for k in range(taps):
            lo = halo - k * R
            part = (here * uext[lo : lo + m, :]).reshape(tb, R, width)
            sums[(k + 1) * R : (k + 2) * R, :] += jnp.sum(part, 0)
            if k:
                du = du + convw[k : k + 1, :] * dext[pl.ds(pl.multiple_of(start + k * R, R), m), :]
        uext[0:halo, :] = uext[m : m + halo, :]
        sums[0:R, :] += jnp.sum((du * xn).reshape(tb, R, width), 0)
        s1 = gain[...] * du
        mean = jnp.mean(s1 * xn, -1, keepdims=True)
        gin = dr1[...] + inv * (s1 - xn * mean)
        grad[...] = row_major(back_pm[...], gin.astype(bf16))


def output_kernel(r1, act, perm, wd, out):
    total = r1[...] + nn(act[...], wd[...])
    out[...] = row_major(perm[...], total.astype(bf16))


def spread_kernel(scal, src, *refs, piece, plan, mate):
    low = scal[2 + mate] & 7
    for a in range(8):
        base = (a ^ low) * piece
        at = 0
        for out, rows, columns in plan:
            ref = refs[len(refs) - len(plan) + out]
            for q in range(columns):
                width = src.shape[1]
                part = src[pl.ds(pl.multiple_of(base + at, 16), rows), :].astype(f32)
                ref[a * rows : (a + 1) * rows, q * width : (q + 1) * width] = part
                at += rows


def last_spread_kernel(scal, src, ride, rest, theirs, *refs, piece, plan, taps):
    norm, conv, mlp, bias = refs[-4:]
    spread_kernel(scal, src, *refs[:-4], piece=piece, plan=plan, mate=1)
    tail = src.shape[0] - 2 * R
    total = ride[...]
    for rows in (rest[...], theirs[...], src[tail:, :]):
        both = rows.astype(f32)
        total = total + (both[:R] + both[R:])
    norm[...] = total[0:1]
    conv[...] = total[1 : taps + 1]
    mlp[...] = total[taps + 1 : taps + 2]
    width = total.shape[1]
    for i in range(bias.shape[1] // width):
        bias[:, i * width : (i + 1) * width] = total[taps + 2 + i : taps + 3 + i]


def last_spread(scal, chunk, held, piece, plan, shapes, taps, hidden):
    src = chunk.their_rest
    width = src.shape[1]
    rows = 2 * R
    tail = pl.BlockSpec((rows, width), lambda g, s: (src.shape[0] // rows - 1, 0))
    small = ((1, width), (taps, width), (1, width), (1, hidden))

    def block(g, s):
        return ((s[1] ^ 1) * 2 + ((s[3] >> 3) ^ 1), 0)

    return pl.pallas_call(
        functools.partial(last_spread_kernel, piece=piece, plan=plan, taps=taps),
        grid_spec=pltpu.PrefetchScalarGridSpec(
            num_scalar_prefetch=1,
            grid=(1,),
            in_specs=[whole(src), whole(chunk.ride), tail, tail] + [ORDER] * len(held),
            out_specs=[pl.BlockSpec((dims[0] // 4, dims[1]), block) for dims in shapes]
            + [pl.BlockSpec(dims, lambda g, s: (0, 0)) for dims in small],
        ),
        out_shape=[pltpu.HBM(dims, f32) for dims in shapes] + [shape(dims) for dims in small],
        input_output_aliases={5 + k: k for k in range(len(held))},
        compiler_params=params(16),
        cost_estimate=SOME,
        name="spread_last",
    )(scal, src, chunk.ride, chunk.rest, chunk.theirs, *held)


def spread(scal, src, held, mate, flip, piece, plan, shapes, name):
    def block(g, s):
        return ((s[1] ^ mate) * 2 + ((s[2 + mate] >> 3) ^ flip), 0)

    count = len(held)
    return pl.pallas_call(
        functools.partial(spread_kernel, piece=piece, plan=plan, mate=mate),
        grid_spec=pltpu.PrefetchScalarGridSpec(
            num_scalar_prefetch=1,
            grid=(1,),
            in_specs=[whole(src)] + [ORDER] * count,
            out_specs=[pl.BlockSpec((dims[0] // 4, dims[1]), block) for dims in shapes],
        ),
        out_shape=[pltpu.HBM(dims, f32) for dims in shapes],
        input_output_aliases={2 + k: k for k in range(count)},
        compiler_params=params(16),
        cost_estimate=SOME,
        name=name,
    )(scal, src, *held)


def params(mib):
    return pltpu.CompilerParams(
        dimension_semantics=("arbitrary",), vmem_limit_bytes=mib * 1024 * 1024
    )


def shape(dims, kind=f32):
    return jax.ShapeDtypeStruct(dims, kind)


LITTLE = pl.CostEstimate(flops=1024, bytes_accessed=1024, transcendentals=0)
MUCH = pl.CostEstimate(flops=3 * 10**10, bytes_accessed=1024, transcendentals=0)
SOME = pl.CostEstimate(flops=10**10, bytes_accessed=1024, transcendentals=0)
ORDER = pl.BlockSpec(memory_space=pl.ANY)


def far(array):
    return pltpu.with_memory_space_constraint(array, pltpu.HBM)


def whole(array):
    zeros = (0,) * array.ndim
    return pl.BlockSpec(array.shape, lambda *a: zeros, pipeline_mode=pl.Buffered(1))


def passed_along(value, axis, steps):
    count = lax.axis_size(axis)
    leading, last = (max(0, -steps), min(count, count - steps))
    return lax.ppermute(value, axis, [(source, source + steps) for source in range(leading, last)])


def flat_permute(value, pairs):
    return lax.ppermute(value, ("seq", "row"), pairs)


def stage_bits():
    row_bits = lax.axis_size("row").bit_length() - 1
    seq_bits = lax.axis_size("seq").bit_length() - 1
    plane = list(range(row_bits))
    line = [row_bits + 1 + z for z in range(seq_bits - 1)]
    cut = row_bits // 2
    return (plane + line, plane[cut:] + plane[:cut] + line[::-1])


def slot_of(flat, bits):
    slot = 0
    for k in range(4):
        slot = slot * 2 + ((flat >> bits[k]) & 1)
    return slot


def halving_pairs(stage):
    row_bits = lax.axis_size("row").bit_length() - 1
    orders = stage_bits()
    devices = lax.axis_size("row") * lax.axis_size("seq")
    return [(d, d ^ (1 << orders[(d >> row_bits) & 1][stage])) for d in range(devices)]


def core_pairs():
    row_bits = lax.axis_size("row").bit_length() - 1
    devices = lax.axis_size("row") * lax.axis_size("seq")
    return [(d, d ^ (1 << row_bits)) for d in range(devices)]


def added(a, b):
    return (a.astype(f32) + b.astype(f32)).astype(bf16)


class Sequence:
    def __init__(self, token):
        self.token = token

    def after(self, *arrays):
        *arrays, _ = lax.optimization_barrier((*arrays, self.token))
        return arrays[0] if len(arrays) == 1 else arrays

    def did(self, array):
        self.token = array
        return array


def split(value):
    high = lax.reduce_precision(value, 8, 7)
    return [high.astype(bf16), (value - high).astype(bf16)]


def join_kernel(mine, recv, ride, out, ride_out):
    rows = mine.shape[0] - 2 * R
    out[0:rows, :] = mine[0:rows, :]
    out[rows : 2 * rows, :] = recv[0:rows, :]
    parts = recv[rows:, :].astype(f32)
    total = ride[...] + (parts[:R] + parts[R:])
    ride_out[...] = total
    high = total.astype(bf16).astype(f32)
    out[2 * rows :, :] = jnp.concatenate([high, total - high], 0).astype(bf16)


def chain_kernel(mine, recv, out):
    rows = mine.shape[0]
    out[0:rows, :] = mine[...]
    out[rows:, :] = recv[...]


def chained(mine, recv):
    rows, width = mine.shape
    return pl.pallas_call(
        chain_kernel,
        in_specs=[pl.BlockSpec(memory_space=pltpu.VMEM)] * 2,
        out_specs=pl.BlockSpec(memory_space=pltpu.VMEM),
        out_shape=shape((2 * rows, width), bf16),
        compiler_params=pltpu.CompilerParams(vmem_limit_bytes=16 * 1024 * 1024),
        cost_estimate=SOME,
        name="chain",
    )(mine, recv)


def joined(mine, recv, ride, estimate):
    rows, width = mine.shape
    return pl.pallas_call(
        join_kernel,
        in_specs=[pl.BlockSpec(memory_space=pltpu.VMEM)] * 3,
        out_specs=[pl.BlockSpec(memory_space=pltpu.VMEM)] * 2,
        out_shape=[shape((2 * rows - 2 * R, width), bf16), shape(ride.shape)],
        compiler_params=pltpu.CompilerParams(vmem_limit_bytes=16 * 1024 * 1024),
        cost_estimate=estimate,
        name="join",
    )(mine, recv, ride)


class Halving:
    def __init__(self, seq, send):
        self.seq = seq
        self.recv = flat_permute(send, core_pairs())
        self.stage = 0
        self.ride = None

    def riders(self):
        return [] if self.ride is None else split(self.ride)

    def step(self, *beside):
        k = self.stage
        self.stage += 1
        stages = len(stage_bits()[0])
        recv, *beside = self.seq.after(self.recv, *beside) if beside else (self.seq.after(self.recv),)
        if k < 4:
            half = self.keep.shape[0] // 2
            send = self.seq.did(added(self.keep[half:], recv[half:]))
            self.recv = flat_permute(send, halving_pairs(k))
            self.keep = added(self.keep[:half], recv[:half])
        elif k == 4:
            total = added(self.keep, recv)
            for extra in range(4, stages):
                total = added(total, flat_permute(total, halving_pairs(extra)))
                if self.ride is not None:
                    self.ride = self.ride + flat_permute(self.ride, halving_pairs(extra))
            self.rows = total.shape[0]
            self.total = self.seq.did(jnp.concatenate([total] + self.riders(), 0))
            self.recv = flat_permute(self.total, halving_pairs(3))
        elif k < 8:
            rows = self.rows
            self.rows = 2 * rows
            if self.ride is None:
                self.total = self.seq.did(chained(self.total, recv))
            else:
                self.total, self.ride = joined(
                    self.total, recv, self.ride, LITTLE if k == 5 else SOME
                )
                self.seq.did(self.total)
            self.recv = flat_permute(self.total, halving_pairs(7 - k))
            if k == 7:
                self.theirs = flat_permute(self.total, core_pairs())
        else:
            self.rest = recv
            self.their_rest = flat_permute(recv, core_pairs())
        return beside


def chip_shift(value, steps):
    return passed_along(value, "seq", 2 * steps)


def per_device(
    inputs,
    lengths,
    norm_gain,
    conv_weight,
    gate_weight,
    gate_bias,
    cand_weight,
    out_weight,
    mlp_gain,
    up_weight,
    down_weight,
    cotangent,
):
    rows, span, width = inputs.shape
    hidden = gate_weight.shape[1]
    feed = up_weight.shape[1]
    taps = conv_weight.shape[0]
    margin = taps - 1
    tokens = rows * span
    tb = 32
    blocks = span // tb
    m = tb * R
    seq = lax.axis_index("seq")
    core = seq & 1
    chips = lax.axis_size("seq") // 2
    hops = chips - 1
    flat = seq * lax.axis_size("row") + lax.axis_index("row")
    slots = [slot_of(flat, bits) for bits in stage_bits()]
    here = jnp.where(core == 0, slots[0], slots[1])
    mate = jnp.where(core == 0, slots[1], slots[0])
    scal = jnp.concatenate([jnp.stack([seq * span, core, here, mate]).astype(jnp.int32), lengths])
    gain1 = norm_gain.reshape(1, width)
    gain2 = mlp_gain.reshape(1, width)
    bias = gate_bias.reshape(1, hidden)
    to_pm, to_rm = token_order()

    edge = inputs[:, span - margin :, :].swapaxes(0, 1).reshape(margin * rows, width)
    edge = passed_along(edge, "seq", 1)

    last = blocks - 1
    clamp = lambda i: jnp.minimum(i, last)
    late = lambda i: jnp.maximum(i - blocks, 0)
    later = lambda i: jnp.minimum(i + 1, last)
    before = lambda i: jnp.maximum(i - 1, 0)

    def rm(index):
        return pl.BlockSpec((rows, tb, width), lambda i, *s: (0, index(i), 0))

    def tok(w, index=clamp):
        return pl.BlockSpec((m, w), lambda i, *s: (index(i), 0))

    def rtok(w):
        return tok(w, lambda i: last - clamp(i))

    def fixed(dims):
        zeros = (0,) * len(dims)
        return pl.BlockSpec(dims, lambda i, *s: zeros)

    def call(kernel, name, grid, ins, outs, scratch, operands, scalars=True, much=False, mib=16):
        spec = pltpu.PrefetchScalarGridSpec(
            num_scalar_prefetch=int(scalars),
            grid=(grid,),
            in_specs=ins,
            out_specs=[o[1] for o in outs],
            scratch_shapes=scratch,
        )
        return pl.pallas_call(
            kernel,
            grid_spec=spec,
            out_shape=[o[0] for o in outs],
            compiler_params=params(mib),
            cost_estimate=MUCH if much else LITTLE,
            name=name,
        )(*operands)

    def rows_of(w, kind, spec=tok, kept=shape):
        return kept((tokens, w), kind), spec(w)

    (normed,) = call(
        norm_kernel, "norm", blocks,
        [rm(clamp), whole(to_pm), whole(gain1)],
        [rows_of(width, bf16)],
        [],
        (far(inputs), far(to_pm), far(gain1)),
        scalars=False,
    )
    edge, normed = lax.optimization_barrier((edge, normed))
    c, zl, kh, ends = call(
        front_kernel, "front", blocks,
        [
            tok(width), whole(edge), whole(gain1), whole(conv_weight),
            whole(gate_weight), whole(bias), whole(cand_weight),
        ],
        [
            rows_of(width, bf16), rows_of(hidden, bf16), rows_of(hidden, bf16),
            (shape((2 * R, hidden)), fixed((2 * R, hidden))),
        ],
        [
            pltpu.VMEM((margin * R + m, width), f32),
            pltpu.VMEM((2 * R, hidden), f32),
            pltpu.VMEM((R, hidden), jnp.int32),
        ],
        (
            scal, normed, edge, far(gain1), far(conv_weight), gate_weight, far(bias),
            cand_weight,
        ),
    )

    other = flat_permute(ends, core_pairs())
    first = jnp.where(core == 0, ends, other)
    second = jnp.where(core == 0, other, ends)
    decay = jnp.log(jnp.maximum(ends[:R] * other[:R], 1e-37))
    message = jnp.concatenate([decay, second[:R] * first[R:] + second[R:]], 0).astype(bf16)
    forward = [chip_shift(message, k) for k in range(1, chips)]

    gl, da = call(
        da_kernel, "da", blocks,
        [rm(clamp), whole(to_pm), whole(down_weight)],
        [rows_of(width, bf16), rows_of(feed, bf16)],
        [],
        (cotangent, to_pm, down_weight),
        scalars=False,
    )

    r1, y, hp, n2, act, dp, dm, dr1, dh, back, mg = call(
        functools.partial(core_kernel, fchunk=256, hops=hops, blocks=blocks), "core", blocks,
        [
            rm(clamp), whole(to_pm), tok(width), tok(feed), tok(hidden), tok(hidden, later), tok(hidden),
            tok(hidden, later), tok(hidden, before), whole(other),
            *[whole(f) for f in forward], whole(out_weight), whole(gain2), whole(up_weight),
        ],
        [
            rows_of(width, f32, kept=pltpu.HBM), rows_of(hidden, bf16), rows_of(hidden, bf16),
            rows_of(width, bf16), rows_of(feed, bf16), rows_of(feed, bf16), rows_of(width, bf16),
            rows_of(width, f32, kept=pltpu.HBM),
            rows_of(hidden, bf16),
            (shape((R, hidden)), fixed((R, hidden))), (shape((R, width)), fixed((R, width))),
        ],
        [
            pltpu.VMEM((R, hidden), f32),
            pltpu.VMEM((R, hidden), jnp.int32),
            pltpu.VMEM((R, hidden), f32),
            pltpu.VMEM((m, width), f32),
            pltpu.VMEM((m, hidden), bf16),
            pltpu.VMEM((m, hidden), bf16),
            pltpu.VMEM((m, hidden), bf16),
        ],
        (
            scal, inputs, to_pm, gl, da, zl, zl, kh, kh, zl, other, *forward, far(out_weight), gain2, up_weight,
        ),
    )

    order = Sequence(back)
    quarter = feed // 4

    def ffn_grads(pick, *beside):
        half = lambda s: s[1] if pick == 0 else 1 - s[1]
        a, d, *beside = order.after(act, dp, *beside)
        (piece,) = call(
            functools.partial(ffn_grad_kernel, pick=pick), "ffn_grad", 2,
            [
                pl.BlockSpec((tokens, quarter), lambda i, s: (0, half(s) * 2 + i)), whole(gl),
                pl.BlockSpec((tokens, width // 2), lambda i, s: (0, half(s))),
                pl.BlockSpec((tokens, feed // 2), lambda i, s: (0, i)),
            ],
            [(shape((SLOTS // 2 * PIECE1, width), bf16), fixed((SLOTS // 2 * PIECE1, width)))],
            [],
            (scal, a, gl, n2, d),
            much=pick == 0,
        )
        return order.did(piece), beside

    def gate_grads(pick):
        half = lambda s: s[1] if pick == 0 else 1 - s[1]
        z, h = order.after(dkz, dkh)
        (piece,) = call(
            functools.partial(gate_grad_kernel, pick=pick), "gate_grad", 1,
            [
                pl.BlockSpec((tokens, width // 2), lambda i, s: (0, half(s))),
                whole(z), whole(h),
                pl.BlockSpec((tokens, hidden // 2), lambda i, s: (0, half(s))), whole(dm),
            ],
            [(shape((SLOTS // 2 * PIECE2, width), bf16), fixed((SLOTS // 2 * PIECE2, width)))],
            [],
            (scal, c, z, h, y, dm),
            much=pick == 0,
            mib=12,
        )
        return order.did(piece)

    fother = flat_permute(back, core_pairs())
    lower = jnp.where(core == 0, back, fother)
    upper = jnp.where(core == 0, fother, back)
    message = jnp.concatenate([decay, lower + first[:R] * upper], 0).astype(bf16)
    backward = [chip_shift(order.did(message), -k) for k in range(1, chips)]
    send1, _ = ffn_grads(1)
    chunk1 = Halving(order, send1)
    chunk1.keep, backward = ffn_grads(0, *backward)
    chunk1.step()

    dkz, dkh, edge_dc, bias_part = call(
        functools.partial(gate_kernel, blocks=blocks, hops=hops), "gates", blocks,
        [
            rtok(hidden), rtok(hidden), rtok(hidden), rtok(hidden),
            whole(other), whole(fother), *[whole(f) for f in backward],
            whole(gate_weight), whole(cand_weight), ORDER,
        ],
        [
            rows_of(hidden, bf16, rtok), rows_of(hidden, bf16, rtok),
            (shape((4 * R, width), bf16), fixed((4 * R, width))),
            (shape((R, hidden)), fixed((R, hidden))),
        ],
        [pltpu.VMEM((R, hidden), f32)],
        (
            scal, dh, zl, kh, hp, other, fother, *backward, gate_weight, cand_weight, order.token,
        ),
    )
    order.did(bias_part)
    after = passed_along(edge_dc[: margin * R], "seq", -1)
    send2 = gate_grads(1)
    chunk2 = Halving(order, send2)
    (output,) = call(
        output_kernel, "output", blocks,
        [tok(width), tok(feed), whole(to_rm), whole(down_weight)],
        [(shape((rows, span, width), bf16), rm(clamp))],
        [],
        (far(r1), order.after(act), to_rm, down_weight),
        scalars=False,
        mib=12,
    )
    order.did(output)
    chunk1.step()
    chunk2.keep = gate_grads(0)
    (after,) = chunk2.step(after)
    input_grad, sums = call(
        functools.partial(tail_kernel, blocks=blocks), "tail", 2 * blocks,
        [
            rm(late), tok(width, late), tok(hidden), tok(hidden), whole(to_pm), whole(to_rm),
            whole(edge), whole(after), whole(gain1), whole(conv_weight), whole(gate_weight),
            whole(cand_weight),
        ],
        [
            (shape((rows, span, width), bf16), rm(late)),
            (shape(((taps + 1) * R, width)), fixed(((taps + 1) * R, width))),
        ],
        [
            pltpu.VMEM((margin * R + m, width), f32),
            pltpu.VMEM((margin * R + tokens, width), f32),
        ],
        (
            far(inputs), far(dr1), order.after(dkz), dkh, far(to_pm), far(to_rm), edge, after,
            far(gain1), far(conv_weight), far(gate_weight), far(cand_weight),
        ),
        scalars=False,
        mib=12,
    )
    order.did(sums)
    small = jnp.concatenate(
        [
            sums.reshape(taps + 1, R, width).sum(1),
            mg.sum(0, keepdims=True),
            bias_part.sum(0).reshape(hidden // width, width),
        ],
        0,
    )

    plan1 = ((0, feed // SLOTS, 1), (1, width // SLOTS, feed // width))
    shapes1 = ((feed, width), (width, feed))
    plan2 = (
        (0, width // SLOTS, hidden // width),
        (1, width // SLOTS, hidden // width),
        (2, hidden // SLOTS, 1),
    )
    shapes2 = ((width, hidden), (width, hidden), (hidden, width))
    held1, held2 = (), ()

    def spread1(src, mate, flip):
        nonlocal held1
        src = order.after(src)
        held1 = spread(scal, src, held1, mate, flip, PIECE1, plan1, shapes1, "spread_ffn")
        order.did(held1[0])

    def spread2(src, mate, flip):
        nonlocal held2
        src = order.after(src)
        held2 = spread(scal, src, held2, mate, flip, PIECE2, plan2, shapes2, "spread_gates")
        order.did(held2[0])

    chunk2.ride = small
    for chunk in (chunk1, chunk2, chunk1, chunk2, chunk1, chunk2, chunk1, chunk2):
        chunk.step()
    chunk2.step()
    chunk1.step()
    chunk2.step()
    chunk1.step()
    chunk2.step()
    spread1(chunk1.total, 0, 0)
    spread1(chunk1.theirs, 1, 0)
    chunk1.step()
    spread1(chunk1.rest, 0, 1)
    spread2(chunk2.total, 0, 0)
    spread1(chunk1.their_rest, 1, 1)
    spread2(chunk2.theirs, 1, 0)
    chunk2.step()
    spread2(chunk2.rest, 0, 1)
    chunk2.their_rest = order.after(chunk2.their_rest)
    *held2, norm_sum, conv_sum, mlp_sum, bias_sum = last_spread(
        scal, chunk2, held2, PIECE2, plan2, shapes2, taps, hidden
    )
    return (
        output,
        input_grad,
        norm_sum.reshape(width),
        conv_sum,
        held2[0],
        bias_sum.reshape(hidden),
        held2[1],
        held2[2],
        mlp_sum.reshape(width),
        held1[1],
        held1[0],
    )


def solution(mesh):
    sharded = P("row", "seq", None)
    in_specs = (sharded, P("row")) + (P(),) * 9 + (sharded,)
    out_specs = (sharded, sharded) + (P(),) * 9
    return jax.shard_map(
        per_device, mesh=mesh, in_specs=in_specs, out_specs=out_specs, check_vma=False
    )
```

```python
import functools

import jax
import jax.numpy as jnp
import numpy as np
from jax import lax
from jax.experimental import pallas as pl
from jax.experimental.pallas import tpu as pltpu
from jax.sharding import PartitionSpec as P

epsilon = 1e-06
f32 = jnp.float32
bf16 = jnp.bfloat16
R = 8
PERM = 256
SCALARS = 4
SLOTS = 32
PIECE1 = 128
PIECE2 = 96


def nn(a, b):
    return lax.dot_general(a, b, (((1,), (0,)), ((), ())), preferred_element_type=f32)


def nt(a, b):
    return lax.dot_general(a, b, (((1,), (1,)), ((), ())), preferred_element_type=f32)


def tn(a, b):
    return lax.dot_general(a, b, (((0,), (0,)), ((), ())), preferred_element_type=f32)


def token_order():
    out = np.arange(PERM)
    source = (out % R) * (PERM // R) + out // R
    to_pm = np.zeros((PERM, PERM), np.float32)
    to_pm[out, source] = 1
    return jnp.asarray(to_pm, bf16), jnp.asarray(to_pm.T, bf16)


def position_major(perm, block):
    span = PERM // R
    parts = []
    for s in range(block.shape[1] // span):
        part = block[:, s * span : (s + 1) * span, :].reshape(PERM, block.shape[2])
        parts.append(nn(perm, part))
    return parts[0] if len(parts) == 1 else jnp.concatenate(parts, 0)


def row_major(perm, tokens):
    span = PERM // R
    parts = []
    for s in range(tokens.shape[0] // PERM):
        part = nn(perm, tokens[s * PERM : (s + 1) * PERM]).astype(bf16)
        parts.append(part.reshape(R, span, tokens.shape[1]))
    return parts[0] if len(parts) == 1 else jnp.concatenate(parts, 1)


def eight(t):
    return pl.ds(pl.multiple_of(t * R, R), R)


def sixteen(t):
    return pl.ds(pl.multiple_of(t * 2 * R, 2 * R), 2 * R)


def normed_edge(edge, gain):
    e = edge.astype(f32)
    inv = lax.rsqrt(jnp.mean(e * e, -1, keepdims=True) + epsilon)
    return (e * inv * gain).astype(bf16).astype(f32)


def set_limits(scal, limit):
    row = lax.broadcasted_iota(jnp.int32, limit.shape, 0)
    value = jnp.zeros(limit.shape, jnp.int32)
    for r in range(R):
        value = jnp.where(row == r, scal[SCALARS + r], value)
    limit[...] = value


def halves(ref, pair):
    both = ref[sixteen(pair), :].astype(f32)
    return both[:R], both[R:]


def norm_kernel(x, perm, gain, u_out):
    xp = position_major(perm[...], x[...])
    inv = lax.rsqrt(jnp.mean(xp * xp, -1, keepdims=True) + epsilon)
    u_out[...] = (xp * inv * gain[...]).astype(bf16)


def front_kernel(scal, u, edge, gain, convw, wg, bias, wc, c_out, zl_out, kh_out, ends, ext, state, limit):
    step = pl.program_id(0)
    m = u.shape[0]
    tb = m // R
    halo = edge.shape[0]
    taps = convw.shape[0]

    @pl.when(step == 0)
    def _():
        set_limits(scal, limit)
        ext[0:halo, :] = normed_edge(edge[...], gain[...])
        state[0:R, :] = jnp.ones((R, state.shape[1]), f32)
        state[R:, :] = jnp.zeros((R, state.shape[1]), f32)

    ext[halo:, :] = u[...].astype(f32)
    conv = convw[0:1, :] * ext[halo:, :]
    for k in range(1, taps):
        lo = halo - k * R
        conv = conv + convw[k : k + 1, :] * ext[lo : lo + m, :]
    ext[0:halo, :] = ext[m : m + halo, :]
    cb = conv.astype(bf16)
    c_out[...] = cb
    kz = nn(cb, wg[...]) + bias[...]
    zs = 1.0 / (1.0 + jnp.exp(-kz))
    width = zs.shape[1]
    zs = zs.reshape(tb, R, width)
    pos = scal[0] + step * tb + lax.broadcasted_iota(jnp.int32, (tb, R, width), 0)
    zl_out[...] = jnp.where(pos < limit[...][None], zs, 0.0).reshape(m, width).astype(bf16)
    kh_out[...] = nn(cb, wc[...]).astype(bf16)

    def body(u, carry):
        prod, h = carry
        za, zb = halves(zl_out, u)
        ka, kb = halves(kh_out, u)
        a = 1.0 - za
        b = 1.0 - zb
        return prod * (a * b), (h * a + za * ka) * b + zb * kb

    prod, h = lax.fori_loop(0, tb // 2, body, (state[0:R, :], state[R:, :]), unroll=4)
    state[0:R, :] = prod
    state[R:, :] = h
    ends[0:R, :] = prod
    ends[R:, :] = h


def gelu_parts(p):
    k0 = 0.7978845608028654
    inner = p * (k0 + (k0 * 0.044715) * (p * p))
    th = jnp.tanh(inner)
    ht = 0.5 + 0.5 * th
    return p * ht, ht + (1.0 - th * th) * (1.5 * inner - k0 * p)


def da_kernel(g, perm, wd, gl_out, da_out):
    gl = position_major(perm[...], g[...]).astype(bf16)
    gl_out[...] = gl
    da_out[...] = nt(gl, wd[...]).astype(bf16)


def core_kernel(scal, x, perm, gl, da, zl, zl_next, kh, kh_next, zl_before, other, *refs, fchunk, hops, blocks):
    msgs = refs[:hops]
    wo, mgain, wu = refs[hops : hops + 3]
    r1_out, y_out, hp_out, n2_out, act_out, dp_out, dm_out, dr1_out, dh_out, back, mg = refs[hops + 3 : hops + 14]
    state, limit, run, acc, ys, hps, dhs = refs[hops + 14 :]
    step = pl.program_id(0)
    tb = x.shape[1]
    m = tb * R
    width, feed = wu.shape
    hidden = wo.shape[0]
    first = scal[0] + step * tb

    def scan_pair(zs, ks, start, u, h):
        t = u * 2
        za, zb = halves(zs, u)
        ka, kb = halves(ks, u)
        ha = h - za * h + za * ka
        hb = ha - zb * ha + zb * kb
        hps[sixteen(u), :] = jnp.concatenate([h, ha], 0).astype(bf16)
        ya = jnp.where(start + t < limit[...], ha, 0.0)
        yb = jnp.where(start + t + 1 < limit[...], hb, 0.0)
        ys[sixteen(u), :] = jnp.concatenate([ya, yb], 0).astype(bf16)
        return hb

    def adjoint_pair(zs, ds, u, prod, total):
        za, zb = halves(zs, u)
        da, db = halves(ds, u)
        pa = prod - za * prod
        pb = pa - zb * pa
        return pb, total + (pa * da + pb * db)

    @pl.when(step == 0)
    def _():
        set_limits(scal, limit)
        h = jnp.zeros((R, hidden), f32)
        for msg in reversed(msgs):
            both = msg[...].astype(f32)
            h = jnp.exp(both[0:R, :]) * h + both[R:, :]
        h = jnp.where(scal[1] == 1, other[0:R, :] * h + other[R:, :], h)
        run[...] = jnp.ones((R, hidden), f32)
        back[...] = jnp.zeros(back.shape, f32)
        mg[...] = jnp.zeros(mg.shape, f32)
        dhs[...] = jnp.zeros(dhs.shape, bf16)
        state[...] = lax.fori_loop(0, tb // 2, lambda u, h: scan_pair(zl, kh, scal[0], u, h), h, unroll=2)

    hp_out[...] = hps[...]
    y = ys[...]
    y_out[...] = y
    r1 = position_major(perm[...], x[...]) + nn(y, wo[...])
    r1_out[...] = r1
    inv = lax.rsqrt(jnp.mean(r1 * r1, -1, keepdims=True) + epsilon)
    n2 = (r1 * inv * mgain[...]).astype(bf16)
    n2_out[...] = n2
    chunks = feed // fchunk
    pairs = tb // 2 // chunks
    for f in range(chunks):
        cols = slice(f * fchunk, (f + 1) * fchunk)
        a, slope = gelu_parts(nn(n2, wu[:, cols]).astype(bf16))
        act_out[:, cols] = a
        dpb = da[:, cols] * slope
        dp_out[:, cols] = dpb
        part = nt(dpb, wu[:, cols])
        acc[...] = acc[...] + part if f else part
        h, prod, total = state[...], run[...], back[...]
        for u in range(f * pairs, (f + 1) * pairs):
            h = scan_pair(zl_next, kh_next, first + tb, u, h)
            prod, total = adjoint_pair(zl_before, dhs, u, prod, total)
        state[...] = h
        run[...] = jnp.where(step == 0, 1.0, prod)
        back[...] = total
    dn2 = acc[...]
    r1 = r1_out[...]
    mg[...] += jnp.sum((dn2 * r1 * inv).reshape(tb, R, width), 0)
    s = mgain[...] * dn2
    mean = jnp.mean(s * r1, -1, keepdims=True)
    dr1 = gl[...].astype(f32) + inv * (s - r1 * (inv * inv * mean))
    dr1_out[...] = dr1
    dm = dr1.astype(bf16)
    dm_out[...] = dm
    dh = nt(dm, wo[...]).reshape(tb, R, hidden)
    pos = first + lax.broadcasted_iota(jnp.int32, (tb, R, hidden), 0)
    dh = jnp.where(pos < limit[...][None], dh, 0.0).reshape(m, hidden).astype(bf16)
    dh_out[...] = dh
    dhs[...] = dh

    @pl.when(step == blocks - 1)
    def _():
        carry = lax.fori_loop(
            0, tb // 2, lambda u, carry: adjoint_pair(zl, dhs, u, *carry), (run[...], back[...]), unroll=4
        )
        back[...] = carry[1]


def put_rows(dst, sel, piece, at, rows, part):
    for i in range(SLOTS // 2):
        pos = pl.multiple_of((i ^ sel) * piece + at, 16)
        dst[pl.ds(pos, rows), :] = part[i * rows : (i + 1) * rows]


def ffn_grad_kernel(scal, act, gl, n2, dp, dst, *, pick):
    step = pl.program_id(0)
    sel = scal[2 + pick]
    width = gl.shape[1]
    rows1 = act.shape[1] * 4 // SLOTS
    rows2 = n2.shape[1] * 2 // SLOTS
    part = tn(act[...], gl[...]).astype(bf16)
    per = act.shape[1] // rows1
    for i in range(per):
        pos = ((step * per + i) ^ sel) * PIECE1
        dst[pl.ds(pl.multiple_of(pos, 16), rows1), :] = part[i * rows1 : (i + 1) * rows1]
    columns = dp.shape[1] // width
    for q in range(columns):
        part = tn(n2[...], dp[:, q * width : (q + 1) * width]).astype(bf16)
        put_rows(dst, sel, PIECE1, rows1 + (step * columns + q) * rows2, rows2, part)


def gate_grad_kernel(scal, c, dkz, dkh, y, dm, dst, *, pick):
    sel = scal[2 + pick]
    width = dm.shape[1]
    rows = c.shape[1] * 2 // SLOTS
    at = 0
    for grads in (dkz, dkh):
        for q in range(grads.shape[1] // width):
            part = tn(c[...], grads[:, q * width : (q + 1) * width]).astype(bf16)
            put_rows(dst, sel, PIECE2, at, rows, part)
            at += rows
    put_rows(dst, sel, PIECE2, at, y.shape[1] * 2 // SLOTS, tn(y[...], dm[...]).astype(bf16))


def gate_kernel(scal, dh, zl, kh, hp, other, fother, *refs, blocks, hops):
    msgs = refs[:hops]
    wg, wc = refs[hops : hops + 2]
    dkz, dkh, edge_out, bias_out = refs[hops + 3 : hops + 7]
    state = refs[hops + 7]
    step = pl.program_id(0)
    m = dh.shape[0]
    tb = m // R
    block = blocks - 1 - step

    @pl.when(step == 0)
    def _():
        mm = jnp.zeros(state.shape, f32)
        for msg in reversed(msgs):
            both = msg[...].astype(f32)
            mm = jnp.exp(both[0:R, :]) * mm + both[R:, :]
        state[...] = jnp.where(scal[1] == 0, fother[...] + other[0:R, :] * mm, mm)
        bias_out[...] = jnp.zeros(bias_out.shape, f32)

    def body(u, carry):
        mm, bias = carry
        w = tb // 2 - 1 - u
        ha, hb = halves(hp, w)
        za, zb = halves(zl, w)
        da, db = halves(dh, w)
        ka, kb = halves(kh, w)
        lam = db + mm
        sb = lam * zb
        mm = lam - sb
        kb = (sb - sb * zb) * (kb - hb)
        lam = da + mm
        sa = lam * za
        mm = lam - sa
        ka = (sa - sa * za) * (ka - ha)
        kk = jnp.concatenate([ka, kb], 0).astype(bf16)
        dkz[sixteen(w), :] = kk
        dkh[sixteen(w), :] = jnp.concatenate([sa, sb], 0).astype(bf16)
        kf = kk.astype(f32)
        return mm, bias + kf[:R, :] + kf[R:, :]

    mm, bias = lax.fori_loop(0, tb // 2, body, (state[...], bias_out[...]), unroll=2)
    state[...] = mm
    bias_out[...] = bias

    @pl.when(block == 0)
    def _():
        span = edge_out.shape[0]
        edge_out[...] = (nt(dkz[0:span, :], wg[...]) + nt(dkh[0:span, :], wc[...])).astype(bf16)


def tail_kernel(x, dr1, dkz, dkh, pm, back_pm, edge, after, gain, convw, wg, wc, grad, sums, uext, dext, *, blocks):
    step = pl.program_id(0)
    tb = x.shape[1]
    m = tb * R
    halo = edge.shape[0]
    taps = convw.shape[0]
    width = gain.shape[1]

    @pl.when(step == 0)
    def _():
        uext[0:halo, :] = normed_edge(edge[...], gain[...])
        dext[blocks * m :, :] = after[...].astype(f32)
        sums[...] = jnp.zeros(sums.shape, f32)

    @pl.when(step < blocks)
    def _():
        rows = pl.ds(pl.multiple_of(step * m, m), m)
        dext[rows, :] = nt(dkz[...], wg[...]) + nt(dkh[...], wc[...])

    @pl.when(step >= blocks)
    def _():
        xp = position_major(pm[...], x[...])
        inv = lax.rsqrt(jnp.mean(xp * xp, -1, keepdims=True) + epsilon)
        xn = xp * inv
        uext[halo:, :] = (xn * gain[...]).astype(bf16).astype(f32)
        start = (step - blocks) * m
        here = dext[pl.ds(pl.multiple_of(start, R), m), :]
        du = convw[0:1, :] * here
        for k in range(taps):
            lo = halo - k * R
            part = (here * uext[lo : lo + m, :]).reshape(tb, R, width)
            sums[(k + 1) * R : (k + 2) * R, :] += jnp.sum(part, 0)
            if k:
                du = du + convw[k : k + 1, :] * dext[pl.ds(pl.multiple_of(start + k * R, R), m), :]
        uext[0:halo, :] = uext[m : m + halo, :]
        sums[0:R, :] += jnp.sum((du * xn).reshape(tb, R, width), 0)
        s1 = gain[...] * du
        mean = jnp.mean(s1 * xn, -1, keepdims=True)
        gin = dr1[...] + inv * (s1 - xn * mean)
        grad[...] = row_major(back_pm[...], gin.astype(bf16))


def output_kernel(r1, act, perm, wd, out):
    total = r1[...] + nn(act[...], wd[...])
    out[...] = row_major(perm[...], total.astype(bf16))


def spread_kernel(scal, src, *refs, piece, plan, mate):
    low = scal[2 + mate] & 7
    for a in range(8):
        base = (a ^ low) * piece
        at = 0
        for out, rows, columns in plan:
            ref = refs[len(refs) - len(plan) + out]
            for q in range(columns):
                width = src.shape[1]
                part = src[pl.ds(pl.multiple_of(base + at, 16), rows), :].astype(f32)
                ref[a * rows : (a + 1) * rows, q * width : (q + 1) * width] = part
                at += rows


def last_spread_kernel(scal, src, ride, rest, theirs, *refs, piece, plan, taps):
    norm, conv, mlp, bias = refs[-4:]
    spread_kernel(scal, src, *refs[:-4], piece=piece, plan=plan, mate=1)
    tail = src.shape[0] - 2 * R
    total = ride[...]
    for rows in (rest[...], theirs[...], src[tail:, :]):
        both = rows.astype(f32)
        total = total + (both[:R] + both[R:])
    norm[...] = total[0:1]
    conv[...] = total[1 : taps + 1]
    mlp[...] = total[taps + 1 : taps + 2]
    width = total.shape[1]
    for i in range(bias.shape[1] // width):
        bias[:, i * width : (i + 1) * width] = total[taps + 2 + i : taps + 3 + i]


def last_spread(scal, chunk, held, piece, plan, shapes, taps, hidden):
    src = chunk.their_rest
    width = src.shape[1]
    rows = 2 * R
    tail = pl.BlockSpec((rows, width), lambda g, s: (src.shape[0] // rows - 1, 0))
    small = ((1, width), (taps, width), (1, width), (1, hidden))

    def block(g, s):
        return ((s[1] ^ 1) * 2 + ((s[3] >> 3) ^ 1), 0)

    return pl.pallas_call(
        functools.partial(last_spread_kernel, piece=piece, plan=plan, taps=taps),
        grid_spec=pltpu.PrefetchScalarGridSpec(
            num_scalar_prefetch=1,
            grid=(1,),
            in_specs=[whole(src), whole(chunk.ride), tail, tail] + [ORDER] * len(held),
            out_specs=[pl.BlockSpec((dims[0] // 4, dims[1]), block) for dims in shapes]
            + [pl.BlockSpec(dims, lambda g, s: (0, 0)) for dims in small],
        ),
        out_shape=[pltpu.HBM(dims, f32) for dims in shapes] + [shape(dims) for dims in small],
        input_output_aliases={5 + k: k for k in range(len(held))},
        compiler_params=params(16),
        cost_estimate=SOME,
        name="spread_last",
    )(scal, src, chunk.ride, chunk.rest, chunk.theirs, *held)


def spread(scal, src, held, mate, flip, piece, plan, shapes, name):
    def block(g, s):
        return ((s[1] ^ mate) * 2 + ((s[2 + mate] >> 3) ^ flip), 0)

    count = len(held)
    return pl.pallas_call(
        functools.partial(spread_kernel, piece=piece, plan=plan, mate=mate),
        grid_spec=pltpu.PrefetchScalarGridSpec(
            num_scalar_prefetch=1,
            grid=(1,),
            in_specs=[whole(src)] + [ORDER] * count,
            out_specs=[pl.BlockSpec((dims[0] // 4, dims[1]), block) for dims in shapes],
        ),
        out_shape=[pltpu.HBM(dims, f32) for dims in shapes],
        input_output_aliases={2 + k: k for k in range(count)},
        compiler_params=params(16),
        cost_estimate=SOME,
        name=name,
    )(scal, src, *held)


def params(mib):
    return pltpu.CompilerParams(
        dimension_semantics=("arbitrary",), vmem_limit_bytes=mib * 1024 * 1024
    )


def shape(dims, kind=f32):
    return jax.ShapeDtypeStruct(dims, kind)


LITTLE = pl.CostEstimate(flops=1024, bytes_accessed=1024, transcendentals=0)
MUCH = pl.CostEstimate(flops=3 * 10**10, bytes_accessed=1024, transcendentals=0)
SOME = pl.CostEstimate(flops=10**10, bytes_accessed=1024, transcendentals=0)
ORDER = pl.BlockSpec(memory_space=pl.ANY)


def far(array):
    return pltpu.with_memory_space_constraint(array, pltpu.HBM)


def whole(array):
    zeros = (0,) * array.ndim
    return pl.BlockSpec(array.shape, lambda *a: zeros, pipeline_mode=pl.Buffered(1))


def passed_along(value, axis, steps):
    count = lax.axis_size(axis)
    leading, last = (max(0, -steps), min(count, count - steps))
    return lax.ppermute(value, axis, [(source, source + steps) for source in range(leading, last)])


def flat_permute(value, pairs):
    return lax.ppermute(value, ("seq", "row"), pairs)


def stage_bits():
    row_bits = lax.axis_size("row").bit_length() - 1
    seq_bits = lax.axis_size("seq").bit_length() - 1
    plane = list(range(row_bits))
    line = [row_bits + 1 + z for z in range(seq_bits - 1)]
    cut = row_bits // 2
    return (plane + line, plane[cut:] + plane[:cut] + line[::-1])


def slot_of(flat, bits):
    slot = 0
    for k in range(4):
        slot = slot * 2 + ((flat >> bits[k]) & 1)
    return slot


def halving_pairs(stage):
    row_bits = lax.axis_size("row").bit_length() - 1
    orders = stage_bits()
    devices = lax.axis_size("row") * lax.axis_size("seq")
    return [(d, d ^ (1 << orders[(d >> row_bits) & 1][stage])) for d in range(devices)]


def core_pairs():
    row_bits = lax.axis_size("row").bit_length() - 1
    devices = lax.axis_size("row") * lax.axis_size("seq")
    return [(d, d ^ (1 << row_bits)) for d in range(devices)]


def added(a, b):
    return (a.astype(f32) + b.astype(f32)).astype(bf16)


class Sequence:
    def __init__(self, token):
        self.token = token

    def after(self, *arrays):
        *arrays, _ = lax.optimization_barrier((*arrays, self.token))
        return arrays[0] if len(arrays) == 1 else arrays

    def did(self, array):
        self.token = array
        return array


def split(value):
    high = lax.reduce_precision(value, 8, 7)
    return [high.astype(bf16), (value - high).astype(bf16)]


def join_kernel(mine, recv, ride, out, ride_out):
    rows = mine.shape[0] - 2 * R
    out[0:rows, :] = mine[0:rows, :]
    out[rows : 2 * rows, :] = recv[0:rows, :]
    parts = recv[rows:, :].astype(f32)
    total = ride[...] + (parts[:R] + parts[R:])
    ride_out[...] = total
    high = total.astype(bf16).astype(f32)
    out[2 * rows :, :] = jnp.concatenate([high, total - high], 0).astype(bf16)


def chain_kernel(mine, recv, out):
    rows = mine.shape[0]
    out[0:rows, :] = mine[...]
    out[rows:, :] = recv[...]


def chained(mine, recv):
    rows, width = mine.shape
    return pl.pallas_call(
        chain_kernel,
        in_specs=[pl.BlockSpec(memory_space=pltpu.VMEM)] * 2,
        out_specs=pl.BlockSpec(memory_space=pltpu.VMEM),
        out_shape=shape((2 * rows, width), bf16),
        compiler_params=pltpu.CompilerParams(vmem_limit_bytes=16 * 1024 * 1024),
        cost_estimate=SOME,
        name="chain",
    )(mine, recv)


def joined(mine, recv, ride, estimate):
    rows, width = mine.shape
    return pl.pallas_call(
        join_kernel,
        in_specs=[pl.BlockSpec(memory_space=pltpu.VMEM)] * 3,
        out_specs=[pl.BlockSpec(memory_space=pltpu.VMEM)] * 2,
        out_shape=[shape((2 * rows - 2 * R, width), bf16), shape(ride.shape)],
        compiler_params=pltpu.CompilerParams(vmem_limit_bytes=16 * 1024 * 1024),
        cost_estimate=estimate,
        name="join",
    )(mine, recv, ride)


class Halving:
    def __init__(self, seq, send):
        self.seq = seq
        self.recv = flat_permute(send, core_pairs())
        self.stage = 0
        self.ride = None

    def riders(self):
        return [] if self.ride is None else split(self.ride)

    def step(self, *beside):
        k = self.stage
        self.stage += 1
        stages = len(stage_bits()[0])
        recv, *beside = self.seq.after(self.recv, *beside) if beside else (self.seq.after(self.recv),)
        if k < 4:
            half = self.keep.shape[0] // 2
            send = self.seq.did(added(self.keep[half:], recv[half:]))
            self.recv = flat_permute(send, halving_pairs(k))
            self.keep = added(self.keep[:half], recv[:half])
        elif k == 4:
            total = added(self.keep, recv)
            for extra in range(4, stages):
                total = added(total, flat_permute(total, halving_pairs(extra)))
                if self.ride is not None:
                    self.ride = self.ride + flat_permute(self.ride, halving_pairs(extra))
            self.rows = total.shape[0]
            self.total = self.seq.did(jnp.concatenate([total] + self.riders(), 0))
            self.recv = flat_permute(self.total, halving_pairs(3))
        elif k < 8:
            rows = self.rows
            self.rows = 2 * rows
            if self.ride is None:
                self.total = self.seq.did(chained(self.total, recv))
            else:
                self.total, self.ride = joined(
                    self.total, recv, self.ride, LITTLE if k == 5 else SOME
                )
                self.seq.did(self.total)
            self.recv = flat_permute(self.total, halving_pairs(7 - k))
            if k == 7:
                self.theirs = flat_permute(self.total, core_pairs())
        else:
            self.rest = recv
            self.their_rest = flat_permute(recv, core_pairs())
        return beside


def chip_shift(value, steps):
    return passed_along(value, "seq", 2 * steps)


def per_device(
    inputs,
    lengths,
    norm_gain,
    conv_weight,
    gate_weight,
    gate_bias,
    cand_weight,
    out_weight,
    mlp_gain,
    up_weight,
    down_weight,
    cotangent,
):
    rows, span, width = inputs.shape
    hidden = gate_weight.shape[1]
    feed = up_weight.shape[1]
    taps = conv_weight.shape[0]
    margin = taps - 1
    tokens = rows * span
    tb = 32
    blocks = span // tb
    m = tb * R
    seq = lax.axis_index("seq")
    core = seq & 1
    chips = lax.axis_size("seq") // 2
    hops = chips - 1
    flat = seq * lax.axis_size("row") + lax.axis_index("row")
    slots = [slot_of(flat, bits) for bits in stage_bits()]
    here = jnp.where(core == 0, slots[0], slots[1])
    mate = jnp.where(core == 0, slots[1], slots[0])
    scal = jnp.concatenate([jnp.stack([seq * span, core, here, mate]).astype(jnp.int32), lengths])
    gain1 = norm_gain.reshape(1, width)
    gain2 = mlp_gain.reshape(1, width)
    bias = gate_bias.reshape(1, hidden)
    to_pm, to_rm = token_order()

    edge = inputs[:, span - margin :, :].swapaxes(0, 1).reshape(margin * rows, width)
    edge = passed_along(edge, "seq", 1)

    last = blocks - 1
    clamp = lambda i: jnp.minimum(i, last)
    late = lambda i: jnp.maximum(i - blocks, 0)
    later = lambda i: jnp.minimum(i + 1, last)
    before = lambda i: jnp.maximum(i - 1, 0)

    def rm(index):
        return pl.BlockSpec((rows, tb, width), lambda i, *s: (0, index(i), 0))

    def tok(w, index=clamp):
        return pl.BlockSpec((m, w), lambda i, *s: (index(i), 0))

    def rtok(w):
        return tok(w, lambda i: last - clamp(i))

    def fixed(dims):
        zeros = (0,) * len(dims)
        return pl.BlockSpec(dims, lambda i, *s: zeros)

    def call(kernel, name, grid, ins, outs, scratch, operands, scalars=True, much=False, mib=16):
        spec = pltpu.PrefetchScalarGridSpec(
            num_scalar_prefetch=int(scalars),
            grid=(grid,),
            in_specs=ins,
            out_specs=[o[1] for o in outs],
            scratch_shapes=scratch,
        )
        return pl.pallas_call(
            kernel,
            grid_spec=spec,
            out_shape=[o[0] for o in outs],
            compiler_params=params(mib),
            cost_estimate=MUCH if much else LITTLE,
            name=name,
        )(*operands)

    def rows_of(w, kind, spec=tok, kept=shape):
        return kept((tokens, w), kind), spec(w)

    (normed,) = call(
        norm_kernel, "norm", blocks,
        [rm(clamp), whole(to_pm), whole(gain1)],
        [rows_of(width, bf16)],
        [],
        (far(inputs), far(to_pm), far(gain1)),
        scalars=False,
    )
    edge, normed = lax.optimization_barrier((edge, normed))
    c, zl, kh, ends = call(
        front_kernel, "front", blocks,
        [
            tok(width), whole(edge), whole(gain1), whole(conv_weight),
            whole(gate_weight), whole(bias), whole(cand_weight),
        ],
        [
            rows_of(width, bf16), rows_of(hidden, bf16), rows_of(hidden, bf16),
            (shape((2 * R, hidden)), fixed((2 * R, hidden))),
        ],
        [
            pltpu.VMEM((margin * R + m, width), f32),
            pltpu.VMEM((2 * R, hidden), f32),
            pltpu.VMEM((R, hidden), jnp.int32),
        ],
        (
            scal, normed, edge, far(gain1), far(conv_weight), gate_weight, far(bias),
            cand_weight,
        ),
    )

    other = flat_permute(ends, core_pairs())
    first = jnp.where(core == 0, ends, other)
    second = jnp.where(core == 0, other, ends)
    decay = jnp.log(jnp.maximum(ends[:R] * other[:R], 1e-37))
    message = jnp.concatenate([decay, second[:R] * first[R:] + second[R:]], 0).astype(bf16)
    forward = [chip_shift(message, k) for k in range(1, chips)]

    gl, da = call(
        da_kernel, "da", blocks,
        [rm(clamp), whole(to_pm), whole(down_weight)],
        [rows_of(width, bf16), rows_of(feed, bf16)],
        [],
        (cotangent, to_pm, down_weight),
        scalars=False,
    )

    r1, y, hp, n2, act, dp, dm, dr1, dh, back, mg = call(
        functools.partial(core_kernel, fchunk=256, hops=hops, blocks=blocks), "core", blocks,
        [
            rm(clamp), whole(to_pm), tok(width), tok(feed), tok(hidden), tok(hidden, later), tok(hidden),
            tok(hidden, later), tok(hidden, before), whole(other),
            *[whole(f) for f in forward], whole(out_weight), whole(gain2), whole(up_weight),
        ],
        [
            rows_of(width, f32, kept=pltpu.HBM), rows_of(hidden, bf16), rows_of(hidden, bf16),
            rows_of(width, bf16), rows_of(feed, bf16), rows_of(feed, bf16), rows_of(width, bf16),
            rows_of(width, f32, kept=pltpu.HBM),
            rows_of(hidden, bf16),
            (shape((R, hidden)), fixed((R, hidden))), (shape((R, width)), fixed((R, width))),
        ],
        [
            pltpu.VMEM((R, hidden), f32),
            pltpu.VMEM((R, hidden), jnp.int32),
            pltpu.VMEM((R, hidden), f32),
            pltpu.VMEM((m, width), f32),
            pltpu.VMEM((m, hidden), bf16),
            pltpu.VMEM((m, hidden), bf16),
            pltpu.VMEM((m, hidden), bf16),
        ],
        (
            scal, inputs, to_pm, gl, da, zl, zl, kh, kh, zl, other, *forward, far(out_weight), gain2, up_weight,
        ),
    )

    order = Sequence(back)
    quarter = feed // 4

    def ffn_grads(pick, *beside):
        half = lambda s: s[1] if pick == 0 else 1 - s[1]
        a, d, *beside = order.after(act, dp, *beside)
        (piece,) = call(
            functools.partial(ffn_grad_kernel, pick=pick), "ffn_grad", 2,
            [
                pl.BlockSpec((tokens, quarter), lambda i, s: (0, half(s) * 2 + i)), whole(gl),
                pl.BlockSpec((tokens, width // 2), lambda i, s: (0, half(s))),
                pl.BlockSpec((tokens, feed // 2), lambda i, s: (0, i)),
            ],
            [(shape((SLOTS // 2 * PIECE1, width), bf16), fixed((SLOTS // 2 * PIECE1, width)))],
            [],
            (scal, a, gl, n2, d),
            much=pick == 0,
        )
        return order.did(piece), beside

    def gate_grads(pick):
        half = lambda s: s[1] if pick == 0 else 1 - s[1]
        z, h = order.after(dkz, dkh)
        (piece,) = call(
            functools.partial(gate_grad_kernel, pick=pick), "gate_grad", 1,
            [
                pl.BlockSpec((tokens, width // 2), lambda i, s: (0, half(s))),
                whole(z), whole(h),
                pl.BlockSpec((tokens, hidden // 2), lambda i, s: (0, half(s))), whole(dm),
            ],
            [(shape((SLOTS // 2 * PIECE2, width), bf16), fixed((SLOTS // 2 * PIECE2, width)))],
            [],
            (scal, c, z, h, y, dm),
            much=pick == 0,
            mib=12,
        )
        return order.did(piece)

    fother = flat_permute(back, core_pairs())
    lower = jnp.where(core == 0, back, fother)
    upper = jnp.where(core == 0, fother, back)
    message = jnp.concatenate([decay, lower + first[:R] * upper], 0).astype(bf16)
    backward = [chip_shift(order.did(message), -k) for k in range(1, chips)]
    send1, _ = ffn_grads(1)
    chunk1 = Halving(order, send1)
    chunk1.keep, backward = ffn_grads(0, *backward)
    chunk1.step()

    dkz, dkh, edge_dc, bias_part = call(
        functools.partial(gate_kernel, blocks=blocks, hops=hops), "gates", blocks,
        [
            rtok(hidden), rtok(hidden), rtok(hidden), rtok(hidden),
            whole(other), whole(fother), *[whole(f) for f in backward],
            whole(gate_weight), whole(cand_weight), ORDER,
        ],
        [
            rows_of(hidden, bf16, rtok), rows_of(hidden, bf16, rtok),
            (shape((4 * R, width), bf16), fixed((4 * R, width))),
            (shape((R, hidden)), fixed((R, hidden))),
        ],
        [pltpu.VMEM((R, hidden), f32)],
        (
            scal, dh, zl, kh, hp, other, fother, *backward, gate_weight, cand_weight, order.token,
        ),
    )
    order.did(bias_part)
    after = passed_along(edge_dc[: margin * R], "seq", -1)
    send2 = gate_grads(1)
    chunk2 = Halving(order, send2)
    (output,) = call(
        output_kernel, "output", blocks,
        [tok(width), tok(feed), whole(to_rm), whole(down_weight)],
        [(shape((rows, span, width), bf16), rm(clamp))],
        [],
        (far(r1), order.after(act), to_rm, down_weight),
        scalars=False,
        mib=12,
    )
    order.did(output)
    chunk1.step()
    chunk2.keep = gate_grads(0)
    (after,) = chunk2.step(after)
    input_grad, sums = call(
        functools.partial(tail_kernel, blocks=blocks), "tail", 2 * blocks,
        [
            rm(late), tok(width, late), tok(hidden), tok(hidden), whole(to_pm), whole(to_rm),
            whole(edge), whole(after), whole(gain1), whole(conv_weight), whole(gate_weight),
            whole(cand_weight),
        ],
        [
            (shape((rows, span, width), bf16), rm(late)),
            (shape(((taps + 1) * R, width)), fixed(((taps + 1) * R, width))),
        ],
        [
            pltpu.VMEM((margin * R + m, width), f32),
            pltpu.VMEM((margin * R + tokens, width), f32),
        ],
        (
            far(inputs), far(dr1), far(order.after(dkz)), far(dkh), far(to_pm), far(to_rm), edge, after,
            far(gain1), far(conv_weight), far(gate_weight), far(cand_weight),
        ),
        scalars=False,
        mib=12,
    )
    order.did(sums)
    small = jnp.concatenate(
        [
            sums.reshape(taps + 1, R, width).sum(1),
            mg.sum(0, keepdims=True),
            bias_part.sum(0).reshape(hidden // width, width),
        ],
        0,
    )

    plan1 = ((0, feed // SLOTS, 1), (1, width // SLOTS, feed // width))
    shapes1 = ((feed, width), (width, feed))
    plan2 = (
        (0, width // SLOTS, hidden // width),
        (1, width // SLOTS, hidden // width),
        (2, hidden // SLOTS, 1),
    )
    shapes2 = ((width, hidden), (width, hidden), (hidden, width))
    held1, held2 = (), ()

    def spread1(src, mate, flip):
        nonlocal held1
        src = order.after(src)
        held1 = spread(scal, src, held1, mate, flip, PIECE1, plan1, shapes1, "spread_ffn")
        order.did(held1[0])

    def spread2(src, mate, flip):
        nonlocal held2
        src = order.after(src)
        held2 = spread(scal, src, held2, mate, flip, PIECE2, plan2, shapes2, "spread_gates")
        order.did(held2[0])

    chunk2.ride = small
    for chunk in (chunk1, chunk2, chunk1, chunk2, chunk1, chunk2, chunk1, chunk2):
        chunk.step()
    chunk2.step()
    chunk1.step()
    chunk2.step()
    chunk1.step()
    chunk2.step()
    spread1(chunk1.total, 0, 0)
    spread1(chunk1.theirs, 1, 0)
    chunk1.step()
    spread1(chunk1.rest, 0, 1)
    spread2(chunk2.total, 0, 0)
    spread1(chunk1.their_rest, 1, 1)
    spread2(chunk2.theirs, 1, 0)
    chunk2.step()
    spread2(chunk2.rest, 0, 1)
    chunk2.their_rest = order.after(chunk2.their_rest)
    *held2, norm_sum, conv_sum, mlp_sum, bias_sum = last_spread(
        scal, chunk2, held2, PIECE2, plan2, shapes2, taps, hidden
    )
    return (
        output,
        input_grad,
        norm_sum.reshape(width),
        conv_sum,
        held2[0],
        bias_sum.reshape(hidden),
        held2[1],
        held2[2],
        mlp_sum.reshape(width),
        held1[1],
        held1[0],
    )


def solution(mesh):
    sharded = P("row", "seq", None)
    in_specs = (sharded, P("row")) + (P(),) * 9 + (sharded,)
    out_specs = (sharded, sharded) + (P(),) * 9
    return jax.shard_map(
        per_device, mesh=mesh, in_specs=in_specs, out_specs=out_specs, check_vma=False
    )
```
